32 devices in a mesh: tm: 4 (over z), space: 8 (over y, x, core).
Axes of the slice: x: 2, y: 2, z: 4, core: 2. Of those that a mesh axis runs over, the one named last changes fastest.
Arguments:
- queries: bfloat16 [512, 1024], P('tm', 'space'), may hold values from -150 to 150
- keys: bfloat16 [4096, 1024], P('tm', 'space'), may hold values from -6 to 6
- values: bfloat16 [4096, 1024], P('tm', 'space'), may hold values from -6 to 6
- saved_out: bfloat16 [512, 1024], P('tm', 'space'), may hold values from -6 to 6
- out_grad: bfloat16 [512, 5120], P('tm', 'space'), may hold values from -6 to 6
- proj_weight: bfloat16 [1024, 5120], P('space'), may hold values from -0.1875 to 0.1875
- gate_table: float32 [16, 5120], replicated, may hold values from 0.1 to 1.9
- noise_levels: int32 [8], replicated, may hold values from 0 to 15
- clip_lengths: int32 [4], replicated, may hold values from 1 to 4, 8 in all
Outputs:
- query_grad: bfloat16 [512, 1024], P('tm', 'space')
- key_grad: bfloat16 [4096, 1024], P('tm', 'space')
- value_grad: bfloat16 [4096, 1024], P('tm', 'space')
- weight_grad: float32 [1024, 5120], P('space', 'tm')
- gate_grad: float32 [16, 5120], replicated
The draws below stay inside these ranges and needn't reach their ends.
All inputs are finite; a program needn't handle non-finite values.
Results may differ from the reference program's by a relative error of at most 0.0065.
Values may be sent and summed in bfloat16 or wider, within the bound.
No kernel may reach another device: no remote copies, remote signals or barrier semaphores. Data moves between devices by JAX's collectives and lax.ppermute only.
A program may use at most 64 MiB of HBM per device.

```python
import math
import jax
import jax.numpy as jnp
import numpy as np
from jax import lax

D = 5120
HD = 128
SPF = 512
QF = 64
LEVELS = 16
NCLIPS = 4
HEADS = 8
HW = 1024
FRAMES = 8
QTOT = 512
KTOT = 4096


def base_keys(key):
    return jnp.clip(jax.random.normal(key, (KTOT, HW), jnp.float32), -6.0, 6.0)


def draw_keys(key, part):
    drawn = base_keys(key)
    return drawn.astype(jnp.bfloat16)


def draw_queries(key, part):
    key = jax.random.fold_in(key, 11)
    first = jax.random.fold_in(key, 0)
    drawn = jnp.clip(jax.random.normal(first, (QTOT, HW), jnp.float32), -6.0, 6.0)
    return drawn.astype(jnp.bfloat16)


def place_ends(values, rng, smallest, top_value):
    longest = values.shape.index(max(values.shape))
    spots = []
    for shift in (0, 1):
        where = [jax.random.randint(jax.random.fold_in(rng, axis), (), 0, length) for axis, length in enumerate(values.shape)]
        where[longest] = (where[longest] + shift) % values.shape[longest]
        spots.append(tuple(where))
    return values.at[spots[0]].set(smallest).at[spots[1]].set(top_value)


def levels(own_key, dims, pieces, low, largest):
    def one(dim, shards_of):
        steps = jax.random.uniform(jax.random.fold_in(jax.random.fold_in(own_key, 6), dim), (shards_of,), jnp.float32, low / len(pieces), largest / len(pieces))
        return jnp.repeat(jnp.exp(steps), dims[dim] // shards_of).reshape((-1,) + (1,) * (len(dims) - dim - 1))

    gain = one(*pieces[0])
    for cut in pieces[1:]:
        gain = gain * one(*cut)
    return gain


def profile(count, total, bound, skew):
    loads = [(1 << 20) // math.isqrt(grade ** skew) + 1 for grade in range(2, count + 1)]
    surplus, holding = total - bound - (count - 1), [1] * (count - 1)
    while surplus > 0:
        candidates = [i for i in range(count - 1) if holding[i] < bound]
        mass, left = sum([loads[i] for i in candidates]), surplus
        for i in candidates:
            addition = min(bound - holding[i], max(1, left * loads[i] // mass), surplus)
            holding[i] = holding[i] + addition
            surplus = surplus - addition
    return np.array([bound] + holding)


def ragged_sizes(key, amount, total, reach, lean):
    if amount == 2:
        one = jax.random.randint(key, (), max(1, total - reach), min(reach, total - 1) + 1)
        return jnp.stack([one, total - one])
    sizes = jnp.asarray(profile(amount, total, reach, lean), jnp.int32)
    couples = (amount - 1) // 2
    donor, receiver = sizes[1:1 + 2 * couples:2], sizes[2:2 + 2 * couples:2]
    room = jnp.minimum(donor - 1, reach - receiver)
    moved = jax.random.randint(jax.random.fold_in(key, 1), (couples,), 0, 1 << 20) % (room + 1)
    sizes = sizes.at[1:1 + 2 * couples:2].set(donor - moved).at[2:2 + 2 * couples:2].set(receiver + moved)
    return sizes[jax.random.permutation(jax.random.fold_in(key, 2), amount)]


def gaussian(rng, dims, width, bound, cuts=(), kind=jnp.bfloat16):
    factor_of = levels(rng, dims, cuts, -0.22, 0.18) if cuts else 1.0
    values = jax.random.normal(rng, dims, jnp.float32) * width * factor_of
    return jnp.minimum(jnp.maximum(values, -bound), bound).astype(kind)


def setup_inputs(seed: int = 0) -> dict:
    streams_of = jax.random.split(jax.random.key(seed), 10)
    queries = draw_queries(jax.random.fold_in(streams_of[9], 71), 0)
    keys = draw_keys(jax.random.fold_in(streams_of[9], 71), 0)
    values = gaussian(streams_of[2], (KTOT, HW), 1.0, 6.0, ((0, 4), (1, 8)))
    saved_out = gaussian(streams_of[3], (QTOT, HW), 1.0, 6.0, ((0, 4), (1, 8)))
    out_grad = gaussian(streams_of[4], (QTOT, D), 1.0, 6.0, ((0, 4), (1, 8)))
    proj_weight = gaussian(streams_of[5], (HW, D), HW ** -0.5, 0.1875, ((0, 8),))
    gate_table = jnp.clip(1.0 + 0.18 * jax.random.normal(streams_of[6], (LEVELS, D), jnp.float32), 0.1, 1.9)
    noise_levels = place_ends(jax.random.randint(streams_of[7], (FRAMES,), 0, LEVELS), jax.random.fold_in(streams_of[7], 1), 0, LEVELS - 1).astype(jnp.int32)
    clip_lengths = ragged_sizes(streams_of[8], NCLIPS, FRAMES, FRAMES // 2, 2).astype(jnp.int32)
    return {"queries": queries, "keys": keys, "values": values, "saved_out": saved_out, "out_grad": out_grad, "proj_weight": proj_weight, "gate_table": gate_table, "noise_levels": noise_levels, "clip_lengths": clip_lengths}


def clip_index(clip_lengths, frame_ids):
    bounds = jnp.cumsum(clip_lengths)
    return lax.optimization_barrier(jnp.sum((frame_ids[:, None] >= bounds[None, :]).astype(jnp.int32), axis=1))

def reference(queries, keys, values, saved_out, out_grad, proj_weight, gate_table, noise_levels, clip_lengths):
    scale = 1.0 / math.sqrt(HD)
    frame_ids = jnp.arange(FRAMES, dtype=jnp.int32)
    clip_of = clip_index(clip_lengths, frame_ids)
    query_frame = jnp.arange(QTOT, dtype=jnp.int32) // QF
    key_frame = jnp.arange(KTOT, dtype=jnp.int32) // SPF
    level_rows = noise_levels[query_frame]
    gate_rows = gate_table[level_rows]
    grad_wide = out_grad.astype(jnp.float32)
    gated = (gate_rows * grad_wide).astype(jnp.bfloat16)
    head_grad = jnp.dot(gated, proj_weight.T, preferred_element_type=jnp.float32).astype(jnp.bfloat16)
    weight_grad = jnp.dot(saved_out.T, gated, preferred_element_type=jnp.float32)
    mixed = jnp.dot(saved_out, proj_weight, preferred_element_type=jnp.float32)
    level_hot = (level_rows[:, None] == jnp.arange(LEVELS, dtype=jnp.int32)[None, :]).astype(jnp.float32)
    gate_grad = jnp.dot(level_hot.T, grad_wide * mixed, precision=lax.Precision.HIGHEST)
    visible = (key_frame[None, :] >= query_frame[:, None]) & (clip_of[key_frame][None, :] == clip_of[query_frame][:, None])

    def split_heads(matrix, rows):
        return matrix.reshape(rows, HEADS, HD).transpose(1, 0, 2)

    def one_head(args):
        q_head, k_head, v_head, o_head, g_head = args
        scores = jnp.dot(q_head, k_head.T, preferred_element_type=jnp.float32) * scale
        masked = jnp.where(visible, scores, -1e+30)
        top = lax.optimization_barrier(jnp.max(masked, axis=1, keepdims=True))
        total = lax.optimization_barrier(jnp.sum(jnp.where(visible, jnp.exp(masked - top), 0.0), axis=1, keepdims=True))
        lse = top + jnp.log(total)
        probs = jnp.where(visible, jnp.exp(masked - lse), 0.0)
        probs_low = probs.astype(jnp.bfloat16)
        value_part = jnp.dot(probs_low.T, g_head, preferred_element_type=jnp.float32)
        delta = lax.optimization_barrier(jnp.sum(g_head.astype(jnp.float32) * o_head.astype(jnp.float32), axis=1, keepdims=True))
        prob_grad = jnp.dot(g_head, v_head.T, preferred_element_type=jnp.float32)
        score_grad = (probs * (prob_grad - delta)).astype(jnp.bfloat16)
        query_part = jnp.dot(score_grad, k_head, preferred_element_type=jnp.float32) * scale
        key_part = jnp.dot(score_grad.T, q_head, preferred_element_type=jnp.float32) * scale
        return (query_part.astype(jnp.bfloat16), key_part.astype(jnp.bfloat16), value_part.astype(jnp.bfloat16))
    query_h, key_h, value_h = lax.map(one_head, (split_heads(queries, QTOT), split_heads(keys, KTOT), split_heads(values, KTOT), split_heads(saved_out, QTOT), split_heads(head_grad, QTOT)))
    query_grad = query_h.transpose(1, 0, 2).reshape(QTOT, HW)
    key_grad = key_h.transpose(1, 0, 2).reshape(KTOT, HW)
    value_grad = value_h.transpose(1, 0, 2).reshape(KTOT, HW)
    return (query_grad, key_grad, value_grad, weight_grad, gate_grad)
```

```python
import functools
import math

import jax
import jax.numpy as jnp
from jax import lax
from jax.experimental import pallas as pl
from jax.experimental.pallas import tpu as pltpu
from jax.sharding import PartitionSpec as P

HD = 128
SPF = 512
QF = 64
NEG_BIG = -1e30
SCALE = 1.0 / math.sqrt(HD)
VMEM_LIMIT = 48 * 1024 * 1024


def dot(a, b, on_a, on_b):
    return lax.dot_general(
        a, b, (((on_a,), (on_b,)), ((), ())), preferred_element_type=jnp.float32
    )


def take_columns(ref, shard, width):
    if len(ref.shape) == 3:
        return ref[shard]
    return ref[:, pl.ds(pl.multiple_of(shard * width, 128), width)]


def gate_row(gate_ref, shard, width, level):
    if len(gate_ref.shape) == 3:
        return gate_ref[shard, pl.ds(level, 1), :]
    return gate_ref[pl.ds(level, 1), pl.ds(pl.multiple_of(shard * width, 128), width)]


def gate_rows(piece, levels_ref, gate_ref, owner, shard, frames):
    wide = piece.astype(jnp.float32)
    rows = []
    for r in range(frames):
        row = gate_row(gate_ref, shard, piece.shape[1], levels_ref[owner * frames + r])
        rows.append((wide[r * QF : (r + 1) * QF] * row).astype(jnp.bfloat16))
    return wide, jnp.concatenate(rows, axis=0)


def head_kernel(n_s, frames, levels_ref, saved_ref, w_ref, gate_ref, *refs):
    pieces, (head_ref, terms_ref) = refs[:n_s], refs[n_s:]
    t, s = lax.axis_index("tm"), lax.axis_index("space")
    width = pieces[0].shape[1]
    saved = saved_ref[...]
    head = jnp.zeros(head_ref.shape, jnp.float32)
    for j in range(n_s):
        shard = s ^ j
        weight = take_columns(w_ref, shard, width)
        wide, gated = gate_rows(pieces[j][...], levels_ref, gate_ref, t, shard, frames)
        head = head + dot(gated, weight, 1, 1)
        product = wide * dot(saved, weight, 1, 0)
        for r in range(frames):
            term = jnp.sum(product[r * QF : (r + 1) * QF], axis=0, keepdims=True)
            if len(terms_ref.shape) == 3:
                terms_ref[shard, r : r + 1, :] = term
            else:
                terms_ref[r : r + 1, pl.ds(pl.multiple_of(shard * width, 128), width)] = term
    head_ref[...] = head.astype(jnp.bfloat16)


def heads_sum_kernel(n_s, *refs):
    pieces, out_ref, held = refs[:n_s], refs[n_s], refs[n_s + 1]
    s = lax.axis_index("space")
    for j in range(n_s):
        held[s ^ j] = pieces[j][...]
    total = held[0]
    for j in range(1, n_s):
        total = total + held[j]
    out_ref[...] = total


def levels_kernel(n_t, frames, levels_ref, *refs):
    pieces, out_ref, held = refs[:n_t], refs[n_t], refs[n_t + 1]
    t = lax.axis_index("tm")
    for k in range(n_t):
        held[t ^ k] = pieces[k][...]
    spot = lax.broadcasted_iota(jnp.int32, out_ref.shape, len(out_ref.shape) - 2)
    total = jnp.zeros(out_ref.shape, jnp.float32)
    for f in range(n_t * frames):
        r = f % frames
        row = held[f // frames, ..., r : r + 1, :]
        total = total + jnp.where(spot == levels_ref[f], row, 0.0)
    out_ref[...] = total


def weight_kernel(n_t, frames, levels_ref, gate_ref, *refs):
    n_s = 2 * n_t
    saved_refs, pieces = refs[:n_t], refs[n_t : n_t + n_s]
    out_ref, held = refs[n_t + n_s], refs[n_t + n_s + 1]
    t, s = lax.axis_index("tm"), lax.axis_index("space")
    chip, core = s // 2, s % 2
    width = pieces[0].shape[1]
    for k in range(n_t):
        held[k] = saved_refs[k][...]
    saved = jnp.concatenate([held[chip ^ k] for k in range(n_t)], axis=0)
    for f in range(2):
        half = core ^ f
        rows = [
            gate_rows(pieces[2 * k + f][...], levels_ref, gate_ref, t ^ chip ^ k, 2 * t + half, frames)[1]
            for k in range(n_t)
        ]
        result = dot(saved, jnp.concatenate(rows, axis=0), 0, 0)
        for h in range(2):

            @pl.when(half == h)
            def _():
                out_ref[:, h * width : (h + 1) * width] = result


def clip_numbers(clips_ref):
    bounds = []
    so_far = 0
    for c in range(clips_ref.shape[0]):
        so_far = so_far + clips_ref[c]
        bounds.append(so_far)
    return lambda frame: sum((frame >= bound).astype(jnp.int32) for bound in bounds)


def bias_row(clip_of, t, k, key_frame, frames, rows):
    lane = lax.broadcasted_iota(jnp.int32, (1, rows), 1)
    row = jnp.full((1, rows), NEG_BIG, jnp.float32)
    for r in range(frames):
        frame = (t ^ k) * frames + r
        visible = (key_frame >= frame) & (clip_of(key_frame) == clip_of(frame))
        value = jnp.where(visible, 0.0, NEG_BIG).astype(jnp.float32)
        row = jnp.where((lane >= r * QF) & (lane < (r + 1) * QF), value, row)
    return row


def stats_kernel(n_t, frames, clips_ref, keys_ref, *refs):
    queries, stats_ref = refs[:n_t], refs[n_t]
    t = lax.axis_index("tm")
    clip_of = clip_numbers(clips_ref)
    rows = queries[0].shape[0]
    for p in range(0, n_t, 2):
        q = jnp.concatenate([queries[p][...], queries[p + 1][...]], axis=0)
        scores = []
        for kf in range(frames):
            bias = jnp.concatenate(
                [bias_row(clip_of, t, k, t * frames + kf, frames, rows) for k in (p, p + 1)], axis=1
            )
            scores.append(dot(keys_ref[kf * SPF : (kf + 1) * SPF, :], q, 1, 1) * SCALE + bias)
        top = functools.reduce(jnp.maximum, [jnp.max(x, axis=0, keepdims=True) for x in scores])
        total = sum(jnp.sum(jnp.exp(x - top), axis=0, keepdims=True) for x in scores)
        stats_ref[0:1, p * rows : (p + 2) * rows] = top
        stats_ref[1:2, p * rows : (p + 2) * rows] = total


def grads_kernel(n_t, frames, clips_ref, keys_ref, values_ref, *refs):
    queries, grads, saved, stats = (refs[i * n_t : (i + 1) * n_t] for i in range(4))
    key_ref, value_ref = refs[4 * n_t : 4 * n_t + 2]
    query_refs = refs[4 * n_t + 2 : 5 * n_t + 2]
    key_acc, value_acc = refs[5 * n_t + 2 :]
    t = lax.axis_index("tm")
    clip_of = clip_numbers(clips_ref)
    rows = queries[0].shape[0]
    ones = jnp.ones((8, HD), jnp.float32)
    keys_t = jnp.transpose(keys_ref[...])
    for p in range(0, n_t, 2):
        q = jnp.concatenate([queries[p][...], queries[p + 1][...]], axis=0)
        g = jnp.concatenate([grads[p][...], grads[p + 1][...]], axis=0)
        o = jnp.concatenate([saved[p][...], saved[p + 1][...]], axis=0)
        delta = lax.dot_general(
            ones,
            g.astype(jnp.float32) * o.astype(jnp.float32),
            (((1,), (1,)), ((), ())),
            precision=lax.Precision.HIGHEST,
            preferred_element_type=jnp.float32,
        )[0:1]
        lse = []
        for i in (p, p + 1):
            tops = [stats[k][0:1, (i ^ k) * rows : ((i ^ k) + 1) * rows] for k in range(n_t)]
            sums = [stats[k][1:2, (i ^ k) * rows : ((i ^ k) + 1) * rows] for k in range(n_t)]
            top = functools.reduce(jnp.maximum, tops)
            lse.append(top + jnp.log(sum(b * jnp.exp(a - top) for a, b in zip(tops, sums))))
        lse = jnp.concatenate(lse, axis=1)
        query_part = None
        for kf in range(frames):
            span = slice(kf * SPF, (kf + 1) * SPF)
            bias = jnp.concatenate(
                [bias_row(clip_of, t, k, t * frames + kf, frames, rows) for k in (p, p + 1)], axis=1
            )
            probs = jnp.exp(dot(keys_ref[span, :], q, 1, 1) * SCALE + (bias - lse))
            score_grad = (probs * (dot(values_ref[span, :], g, 1, 1) - delta)).astype(jnp.bfloat16)
            value_add = dot(probs.astype(jnp.bfloat16), g, 1, 0)
            key_add = dot(score_grad, q, 1, 0)
            if p > 0:
                value_add = value_add + value_acc[span, :]
                key_add = key_add + key_acc[span, :]
            if p + 2 < n_t:
                value_acc[span, :] = value_add
                key_acc[span, :] = key_add
            else:
                value_ref[span, :] = value_add.astype(jnp.bfloat16)
                key_ref[span, :] = (key_add * SCALE).astype(jnp.bfloat16)
            part = dot(keys_t[:, span], score_grad, 1, 0)
            query_part = part if query_part is None else query_part + part
        query_refs[p][...] = query_part[:, :rows]
        query_refs[p + 1][...] = query_part[:, rows:]


def query_kernel(n_t, *refs):
    total = refs[0][...]
    for k in range(1, n_t):
        total = total + refs[k][...]
    refs[n_t][...] = jnp.transpose(total * SCALE).astype(jnp.bfloat16)


def call(kernel, in_smem, args, out_shape, scratch=(), flops=0):
    whole = pl.BlockSpec(memory_space=pltpu.VMEM)
    single = not isinstance(out_shape, (list, tuple))
    nbytes = sum(a.size * a.dtype.itemsize for a in args)
    return pl.pallas_call(
        kernel,
        out_shape=out_shape,
        in_specs=[pl.BlockSpec(memory_space=pltpu.SMEM)] * in_smem + [whole] * (len(args) - in_smem),
        out_specs=whole if single else [whole] * len(out_shape),
        scratch_shapes=list(scratch),
        compiler_params=pltpu.CompilerParams(vmem_limit_bytes=VMEM_LIMIT),
        cost_estimate=pl.CostEstimate(flops=flops, bytes_accessed=nbytes, transcendentals=0),
    )(*args)


def body(
    queries, keys, values, saved_out, out_grad, proj_weight, gate_table, noise_levels, clip_lengths
):
    n_t, n_s = lax.axis_size("tm"), lax.axis_size("space")
    chips = n_s // 2
    rows, width = out_grad.shape
    k_rows = keys.shape[0]
    frames = rows // QF
    levels, columns = gate_table.shape
    shape = jax.ShapeDtypeStruct

    def over_chips(x, k):
        return lax.ppermute(x, "space", [(s, s ^ (2 * k)) for s in range(n_s)])

    def over_cores(x):
        return lax.ppermute(x, "space", [(s, s ^ 1) for s in range(n_s)])

    def over_time(x, k, up_only=False, down_only=False):
        pairs = [(t, t ^ k) for t in range(n_t)]
        if up_only:
            pairs = [(a, b) for a, b in pairs if a < b]
        if down_only:
            pairs = [(a, b) for a, b in pairs if a > b]
        return lax.ppermute(x, "tm", pairs)

    def plane_gather(x):
        same_core = [x] + [over_chips(x, k) for k in range(1, chips)]
        return [y for piece in same_core for y in (piece, over_cores(piece))]

    pieces = plane_gather(out_grad)
    queries_all = [queries] + [over_time(queries, k, up_only=True) for k in range(1, n_t)]
    saved_all = [saved_out] + [over_time(saved_out, k) for k in range(1, n_t)]
    moves = [
        (t * n_s + 2 * c + e, c * n_s + 2 * (c ^ t) + e)
        for t in range(n_t)
        for c in range(chips)
        for e in range(2)
    ]
    moved = lax.ppermute(out_grad, ("tm", "space"), moves)
    row_pieces = plane_gather(moved)

    cut = width % 128 != 0
    w_table, g_table = proj_weight, gate_table
    if cut:
        w_table = proj_weight.reshape(HD, n_s, width).transpose(1, 0, 2)
        g_table = gate_table.reshape(levels, n_s, width).transpose(1, 0, 2)
    terms_shape = (n_s, frames, width) if cut else (frames, columns)

    stats = call(
        functools.partial(stats_kernel, n_t, frames),
        1,
        [clip_lengths, keys] + queries_all,
        shape((2, n_t * rows), jnp.float32),
        flops=2 * n_t * rows * k_rows * HD,
    )
    stats_all = [stats] + [over_time(stats, k) for k in range(1, n_t)]

    head_grad, terms = call(
        functools.partial(head_kernel, n_s, frames),
        1,
        [noise_levels, saved_out, w_table, g_table] + pieces,
        [shape((rows, HD), jnp.bfloat16), shape(terms_shape, jnp.float32)],
        flops=4 * rows * columns * HD,
    )
    grads_all = [head_grad] + [over_time(head_grad, k, up_only=True) for k in range(1, n_t)]
    terms_all = [terms] + [
        lax.ppermute(terms, "space", [(s, s ^ j) for s in range(n_s)]) for j in range(1, n_s)
    ]
    terms_sum = call(
        functools.partial(heads_sum_kernel, n_s),
        0,
        terms_all,
        shape(terms_shape, jnp.float32),
        [pltpu.VMEM((n_s,) + terms_shape, jnp.float32)],
    )
    sums_all = [terms_sum] + [over_time(terms_sum, k) for k in range(1, n_t)]

    outs = call(
        functools.partial(grads_kernel, n_t, frames),
        1,
        [clip_lengths, keys, values] + queries_all + grads_all + saved_all + stats_all,
        [shape((k_rows, HD), jnp.bfloat16)] * 2 + [shape((HD, rows), jnp.float32)] * n_t,
        [pltpu.VMEM((k_rows, HD), jnp.float32)] * 2,
        flops=10 * n_t * rows * k_rows * HD,
    )
    key_grad, value_grad, query_parts = outs[0], outs[1], outs[2:]
    query_terms = [query_parts[0]] + [
        over_time(query_parts[k], k, down_only=True) for k in range(1, n_t)
    ]

    weight_grad = call(
        functools.partial(weight_kernel, n_t, frames),
        1,
        [noise_levels, g_table] + saved_all + row_pieces,
        shape((HD, 2 * width), jnp.float32),
        [pltpu.VMEM((n_t, rows, HD), jnp.bfloat16)],
        flops=4 * n_t * rows * width * HD,
    )
    gate_grad = call(
        functools.partial(levels_kernel, n_t, frames),
        1,
        [noise_levels] + sums_all,
        shape((n_s, levels, width) if cut else (levels, columns), jnp.float32),
        [pltpu.VMEM((n_t,) + terms_shape, jnp.float32)],
    )
    if cut:
        gate_grad = gate_grad.transpose(1, 0, 2).reshape(levels, columns)
    query_grad = call(
        functools.partial(query_kernel, n_t),
        0,
        query_terms,
        shape((rows, HD), jnp.bfloat16),
    )
    return (query_grad, key_grad, value_grad, weight_grad, gate_grad)


def solution(mesh):
    return jax.shard_map(
        body,
        mesh=mesh,
        in_specs=(
            P("tm", "space"),
            P("tm", "space"),
            P("tm", "space"),
            P("tm", "space"),
            P("tm", "space"),
            P("space", None),
            P(),
            P(),
            P(),
        ),
        out_specs=(P("tm", "space"), P("tm", "space"), P("tm", "space"), P("space", "tm"), P()),
        check_vma=False,
    )
```

```python
import functools
import math

import jax
import jax.numpy as jnp
from jax import lax
from jax.experimental import pallas as pl
from jax.experimental.pallas import tpu as pltpu
from jax.sharding import PartitionSpec as P

HD = 128
SPF = 512
QF = 64
NEG_BIG = -1e30
SCALE = 1.0 / math.sqrt(HD)
VMEM_LIMIT = 48 * 1024 * 1024


def dot(a, b, on_a, on_b):
    return lax.dot_general(
        a, b, (((on_a,), (on_b,)), ((), ())), preferred_element_type=jnp.float32
    )


def take_columns(ref, shard, width):
    if len(ref.shape) == 3:
        return ref[shard]
    return ref[:, pl.ds(pl.multiple_of(shard * width, 128), width)]


def gate_row(gate_ref, shard, width, level):
    if len(gate_ref.shape) == 3:
        return gate_ref[shard, pl.ds(level, 1), :]
    return gate_ref[pl.ds(level, 1), pl.ds(pl.multiple_of(shard * width, 128), width)]


def gate_rows(piece, levels_ref, gate_ref, owner, shard, frames):
    wide = piece.astype(jnp.float32)
    rows = []
    for r in range(frames):
        row = gate_row(gate_ref, shard, piece.shape[1], levels_ref[owner * frames + r])
        rows.append((wide[r * QF : (r + 1) * QF] * row).astype(jnp.bfloat16))
    return wide, jnp.concatenate(rows, axis=0)


def pack_kernel(queries_ref, saved_ref, out_ref):
    for i in range(out_ref.shape[0]):
        out_ref[i, 0] = queries_ref[...]
        out_ref[i, 1] = saved_ref[...]


def head_kernel(n_s, frames, levels_ref, saved_ref, w_ref, gate_ref, *refs):
    pieces, (head_out, terms_out, terms_ref) = refs[:n_s], refs[n_s:]
    t, s = lax.axis_index("tm"), lax.axis_index("space")
    width = pieces[0].shape[1]
    saved = saved_ref[...]
    head = jnp.zeros(head_out.shape[1:], jnp.float32)
    for j in range(n_s):
        shard = s ^ j
        weight = take_columns(w_ref, shard, width)
        wide, gated = gate_rows(pieces[j][...], levels_ref, gate_ref, t, shard, frames)
        head = head + dot(gated, weight, 1, 1)
        product = wide * dot(saved, weight, 1, 0)
        for r in range(frames):
            term = jnp.sum(product[r * QF : (r + 1) * QF], axis=0, keepdims=True)
            if len(terms_ref.shape) == 3:
                terms_ref[shard, r : r + 1, :] = term
            else:
                terms_ref[r : r + 1, pl.ds(pl.multiple_of(shard * width, 128), width)] = term
    for i in range(head_out.shape[0]):
        head_out[i] = head.astype(jnp.bfloat16)
    for i in range(n_s):
        terms_out[i] = terms_ref[...]


def heads_sum_kernel(terms_ref, out_ref):
    total = terms_ref[0]
    for j in range(1, terms_ref.shape[0]):
        total = total + terms_ref[j]
    for i in range(out_ref.shape[0]):
        out_ref[i] = total


def levels_kernel(n_t, frames, levels_ref, held, out_ref):
    spot = lax.broadcasted_iota(jnp.int32, out_ref.shape, len(out_ref.shape) - 2)
    total = jnp.zeros(out_ref.shape, jnp.float32)
    for f in range(n_t * frames):
        r = f % frames
        row = held[f // frames, ..., r : r + 1, :]
        total = total + jnp.where(spot == levels_ref[f], row, 0.0)
    out_ref[...] = total


def weight_kernel(n_t, frames, levels_ref, gate_ref, packed_ref, *refs):
    n_s = 2 * n_t
    pieces, out_ref = refs[:n_s], refs[n_s]
    t, s = lax.axis_index("tm"), lax.axis_index("space")
    chip, core = s // 2, s % 2
    width = pieces[0].shape[1]
    saved = jnp.concatenate([packed_ref[t ^ chip ^ k, 1] for k in range(n_t)], axis=0)
    for f in range(2):
        half = core ^ f
        rows = [
            gate_rows(pieces[2 * k + f][...], levels_ref, gate_ref, t ^ chip ^ k, 2 * t + half, frames)[1]
            for k in range(n_t)
        ]
        result = dot(saved, jnp.concatenate(rows, axis=0), 0, 0)
        for h in range(2):

            @pl.when(half == h)
            def _():
                out_ref[:, h * width : (h + 1) * width] = result


def clip_numbers(clips_ref):
    bounds = []
    so_far = 0
    for c in range(clips_ref.shape[0]):
        so_far = so_far + clips_ref[c]
        bounds.append(so_far)
    return lambda frame: sum((frame >= bound).astype(jnp.int32) for bound in bounds)


def bias_row(clip_of, owner, key_frame, frames, rows):
    lane = lax.broadcasted_iota(jnp.int32, (1, rows), 1)
    row = jnp.full((1, rows), NEG_BIG, jnp.float32)
    for r in range(frames):
        frame = owner * frames + r
        visible = (key_frame >= frame) & (clip_of(key_frame) == clip_of(frame))
        value = jnp.where(visible, 0.0, NEG_BIG).astype(jnp.float32)
        row = jnp.where((lane >= r * QF) & (lane < (r + 1) * QF), value, row)
    return row


def stats_kernel(n_t, frames, clips_ref, keys_ref, packed_ref, stats_ref):
    t = lax.axis_index("tm")
    clip_of = clip_numbers(clips_ref)
    rows = packed_ref.shape[2]
    for p in range(0, n_t, 2):
        q = jnp.concatenate([packed_ref[p, 0], packed_ref[p + 1, 0]], axis=0)
        scores = []
        for kf in range(frames):
            bias = jnp.concatenate(
                [bias_row(clip_of, k, t * frames + kf, frames, rows) for k in (p, p + 1)], axis=1
            )
            scores.append(dot(keys_ref[kf * SPF : (kf + 1) * SPF, :], q, 1, 1) * SCALE + bias)
        top = functools.reduce(jnp.maximum, [jnp.max(x, axis=0, keepdims=True) for x in scores])
        total = sum(jnp.sum(jnp.exp(x - top), axis=0, keepdims=True) for x in scores)
        for i in range(n_t):
            stats_ref[i, 0:1, p * rows : (p + 2) * rows] = top
            stats_ref[i, 1:2, p * rows : (p + 2) * rows] = total


def grads_kernel(
    n_t, frames, clips_ref, keys_ref, values_ref, packed_ref, grads_ref, stats_ref,
    key_ref, value_ref, query_ref, key_acc, value_acc,
):
    t = lax.axis_index("tm")
    clip_of = clip_numbers(clips_ref)
    rows = packed_ref.shape[2]
    ones = jnp.ones((8, HD), jnp.float32)
    keys_t = jnp.transpose(keys_ref[...])
    for p in range(0, n_t, 2):
        q = jnp.concatenate([packed_ref[p, 0], packed_ref[p + 1, 0]], axis=0)
        g = jnp.concatenate([grads_ref[p], grads_ref[p + 1]], axis=0)
        o = jnp.concatenate([packed_ref[p, 1], packed_ref[p + 1, 1]], axis=0)
        delta = lax.dot_general(
            ones,
            g.astype(jnp.float32) * o.astype(jnp.float32),
            (((1,), (1,)), ((), ())),
            precision=lax.Precision.HIGHEST,
            preferred_element_type=jnp.float32,
        )[0:1]
        span = slice(p * rows, (p + 2) * rows)
        tops = [stats_ref[i, 0:1, span] for i in range(n_t)]
        sums = [stats_ref[i, 1:2, span] for i in range(n_t)]
        top = functools.reduce(jnp.maximum, tops)
        lse = top + jnp.log(sum(b * jnp.exp(a - top) for a, b in zip(tops, sums)))
        query_part = None
        for kf in range(frames):
            span = slice(kf * SPF, (kf + 1) * SPF)
            bias = jnp.concatenate(
                [bias_row(clip_of, k, t * frames + kf, frames, rows) for k in (p, p + 1)], axis=1
            )
            probs = jnp.exp(dot(keys_ref[span, :], q, 1, 1) * SCALE + (bias - lse))
            score_grad = (probs * (dot(values_ref[span, :], g, 1, 1) - delta)).astype(jnp.bfloat16)
            value_add = dot(probs.astype(jnp.bfloat16), g, 1, 0)
            key_add = dot(score_grad, q, 1, 0)
            if p > 0:
                value_add = value_add + value_acc[span, :]
                key_add = key_add + key_acc[span, :]
            if p + 2 < n_t:
                value_acc[span, :] = value_add
                key_acc[span, :] = key_add
            else:
                value_ref[span, :] = value_add.astype(jnp.bfloat16)
                key_ref[span, :] = (key_add * SCALE).astype(jnp.bfloat16)
            part = dot(keys_t[:, span], score_grad, 1, 0)
            query_part = part if query_part is None else query_part + part
        query_ref[p] = query_part[:, :rows]
        query_ref[p + 1] = query_part[:, rows:]


def query_kernel(parts_ref, out_ref):
    total = parts_ref[0]
    for k in range(1, parts_ref.shape[0]):
        total = total + parts_ref[k]
    out_ref[...] = jnp.transpose(total * SCALE).astype(jnp.bfloat16)


def call(kernel, in_smem, args, out_shape, scratch=(), flops=0):
    whole = pl.BlockSpec(memory_space=pltpu.VMEM)
    single = not isinstance(out_shape, (list, tuple))
    nbytes = sum(a.size * a.dtype.itemsize for a in args)
    return pl.pallas_call(
        kernel,
        out_shape=out_shape,
        in_specs=[pl.BlockSpec(memory_space=pltpu.SMEM)] * in_smem + [whole] * (len(args) - in_smem),
        out_specs=whole if single else [whole] * len(out_shape),
        scratch_shapes=list(scratch),
        compiler_params=pltpu.CompilerParams(vmem_limit_bytes=VMEM_LIMIT),
        cost_estimate=pl.CostEstimate(flops=flops, bytes_accessed=nbytes, transcendentals=0),
    )(*args)


def body(
    queries, keys, values, saved_out, out_grad, proj_weight, gate_table, noise_levels, clip_lengths
):
    n_t, n_s = lax.axis_size("tm"), lax.axis_size("space")
    chips = n_s // 2
    rows, width = out_grad.shape
    k_rows = keys.shape[0]
    frames = rows // QF
    levels, columns = gate_table.shape
    shape = jax.ShapeDtypeStruct

    def over_chips(x, k):
        return lax.ppermute(x, "space", [(s, s ^ (2 * k)) for s in range(n_s)])

    def over_cores(x):
        return lax.ppermute(x, "space", [(s, s ^ 1) for s in range(n_s)])

    def swap(x, axis):
        return lax.all_to_all(x, axis, 0, 0)

    def plane_gather(x):
        same_core = [x] + [over_chips(x, k) for k in range(1, chips)]
        return [y for piece in same_core for y in (piece, over_cores(piece))]

    pieces = plane_gather(out_grad)
    packed = swap(
        call(pack_kernel, 0, [queries, saved_out], shape((n_t, 2, rows, HD), jnp.bfloat16)), "tm"
    )
    moves = [
        (t * n_s + 2 * c + e, c * n_s + 2 * (c ^ t) + e)
        for t in range(n_t)
        for c in range(chips)
        for e in range(2)
    ]
    moved = lax.ppermute(out_grad, ("tm", "space"), moves)
    row_pieces = plane_gather(moved)

    cut = width % 128 != 0
    w_table, g_table = proj_weight, gate_table
    if cut:
        w_table = proj_weight.reshape(HD, n_s, width).transpose(1, 0, 2)
        g_table = gate_table.reshape(levels, n_s, width).transpose(1, 0, 2)
    terms_shape = (n_s, frames, width) if cut else (frames, columns)

    stats = call(
        functools.partial(stats_kernel, n_t, frames),
        1,
        [clip_lengths, keys, packed],
        shape((n_t, 2, n_t * rows), jnp.float32),
        flops=2 * n_t * rows * k_rows * HD,
    )
    stats = swap(stats, "tm")

    head_grad, terms = call(
        functools.partial(head_kernel, n_s, frames),
        1,
        [noise_levels, saved_out, w_table, g_table] + pieces,
        [shape((n_t, rows, HD), jnp.bfloat16), shape((n_s,) + terms_shape, jnp.float32)],
        [pltpu.VMEM(terms_shape, jnp.float32)],
        flops=4 * rows * columns * HD,
    )
    grads_all = swap(head_grad, "tm")
    terms_sum = call(
        heads_sum_kernel, 0, [swap(terms, "space")], shape((n_t,) + terms_shape, jnp.float32)
    )
    terms_sum = swap(terms_sum, "tm")

    key_grad, value_grad, query_parts = call(
        functools.partial(grads_kernel, n_t, frames),
        1,
        [clip_lengths, keys, values, packed, grads_all, stats],
        [shape((k_rows, HD), jnp.bfloat16)] * 2 + [shape((n_t, HD, rows), jnp.float32)],
        [pltpu.VMEM((k_rows, HD), jnp.float32)] * 2,
        flops=10 * n_t * rows * k_rows * HD,
    )
    query_parts = swap(query_parts, "tm")

    weight_grad = call(
        functools.partial(weight_kernel, n_t, frames),
        1,
        [noise_levels, g_table, packed] + row_pieces,
        shape((HD, 2 * width), jnp.float32),
        flops=4 * n_t * rows * width * HD,
    )
    gate_grad = call(
        functools.partial(levels_kernel, n_t, frames),
        1,
        [noise_levels, terms_sum],
        shape((n_s, levels, width) if cut else (levels, columns), jnp.float32),
    )
    if cut:
        gate_grad = gate_grad.transpose(1, 0, 2).reshape(levels, columns)
    query_grad = call(query_kernel, 0, [query_parts], shape((rows, HD), jnp.bfloat16))
    return (query_grad, key_grad, value_grad, weight_grad, gate_grad)


def solution(mesh):
    return jax.shard_map(
        body,
        mesh=mesh,
        in_specs=(
            P("tm", "space"),
            P("tm", "space"),
            P("tm", "space"),
            P("tm", "space"),
            P("tm", "space"),
            P("space", None),
            P(),
            P(),
            P(),
        ),
        out_specs=(P("tm", "space"), P("tm", "space"), P("tm", "space"), P("space", "tm"), P()),
        check_vma=False,
    )
```

```python
import functools
import math

import jax
import jax.numpy as jnp
from jax import lax
from jax.experimental import pallas as pl
from jax.experimental.pallas import tpu as pltpu
from jax.sharding import PartitionSpec as P

HD = 128
SPF = 512
QF = 64
LANES = 128
NEG_BIG = -1e30
SCALE = 1.0 / math.sqrt(HD)
VMEM_LIMIT = 32 * 1024 * 1024
SPLIT = 3


def dot(a, b, on_a, on_b):
    return lax.dot_general(
        a, b, (((on_a,), (on_b,)), ((), ())), preferred_element_type=jnp.float32
    )


def place():
    s = lax.axis_index("space")
    return lax.axis_index("tm"), s // 2, s % 2


def clip_numbers(clips_ref):
    bounds = []
    so_far = 0
    for c in range(clips_ref.shape[0]):
        so_far = so_far + clips_ref[c]
        bounds.append(so_far)
    return lambda frame: sum((frame >= bound).astype(jnp.int32) for bound in bounds)


def prep_kernel(
    n_t, chips, frames, levels_in, clips_in, queries_in, saved_in, keys_in, values_in, grad_in,
    weight_in, gate_in, packed, kept, sent, keys, values, grad, bias, gate_a, gate_b, hot,
    gate, levels, clips, sems,
):
    t, chip, core = place()
    rows = grad.shape[0]
    width = grad.shape[1]

    def columns(k, c):
        return pl.ds(pl.multiple_of((2 * (chip ^ k) + c) * width, LANES), width)

    moves = [(levels_in, levels), (clips_in, clips), (queries_in, packed.at[0]), (saved_in, packed.at[1])]
    for k in range(chips):
        moves.append((weight_in.at[:, columns(k, 1 - core)], sent.at[:, k * width : (k + 1) * width]))
    moves.append((saved_in, sent.at[:, chips * width : chips * width + HD]))
    moves.append((gate_in, gate))
    moves.append((keys_in, keys))
    for k in range(chips):
        moves.append((weight_in.at[:, columns(k, core)], kept.at[k]))
    moves.append((grad_in, grad))
    moves.append((values_in, values))
    copies = [pltpu.make_async_copy(a, b, sems.at[i]) for i, (a, b) in enumerate(moves)]
    for copy in copies:
        copy.start()
    copies[0].wait()
    copies[1].wait()
    clip_of = clip_numbers(clips)
    lane = lax.broadcasted_iota(jnp.int32, (1, rows), 1)
    for kf in range(frames):
        key_frame = t * frames + kf
        key_clip = clip_of(key_frame)
        for k in range(n_t):
            row = jnp.full((1, rows), NEG_BIG, jnp.float32)
            for r in range(frames):
                frame = (t ^ k) * frames + r
                visible = (key_frame >= frame) & (clip_of(frame) == key_clip)
                value = jnp.where(visible, 0.0, NEG_BIG).astype(jnp.float32)
                row = jnp.where((lane >= r * QF) & (lane < (r + 1) * QF), value, row)
            bias[kf : kf + 1, k * rows : (k + 1) * rows] = row
    spot = lax.broadcasted_iota(jnp.int32, hot.shape[1:], 0)
    for f in range(n_t * frames):
        hot[f] = (spot == levels[f]).astype(jnp.float32)
    for copy in copies[2:]:
        copy.wait()
    for r in range(frames):
        level = levels[t * frames + r]
        for k in range(chips):
            gate_a[k, r : r + 1, :] = gate[pl.ds(level, 1), columns(k, core)]
        for k in range(n_t):
            level = levels[(t ^ chip ^ k) * frames + r]
            mine = pl.ds(pl.multiple_of((2 * t + core) * width, LANES), width)
            gate_b[k, r : r + 1, :] = gate[pl.ds(level, 1), mine]


def stats_kernel(n_t, bias, keys, *refs):
    packed, out = refs[:n_t], refs[n_t]
    rows = packed[0].shape[1]
    for p in range(0, n_t, 2):
        q = jnp.concatenate([packed[p][0], packed[p + 1][0]], axis=0)
        scores = []
        for kf in range(bias.shape[0]):
            mask = bias[kf : kf + 1, p * rows : (p + 2) * rows]
            scores.append(dot(keys[kf * SPF : (kf + 1) * SPF, :], q, 1, 1) * SCALE + mask)
        top = functools.reduce(jnp.maximum, [jnp.max(x, axis=0, keepdims=True) for x in scores])
        total = sum(jnp.sum(jnp.exp(x - top), axis=0, keepdims=True) for x in scores)
        for i in range(2):
            out[p + i : p + i + 1, :] = top[:, i * rows : (i + 1) * rows]
            out[n_t + p + i : n_t + p + i + 1, :] = total[:, i * rows : (i + 1) * rows]


def head_kernel(chips, frames, packed, kept, received, gate_a, *refs):
    pieces, (mine, other, terms) = refs[:chips], refs[chips:]
    _, chip, _ = place()
    width = pieces[0].shape[1]
    saved = jnp.concatenate([packed[1], received[:, chips * width : chips * width + HD]], axis=1)
    head = None
    for k in range(chips):
        weight = jnp.concatenate([kept[k], received[:, k * width : (k + 1) * width]], axis=0)
        wide = pieces[k][...].astype(jnp.float32)
        gated = jnp.concatenate(
            [
                (wide[r * QF : (r + 1) * QF] * gate_a[k, r : r + 1, :]).astype(jnp.bfloat16)
                for r in range(frames)
            ],
            axis=0,
        )
        part = dot(gated, weight, 1, 1)
        head = part if head is None else head + part
        product = wide * dot(saved, weight, 1, 0)
        for r in range(frames):
            term = jnp.sum(product[r * QF : (r + 1) * QF], axis=0, keepdims=True)
            terms[chip ^ k, r : r + 1, :] = term
    mine[...] = head[:, :HD]
    other[...] = head[:, HD:]


def join_kernel(mine, received, stats, out):
    rows = mine.shape[0]
    out[:rows, :] = (mine[...] + received[...]).astype(jnp.bfloat16)
    rest = stats[...]
    parts = []
    for _ in range(SPLIT):
        part = rest.astype(jnp.bfloat16).astype(jnp.float32)
        parts.append(part)
        rest = rest - part
    pad = out.shape[0] - rows - SPLIT * rest.shape[0]
    if pad:
        parts.append(jnp.zeros((pad, LANES), jnp.float32))
    out[rows:, :] = jnp.concatenate(parts, axis=0).astype(jnp.bfloat16)


def terms_kernel(chips, *refs):
    pieces, out, held = refs[:chips], refs[chips], refs[chips + 1]
    _, chip, _ = place()
    for k in range(chips):
        held[chip ^ k] = pieces[k][...]
    total = held[0]
    for k in range(1, chips):
        total = total + held[k]
    row = 0
    for a in range(total.shape[0]):
        for r in range(total.shape[1]):
            for j in range(0, total.shape[2], LANES):
                out[row : row + 1, :] = total[a, r : r + 1, j : j + LANES]
                row += 1


def grads_kernel(n_t, bias, keys, values, own_terms, other_terms, *refs):
    packed, heads = refs[:n_t], refs[n_t : 2 * n_t]
    key_out, value_out = refs[2 * n_t : 2 * n_t + 2]
    outs = refs[2 * n_t + 2 : 3 * n_t + 2]
    key_acc, value_acc = refs[3 * n_t + 2 :]
    core = place()[2]
    rows = packed[0].shape[1]
    count = own_terms.shape[0]
    ones = jnp.ones((8, HD), jnp.float32)
    keys_t = jnp.transpose(keys[...])
    stats = []
    for k in range(n_t):
        parts = heads[k][rows:, :].astype(jnp.float32)
        stats.append(sum(parts[i * 2 * n_t : (i + 1) * 2 * n_t] for i in range(SPLIT)))
    own, other = own_terms[...], other_terms[...]
    first, second = jnp.where(core == 0, own, other), jnp.where(core == 0, other, own)
    for k in range(n_t):
        outs[k][rows : rows + count, :] = first
        outs[k][rows + count :, :] = second
    for p in range(0, n_t, 2):
        q = jnp.concatenate([packed[p][0], packed[p + 1][0]], axis=0)
        o = jnp.concatenate([packed[p][1], packed[p + 1][1]], axis=0)
        g = jnp.concatenate([heads[p][:rows, :], heads[p + 1][:rows, :]], axis=0)
        delta = lax.dot_general(
            ones,
            g.astype(jnp.float32) * o.astype(jnp.float32),
            (((1,), (1,)), ((), ())),
            precision=lax.Precision.HIGHEST,
            preferred_element_type=jnp.float32,
        )[0:1]
        lse = []
        for i in (p, p + 1):
            tops = [stats[k][i ^ k : (i ^ k) + 1] for k in range(n_t)]
            sums = [stats[k][n_t + (i ^ k) : n_t + (i ^ k) + 1] for k in range(n_t)]
            top = functools.reduce(jnp.maximum, tops)
            lse.append(top + jnp.log(sum(b * jnp.exp(a - top) for a, b in zip(tops, sums))))
        lse = jnp.concatenate(lse, axis=1)
        query_part = None
        for kf in range(bias.shape[0]):
            span = slice(kf * SPF, (kf + 1) * SPF)
            shift = bias[kf : kf + 1, p * rows : (p + 2) * rows] - lse
            probs = jnp.exp(dot(keys[span, :], q, 1, 1) * SCALE + shift)
            score_grad = (probs * (dot(values[span, :], g, 1, 1) - delta)).astype(jnp.bfloat16)
            value_add = dot(probs.astype(jnp.bfloat16), g, 1, 0)
            key_add = dot(score_grad, q, 1, 0)
            if p > 0:
                value_add = value_add + value_acc[span, :]
                key_add = key_add + key_acc[span, :]
            if p + 2 < n_t:
                value_acc[span, :] = value_add
                key_acc[span, :] = key_add
            else:
                value_out[span, :] = value_add.astype(jnp.bfloat16)
                key_out[span, :] = (key_add * SCALE).astype(jnp.bfloat16)
            part = dot(keys_t[:, span], score_grad, 1, 0)
            query_part = part if query_part is None else query_part + part
        outs[p][:rows, :] = query_part[:, :rows]
        outs[p + 1][:rows, :] = query_part[:, rows:]


def finish_kernel(n_t, chips, frames, hot, *refs):
    parts, (query_out, gate_out, held) = refs[:n_t], refs[n_t:]
    t = lax.axis_index("tm")
    rows = query_out.shape[0]
    total = parts[0][:rows, :]
    for k in range(1, n_t):
        total = total + parts[k][:rows, :]
    query_out[...] = jnp.transpose(total * SCALE).astype(jnp.bfloat16)
    for k in range(n_t):
        held[t ^ k] = parts[k][rows:, :]
    tiles = gate_out.shape[1] // (2 * chips * LANES)
    for core in range(2):
        for a in range(chips):
            for j in range(tiles):
                total = jnp.zeros(hot.shape[1:], jnp.float32)
                for f in range(n_t * frames):
                    row = ((core * chips + a) * frames + f % frames) * tiles + j
                    total = total + hot[f] * held[f // frames, row : row + 1, :]
                column = ((2 * a + core) * tiles + j) * LANES
                gate_out[:, column : column + LANES] = total


def gated_kernel(n_t, frames, gate_b, *refs):
    pieces, out = refs[:n_t], refs[n_t]
    for k in range(n_t):
        for r in range(frames):
            span = slice(r * QF, (r + 1) * QF)
            wide = pieces[k][span, :].astype(jnp.float32)
            out[k, span, :] = (wide * gate_b[k, r : r + 1, :]).astype(jnp.bfloat16)


def weight_kernel(n_t, own, other, *refs):
    packed, out, held = refs[:n_t], refs[n_t], refs[n_t + 1]
    _, chip, core = place()
    width = own.shape[2]
    for k in range(n_t):
        held[k] = packed[k][1]
    saved = jnp.concatenate([held[chip ^ k] for k in range(n_t)], axis=0)
    for ref, half in ((own, core), (other, 1 - core)):
        gated = jnp.concatenate([ref[k] for k in range(n_t)], axis=0)
        result = dot(saved, gated, 0, 0)
        for h in range(2):

            @pl.when(half == h)
            def _():
                out[:, h * width : (h + 1) * width] = result


def call(kernel, args, out_shape, scratch=(), flops=0, in_place=False):
    vmem = pl.BlockSpec(memory_space=pltpu.VMEM)
    single = not isinstance(out_shape, (list, tuple))
    nbytes = sum(a.size * a.dtype.itemsize for a in args)
    return pl.pallas_call(
        kernel,
        out_shape=out_shape,
        in_specs=[pl.BlockSpec(memory_space=pltpu.HBM) if in_place else vmem] * len(args),
        out_specs=vmem if single else [vmem] * len(out_shape),
        scratch_shapes=list(scratch),
        compiler_params=pltpu.CompilerParams(vmem_limit_bytes=VMEM_LIMIT),
        cost_estimate=pl.CostEstimate(flops=flops, bytes_accessed=nbytes, transcendentals=0),
    )(*args)


def padded_shards(table, n_s, width):
    rows, columns = table.shape
    cut = table.reshape(rows, n_s, columns // n_s)
    cut = jnp.pad(cut, ((0, 0), (0, 0), (0, width - columns // n_s)))
    return cut.reshape(rows, n_s * width)


def without_padding(table, shards, shard):
    rows, columns = table.shape
    return table.reshape(rows, shards, columns // shards)[:, :, :shard].reshape(rows, shards * shard)


def body(
    queries, keys, values, saved_out, out_grad, proj_weight, gate_table, noise_levels, clip_lengths
):
    n_t, n_s = lax.axis_size("tm"), lax.axis_size("space")
    chips = n_s // 2
    rows, shard = out_grad.shape
    k_rows = keys.shape[0]
    frames = rows // QF
    levels = gate_table.shape[0]
    bf16, f32 = jnp.bfloat16, jnp.float32
    width = -(-shard // LANES) * LANES
    if width != shard:
        out_grad = jnp.pad(out_grad, ((0, 0), (0, width - shard)))
        proj_weight = padded_shards(proj_weight, n_s, width)
        gate_table = padded_shards(gate_table, n_s, width)

    def shape(dtype, *dims):
        return jax.ShapeDtypeStruct(dims, dtype)

    def over_chips(x):
        return [x] + [
            lax.ppermute(x, "space", [(s, s ^ (2 * k)) for s in range(n_s)]) for k in range(1, chips)
        ]

    def over_cores(x):
        return lax.ppermute(x, "space", [(s, s ^ 1) for s in range(n_s)])

    def over_time(x, k):
        return lax.ppermute(x, "tm", [(t, t ^ k) for t in range(n_t)])

    pieces = over_chips(out_grad)
    moves = [
        (t * n_s + 2 * c + e, c * n_s + 2 * (c ^ t) + e)
        for t in range(n_t)
        for c in range(chips)
        for e in range(2)
    ]
    moved = lax.ppermute(out_grad, ("tm", "space"), moves)
    packed, kept, sent, keys, values, own_grad, bias, gate_a, gate_b, hot = call(
        functools.partial(prep_kernel, n_t, chips, frames),
        [noise_levels, clip_lengths, queries, saved_out, keys, values, out_grad, proj_weight, gate_table],
        [
            shape(bf16, 2, rows, HD),
            shape(bf16, chips, HD, width),
            shape(bf16, HD, chips * width + HD),
            shape(bf16, k_rows, HD),
            shape(bf16, k_rows, HD),
            shape(bf16, rows, width),
            shape(f32, frames, n_t * rows),
            shape(f32, chips, frames, width),
            shape(f32, n_t, frames, width),
            shape(f32, n_t * frames, levels, LANES),
        ],
        [
            pltpu.VMEM((levels, n_s * width), f32),
            pltpu.SMEM(noise_levels.shape, jnp.int32),
            pltpu.SMEM(clip_lengths.shape, jnp.int32),
            pltpu.SemaphoreType.DMA((2 * chips + 9,)),
        ],
        in_place=True,
    )
    received = over_cores(sent)
    packed_all = [packed] + [over_time(packed, k) for k in range(1, n_t)]
    stats = call(
        functools.partial(stats_kernel, n_t),
        [bias, keys] + packed_all,
        shape(f32, 2 * n_t, LANES),
        flops=2 * n_t * rows * k_rows * HD,
    )
    gate_a, _ = lax.optimization_barrier((gate_a, stats))
    mine, other, terms = call(
        functools.partial(head_kernel, chips, frames),
        [packed, kept, received, gate_a, own_grad] + pieces[1:],
        [shape(f32, rows, HD), shape(f32, rows, HD), shape(f32, chips, frames, width)],
        flops=4 * rows * chips * width * 2 * HD,
    )
    extra = -(-SPLIT * 2 * n_t // 16) * 16
    joined = call(join_kernel, [mine, over_cores(other), stats], shape(bf16, rows + extra, HD))
    moved, joined = lax.optimization_barrier((moved, joined))
    row_pieces = over_chips(moved)
    heads_all = [joined] + [over_time(joined, k) for k in range(1, n_t)]

    count = chips * frames * width // LANES
    own_terms = call(
        functools.partial(terms_kernel, chips),
        over_chips(terms),
        shape(f32, count, LANES),
        [pltpu.VMEM((chips, chips, frames, width), f32)],
    )
    outs = call(
        functools.partial(grads_kernel, n_t),
        [bias, keys, values, own_terms, over_cores(own_terms)] + packed_all + heads_all,
        [shape(bf16, k_rows, HD)] * 2 + [shape(f32, rows + 2 * count, LANES)] * n_t,
        [pltpu.VMEM((k_rows, HD), f32)] * 2,
        flops=10 * n_t * rows * k_rows * HD,
    )
    key_grad, value_grad, parts = outs[0], outs[1], outs[2:]
    row_pieces, _ = lax.optimization_barrier((row_pieces, parts[0]))
    parts = [parts[0]] + [over_time(parts[k], k) for k in range(1, n_t)]

    gated = call(
        functools.partial(gated_kernel, n_t, frames),
        [gate_b] + row_pieces,
        shape(bf16, n_t, rows, width),
    )
    weight_grad = call(
        functools.partial(weight_kernel, n_t),
        [gated, over_cores(gated)] + packed_all,
        shape(f32, HD, 2 * width),
        [pltpu.VMEM((n_t, rows, HD), bf16)],
        flops=4 * n_t * rows * width * HD,
    )
    query_grad, gate_grad = call(
        functools.partial(finish_kernel, n_t, chips, frames),
        [hot] + parts,
        [shape(bf16, rows, HD), shape(f32, levels, n_s * width)],
        [pltpu.VMEM((n_t, 2 * count, LANES), f32)],
    )
    if width != shard:
        weight_grad = without_padding(weight_grad, 2, shard)
        gate_grad = without_padding(gate_grad, n_s, shard)
    return (query_grad, key_grad, value_grad, weight_grad, gate_grad)


def solution(mesh):
    return jax.shard_map(
        body,
        mesh=mesh,
        in_specs=(
            P("tm", "space"),
            P("tm", "space"),
            P("tm", "space"),
            P("tm", "space"),
            P("tm", "space"),
            P("space", None),
            P(),
            P(),
            P(),
        ),
        out_specs=(P("tm", "space"), P("tm", "space"), P("tm", "space"), P("space", "tm"), P()),
        check_vma=False,
    )
```

```python
import functools
import math

import jax
import jax.numpy as jnp
from jax import lax
from jax.experimental import pallas as pl
from jax.experimental.pallas import tpu as pltpu
from jax.sharding import PartitionSpec as P

HD = 128
SPF = 512
QF = 64
LANES = 128
NEG_BIG = -1e30
SCALE = 1.0 / math.sqrt(HD)
VMEM_LIMIT = 32 * 1024 * 1024
PREP_VMEM = 52 * 1024 * 1024
SPLIT = 3


def dot(a, b, on_a, on_b):
    return lax.dot_general(
        a, b, (((on_a,), (on_b,)), ((), ())), preferred_element_type=jnp.float32
    )


def place():
    s = lax.axis_index("space")
    return lax.axis_index("tm"), s // 2, s % 2


def clip_numbers(clips_ref):
    bounds = []
    so_far = 0
    for c in range(clips_ref.shape[0]):
        so_far = so_far + clips_ref[c]
        bounds.append(so_far)
    return lambda frame: sum((frame >= bound).astype(jnp.int32) for bound in bounds)


def cut_kernel(chips, weight_in, kept, sent, sems):
    _, chip, core = place()
    width = kept.shape[2]
    copies = []
    for k in range(chips):
        for c, out in ((1 - core, sent), (core, kept)):
            columns = pl.ds(pl.multiple_of((2 * (chip ^ k) + c) * width, LANES), width)
            copies.append(
                pltpu.make_async_copy(weight_in.at[:, columns], out.at[k], sems.at[len(copies)])
            )
    for copy in copies:
        copy.start()
    for copy in copies:
        copy.wait()


def masks_kernel(n_t, chips, frames, rows, levels, clips, gate, bias, gate_a, gate_b, hot):
    t, chip, core = place()
    width = gate_a.shape[2]
    clip_of = clip_numbers(clips)
    lane = lax.broadcasted_iota(jnp.int32, (1, rows), 1)
    for kf in range(frames):
        key_frame = t * frames + kf
        key_clip = clip_of(key_frame)
        for k in range(n_t):
            row = jnp.full((1, rows), NEG_BIG, jnp.float32)
            for r in range(frames):
                frame = (t ^ k) * frames + r
                visible = (key_frame >= frame) & (clip_of(frame) == key_clip)
                value = jnp.where(visible, 0.0, NEG_BIG).astype(jnp.float32)
                row = jnp.where((lane >= r * QF) & (lane < (r + 1) * QF), value, row)
            bias[kf : kf + 1, k * rows : (k + 1) * rows] = row
    spot = lax.broadcasted_iota(jnp.int32, hot.shape[1:], 0)
    for f in range(n_t * frames):
        hot[f] = (spot == levels[f]).astype(jnp.float32)
    for r in range(frames):
        level = levels[t * frames + r]
        for k in range(chips):
            columns = pl.ds(pl.multiple_of((2 * (chip ^ k) + core) * width, LANES), width)
            gate_a[k, r : r + 1, :] = gate[pl.ds(level, 1), columns]
        for k in range(n_t):
            level = levels[(t ^ chip ^ k) * frames + r]
            mine = pl.ds(pl.multiple_of((2 * t + core) * width, LANES), width)
            gate_b[k, r : r + 1, :] = gate[pl.ds(level, 1), mine]


def stats_kernel(n_t, bias, keys, *refs):
    packed, out = refs[:n_t], refs[n_t]
    rows = packed[0].shape[1]
    for p in range(0, n_t, 2):
        q = jnp.concatenate([packed[p][0], packed[p + 1][0]], axis=0)
        scores = []
        for kf in range(bias.shape[0]):
            mask = bias[kf : kf + 1, p * rows : (p + 2) * rows]
            scores.append(dot(keys[kf * SPF : (kf + 1) * SPF, :], q, 1, 1) * SCALE + mask)
        top = functools.reduce(jnp.maximum, [jnp.max(x, axis=0, keepdims=True) for x in scores])
        total = sum(jnp.sum(jnp.exp(x - top), axis=0, keepdims=True) for x in scores)
        for i in range(2):
            out[p + i : p + i + 1, :] = top[:, i * rows : (i + 1) * rows]
            out[n_t + p + i : n_t + p + i + 1, :] = total[:, i * rows : (i + 1) * rows]


def head_kernel(chips, frames, packed, other_saved, kept, received, gate_a, *refs):
    pieces, (mine, other) = refs[:chips], refs[chips:]
    _, chip, _ = place()
    rows = mine.shape[0]
    tiles = pieces[0].shape[1] // LANES
    saved = jnp.concatenate([packed[1], other_saved[...]], axis=1)
    head = None
    for k in range(chips):
        weight = jnp.concatenate([kept[k], received[k]], axis=0)
        wide = pieces[k][...].astype(jnp.float32)
        gated = jnp.concatenate(
            [
                (wide[r * QF : (r + 1) * QF] * gate_a[k, r : r + 1, :]).astype(jnp.bfloat16)
                for r in range(frames)
            ],
            axis=0,
        )
        part = dot(gated, weight, 1, 1)
        head = part if head is None else head + part
        product = wide * dot(saved, weight, 1, 0)
        for r in range(frames):
            term = jnp.sum(product[r * QF : (r + 1) * QF], axis=0, keepdims=True)
            for j in range(tiles):
                row = rows + ((chip ^ k) * frames + r) * tiles + j
                other[pl.ds(row, 1), :] = term[:, j * LANES : (j + 1) * LANES]
    mine[...] = head[:, :HD]
    other[:rows, :] = head[:, HD:]


def join_kernel(mine, sent, received, stats, out, terms):
    core = place()[2]
    rows = mine.shape[0]
    out[:rows, :] = (mine[...] + received[:rows, :]).astype(jnp.bfloat16)
    own, other = sent[rows:, :], received[rows:, :]
    count = own.shape[0]
    terms[:count, :] = jnp.where(core == 0, own, other)
    terms[count:, :] = jnp.where(core == 0, other, own)
    rest = stats[...]
    parts = []
    for _ in range(SPLIT):
        part = rest.astype(jnp.bfloat16).astype(jnp.float32)
        parts.append(part)
        rest = rest - part
    pad = out.shape[0] - rows - SPLIT * rest.shape[0]
    if pad:
        parts.append(jnp.zeros((pad, LANES), jnp.float32))
    out[rows:, :] = jnp.concatenate(parts, axis=0).astype(jnp.bfloat16)


def grads_kernel(n_t, chips, bias, keys, values, *refs):
    terms, refs = refs[:chips], refs[chips:]
    packed, heads = refs[:n_t], refs[n_t : 2 * n_t]
    key_out, value_out = refs[2 * n_t : 2 * n_t + 2]
    outs = refs[2 * n_t + 2 : 3 * n_t + 2]
    key_acc, value_acc, held = refs[3 * n_t + 2 :]
    chip = place()[1]
    rows = packed[0].shape[1]
    ones = jnp.ones((8, HD), jnp.float32)
    keys_t = jnp.transpose(keys[...])
    stats = []
    for k in range(n_t):
        parts = heads[k][rows:, :].astype(jnp.float32)
        stats.append(sum(parts[i * 2 * n_t : (i + 1) * 2 * n_t] for i in range(SPLIT)))
    for k in range(chips):
        held[chip ^ k] = terms[k][...]
    total = held[0]
    for k in range(1, chips):
        total = total + held[k]
    for k in range(n_t):
        outs[k][rows:, :] = total.astype(jnp.bfloat16)
    for p in range(0, n_t, 2):
        q = jnp.concatenate([packed[p][0], packed[p + 1][0]], axis=0)
        o = jnp.concatenate([packed[p][1], packed[p + 1][1]], axis=0)
        g = jnp.concatenate([heads[p][:rows, :], heads[p + 1][:rows, :]], axis=0)
        delta = lax.dot_general(
            ones,
            g.astype(jnp.float32) * o.astype(jnp.float32),
            (((1,), (1,)), ((), ())),
            precision=lax.Precision.HIGHEST,
            preferred_element_type=jnp.float32,
        )[0:1]
        lse = []
        for i in (p, p + 1):
            tops = [stats[k][i ^ k : (i ^ k) + 1] for k in range(n_t)]
            sums = [stats[k][n_t + (i ^ k) : n_t + (i ^ k) + 1] for k in range(n_t)]
            top = functools.reduce(jnp.maximum, tops)
            lse.append(top + jnp.log(sum(b * jnp.exp(a - top) for a, b in zip(tops, sums))))
        lse = jnp.concatenate(lse, axis=1)
        query_part = None
        for kf in range(bias.shape[0]):
            span = slice(kf * SPF, (kf + 1) * SPF)
            shift = bias[kf : kf + 1, p * rows : (p + 2) * rows] - lse
            probs = jnp.exp(dot(keys[span, :], q, 1, 1) * SCALE + shift)
            score_grad = (probs * (dot(values[span, :], g, 1, 1) - delta)).astype(jnp.bfloat16)
            value_add = dot(probs.astype(jnp.bfloat16), g, 1, 0)
            key_add = dot(score_grad, q, 1, 0)
            if p > 0:
                value_add = value_add + value_acc[span, :]
                key_add = key_add + key_acc[span, :]
            if p + 2 < n_t:
                value_acc[span, :] = value_add
                key_acc[span, :] = key_add
            else:
                value_out[span, :] = value_add.astype(jnp.bfloat16)
                key_out[span, :] = (key_add * SCALE).astype(jnp.bfloat16)
            part = dot(keys_t[:, span], score_grad, 1, 0)
            query_part = part if query_part is None else query_part + part
        outs[p][:rows, :] = query_part[:, :rows].astype(jnp.bfloat16)
        outs[p + 1][:rows, :] = query_part[:, rows:].astype(jnp.bfloat16)


def finish_kernel(n_t, chips, frames, hot, *refs):
    parts, (query_out, gate_out, held) = refs[:n_t], refs[n_t:]
    t = lax.axis_index("tm")
    rows = query_out.shape[0]
    total = parts[0][:rows, :].astype(jnp.float32)
    for k in range(1, n_t):
        total = total + parts[k][:rows, :].astype(jnp.float32)
    query_out[...] = jnp.transpose(total * SCALE).astype(jnp.bfloat16)
    for k in range(n_t):
        held[t ^ k] = parts[k][rows:, :].astype(jnp.float32)
    tiles = gate_out.shape[1] // (2 * chips * LANES)
    for core in range(2):
        for a in range(chips):
            for j in range(tiles):
                total = jnp.zeros(hot.shape[1:], jnp.float32)
                for f in range(n_t * frames):
                    row = ((core * chips + a) * frames + f % frames) * tiles + j
                    total = total + hot[f] * held[f // frames, row : row + 1, :]
                column = ((2 * a + core) * tiles + j) * LANES
                gate_out[:, column : column + LANES] = total


def gated_kernel(n_t, frames, gate_b, *refs):
    pieces, out = refs[:n_t], refs[n_t]
    for k in range(n_t):
        for r in range(frames):
            span = slice(r * QF, (r + 1) * QF)
            wide = pieces[k][span, :].astype(jnp.float32)
            out[k, span, :] = (wide * gate_b[k, r : r + 1, :]).astype(jnp.bfloat16)


def weight_kernel(n_t, own, other, *refs):
    packed, out, held = refs[:n_t], refs[n_t], refs[n_t + 1]
    _, chip, core = place()
    width = own.shape[2]
    for k in range(n_t):
        held[k] = packed[k][1]
    saved = jnp.concatenate([held[chip ^ k] for k in range(n_t)], axis=0)
    for ref, half in ((own, core), (other, 1 - core)):
        gated = jnp.concatenate([ref[k] for k in range(n_t)], axis=0)
        result = dot(saved, gated, 0, 0)
        for h in range(2):

            @pl.when(half == h)
            def _():
                out[:, h * width : (h + 1) * width] = result


def call(kernel, args, out_shape, scratch=(), flops=0, in_place=False, in_smem=0):
    vmem = pl.BlockSpec(memory_space=pltpu.VMEM)
    single = not isinstance(out_shape, (list, tuple))
    nbytes = sum(a.size * a.dtype.itemsize for a in args)
    return pl.pallas_call(
        kernel,
        out_shape=out_shape,
        in_specs=[pl.BlockSpec(memory_space=pltpu.SMEM)] * in_smem
        + [pl.BlockSpec(memory_space=pltpu.HBM) if in_place else vmem] * (len(args) - in_smem),
        out_specs=vmem if single else [vmem] * len(out_shape),
        scratch_shapes=list(scratch),
        compiler_params=pltpu.CompilerParams(vmem_limit_bytes=PREP_VMEM if in_place else VMEM_LIMIT),
        cost_estimate=pl.CostEstimate(flops=flops, bytes_accessed=nbytes, transcendentals=0),
    )(*args)


def padded_shards(table, n_s, width):
    rows, columns = table.shape
    cut = table.reshape(rows, n_s, columns // n_s)
    cut = jnp.pad(cut, ((0, 0), (0, 0), (0, width - columns // n_s)))
    return cut.reshape(rows, n_s * width)


def without_padding(table, shards, shard):
    rows, columns = table.shape
    return table.reshape(rows, shards, columns // shards)[:, :, :shard].reshape(rows, shards * shard)


def body(
    queries, keys, values, saved_out, out_grad, proj_weight, gate_table, noise_levels, clip_lengths
):
    n_t, n_s = lax.axis_size("tm"), lax.axis_size("space")
    chips = n_s // 2
    rows, shard = out_grad.shape
    k_rows = keys.shape[0]
    frames = rows // QF
    levels = gate_table.shape[0]
    bf16, f32 = jnp.bfloat16, jnp.float32
    width = -(-shard // LANES) * LANES
    if width != shard:
        out_grad = jnp.pad(out_grad, ((0, 0), (0, width - shard)))
        proj_weight = padded_shards(proj_weight, n_s, width)
        gate_table = padded_shards(gate_table, n_s, width)

    def shape(dtype, *dims):
        return jax.ShapeDtypeStruct(dims, dtype)

    def over_chips(x):
        return [x] + [
            lax.ppermute(x, "space", [(s, s ^ (2 * k)) for s in range(n_s)]) for k in range(1, chips)
        ]

    def over_cores(x):
        return lax.ppermute(x, "space", [(s, s ^ 1) for s in range(n_s)])

    def over_time(x, k):
        return lax.ppermute(x, "tm", [(t, t ^ k) for t in range(n_t)])

    pieces = over_chips(out_grad)
    kept, sent = call(
        functools.partial(cut_kernel, chips),
        [proj_weight],
        [shape(bf16, chips, HD, width)] * 2,
        [pltpu.SemaphoreType.DMA((2 * chips,))],
        in_place=True,
    )
    received, other_saved = over_cores(sent), over_cores(saved_out)
    packed, _ = lax.optimization_barrier((jnp.stack([queries, saved_out]), (received, other_saved)))
    packed_all = [packed]
    for k in range(1, n_t):
        high = 1 << (k.bit_length() - 1)
        packed_all.append(over_time(packed_all[k - high], high))
    moves = [
        (t * n_s + 2 * c + e, c * n_s + 2 * (c ^ t) + e)
        for t in range(n_t)
        for c in range(chips)
        for e in range(2)
    ]
    to_move, _ = lax.optimization_barrier((out_grad, packed_all[n_t // 2]))
    moved = lax.ppermute(to_move, ("tm", "space"), moves)
    gate_table, _ = lax.optimization_barrier((gate_table, received))
    bias, gate_a, gate_b, hot = call(
        functools.partial(masks_kernel, n_t, chips, frames, rows),
        [noise_levels, clip_lengths, gate_table],
        [
            shape(f32, frames, n_t * rows),
            shape(f32, chips, frames, width),
            shape(f32, n_t, frames, width),
            shape(f32, n_t * frames, levels, LANES),
        ],
        in_smem=2,
    )
    kept, _ = lax.optimization_barrier((kept, packed_all))
    count = chips * frames * width // LANES
    mine, other = call(
        functools.partial(head_kernel, chips, frames),
        [packed, other_saved, kept, received, gate_a] + pieces,
        [shape(f32, rows, HD), shape(f32, rows + count, HD)],
        flops=4 * rows * chips * width * 2 * HD,
    )
    later_bias, _ = lax.optimization_barrier((bias, mine))
    stats = call(
        functools.partial(stats_kernel, n_t),
        [later_bias, keys] + packed_all,
        shape(f32, 2 * n_t, LANES),
        flops=2 * n_t * rows * k_rows * HD,
    )
    extra = -(-SPLIT * 2 * n_t // 16) * 16
    joined, terms = call(
        join_kernel,
        [mine, other, over_cores(other), stats],
        [shape(bf16, rows + extra, HD), shape(f32, 2 * count, LANES)],
    )
    heads_all = [joined] + [over_time(joined, k) for k in range(1, n_t)]
    terms_all = over_chips(terms)
    moved, _ = lax.optimization_barrier((moved, terms_all))
    row_pieces = over_chips(moved)
    outs = call(
        functools.partial(grads_kernel, n_t, chips),
        [bias, keys, values] + terms_all + packed_all + heads_all,
        [shape(bf16, k_rows, HD)] * 2 + [shape(bf16, rows + 2 * count, LANES)] * n_t,
        [pltpu.VMEM((k_rows, HD), f32)] * 2 + [pltpu.VMEM((chips, 2 * count, LANES), f32)],
        flops=10 * n_t * rows * k_rows * HD,
    )
    key_grad, value_grad, parts = outs[0], outs[1], outs[2:]
    parts = [parts[0]] + [over_time(parts[k], k) for k in range(1, n_t)]
    row_pieces, _ = lax.optimization_barrier((row_pieces, parts))

    gated = call(
        functools.partial(gated_kernel, n_t, frames),
        [gate_b] + row_pieces,
        shape(bf16, n_t, rows, width),
    )
    weight_grad = call(
        functools.partial(weight_kernel, n_t),
        [gated, over_cores(gated)] + packed_all,
        shape(f32, HD, 2 * width),
        [pltpu.VMEM((n_t, rows, HD), bf16)],
        flops=4 * n_t * rows * width * HD,
    )
    query_grad, gate_grad = call(
        functools.partial(finish_kernel, n_t, chips, frames),
        [hot] + parts,
        [shape(bf16, rows, HD), shape(f32, levels, n_s * width)],
        [pltpu.VMEM((n_t, 2 * count, LANES), f32)],
    )
    if width != shard:
        weight_grad = without_padding(weight_grad, 2, shard)
        gate_grad = without_padding(gate_grad, n_s, shard)
    return (query_grad, key_grad, value_grad, weight_grad, gate_grad)


def solution(mesh):
    return jax.shard_map(
        body,
        mesh=mesh,
        in_specs=(
            P("tm", "space"),
            P("tm", "space"),
            P("tm", "space"),
            P("tm", "space"),
            P("tm", "space"),
            P("space", None),
            P(),
            P(),
            P(),
        ),
        out_specs=(P("tm", "space"), P("tm", "space"), P("tm", "space"), P("space", "tm"), P()),
        check_vma=False,
    )
```

```python
import functools
import math

import jax
import jax.numpy as jnp
from jax import lax
from jax.experimental import pallas as pl
from jax.experimental.pallas import tpu as pltpu
from jax.sharding import PartitionSpec as P

HD = 128
SPF = 512
QF = 64
LANES = 128
NEG_BIG = -1e30
SCALE = 1.0 / math.sqrt(HD)
VMEM_LIMIT = 32 * 1024 * 1024
PREP_VMEM = 52 * 1024 * 1024
SPLIT = 3


def dot(a, b, on_a, on_b):
    return lax.dot_general(
        a, b, (((on_a,), (on_b,)), ((), ())), preferred_element_type=jnp.float32
    )


def place():
    s = lax.axis_index("space")
    return lax.axis_index("tm"), s // 2, s % 2


def clip_numbers(clips_ref):
    bounds = []
    so_far = 0
    for c in range(clips_ref.shape[0]):
        so_far = so_far + clips_ref[c]
        bounds.append(so_far)
    return lambda frame: sum((frame >= bound).astype(jnp.int32) for bound in bounds)


def cut_kernel(chips, weight_in, saved_in, kept, sent, sems):
    _, chip, core = place()
    width = kept.shape[2]
    moves = [(saved_in, sent.at[:, chips * width : chips * width + HD])]
    for k in range(chips):
        for c, out in ((1 - core, sent.at[:, k * width : (k + 1) * width]), (core, kept.at[k])):
            columns = pl.ds(pl.multiple_of((2 * (chip ^ k) + c) * width, LANES), width)
            moves.append((weight_in.at[:, columns], out))
    copies = [pltpu.make_async_copy(a, b, sems.at[i]) for i, (a, b) in enumerate(moves)]
    for copy in copies:
        copy.start()
    for copy in copies:
        copy.wait()


def masks_kernel(n_t, chips, frames, rows, levels, clips, gate, bias, gate_a, gate_b, hot):
    t, chip, core = place()
    width = gate_a.shape[2]
    clip_of = clip_numbers(clips)
    lane = lax.broadcasted_iota(jnp.int32, (1, rows), 1)
    for kf in range(frames):
        key_frame = t * frames + kf
        key_clip = clip_of(key_frame)
        for k in range(n_t):
            row = jnp.full((1, rows), NEG_BIG, jnp.float32)
            for r in range(frames):
                frame = (t ^ k) * frames + r
                visible = (key_frame >= frame) & (clip_of(frame) == key_clip)
                value = jnp.where(visible, 0.0, NEG_BIG).astype(jnp.float32)
                row = jnp.where((lane >= r * QF) & (lane < (r + 1) * QF), value, row)
            bias[kf : kf + 1, k * rows : (k + 1) * rows] = row
    spot = lax.broadcasted_iota(jnp.int32, hot.shape[1:], 0)
    for f in range(n_t * frames):
        hot[f] = (spot == levels[f]).astype(jnp.float32)
    for r in range(frames):
        level = levels[t * frames + r]
        for k in range(chips):
            columns = pl.ds(pl.multiple_of((2 * (chip ^ k) + core) * width, LANES), width)
            gate_a[k, r : r + 1, :] = gate[pl.ds(level, 1), columns]
    mine = pl.ds(pl.multiple_of((2 * t + core) * width, LANES), width)
    for k in range(n_t):
        level = levels[(t ^ k) * frames + chip * (rows // chips) // QF]
        gate_b[k] = gate[pl.ds(level, 1), mine]


def stats_kernel(n_t, bias, keys, *refs):
    packed, out = refs[:n_t], refs[n_t]
    rows = packed[0].shape[1]
    for p in range(0, n_t, 2):
        q = jnp.concatenate([packed[p][0], packed[p + 1][0]], axis=0)
        scores = []
        for kf in range(bias.shape[0]):
            mask = bias[kf : kf + 1, p * rows : (p + 2) * rows]
            scores.append(dot(keys[kf * SPF : (kf + 1) * SPF, :], q, 1, 1) * SCALE + mask)
        top = functools.reduce(jnp.maximum, [jnp.max(x, axis=0, keepdims=True) for x in scores])
        total = sum(jnp.sum(jnp.exp(x - top), axis=0, keepdims=True) for x in scores)
        for i in range(2):
            out[p + i : p + i + 1, :] = top[:, i * rows : (i + 1) * rows]
            out[n_t + p + i : n_t + p + i + 1, :] = total[:, i * rows : (i + 1) * rows]


def head_kernel(chips, frames, packed, kept, received, gate_a, *refs):
    pieces, (mine, other, terms) = refs[:chips], refs[chips:]
    _, chip, _ = place()
    width = pieces[0].shape[1]
    tiles = width // LANES
    saved = jnp.concatenate([packed[1], received[:, chips * width : chips * width + HD]], axis=1)
    head = None
    for k in range(chips):
        weight = jnp.concatenate([kept[k], received[:, k * width : (k + 1) * width]], axis=0)
        wide = pieces[k][...].astype(jnp.float32)
        gated = jnp.concatenate(
            [
                (wide[r * QF : (r + 1) * QF] * gate_a[k, r : r + 1, :]).astype(jnp.bfloat16)
                for r in range(frames)
            ],
            axis=0,
        )
        part = dot(gated, weight, 1, 1)
        head = part if head is None else head + part
        product = wide * dot(saved, weight, 1, 0)
        for r in range(frames):
            term = jnp.sum(product[r * QF : (r + 1) * QF], axis=0, keepdims=True)
            for j in range(tiles):
                row = ((chip ^ k) * frames + r) * tiles + j
                terms[pl.ds(row, 1), :] = term[:, j * LANES : (j + 1) * LANES]
    mine[...] = head[:, :HD]
    other[...] = head[:, HD:]


def sections(rows, chips, tiles, n_t, count):
    starts = [0, rows]
    starts.append(starts[-1] + -(-SPLIT * 2 * n_t // 16) * 16)
    starts.append(starts[-1] + tiles * (rows // chips))
    starts.append(starts[-1] + -(-count // 16) * 16)
    return starts


def padded(x, rows):
    if x.shape[0] == rows:
        return x
    return jnp.concatenate([x, jnp.zeros((rows - x.shape[0], x.shape[1]), x.dtype)], axis=0)


def join_kernel(n_t, chips, starts, mine, received, stats, terms, *refs):
    pieces, outs, (wide, held) = refs[:chips], refs[chips : chips + n_t][::-1], refs[chips + n_t :]
    t, chip, _ = place()
    part, tiles = held.shape[1], held.shape[2] // LANES
    for k in range(chips):
        wide[...] = pieces[k][...].astype(jnp.float32)
        held[k] = wide[pl.ds(pl.multiple_of(chip * part, part), part), :]
    head = (mine[...] + received[...]).astype(jnp.bfloat16)
    rest = stats[...]
    split = []
    for _ in range(SPLIT):
        piece = rest.astype(jnp.bfloat16).astype(jnp.float32)
        split.append(piece)
        rest = rest - piece
    split = padded(jnp.concatenate(split, axis=0), starts[2] - starts[1]).astype(jnp.bfloat16)
    last = padded(terms[...], starts[4] - starts[3]).astype(jnp.bfloat16)
    for k in range(n_t):
        rows = held[chip ^ t ^ k]
        rows = jnp.concatenate([rows[:, j * LANES : (j + 1) * LANES] for j in range(tiles)], axis=0)
        outs[k][: starts[1], :] = head
        outs[k][starts[1] : starts[2], :] = split
        outs[k][starts[2] : starts[3], :] = rows.astype(jnp.bfloat16)
        outs[k][starts[3] :, :] = last


def bundle_kernel(n_t, starts, count, gate_b, *refs):
    heads, out = refs[:n_t][::-1], refs[n_t]
    tiles = gate_b.shape[2] // LANES
    part = (starts[3] - starts[2]) // tiles
    wide = [heads[k][starts[2] : starts[3], :].astype(jnp.float32) for k in range(n_t)]
    for j in range(tiles):
        gated = jnp.concatenate(
            [
                wide[k][j * part : (j + 1) * part] * gate_b[k, :, j * LANES : (j + 1) * LANES]
                for k in range(n_t)
            ],
            axis=0,
        )
        out[j * n_t * part : (j + 1) * n_t * part, :] = gated.astype(jnp.bfloat16)
    terms = [heads[k][starts[3] :, :].astype(jnp.float32)[:count] for k in range(n_t)]
    out[tiles * n_t * part :, :] = jnp.concatenate(terms, axis=0).astype(jnp.bfloat16)


def collect_kernel(chips, base, *refs):
    pieces, out, held = refs[:chips], refs[chips], refs[chips + 1]
    chip = place()[1]
    for k in range(chips):
        out[k * base : (k + 1) * base, :] = pieces[k][:base, :]
        held[chip ^ k] = pieces[k][base:, :].astype(jnp.float32)
    total = held[0]
    for k in range(1, chips):
        total = total + held[k]
    high = total.astype(jnp.bfloat16)
    count = total.shape[0]
    out[chips * base : chips * base + count, :] = high
    out[chips * base + count :, :] = (total - high.astype(jnp.float32)).astype(jnp.bfloat16)


def grads_kernel(n_t, bias, keys, values, *refs):
    packed, heads = refs[:n_t], refs[n_t : 2 * n_t][::-1]
    key_out, value_out = refs[2 * n_t : 2 * n_t + 2]
    outs = refs[2 * n_t + 2 : 3 * n_t + 2][::-1]
    key_acc, value_acc = refs[3 * n_t + 2 :]
    rows = packed[0].shape[1]
    ones = jnp.ones((8, HD), jnp.float32)
    keys_t = jnp.transpose(keys[...])
    stats = []
    for k in range(n_t):
        parts = heads[k][rows : rows + -(-SPLIT * 2 * n_t // 16) * 16, :].astype(jnp.float32)
        stats.append(sum(parts[i * 2 * n_t : (i + 1) * 2 * n_t] for i in range(SPLIT)))
    for p in range(0, n_t, 2):
        q = jnp.concatenate([packed[p][0], packed[p + 1][0]], axis=0)
        o = jnp.concatenate([packed[p][1], packed[p + 1][1]], axis=0)
        g = jnp.concatenate([heads[p][:rows, :], heads[p + 1][:rows, :]], axis=0)
        delta = lax.dot_general(
            ones,
            g.astype(jnp.float32) * o.astype(jnp.float32),
            (((1,), (1,)), ((), ())),
            precision=lax.Precision.HIGHEST,
            preferred_element_type=jnp.float32,
        )[0:1]
        lse = []
        for i in (p, p + 1):
            tops = [stats[k][i ^ k : (i ^ k) + 1] for k in range(n_t)]
            sums = [stats[k][n_t + (i ^ k) : n_t + (i ^ k) + 1] for k in range(n_t)]
            top = functools.reduce(jnp.maximum, tops)
            lse.append(top + jnp.log(sum(b * jnp.exp(a - top) for a, b in zip(tops, sums))))
        lse = jnp.concatenate(lse, axis=1)
        query_part = None
        for kf in range(bias.shape[0]):
            span = slice(kf * SPF, (kf + 1) * SPF)
            shift = bias[kf : kf + 1, p * rows : (p + 2) * rows] - lse
            probs = jnp.exp(dot(keys[span, :], q, 1, 1) * SCALE + shift)
            score_grad = (probs * (dot(values[span, :], g, 1, 1) - delta)).astype(jnp.bfloat16)
            value_add = dot(probs.astype(jnp.bfloat16), g, 1, 0)
            key_add = dot(score_grad, q, 1, 0)
            if p > 0:
                value_add = value_add + value_acc[span, :]
                key_add = key_add + key_acc[span, :]
            if p + 2 < n_t:
                value_acc[span, :] = value_add
                key_acc[span, :] = key_add
            else:
                value_out[span, :] = value_add.astype(jnp.bfloat16)
                key_out[span, :] = (key_add * SCALE).astype(jnp.bfloat16)
            part = dot(keys_t[:, span], score_grad, 1, 0)
            query_part = part if query_part is None else query_part + part
        outs[p][...] = query_part[:, :rows].astype(jnp.bfloat16)
        outs[p + 1][...] = query_part[:, rows:].astype(jnp.bfloat16)


def query_kernel(n_t, *refs):
    total = refs[0][...].astype(jnp.float32)
    for k in range(1, n_t):
        total = total + refs[k][...].astype(jnp.float32)
    refs[n_t][...] = jnp.transpose(total * SCALE).astype(jnp.bfloat16)


def final_kernel(n_t, chips, frames, hot, own, other, *refs):
    packed, (weight_out, gate_out, saved, held) = refs[:n_t], refs[n_t:]
    t, chip, core = place()
    width = weight_out.shape[1] // 2
    tiles = width // LANES
    rows = saved.shape[1]
    part = rows // chips
    base = tiles * n_t * part
    for k in range(n_t):
        saved[k] = packed[k][1].astype(jnp.float32)
    ordered = []
    for c in range(chips):
        mine = pl.ds(pl.multiple_of((chip ^ c) * part, part), part)
        ordered += [saved[k, mine, :] for k in range(n_t)]
    ordered = jnp.transpose(jnp.concatenate(ordered, axis=0)).astype(jnp.bfloat16)
    count = (own.shape[0] - chips * base) // 2
    each = count // n_t
    for ref, half in ((own, core), (other, 1 - core)):
        gated = jnp.concatenate(
            [
                jnp.concatenate(
                    [
                        ref[c * base + j * n_t * part : c * base + (j + 1) * n_t * part, :]
                        for c in range(chips)
                    ],
                    axis=0,
                )
                for j in range(tiles)
            ],
            axis=1,
        )
        result = dot(ordered, gated, 1, 0)
        terms = ref[chips * base : chips * base + count, :].astype(jnp.float32)
        terms = terms + ref[chips * base + count :, :].astype(jnp.float32)
        for k in range(n_t):
            held[half, t ^ k] = terms[k * each : (k + 1) * each]
        for h in range(2):

            @pl.when(half == h)
            def _():
                weight_out[:, h * width : (h + 1) * width] = result

    for half in range(2):
        for a in range(chips):
            for j in range(tiles):
                total = jnp.zeros(hot.shape[1:], jnp.float32)
                for f in range(n_t * frames):
                    row = (a * frames + f % frames) * tiles + j
                    total = total + hot[f] * held[half, f // frames, row : row + 1, :]
                column = ((2 * a + half) * tiles + j) * LANES
                gate_out[:, column : column + LANES] = total


def call(kernel, args, out_shape, scratch=(), flops=0, in_place=False, in_smem=0):
    vmem = pl.BlockSpec(memory_space=pltpu.VMEM)
    single = not isinstance(out_shape, (list, tuple))
    nbytes = sum(a.size * a.dtype.itemsize for a in args)
    return pl.pallas_call(
        kernel,
        out_shape=out_shape,
        in_specs=[pl.BlockSpec(memory_space=pltpu.SMEM)] * in_smem
        + [pl.BlockSpec(memory_space=pltpu.HBM) if in_place else vmem] * (len(args) - in_smem),
        out_specs=vmem if single else [vmem] * len(out_shape),
        scratch_shapes=list(scratch),
        compiler_params=pltpu.CompilerParams(vmem_limit_bytes=PREP_VMEM if in_place else VMEM_LIMIT),
        cost_estimate=pl.CostEstimate(flops=flops, bytes_accessed=nbytes, transcendentals=0),
    )(*args)


def padded_shards(table, n_s, width):
    rows, columns = table.shape
    cut = table.reshape(rows, n_s, columns // n_s)
    cut = jnp.pad(cut, ((0, 0), (0, 0), (0, width - columns // n_s)))
    return cut.reshape(rows, n_s * width)


def without_padding(table, shards, shard):
    rows, columns = table.shape
    return table.reshape(rows, shards, columns // shards)[:, :, :shard].reshape(rows, shards * shard)


def body(
    queries, keys, values, saved_out, out_grad, proj_weight, gate_table, noise_levels, clip_lengths
):
    n_t, n_s = lax.axis_size("tm"), lax.axis_size("space")
    chips = n_s // 2
    rows, shard = out_grad.shape
    k_rows = keys.shape[0]
    frames = rows // QF
    levels = gate_table.shape[0]
    bf16, f32 = jnp.bfloat16, jnp.float32
    width = -(-shard // LANES) * LANES
    if width != shard:
        out_grad = jnp.pad(out_grad, ((0, 0), (0, width - shard)))
        proj_weight = padded_shards(proj_weight, n_s, width)
        gate_table = padded_shards(gate_table, n_s, width)

    def shape(dtype, *dims):
        return jax.ShapeDtypeStruct(dims, dtype)

    def over_chips(x):
        return [x] + [
            lax.ppermute(x, "space", [(s, s ^ (2 * k)) for s in range(n_s)]) for k in range(1, chips)
        ]

    def over_cores(x):
        return lax.ppermute(x, "space", [(s, s ^ 1) for s in range(n_s)])

    def over_time(x, k):
        return lax.ppermute(x, "tm", [(t, t ^ k) for t in range(n_t)])

    tiles = width // LANES
    part = rows // chips
    count = chips * frames * tiles
    starts = sections(rows, chips, tiles, n_t, count)

    def time_swaps(messages):
        got = {k: over_time(messages[k], k) for k in range(n_t - 1, 0, -1)}
        return [messages[0]] + [got[k] for k in range(1, n_t)]

    pieces = over_chips(out_grad)
    kept, sent = call(
        functools.partial(cut_kernel, chips),
        [proj_weight, saved_out],
        [shape(bf16, chips, HD, width), shape(bf16, HD, chips * width + HD)],
        [pltpu.SemaphoreType.DMA((2 * chips + 1,))],
        in_place=True,
    )
    received = over_cores(sent)
    packed, _ = lax.optimization_barrier((jnp.stack([queries, saved_out]), received))
    packed_all = [packed]
    for k in range(1, n_t):
        high = 1 << (k.bit_length() - 1)
        packed_all.append(over_time(packed_all[k - high], high))
    gate_table, _ = lax.optimization_barrier((gate_table, received))
    bias, gate_a, gate_b, hot = call(
        functools.partial(masks_kernel, n_t, chips, frames, rows),
        [noise_levels, clip_lengths, gate_table],
        [
            shape(f32, frames, n_t * rows),
            shape(f32, chips, frames, width),
            shape(f32, n_t, 1, width),
            shape(f32, n_t * frames, levels, LANES),
        ],
        in_smem=2,
    )
    mine, other, terms = call(
        functools.partial(head_kernel, chips, frames),
        [packed, kept, received, gate_a] + pieces,
        [shape(f32, rows, HD), shape(f32, rows, HD), shape(f32, count, LANES)],
        flops=4 * rows * chips * width * 2 * HD,
    )
    later_bias, _ = lax.optimization_barrier((bias, mine))
    stats = call(
        functools.partial(stats_kernel, n_t),
        [later_bias, keys] + packed_all,
        shape(f32, 2 * n_t, LANES),
        flops=2 * n_t * rows * k_rows * HD,
    )
    heads = call(
        functools.partial(join_kernel, n_t, chips, starts),
        [mine, over_cores(other), stats, terms] + pieces,
        [shape(bf16, starts[-1], LANES)] * n_t,
        [pltpu.VMEM((rows, width), f32), pltpu.VMEM((chips, part, width), f32)],
    )
    heads_all = time_swaps(heads[::-1])
    base = tiles * n_t * part
    bundle = call(
        functools.partial(bundle_kernel, n_t, starts, count),
        [gate_b] + heads_all[::-1],
        shape(bf16, base + n_t * count, LANES),
    )
    bundles = over_chips(bundle)
    later_bias, _ = lax.optimization_barrier((bias, bundle))
    outs = call(
        functools.partial(grads_kernel, n_t),
        [later_bias, keys, values] + packed_all + heads_all[::-1],
        [shape(bf16, k_rows, HD)] * 2 + [shape(bf16, HD, rows)] * n_t,
        [pltpu.VMEM((k_rows, HD), f32)] * 2,
        flops=10 * n_t * rows * k_rows * HD,
    )
    key_grad, value_grad = outs[:2]
    parts = time_swaps(outs[2:][::-1])
    bundles, _ = lax.optimization_barrier((bundles, parts[::-1]))
    collected = call(
        functools.partial(collect_kernel, chips, base),
        bundles,
        shape(bf16, chips * base + 2 * n_t * count, LANES),
        [pltpu.VMEM((chips, n_t * count, LANES), f32)],
    )
    query_grad = call(functools.partial(query_kernel, n_t), parts[::-1], shape(bf16, rows, HD))
    weight_grad, gate_grad = call(
        functools.partial(final_kernel, n_t, chips, frames),
        [hot, collected, over_cores(collected)] + packed_all,
        [shape(f32, HD, 2 * width), shape(f32, levels, n_s * width)],
        [pltpu.VMEM((n_t, rows, HD), f32), pltpu.VMEM((2, n_t, count, LANES), f32)],
        flops=4 * n_t * rows * width * HD,
    )
    if width != shard:
        weight_grad = without_padding(weight_grad, 2, shard)
        gate_grad = without_padding(gate_grad, n_s, shard)
    return (query_grad, key_grad, value_grad, weight_grad, gate_grad)


def solution(mesh):
    return jax.shard_map(
        body,
        mesh=mesh,
        in_specs=(
            P("tm", "space"),
            P("tm", "space"),
            P("tm", "space"),
            P("tm", "space"),
            P("tm", "space"),
            P("space", None),
            P(),
            P(),
            P(),
        ),
        out_specs=(P("tm", "space"), P("tm", "space"), P("tm", "space"), P("space", "tm"), P()),
        check_vma=False,
    )
```

```python
import functools
import math

import jax
import jax.numpy as jnp
from jax import lax
from jax.experimental import pallas as pl
from jax.experimental.pallas import tpu as pltpu
from jax.sharding import PartitionSpec as P

HD = 128
SPF = 512
QF = 64
LANES = 128
NEG_BIG = -1e30
SCALE = 1.0 / math.sqrt(HD)
VMEM_LIMIT = 32 * 1024 * 1024
PREP_VMEM = 52 * 1024 * 1024
SPLIT = 3


def dot(a, b, on_a, on_b):
    return lax.dot_general(
        a, b, (((on_a,), (on_b,)), ((), ())), preferred_element_type=jnp.float32
    )


def piece(refs, k):
    each = refs[0].shape[0]
    return refs[k // each][k % each]


def place():
    s = lax.axis_index("space")
    return lax.axis_index("tm"), s // 2, s % 2


def clip_numbers(clips_ref):
    bounds = []
    so_far = 0
    for c in range(clips_ref.shape[0]):
        so_far = so_far + clips_ref[c]
        bounds.append(so_far)
    return lambda frame: sum((frame >= bound).astype(jnp.int32) for bound in bounds)


def cut_kernel(chips, weight_in, saved_in, kept, sent, sems):
    _, chip, core = place()
    width = kept.shape[2]
    moves = [(saved_in, sent.at[:, chips * width : chips * width + HD])]
    for k in range(chips):
        for c, out in ((1 - core, sent.at[:, k * width : (k + 1) * width]), (core, kept.at[k])):
            columns = pl.ds(pl.multiple_of((2 * (chip ^ k) + c) * width, LANES), width)
            moves.append((weight_in.at[:, columns], out))
    copies = [pltpu.make_async_copy(a, b, sems.at[i]) for i, (a, b) in enumerate(moves)]
    for copy in copies:
        copy.start()
    for copy in copies:
        copy.wait()


def masks_kernel(n_t, chips, frames, rows, levels, clips, gate, bias, gate_a, gate_b, hot):
    t, chip, core = place()
    width = gate_a.shape[2]
    clip_of = clip_numbers(clips)
    lane = lax.broadcasted_iota(jnp.int32, (1, rows), 1)
    for kf in range(frames):
        key_frame = t * frames + kf
        key_clip = clip_of(key_frame)
        for k in range(n_t):
            row = jnp.full((1, rows), NEG_BIG, jnp.float32)
            for r in range(frames):
                frame = (t ^ k) * frames + r
                visible = (key_frame >= frame) & (clip_of(frame) == key_clip)
                value = jnp.where(visible, 0.0, NEG_BIG).astype(jnp.float32)
                row = jnp.where((lane >= r * QF) & (lane < (r + 1) * QF), value, row)
            bias[kf : kf + 1, k * rows : (k + 1) * rows] = row
    spot = lax.broadcasted_iota(jnp.int32, hot.shape[1:], 0)
    for f in range(n_t * frames):
        hot[f] = (spot == levels[f]).astype(jnp.float32)
    for r in range(frames):
        level = levels[t * frames + r]
        for k in range(chips):
            columns = pl.ds(pl.multiple_of((2 * (chip ^ k) + core) * width, LANES), width)
            gate_a[k, r : r + 1, :] = gate[pl.ds(level, 1), columns]
    mine = pl.ds(pl.multiple_of((2 * t + core) * width, LANES), width)
    for r in range(frames):
        level = levels[(t ^ chip) * frames + r]
        gate_b[r : r + 1, :] = gate[pl.ds(level, 1), mine]


def stats_kernel(n_t, bias, keys, *refs):
    packed, out = refs[:-1], refs[-1]
    rows = packed[0].shape[2]
    for p in range(0, n_t, 2):
        q = jnp.concatenate([piece(packed, p)[0], piece(packed, p + 1)[0]], axis=0)
        scores = []
        for kf in range(bias.shape[0]):
            mask = bias[kf : kf + 1, p * rows : (p + 2) * rows]
            scores.append(dot(keys[kf * SPF : (kf + 1) * SPF, :], q, 1, 1) * SCALE + mask)
        top = functools.reduce(jnp.maximum, [jnp.max(x, axis=0, keepdims=True) for x in scores])
        total = sum(jnp.sum(jnp.exp(x - top), axis=0, keepdims=True) for x in scores)
        for i in range(2):
            out[p + i : p + i + 1, :] = top[:, i * rows : (i + 1) * rows]
            out[n_t + p + i : n_t + p + i + 1, :] = total[:, i * rows : (i + 1) * rows]


def head_kernel(chips, frames, packed, kept, received, gate_a, *refs):
    pieces, (mine, other) = refs[:chips], refs[chips:]
    _, chip, _ = place()
    rows, width = pieces[0].shape
    tiles = width // LANES
    saved = jnp.concatenate([packed[0, 1], received[:, chips * width : chips * width + HD]], axis=1)
    head = None
    for k in range(chips):
        weight = jnp.concatenate([kept[k], received[:, k * width : (k + 1) * width]], axis=0)
        wide = pieces[k][...].astype(jnp.float32)
        gated = jnp.concatenate(
            [
                (wide[r * QF : (r + 1) * QF] * gate_a[k, r : r + 1, :]).astype(jnp.bfloat16)
                for r in range(frames)
            ],
            axis=0,
        )
        part = dot(gated, weight, 1, 1)
        head = part if head is None else head + part
        product = wide * dot(saved, weight, 1, 0)
        for r in range(frames):
            term = jnp.sum(product[r * QF : (r + 1) * QF], axis=0, keepdims=True)
            for j in range(tiles):
                row = rows + ((chip ^ k) * frames + r) * tiles + j
                other[pl.ds(row, 1), :] = term[:, j * LANES : (j + 1) * LANES]
    mine[...] = head[:, :HD]
    other[:rows, :] = head[:, HD:]


def rows_of_split(n_t):
    return -(-SPLIT * 2 * n_t // 16) * 16


def split_up(x, count):
    terms = []
    for _ in range(count):
        term = x.astype(jnp.bfloat16).astype(jnp.float32)
        terms.append(term)
        x = x - term
    return jnp.concatenate(terms, axis=0)


def padded(x, rows):
    if x.shape[0] == rows:
        return x
    return jnp.concatenate([x, jnp.zeros((rows - x.shape[0], x.shape[1]), x.dtype)], axis=0)


def join_kernel(mine, received, stats, out):
    rows = mine.shape[0]
    out[0, :rows, :] = (mine[...] + received[:rows, :]).astype(jnp.bfloat16)
    split = padded(split_up(stats[...], SPLIT), out.shape[1] - rows)
    out[0, rows:, :] = split.astype(jnp.bfloat16)


def bundle_kernel(frames, gate_b, moved, sent, received, out):
    core = place()[2]
    rows, width = moved.shape
    wide = moved[...].astype(jnp.float32)
    gated = jnp.concatenate(
        [wide[r * QF : (r + 1) * QF] * gate_b[r : r + 1, :] for r in range(frames)], axis=0
    ).astype(jnp.bfloat16)
    base = rows * (width // LANES)
    for j in range(width // LANES):
        out[j * rows : (j + 1) * rows, :] = gated[:, j * LANES : (j + 1) * LANES]
    own, other = sent[rows:, :], received[rows:, :]
    terms = [jnp.where(core == 0, own, other), jnp.where(core == 0, other, own)]
    out[base:, :] = split_up(jnp.concatenate(terms, axis=0), 2).astype(jnp.bfloat16)


def collect_kernel(chips, base, *refs):
    pieces, (gated, terms_out, held) = refs[:chips], refs[chips:]
    chip = place()[1]
    count = held.shape[1]
    for k in range(chips):
        gated[k * base : (k + 1) * base, :] = pieces[k][:base, :]
        terms = pieces[k][base:, :].astype(jnp.float32)
        held[chip ^ k] = terms[:count] + terms[count:]
    total = held[0]
    for k in range(1, chips):
        total = total + held[k]
    terms_out[...] = total.astype(jnp.bfloat16)


def grads_kernel(n_t, parts, bias, keys, values, terms, *refs):
    packed, heads = refs[:parts], refs[parts : 2 * parts]
    key_out, value_out = refs[2 * parts : 2 * parts + 2]
    outs = refs[2 * parts + 2 : 2 * parts + 2 + n_t][::-1]
    key_acc, value_acc = refs[2 * parts + 2 + n_t :]
    rows = packed[0].shape[2]
    ones = jnp.ones((8, HD), jnp.float32)
    keys_t = jnp.transpose(keys[...])
    stats = []
    for k in range(n_t):
        split = piece(heads, k)[rows:].astype(jnp.float32)
        stats.append(sum(split[i * 2 * n_t : (i + 1) * 2 * n_t] for i in range(SPLIT)))
    for k in range(n_t):
        outs[k][rows:, :] = terms[...]
    for p in range(0, n_t, 2):
        q = jnp.concatenate([piece(packed, p)[0], piece(packed, p + 1)[0]], axis=0)
        o = jnp.concatenate([piece(packed, p)[1], piece(packed, p + 1)[1]], axis=0)
        g = jnp.concatenate([piece(heads, p)[:rows], piece(heads, p + 1)[:rows]], axis=0)
        delta = lax.dot_general(
            ones,
            g.astype(jnp.float32) * o.astype(jnp.float32),
            (((1,), (1,)), ((), ())),
            precision=lax.Precision.HIGHEST,
            preferred_element_type=jnp.float32,
        )[0:1]
        lse = []
        for i in (p, p + 1):
            tops = [stats[k][i ^ k : (i ^ k) + 1] for k in range(n_t)]
            sums = [stats[k][n_t + (i ^ k) : n_t + (i ^ k) + 1] for k in range(n_t)]
            top = functools.reduce(jnp.maximum, tops)
            lse.append(top + jnp.log(sum(b * jnp.exp(a - top) for a, b in zip(tops, sums))))
        lse = jnp.concatenate(lse, axis=1)
        query_part = None
        for kf in range(bias.shape[0]):
            span = slice(kf * SPF, (kf + 1) * SPF)
            shift = bias[kf : kf + 1, p * rows : (p + 2) * rows] - lse
            probs = jnp.exp(dot(keys[span, :], q, 1, 1) * SCALE + shift)
            score_grad = (probs * (dot(values[span, :], g, 1, 1) - delta)).astype(jnp.bfloat16)
            value_add = dot(probs.astype(jnp.bfloat16), g, 1, 0)
            key_add = dot(score_grad, q, 1, 0)
            if p > 0:
                value_add = value_add + value_acc[span, :]
                key_add = key_add + key_acc[span, :]
            if p + 2 < n_t:
                value_acc[span, :] = value_add
                key_acc[span, :] = key_add
            else:
                value_out[span, :] = value_add.astype(jnp.bfloat16)
                key_out[span, :] = (key_add * SCALE).astype(jnp.bfloat16)
            part = dot(keys_t[:, span], score_grad, 1, 0)
            query_part = part if query_part is None else query_part + part
        outs[p][:rows, :] = query_part[:, :rows].astype(jnp.bfloat16)
        outs[p + 1][:rows, :] = query_part[:, rows:].astype(jnp.bfloat16)


def finish_kernel(n_t, chips, frames, hot, *refs):
    parts, (query_out, gate_out, held) = refs[:n_t][::-1], refs[n_t:]
    t = lax.axis_index("tm")
    rows = query_out.shape[0]
    total = parts[0][:rows, :].astype(jnp.float32)
    for k in range(1, n_t):
        total = total + parts[k][:rows, :].astype(jnp.float32)
    query_out[...] = jnp.transpose(total * SCALE).astype(jnp.bfloat16)
    for k in range(n_t):
        held[t ^ k] = parts[k][rows:, :].astype(jnp.float32)
    tiles = gate_out.shape[1] // (2 * chips * LANES)
    for core in range(2):
        for a in range(chips):
            for j in range(tiles):
                total = jnp.zeros(hot.shape[1:], jnp.float32)
                for f in range(n_t * frames):
                    row = ((core * chips + a) * frames + f % frames) * tiles + j
                    total = total + hot[f] * held[f // frames, row : row + 1, :]
                column = ((2 * a + core) * tiles + j) * LANES
                gate_out[:, column : column + LANES] = total


def weight_kernel(n_t, own, other, *refs):
    packed, (out, saved) = refs[:-2], refs[-2:]
    _, chip, core = place()
    rows = saved.shape[1]
    width = out.shape[1] // 2
    tiles = width // LANES
    base = tiles * rows
    for k in range(n_t):
        saved[k] = piece(packed, k)[1].astype(jnp.float32)
    ordered = jnp.concatenate([saved[chip ^ k] for k in range(n_t)], axis=0)
    ordered = jnp.transpose(ordered).astype(jnp.bfloat16)
    for ref, half in ((own, core), (other, 1 - core)):
        gated = jnp.concatenate(
            [
                jnp.concatenate(
                    [ref[k * base + j * rows : k * base + (j + 1) * rows, :] for k in range(n_t)],
                    axis=0,
                )
                for j in range(tiles)
            ],
            axis=1,
        )
        result = dot(ordered, gated, 1, 0)
        for h in range(2):

            @pl.when(half == h)
            def _():
                out[:, h * width : (h + 1) * width] = result


def call(kernel, args, out_shape, scratch=(), flops=0, in_place=False, in_smem=0):
    vmem = pl.BlockSpec(memory_space=pltpu.VMEM)
    single = not isinstance(out_shape, (list, tuple))
    nbytes = sum(a.size * a.dtype.itemsize for a in args)
    return pl.pallas_call(
        kernel,
        out_shape=out_shape,
        in_specs=[pl.BlockSpec(memory_space=pltpu.SMEM)] * in_smem
        + [pl.BlockSpec(memory_space=pltpu.HBM) if in_place else vmem] * (len(args) - in_smem),
        out_specs=vmem if single else [vmem] * len(out_shape),
        scratch_shapes=list(scratch),
        compiler_params=pltpu.CompilerParams(vmem_limit_bytes=PREP_VMEM if in_place else VMEM_LIMIT),
        cost_estimate=pl.CostEstimate(flops=flops, bytes_accessed=nbytes, transcendentals=0),
    )(*args)


def padded_shards(table, n_s, width):
    rows, columns = table.shape
    cut = table.reshape(rows, n_s, columns // n_s)
    cut = jnp.pad(cut, ((0, 0), (0, 0), (0, width - columns // n_s)))
    return cut.reshape(rows, n_s * width)


def without_padding(table, shards, shard):
    rows, columns = table.shape
    return table.reshape(rows, shards, columns // shards)[:, :, :shard].reshape(rows, shards * shard)


def body(
    queries, keys, values, saved_out, out_grad, proj_weight, gate_table, noise_levels, clip_lengths
):
    n_t, n_s = lax.axis_size("tm"), lax.axis_size("space")
    chips = n_s // 2
    rows, shard = out_grad.shape
    k_rows = keys.shape[0]
    frames = rows // QF
    levels = gate_table.shape[0]
    bf16, f32 = jnp.bfloat16, jnp.float32
    width = -(-shard // LANES) * LANES
    if width != shard:
        out_grad = jnp.pad(out_grad, ((0, 0), (0, width - shard)))
        proj_weight = padded_shards(proj_weight, n_s, width)
        gate_table = padded_shards(gate_table, n_s, width)

    def shape(dtype, *dims):
        return jax.ShapeDtypeStruct(dims, dtype)

    def over_chips(x):
        return [x] + [
            lax.ppermute(x, "space", [(s, s ^ (2 * k)) for s in range(n_s)]) for k in range(1, chips)
        ]

    def over_cores(x):
        return lax.ppermute(x, "space", [(s, s ^ 1) for s in range(n_s)])

    def over_time(x, k):
        return lax.ppermute(x, "tm", [(t, t ^ k) for t in range(n_t)])

    tiles = width // LANES
    count = chips * frames * tiles
    base = tiles * rows

    def time_swaps(messages):
        got = {k: over_time(messages[k], k) for k in range(n_t - 1, 0, -1)}
        return [messages[0]] + [got[k] for k in range(1, n_t)]

    def time_gather(x):
        step = 1
        while True:
            got = over_time(x, step)
            step *= 2
            if step >= n_t:
                return [x, got]
            x = jnp.concatenate([x, got], axis=0)

    pieces = over_chips(out_grad)
    moves = [
        (t * n_s + 2 * c + e, c * n_s + 2 * (c ^ t) + e)
        for t in range(n_t)
        for c in range(chips)
        for e in range(2)
    ]
    moved = lax.ppermute(out_grad, ("tm", "space"), moves)
    kept, sent = call(
        functools.partial(cut_kernel, chips),
        [proj_weight, saved_out],
        [shape(bf16, chips, HD, width), shape(bf16, HD, chips * width + HD)],
        [pltpu.SemaphoreType.DMA((2 * chips + 1,))],
        in_place=True,
    )
    received = over_cores(sent)
    packed, _ = lax.optimization_barrier((jnp.stack([queries, saved_out])[None], received))
    packed_all = time_gather(packed)
    gate_table, _ = lax.optimization_barrier((gate_table, received))
    bias, gate_a, gate_b, hot = call(
        functools.partial(masks_kernel, n_t, chips, frames, rows),
        [noise_levels, clip_lengths, gate_table],
        [
            shape(f32, frames, n_t * rows),
            shape(f32, chips, frames, width),
            shape(f32, frames, width),
            shape(f32, n_t * frames, levels, LANES),
        ],
        in_smem=2,
    )
    mine, other = call(
        functools.partial(head_kernel, chips, frames),
        [packed, kept, received, gate_a] + pieces,
        [shape(f32, rows, HD), shape(f32, rows + count, HD)],
        flops=4 * rows * chips * width * 2 * HD,
    )
    later_bias, _ = lax.optimization_barrier((bias, mine))
    stats = call(
        functools.partial(stats_kernel, n_t),
        [later_bias, keys] + packed_all,
        shape(f32, 2 * n_t, LANES),
        flops=2 * n_t * rows * k_rows * HD,
    )
    from_core = over_cores(other)
    joined = call(
        join_kernel,
        [mine, from_core, stats],
        shape(bf16, 1, rows + rows_of_split(n_t), HD),
    )
    heads_all = time_gather(joined)
    bundle = call(
        functools.partial(bundle_kernel, frames),
        [gate_b, moved, other, from_core],
        shape(bf16, base + 4 * count, LANES),
    )
    bundles, _ = lax.optimization_barrier((over_chips(bundle), heads_all[1]))
    collected, terms = call(
        functools.partial(collect_kernel, chips, base),
        bundles,
        [shape(bf16, chips * base, LANES), shape(bf16, 2 * count, LANES)],
        [pltpu.VMEM((chips, 2 * count, LANES), f32)],
    )
    outs = call(
        functools.partial(grads_kernel, n_t, len(packed_all)),
        [bias, keys, values, terms] + packed_all + heads_all,
        [shape(bf16, k_rows, HD)] * 2 + [shape(bf16, HD + 2 * count, rows)] * n_t,
        [pltpu.VMEM((k_rows, HD), f32)] * 2,
        flops=10 * n_t * rows * k_rows * HD,
    )
    key_grad, value_grad = outs[:2]
    parts = time_swaps(outs[2:][::-1])
    to_core, _ = lax.optimization_barrier((collected, outs[2]))
    exchanged = over_cores(to_core)
    later, _ = lax.optimization_barrier((collected, parts[n_t - 1]))
    weight_grad = call(
        functools.partial(weight_kernel, n_t),
        [later, exchanged] + packed_all,
        shape(f32, HD, 2 * width),
        [pltpu.VMEM((n_t, rows, HD), f32)],
        flops=4 * n_t * rows * width * HD,
    )
    hot, _ = lax.optimization_barrier((hot, weight_grad))
    query_grad, gate_grad = call(
        functools.partial(finish_kernel, n_t, chips, frames),
        [hot] + parts[::-1],
        [shape(bf16, rows, HD), shape(f32, levels, n_s * width)],
        [pltpu.VMEM((n_t, 2 * count, LANES), f32)],
    )
    if width != shard:
        weight_grad = without_padding(weight_grad, 2, shard)
        gate_grad = without_padding(gate_grad, n_s, shard)
    return (query_grad, key_grad, value_grad, weight_grad, gate_grad)


def solution(mesh):
    return jax.shard_map(
        body,
        mesh=mesh,
        in_specs=(
            P("tm", "space"),
            P("tm", "space"),
            P("tm", "space"),
            P("tm", "space"),
            P("tm", "space"),
            P("space", None),
            P(),
            P(),
            P(),
        ),
        out_specs=(P("tm", "space"), P("tm", "space"), P("tm", "space"), P("space", "tm"), P()),
        check_vma=False,
    )
```

```python
import functools
import math

import jax
import jax.numpy as jnp
from jax import lax
from jax.experimental import pallas as pl
from jax.experimental.pallas import tpu as pltpu
from jax.sharding import PartitionSpec as P

HD = 128
SPF = 512
QF = 64
LANES = 128
NEG_BIG = -1e30
SCALE = 1.0 / math.sqrt(HD)
VMEM_LIMIT = 32 * 1024 * 1024
PREP_VMEM = 52 * 1024 * 1024
SPLIT = 3


def dot(a, b, on_a, on_b):
    return lax.dot_general(
        a, b, (((on_a,), (on_b,)), ((), ())), preferred_element_type=jnp.float32
    )


def place():
    s = lax.axis_index("space")
    return lax.axis_index("tm"), s // 2, s % 2


def clip_numbers(clips_ref):
    bounds = []
    so_far = 0
    for c in range(clips_ref.shape[0]):
        so_far = so_far + clips_ref[c]
        bounds.append(so_far)
    return lambda frame: sum((frame >= bound).astype(jnp.int32) for bound in bounds)


def masks_kernel(
    n_t, n_s, frames, rows, levels, clips, gate, grad_in, bias, gate_a, gate_b, hot, grad
):
    grad[...] = grad_in[...]
    t, chip, core = place()
    width = gate_a.shape[2]
    clip_of = clip_numbers(clips)
    lane = lax.broadcasted_iota(jnp.int32, (1, rows), 1)
    for kf in range(frames):
        key_frame = t * frames + kf
        key_clip = clip_of(key_frame)
        for k in range(n_t):
            row = jnp.full((1, rows), NEG_BIG, jnp.float32)
            for r in range(frames):
                frame = (t ^ k) * frames + r
                visible = (key_frame >= frame) & (clip_of(frame) == key_clip)
                value = jnp.where(visible, 0.0, NEG_BIG).astype(jnp.float32)
                row = jnp.where((lane >= r * QF) & (lane < (r + 1) * QF), value, row)
            bias[kf : kf + 1, k * rows : (k + 1) * rows] = row
    spot = lax.broadcasted_iota(jnp.int32, hot.shape[1:], 0)
    for f in range(n_t * frames):
        hot[f] = (spot == levels[f]).astype(jnp.float32)
    for r in range(frames):
        level = levels[t * frames + r]
        for k in range(n_s):
            shard = (2 * chip + core) ^ k
            columns = pl.ds(pl.multiple_of(shard * width, LANES), width)
            gate_a[k, r : r + 1, :] = gate[pl.ds(level, 1), columns]
    mine = pl.ds(pl.multiple_of((2 * t + core) * width, LANES), width)
    for k in range(n_t):
        level = levels[(t ^ k) * frames + chip * (rows // (n_s // 2)) // QF]
        gate_b[k] = gate[pl.ds(level, 1), mine]


def stats_kernel(n_t, bias, keys, *refs):
    packed, out = refs[:n_t], refs[n_t]
    rows = packed[0].shape[1]
    for p in range(0, n_t, 2):
        q = jnp.concatenate([packed[p][0], packed[p + 1][0]], axis=0)
        scores = []
        for kf in range(bias.shape[0]):
            mask = bias[kf : kf + 1, p * rows : (p + 2) * rows]
            scores.append(dot(keys[kf * SPF : (kf + 1) * SPF, :], q, 1, 1) * SCALE + mask)
        top = functools.reduce(jnp.maximum, [jnp.max(x, axis=0, keepdims=True) for x in scores])
        total = sum(jnp.sum(jnp.exp(x - top), axis=0, keepdims=True) for x in scores)
        for i in range(2):
            out[p + i : p + i + 1, :] = top[:, i * rows : (i + 1) * rows]
            out[n_t + p + i : n_t + p + i + 1, :] = total[:, i * rows : (i + 1) * rows]


def head_kernel(n_s, frames, weight_in, packed, gate_a, *refs):
    pieces, (head_out, terms, weight_ref, sems) = refs[:n_s], refs[n_s:]
    s = lax.axis_index("space")
    width = pieces[0].shape[1]
    copies = []
    for k in range(n_s):
        columns = pl.ds(pl.multiple_of((s ^ k) * width, LANES), width)
        copies.append(pltpu.make_async_copy(weight_in.at[:, columns], weight_ref.at[k], sems.at[k]))
    for copy in copies:
        copy.start()
    tiles = width // LANES
    saved = packed[1]
    head = None
    for k in range(n_s):
        shard = s ^ k
        copies[k].wait()
        weight = weight_ref[k]
        wide = pieces[k][...].astype(jnp.float32)
        gated = jnp.concatenate(
            [
                (wide[r * QF : (r + 1) * QF] * gate_a[k, r : r + 1, :]).astype(jnp.bfloat16)
                for r in range(frames)
            ],
            axis=0,
        )
        part = dot(gated, weight, 1, 1)
        head = part if head is None else head + part
        product = wide * dot(saved, weight, 1, 0)
        place_of = (shard % 2) * (n_s // 2) + shard // 2
        for r in range(frames):
            term = jnp.sum(product[r * QF : (r + 1) * QF], axis=0, keepdims=True)
            for j in range(tiles):
                row = (place_of * frames + r) * tiles + j
                terms[pl.ds(row, 1), :] = term[:, j * LANES : (j + 1) * LANES]
    head_out[...] = head.astype(jnp.bfloat16)


def sections(rows, chips, tiles, n_t):
    starts = [0, rows]
    starts.append(starts[-1] + -(-SPLIT * 2 * n_t // 16) * 16)
    starts.append(starts[-1] + tiles * (rows // chips))
    return starts


def padded(x, rows):
    if x.shape[0] == rows:
        return x
    return jnp.concatenate([x, jnp.zeros((rows - x.shape[0], x.shape[1]), x.dtype)], axis=0)


def join_kernel(n_t, chips, starts, head, stats, *refs):
    pieces, outs, (wide, held) = refs[:chips], refs[chips : chips + n_t][::-1], refs[chips + n_t :]
    t, chip, _ = place()
    part, tiles = held.shape[1], held.shape[2] // LANES
    for k in range(chips):
        wide[...] = pieces[k][...].astype(jnp.float32)
        held[k] = wide[pl.ds(pl.multiple_of(chip * part, part), part), :]
    rest = stats[...]
    split = []
    for _ in range(SPLIT):
        piece = rest.astype(jnp.bfloat16).astype(jnp.float32)
        split.append(piece)
        rest = rest - piece
    split = padded(jnp.concatenate(split, axis=0), starts[2] - starts[1]).astype(jnp.bfloat16)
    for k in range(n_t):
        rows = held[chip ^ t ^ k]
        rows = jnp.concatenate([rows[:, j * LANES : (j + 1) * LANES] for j in range(tiles)], axis=0)
        outs[k][: starts[1], :] = head[...]
        outs[k][starts[1] : starts[2], :] = split
        outs[k][starts[2] : starts[3], :] = rows.astype(jnp.bfloat16)


def bundle_kernel(n_t, starts, gate_b, *refs):
    heads, out = refs[:n_t][::-1], refs[n_t]
    tiles = gate_b.shape[2] // LANES
    part = (starts[3] - starts[2]) // tiles
    wide = [heads[k][starts[2] : starts[3], :].astype(jnp.float32) for k in range(n_t)]
    for j in range(tiles):
        gated = jnp.concatenate(
            [
                wide[k][j * part : (j + 1) * part] * gate_b[k, :, j * LANES : (j + 1) * LANES]
                for k in range(n_t)
            ],
            axis=0,
        )
        out[j * n_t * part : (j + 1) * n_t * part, :] = gated.astype(jnp.bfloat16)


def collect_kernel(chips, *refs):
    base = refs[0].shape[0]
    for k in range(chips):
        refs[chips][k * base : (k + 1) * base, :] = refs[k][...]


def grads_kernel(n_t, bias, keys, values, terms, *refs):
    packed, heads = refs[:n_t], refs[n_t : 2 * n_t][::-1]
    key_out, value_out = refs[2 * n_t : 2 * n_t + 2]
    outs = refs[2 * n_t + 2 : 3 * n_t + 2][::-1]
    key_acc, value_acc = refs[3 * n_t + 2 :]
    rows = packed[0].shape[1]
    ones = jnp.ones((8, HD), jnp.float32)
    keys_t = jnp.transpose(keys[...])
    stats = []
    for k in range(n_t):
        parts = heads[k][rows : rows + -(-SPLIT * 2 * n_t // 16) * 16, :].astype(jnp.float32)
        stats.append(sum(parts[i * 2 * n_t : (i + 1) * 2 * n_t] for i in range(SPLIT)))
    for k in range(n_t):
        outs[k][rows:, :] = terms[...].astype(jnp.bfloat16)
    for p in range(0, n_t, 2):
        q = jnp.concatenate([packed[p][0], packed[p + 1][0]], axis=0)
        o = jnp.concatenate([packed[p][1], packed[p + 1][1]], axis=0)
        g = jnp.concatenate([heads[p][:rows, :], heads[p + 1][:rows, :]], axis=0)
        delta = lax.dot_general(
            ones,
            g.astype(jnp.float32) * o.astype(jnp.float32),
            (((1,), (1,)), ((), ())),
            precision=lax.Precision.HIGHEST,
            preferred_element_type=jnp.float32,
        )[0:1]
        lse = []
        for i in (p, p + 1):
            tops = [stats[k][i ^ k : (i ^ k) + 1] for k in range(n_t)]
            sums = [stats[k][n_t + (i ^ k) : n_t + (i ^ k) + 1] for k in range(n_t)]
            top = functools.reduce(jnp.maximum, tops)
            lse.append(top + jnp.log(sum(b * jnp.exp(a - top) for a, b in zip(tops, sums))))
        lse = jnp.concatenate(lse, axis=1)
        query_part = None
        for kf in range(bias.shape[0]):
            span = slice(kf * SPF, (kf + 1) * SPF)
            shift = bias[kf : kf + 1, p * rows : (p + 2) * rows] - lse
            probs = jnp.exp(dot(keys[span, :], q, 1, 1) * SCALE + shift)
            score_grad = (probs * (dot(values[span, :], g, 1, 1) - delta)).astype(jnp.bfloat16)
            value_add = dot(probs.astype(jnp.bfloat16), g, 1, 0)
            key_add = dot(score_grad, q, 1, 0)
            if p > 0:
                value_add = value_add + value_acc[span, :]
                key_add = key_add + key_acc[span, :]
            if p + 2 < n_t:
                value_acc[span, :] = value_add
                key_acc[span, :] = key_add
            else:
                value_out[span, :] = value_add.astype(jnp.bfloat16)
                key_out[span, :] = (key_add * SCALE).astype(jnp.bfloat16)
            part = dot(keys_t[:, span], score_grad, 1, 0)
            query_part = part if query_part is None else query_part + part
        outs[p][:rows, :] = query_part[:, :rows].astype(jnp.bfloat16)
        outs[p + 1][:rows, :] = query_part[:, rows:].astype(jnp.bfloat16)


def finish_kernel(n_t, chips, frames, hot, *refs):
    parts, (query_out, gate_out, held) = refs[:n_t][::-1], refs[n_t:]
    t = lax.axis_index("tm")
    rows = query_out.shape[0]
    total = parts[0][:rows, :].astype(jnp.float32)
    for k in range(1, n_t):
        total = total + parts[k][:rows, :].astype(jnp.float32)
    query_out[...] = jnp.transpose(total * SCALE).astype(jnp.bfloat16)
    for k in range(n_t):
        held[t ^ k] = parts[k][rows:, :].astype(jnp.float32)
    tiles = gate_out.shape[1] // (2 * chips * LANES)
    for core in range(2):
        for a in range(chips):
            for j in range(tiles):
                total = jnp.zeros(hot.shape[1:], jnp.float32)
                for f in range(n_t * frames):
                    row = ((core * chips + a) * frames + f % frames) * tiles + j
                    total = total + hot[f] * held[f // frames, row : row + 1, :]
                column = ((2 * a + core) * tiles + j) * LANES
                gate_out[:, column : column + LANES] = total


def weight_kernel(n_t, chips, own, other, *refs):
    packed, (out, saved) = refs[:n_t], refs[n_t:]
    _, chip, core = place()
    width = out.shape[1] // 2
    tiles = width // LANES
    rows = saved.shape[1]
    part = rows // chips
    base = tiles * n_t * part
    for k in range(n_t):
        saved[k] = packed[k][1].astype(jnp.float32)
    ordered = []
    for c in range(chips):
        mine = pl.ds(pl.multiple_of((chip ^ c) * part, part), part)
        ordered += [saved[k, mine, :] for k in range(n_t)]
    ordered = jnp.transpose(jnp.concatenate(ordered, axis=0)).astype(jnp.bfloat16)
    for ref, half in ((own, core), (other, 1 - core)):
        gated = jnp.concatenate(
            [
                jnp.concatenate(
                    [
                        ref[c * base + j * n_t * part : c * base + (j + 1) * n_t * part, :]
                        for c in range(chips)
                    ],
                    axis=0,
                )
                for j in range(tiles)
            ],
            axis=1,
        )
        result = dot(ordered, gated, 1, 0)
        for h in range(2):

            @pl.when(half == h)
            def _():
                out[:, h * width : (h + 1) * width] = result


def call(kernel, args, out_shape, scratch=(), flops=0, in_place=0, in_smem=0):
    vmem = pl.BlockSpec(memory_space=pltpu.VMEM)
    single = not isinstance(out_shape, (list, tuple))
    nbytes = sum(a.size * a.dtype.itemsize for a in args)
    return pl.pallas_call(
        kernel,
        out_shape=out_shape,
        in_specs=[pl.BlockSpec(memory_space=pltpu.SMEM)] * in_smem
        + [pl.BlockSpec(memory_space=pltpu.HBM)] * in_place
        + [vmem] * (len(args) - in_smem - in_place),
        out_specs=vmem if single else [vmem] * len(out_shape),
        scratch_shapes=list(scratch),
        compiler_params=pltpu.CompilerParams(vmem_limit_bytes=PREP_VMEM if in_place else VMEM_LIMIT),
        cost_estimate=pl.CostEstimate(flops=flops, bytes_accessed=nbytes, transcendentals=0),
    )(*args)


def padded_shards(table, n_s, width):
    rows, columns = table.shape
    cut = table.reshape(rows, n_s, columns // n_s)
    cut = jnp.pad(cut, ((0, 0), (0, 0), (0, width - columns // n_s)))
    return cut.reshape(rows, n_s * width)


def without_padding(table, shards, shard):
    rows, columns = table.shape
    return table.reshape(rows, shards, columns // shards)[:, :, :shard].reshape(rows, shards * shard)


def body(
    queries, keys, values, saved_out, out_grad, proj_weight, gate_table, noise_levels, clip_lengths
):
    n_t, n_s = lax.axis_size("tm"), lax.axis_size("space")
    chips = n_s // 2
    rows, shard = out_grad.shape
    k_rows = keys.shape[0]
    frames = rows // QF
    levels = gate_table.shape[0]
    bf16, f32 = jnp.bfloat16, jnp.float32
    width = -(-shard // LANES) * LANES
    if width != shard:
        out_grad = jnp.pad(out_grad, ((0, 0), (0, width - shard)))
        proj_weight = padded_shards(proj_weight, n_s, width)
        gate_table = padded_shards(gate_table, n_s, width)

    def shape(dtype, *dims):
        return jax.ShapeDtypeStruct(dims, dtype)

    def over_chips(x):
        return [x] + [
            lax.ppermute(x, "space", [(s, s ^ (2 * k)) for s in range(n_s)]) for k in range(1, chips)
        ]

    def over_space(x, k):
        return lax.ppermute(x, "space", [(s, s ^ k) for s in range(n_s)])

    def over_cores(x):
        return lax.ppermute(x, "space", [(s, s ^ 1) for s in range(n_s)])

    def over_time(x, k):
        return lax.ppermute(x, "tm", [(t, t ^ k) for t in range(n_t)])

    tiles = width // LANES
    part = rows // chips
    count = chips * frames * tiles
    starts = sections(rows, chips, tiles, n_t)

    def time_swaps(messages):
        got = {k: over_time(messages[k], k) for k in range(n_t - 1, 0, -1)}
        return [messages[0]] + [got[k] for k in range(1, n_t)]

    packed = jnp.stack([queries, saved_out])
    packed_all = [packed]
    for k in range(1, n_t):
        high = 1 << (k.bit_length() - 1)
        packed_all.append(over_time(packed_all[k - high], high))
    pieces = over_chips(out_grad)
    bias, gate_a, gate_b, hot, own_piece = call(
        functools.partial(masks_kernel, n_t, n_s, frames, rows),
        [noise_levels, clip_lengths, gate_table, out_grad],
        [
            shape(f32, frames, n_t * rows),
            shape(f32, n_s, frames, width),
            shape(f32, n_t, 1, width),
            shape(f32, n_t * frames, levels, LANES),
            shape(bf16, rows, width),
        ],
        in_smem=2,
    )
    pieces[1:], _ = lax.optimization_barrier((pieces[1:], (packed_all[1:], gate_a)))
    pieces = [y for x in pieces for y in (x, over_cores(x))]
    pieces[0] = own_piece
    head, terms = call(
        functools.partial(head_kernel, n_s, frames),
        [proj_weight, packed, gate_a] + pieces,
        [shape(bf16, rows, HD), shape(f32, 2 * count, LANES)],
        [
            pltpu.VMEM((n_s, HD, width), bf16),
            pltpu.SemaphoreType.DMA((n_s,)),
        ],
        in_place=1,
        flops=4 * rows * n_s * width * HD,
    )
    later_bias, _ = lax.optimization_barrier((bias, head))
    stats = call(
        functools.partial(stats_kernel, n_t),
        [later_bias, keys] + packed_all,
        shape(f32, 2 * n_t, LANES),
        flops=2 * n_t * rows * k_rows * HD,
    )
    messages = call(
        functools.partial(join_kernel, n_t, chips, starts),
        [head, stats] + pieces[::2],
        [shape(bf16, starts[-1], LANES)] * n_t,
        [pltpu.VMEM((rows, width), f32), pltpu.VMEM((chips, part, width), f32)],
    )
    heads_all = time_swaps(messages[::-1])
    step = 1
    while step < n_s:
        terms = terms + over_space(terms, step)
        step *= 2
    base = tiles * n_t * part
    bundle = call(
        functools.partial(bundle_kernel, n_t, starts),
        [gate_b] + heads_all[::-1],
        shape(bf16, base, LANES),
    )
    bundles = over_chips(bundle)
    later_bias, _ = lax.optimization_barrier((bias, bundle))
    outs = call(
        functools.partial(grads_kernel, n_t),
        [later_bias, keys, values, terms] + packed_all + heads_all[::-1],
        [shape(bf16, k_rows, HD)] * 2 + [shape(bf16, HD + 2 * count, rows)] * n_t,
        [pltpu.VMEM((k_rows, HD), f32)] * 2,
        flops=10 * n_t * rows * k_rows * HD,
    )
    key_grad, value_grad = outs[:2]
    parts = time_swaps(outs[2:][::-1])
    bundles, _ = lax.optimization_barrier((bundles, parts[::-1]))
    collected = call(
        functools.partial(collect_kernel, chips), bundles, shape(bf16, chips * base, LANES)
    )
    weight_grad = call(
        functools.partial(weight_kernel, n_t, chips),
        [collected, over_cores(collected)] + packed_all,
        shape(f32, HD, 2 * width),
        [pltpu.VMEM((n_t, rows, HD), f32)],
        flops=4 * n_t * rows * width * HD,
    )
    query_grad, gate_grad = call(
        functools.partial(finish_kernel, n_t, chips, frames),
        [hot] + parts[::-1],
        [shape(bf16, rows, HD), shape(f32, levels, n_s * width)],
        [pltpu.VMEM((n_t, 2 * count, LANES), f32)],
    )
    if width != shard:
        weight_grad = without_padding(weight_grad, 2, shard)
        gate_grad = without_padding(gate_grad, n_s, shard)
    return (query_grad, key_grad, value_grad, weight_grad, gate_grad)


def solution(mesh):
    return jax.shard_map(
        body,
        mesh=mesh,
        in_specs=(
            P("tm", "space"),
            P("tm", "space"),
            P("tm", "space"),
            P("tm", "space"),
            P("tm", "space"),
            P("space", None),
            P(),
            P(),
            P(),
        ),
        out_specs=(P("tm", "space"), P("tm", "space"), P("tm", "space"), P("space", "tm"), P()),
        check_vma=False,
    )
```

```python
import functools
import math

import jax
import jax.numpy as jnp
from jax import lax
from jax.experimental import pallas as pl
from jax.experimental.pallas import tpu as pltpu
from jax.sharding import PartitionSpec as P

HD = 128
SPF = 512
QF = 64
LANES = 128
NEG_BIG = -1e30
SCALE = 1.0 / math.sqrt(HD)
VMEM_LIMIT = 32 * 1024 * 1024
PREP_VMEM = 52 * 1024 * 1024
SPLIT = 3


def dot(a, b, on_a, on_b):
    return lax.dot_general(
        a, b, (((on_a,), (on_b,)), ((), ())), preferred_element_type=jnp.float32
    )


def place():
    s = lax.axis_index("space")
    return lax.axis_index("tm"), s // 2, s % 2


def clip_numbers(clips_ref):
    bounds = []
    so_far = 0
    for c in range(clips_ref.shape[0]):
        so_far = so_far + clips_ref[c]
        bounds.append(so_far)
    return lambda frame: sum((frame >= bound).astype(jnp.int32) for bound in bounds)


def cut_kernel(chips, weight_in, saved_in, kept, sent, sems):
    _, chip, core = place()
    width = kept.shape[2]
    moves = [(saved_in, sent.at[:, chips * width : chips * width + HD])]
    for k in range(chips):
        for c, out in ((1 - core, sent.at[:, k * width : (k + 1) * width]), (core, kept.at[k])):
            columns = pl.ds(pl.multiple_of((2 * (chip ^ k) + c) * width, LANES), width)
            moves.append((weight_in.at[:, columns], out))
    copies = [pltpu.make_async_copy(a, b, sems.at[i]) for i, (a, b) in enumerate(moves)]
    for copy in copies:
        copy.start()
    for copy in copies:
        copy.wait()


def masks_kernel(n_t, chips, frames, rows, levels, clips, gate, bias, gate_a, gate_b, hot):
    t, chip, core = place()
    width = gate_a.shape[2]
    clip_of = clip_numbers(clips)
    lane = lax.broadcasted_iota(jnp.int32, (1, rows), 1)
    for kf in range(frames):
        key_frame = t * frames + kf
        key_clip = clip_of(key_frame)
        for k in range(n_t):
            row = jnp.full((1, rows), NEG_BIG, jnp.float32)
            for r in range(frames):
                frame = (t ^ k) * frames + r
                visible = (key_frame >= frame) & (clip_of(frame) == key_clip)
                value = jnp.where(visible, 0.0, NEG_BIG).astype(jnp.float32)
                row = jnp.where((lane >= r * QF) & (lane < (r + 1) * QF), value, row)
            bias[kf : kf + 1, k * rows : (k + 1) * rows] = row
    spot = lax.broadcasted_iota(jnp.int32, hot.shape[1:], 0)
    for f in range(n_t * frames):
        hot[f] = (spot == levels[f]).astype(jnp.float32)
    for r in range(frames):
        level = levels[t * frames + r]
        for k in range(chips):
            columns = pl.ds(pl.multiple_of((2 * (chip ^ k) + core) * width, LANES), width)
            gate_a[k, r : r + 1, :] = gate[pl.ds(level, 1), columns]
    mine = pl.ds(pl.multiple_of((2 * t + core) * width, LANES), width)
    for r in range(frames):
        level = levels[(t ^ chip) * frames + r]
        gate_b[r : r + 1, :] = gate[pl.ds(level, 1), mine]


def stats_kernel(n_t, bias, keys, *refs):
    packed, out = refs[:n_t], refs[n_t]
    rows = packed[0].shape[1]
    for p in range(0, n_t, 2):
        q = jnp.concatenate([packed[p][0], packed[p + 1][0]], axis=0)
        scores = []
        for kf in range(bias.shape[0]):
            mask = bias[kf : kf + 1, p * rows : (p + 2) * rows]
            scores.append(dot(keys[kf * SPF : (kf + 1) * SPF, :], q, 1, 1) * SCALE + mask)
        top = functools.reduce(jnp.maximum, [jnp.max(x, axis=0, keepdims=True) for x in scores])
        total = sum(jnp.sum(jnp.exp(x - top), axis=0, keepdims=True) for x in scores)
        for i in range(2):
            out[p + i : p + i + 1, :] = top[:, i * rows : (i + 1) * rows]
            out[n_t + p + i : n_t + p + i + 1, :] = total[:, i * rows : (i + 1) * rows]


def head_kernel(chips, frames, packed, kept, received, gate_a, *refs):
    pieces, (mine, other, terms, move) = refs[:chips], refs[chips:]
    t, chip, _ = place()
    for k in range(chips):

        @pl.when(t == k)
        def _():
            move[...] = pieces[k][...]

    width = pieces[0].shape[1]
    tiles = width // LANES
    saved = jnp.concatenate([packed[1], received[:, chips * width : chips * width + HD]], axis=1)
    head = None
    for k in range(chips):
        weight = jnp.concatenate([kept[k], received[:, k * width : (k + 1) * width]], axis=0)
        wide = pieces[k][...].astype(jnp.float32)
        gated = jnp.concatenate(
            [
                (wide[r * QF : (r + 1) * QF] * gate_a[k, r : r + 1, :]).astype(jnp.bfloat16)
                for r in range(frames)
            ],
            axis=0,
        )
        part = dot(gated, weight, 1, 1)
        head = part if head is None else head + part
        product = wide * dot(saved, weight, 1, 0)
        for r in range(frames):
            term = jnp.sum(product[r * QF : (r + 1) * QF], axis=0, keepdims=True)
            for j in range(tiles):
                row = ((chip ^ k) * frames + r) * tiles + j
                terms[pl.ds(row, 1), :] = term[:, j * LANES : (j + 1) * LANES]
    mine[...] = head[:, :HD]
    other[...] = head[:, HD:]


def sections(rows, n_t, count):
    starts = [0, rows]
    starts.append(starts[-1] + -(-SPLIT * 2 * n_t // 16) * 16)
    starts.append(starts[-1] + -(-count // 16) * 16)
    return starts


def padded(x, rows):
    if x.shape[0] == rows:
        return x
    return jnp.concatenate([x, jnp.zeros((rows - x.shape[0], x.shape[1]), x.dtype)], axis=0)


def join_kernel(starts, mine, received, stats, terms, out):
    out[: starts[1], :] = (mine[...] + received[...]).astype(jnp.bfloat16)
    rest = stats[...]
    split = []
    for _ in range(SPLIT):
        piece = rest.astype(jnp.bfloat16).astype(jnp.float32)
        split.append(piece)
        rest = rest - piece
    split = padded(jnp.concatenate(split, axis=0), starts[2] - starts[1])
    out[starts[1] : starts[2], :] = split.astype(jnp.bfloat16)
    out[starts[2] :, :] = padded(terms[...], starts[3] - starts[2]).astype(jnp.bfloat16)


def bundle_kernel(n_t, frames, starts, count, gate_b, moved, *refs):
    heads, out = refs[:n_t], refs[n_t]
    rows, width = moved.shape
    tiles = width // LANES
    wide = moved[...].astype(jnp.float32)
    gated = jnp.concatenate(
        [wide[r * QF : (r + 1) * QF] * gate_b[r : r + 1, :] for r in range(frames)], axis=0
    ).astype(jnp.bfloat16)
    for j in range(tiles):
        out[j * rows : (j + 1) * rows, :] = gated[:, j * LANES : (j + 1) * LANES]
    terms = [heads[k][starts[2] :, :].astype(jnp.float32)[:count] for k in range(n_t)]
    out[tiles * rows :, :] = jnp.concatenate(terms, axis=0).astype(jnp.bfloat16)


def collect_kernel(chips, base, *refs):
    pieces, out, held = refs[:chips], refs[chips], refs[chips + 1]
    chip = place()[1]
    for k in range(chips):
        out[k * base : (k + 1) * base, :] = pieces[k][:base, :]
        held[chip ^ k] = pieces[k][base:, :].astype(jnp.float32)
    total = held[0]
    for k in range(1, chips):
        total = total + held[k]
    high = total.astype(jnp.bfloat16)
    count = total.shape[0]
    out[chips * base : chips * base + count, :] = high
    out[chips * base + count :, :] = (total - high.astype(jnp.float32)).astype(jnp.bfloat16)


def grads_kernel(n_t, bias, keys, values, *refs):
    packed, heads = refs[:n_t], refs[n_t : 2 * n_t]
    key_out, value_out = refs[2 * n_t : 2 * n_t + 2]
    outs = refs[2 * n_t + 2 : 3 * n_t + 2][::-1]
    key_acc, value_acc = refs[3 * n_t + 2 :]
    rows = packed[0].shape[1]
    ones = jnp.ones((8, HD), jnp.float32)
    keys_t = jnp.transpose(keys[...])
    stats = []
    for k in range(n_t):
        parts = heads[k][rows : rows + -(-SPLIT * 2 * n_t // 16) * 16, :].astype(jnp.float32)
        stats.append(sum(parts[i * 2 * n_t : (i + 1) * 2 * n_t] for i in range(SPLIT)))
    for p in range(0, n_t, 2):
        q = jnp.concatenate([packed[p][0], packed[p + 1][0]], axis=0)
        o = jnp.concatenate([packed[p][1], packed[p + 1][1]], axis=0)
        g = jnp.concatenate([heads[p][:rows, :], heads[p + 1][:rows, :]], axis=0)
        delta = lax.dot_general(
            ones,
            g.astype(jnp.float32) * o.astype(jnp.float32),
            (((1,), (1,)), ((), ())),
            precision=lax.Precision.HIGHEST,
            preferred_element_type=jnp.float32,
        )[0:1]
        lse = []
        for i in (p, p + 1):
            tops = [stats[k][i ^ k : (i ^ k) + 1] for k in range(n_t)]
            sums = [stats[k][n_t + (i ^ k) : n_t + (i ^ k) + 1] for k in range(n_t)]
            top = functools.reduce(jnp.maximum, tops)
            lse.append(top + jnp.log(sum(b * jnp.exp(a - top) for a, b in zip(tops, sums))))
        lse = jnp.concatenate(lse, axis=1)
        query_part = None
        for kf in range(bias.shape[0]):
            span = slice(kf * SPF, (kf + 1) * SPF)
            shift = bias[kf : kf + 1, p * rows : (p + 2) * rows] - lse
            probs = jnp.exp(dot(keys[span, :], q, 1, 1) * SCALE + shift)
            score_grad = (probs * (dot(values[span, :], g, 1, 1) - delta)).astype(jnp.bfloat16)
            value_add = dot(probs.astype(jnp.bfloat16), g, 1, 0)
            key_add = dot(score_grad, q, 1, 0)
            if p > 0:
                value_add = value_add + value_acc[span, :]
                key_add = key_add + key_acc[span, :]
            if p + 2 < n_t:
                value_acc[span, :] = value_add
                key_acc[span, :] = key_add
            else:
                value_out[span, :] = value_add.astype(jnp.bfloat16)
                key_out[span, :] = (key_add * SCALE).astype(jnp.bfloat16)
            part = dot(keys_t[:, span], score_grad, 1, 0)
            query_part = part if query_part is None else query_part + part
        outs[p][...] = query_part[:, :rows].astype(jnp.bfloat16)
        outs[p + 1][...] = query_part[:, rows:].astype(jnp.bfloat16)


def query_kernel(n_t, *refs):
    total = refs[0][...].astype(jnp.float32)
    for k in range(1, n_t):
        total = total + refs[k][...].astype(jnp.float32)
    refs[n_t][...] = jnp.transpose(total * SCALE).astype(jnp.bfloat16)


def final_kernel(n_t, chips, frames, hot, own, other, *refs):
    packed, (weight_out, gate_out, saved, held) = refs[:n_t], refs[n_t:]
    t, chip, core = place()
    width = weight_out.shape[1] // 2
    tiles = width // LANES
    rows = saved.shape[1]
    base = tiles * rows
    for k in range(n_t):
        saved[k] = packed[k][1].astype(jnp.float32)
    ordered = jnp.concatenate([saved[chip ^ c] for c in range(chips)], axis=0)
    ordered = jnp.transpose(ordered).astype(jnp.bfloat16)
    count = (own.shape[0] - chips * base) // 2
    each = count // n_t
    for ref, half in ((own, core), (other, 1 - core)):
        gated = jnp.concatenate(
            [
                jnp.concatenate(
                    [
                        ref[c * base + j * rows : c * base + (j + 1) * rows, :]
                        for c in range(chips)
                    ],
                    axis=0,
                )
                for j in range(tiles)
            ],
            axis=1,
        )
        result = dot(ordered, gated, 1, 0)
        terms = ref[chips * base : chips * base + count, :].astype(jnp.float32)
        terms = terms + ref[chips * base + count :, :].astype(jnp.float32)
        for k in range(n_t):
            held[half, t ^ k] = terms[k * each : (k + 1) * each]
        for h in range(2):

            @pl.when(half == h)
            def _():
                weight_out[:, h * width : (h + 1) * width] = result

    for half in range(2):
        for a in range(chips):
            for j in range(tiles):
                total = jnp.zeros(hot.shape[1:], jnp.float32)
                for f in range(n_t * frames):
                    row = (a * frames + f % frames) * tiles + j
                    total = total + hot[f] * held[half, f // frames, row : row + 1, :]
                column = ((2 * a + half) * tiles + j) * LANES
                gate_out[:, column : column + LANES] = total


def call(kernel, args, out_shape, scratch=(), flops=0, in_place=False, in_smem=0):
    vmem = pl.BlockSpec(memory_space=pltpu.VMEM)
    single = not isinstance(out_shape, (list, tuple))
    nbytes = sum(a.size * a.dtype.itemsize for a in args)
    return pl.pallas_call(
        kernel,
        out_shape=out_shape,
        in_specs=[pl.BlockSpec(memory_space=pltpu.SMEM)] * in_smem
        + [pl.BlockSpec(memory_space=pltpu.HBM) if in_place else vmem] * (len(args) - in_smem),
        out_specs=vmem if single else [vmem] * len(out_shape),
        scratch_shapes=list(scratch),
        compiler_params=pltpu.CompilerParams(vmem_limit_bytes=PREP_VMEM if in_place else VMEM_LIMIT),
        cost_estimate=pl.CostEstimate(flops=flops, bytes_accessed=nbytes, transcendentals=0),
    )(*args)


def padded_shards(table, n_s, width):
    rows, columns = table.shape
    cut = table.reshape(rows, n_s, columns // n_s)
    cut = jnp.pad(cut, ((0, 0), (0, 0), (0, width - columns // n_s)))
    return cut.reshape(rows, n_s * width)


def without_padding(table, shards, shard):
    rows, columns = table.shape
    return table.reshape(rows, shards, columns // shards)[:, :, :shard].reshape(rows, shards * shard)


def body(
    queries, keys, values, saved_out, out_grad, proj_weight, gate_table, noise_levels, clip_lengths
):
    n_t, n_s = lax.axis_size("tm"), lax.axis_size("space")
    chips = n_s // 2
    rows, shard = out_grad.shape
    k_rows = keys.shape[0]
    frames = rows // QF
    levels = gate_table.shape[0]
    bf16, f32 = jnp.bfloat16, jnp.float32
    width = -(-shard // LANES) * LANES
    if width != shard:
        out_grad = jnp.pad(out_grad, ((0, 0), (0, width - shard)))
        proj_weight = padded_shards(proj_weight, n_s, width)
        gate_table = padded_shards(gate_table, n_s, width)

    def shape(dtype, *dims):
        return jax.ShapeDtypeStruct(dims, dtype)

    def over_chips(x):
        return [x] + [
            lax.ppermute(x, "space", [(s, s ^ (2 * k)) for s in range(n_s)]) for k in range(1, chips)
        ]

    def over_cores(x):
        return lax.ppermute(x, "space", [(s, s ^ 1) for s in range(n_s)])

    def over_time(x, k):
        return lax.ppermute(x, "tm", [(t, t ^ k) for t in range(n_t)])

    tiles = width // LANES
    count = chips * frames * tiles
    starts = sections(rows, n_t, count)

    def time_swaps(messages):
        got = {k: over_time(messages[k], k) for k in range(n_t - 1, 0, -1)}
        return [messages[0]] + [got[k] for k in range(1, n_t)]

    pieces = over_chips(out_grad)
    kept, sent = call(
        functools.partial(cut_kernel, chips),
        [proj_weight, saved_out],
        [shape(bf16, chips, HD, width), shape(bf16, HD, chips * width + HD)],
        [pltpu.SemaphoreType.DMA((2 * chips + 1,))],
        in_place=True,
    )
    received = over_cores(sent)
    packed, _ = lax.optimization_barrier((jnp.stack([queries, saved_out]), received))
    packed_all = [packed]
    for k in range(1, n_t):
        high = 1 << (k.bit_length() - 1)
        packed_all.append(over_time(packed_all[k - high], high))
    gate_table, _ = lax.optimization_barrier((gate_table, received))
    bias, gate_a, gate_b, hot = call(
        functools.partial(masks_kernel, n_t, chips, frames, rows),
        [noise_levels, clip_lengths, gate_table],
        [
            shape(f32, frames, n_t * rows),
            shape(f32, chips, frames, width),
            shape(f32, frames, width),
            shape(f32, n_t * frames, levels, LANES),
        ],
        in_smem=2,
    )
    kept, _ = lax.optimization_barrier((kept, packed_all[1 : n_t // 2 + 1]))
    mine, other, terms, to_move = call(
        functools.partial(head_kernel, chips, frames),
        [packed, kept, received, gate_a] + pieces,
        [
            shape(f32, rows, HD),
            shape(f32, rows, HD),
            shape(f32, count, LANES),
            shape(bf16, rows, width),
        ],
        flops=4 * rows * chips * width * 2 * HD,
    )
    later_bias, _ = lax.optimization_barrier((bias, mine))
    stats = call(
        functools.partial(stats_kernel, n_t),
        [later_bias, keys] + packed_all,
        shape(f32, 2 * n_t, LANES),
        flops=2 * n_t * rows * k_rows * HD,
    )
    moves = [
        (t * n_s + s, (t ^ (s // 2)) * n_s + s) for t in range(n_t) for s in range(n_s)
    ]
    moved = lax.ppermute(to_move, ("tm", "space"), moves)
    message = call(
        functools.partial(join_kernel, starts),
        [mine, over_cores(other), stats, terms],
        shape(bf16, starts[-1], LANES),
    )
    heads_all = time_swaps([message] * n_t)
    base = tiles * rows
    bundle = call(
        functools.partial(bundle_kernel, n_t, frames, starts, count),
        [gate_b, moved] + heads_all,
        shape(bf16, base + n_t * count, LANES),
    )
    bundles = over_chips(bundle)
    later_bias, _ = lax.optimization_barrier((bias, bundle))
    outs = call(
        functools.partial(grads_kernel, n_t),
        [later_bias, keys, values] + packed_all + heads_all,
        [shape(bf16, k_rows, HD)] * 2 + [shape(bf16, HD, rows)] * n_t,
        [pltpu.VMEM((k_rows, HD), f32)] * 2,
        flops=10 * n_t * rows * k_rows * HD,
    )
    key_grad, value_grad = outs[:2]
    parts = time_swaps(outs[2:][::-1])
    bundles, _ = lax.optimization_barrier((bundles, parts[::-1]))
    collected = call(
        functools.partial(collect_kernel, chips, base),
        bundles,
        shape(bf16, chips * base + 2 * n_t * count, LANES),
        [pltpu.VMEM((chips, n_t * count, LANES), f32)],
    )
    query_grad = call(functools.partial(query_kernel, n_t), parts[::-1], shape(bf16, rows, HD))
    weight_grad, gate_grad = call(
        functools.partial(final_kernel, n_t, chips, frames),
        [hot, collected, over_cores(collected)] + packed_all,
        [shape(f32, HD, 2 * width), shape(f32, levels, n_s * width)],
        [pltpu.VMEM((n_t, rows, HD), f32), pltpu.VMEM((2, n_t, count, LANES), f32)],
        flops=4 * n_t * rows * width * HD,
    )
    if width != shard:
        weight_grad = without_padding(weight_grad, 2, shard)
        gate_grad = without_padding(gate_grad, n_s, shard)
    return (query_grad, key_grad, value_grad, weight_grad, gate_grad)


def solution(mesh):
    return jax.shard_map(
        body,
        mesh=mesh,
        in_specs=(
            P("tm", "space"),
            P("tm", "space"),
            P("tm", "space"),
            P("tm", "space"),
            P("tm", "space"),
            P("space", None),
            P(),
            P(),
            P(),
        ),
        out_specs=(P("tm", "space"), P("tm", "space"), P("tm", "space"), P("space", "tm"), P()),
        check_vma=False,
    )
```

```python
import functools
import math

import jax
import jax.numpy as jnp
from jax import lax
from jax.experimental import pallas as pl
from jax.experimental.pallas import tpu as pltpu
from jax.sharding import PartitionSpec as P

HD = 128
SPF = 512
QF = 64
LANES = 128
NEG_BIG = -1e30
SCALE = 1.0 / math.sqrt(HD)
VMEM_LIMIT = 32 * 1024 * 1024
PREP_VMEM = 52 * 1024 * 1024
SPLIT = 3


def dot(a, b, on_a, on_b):
    return lax.dot_general(
        a, b, (((on_a,), (on_b,)), ((), ())), preferred_element_type=jnp.float32
    )


def place():
    s = lax.axis_index("space")
    return lax.axis_index("tm"), s // 2, s % 2


def clip_numbers(clips_ref):
    bounds = []
    so_far = 0
    for c in range(clips_ref.shape[0]):
        so_far = so_far + clips_ref[c]
        bounds.append(so_far)
    return lambda frame: sum((frame >= bound).astype(jnp.int32) for bound in bounds)


def cut_kernel(chips, weight_in, saved_in, kept, sent, sems):
    _, chip, core = place()
    width = kept.shape[2]
    moves = [(saved_in, sent.at[:, chips * width : chips * width + HD])]
    for k in range(chips):
        for c, out in ((1 - core, sent.at[:, k * width : (k + 1) * width]), (core, kept.at[k])):
            columns = pl.ds(pl.multiple_of((2 * (chip ^ k) + c) * width, LANES), width)
            moves.append((weight_in.at[:, columns], out))
    copies = [pltpu.make_async_copy(a, b, sems.at[i]) for i, (a, b) in enumerate(moves)]
    for copy in copies:
        copy.start()
    for copy in copies:
        copy.wait()


def masks_kernel(n_t, chips, frames, rows, levels, clips, gate, bias, gate_a, gate_b, hot):
    t, chip, core = place()
    width = gate_a.shape[2]
    clip_of = clip_numbers(clips)
    lane = lax.broadcasted_iota(jnp.int32, (1, rows), 1)
    for kf in range(frames):
        key_frame = t * frames + kf
        key_clip = clip_of(key_frame)
        for k in range(n_t):
            row = jnp.full((1, rows), NEG_BIG, jnp.float32)
            for r in range(frames):
                frame = (t ^ k) * frames + r
                visible = (key_frame >= frame) & (clip_of(frame) == key_clip)
                value = jnp.where(visible, 0.0, NEG_BIG).astype(jnp.float32)
                row = jnp.where((lane >= r * QF) & (lane < (r + 1) * QF), value, row)
            bias[kf : kf + 1, k * rows : (k + 1) * rows] = row
    spot = lax.broadcasted_iota(jnp.int32, hot.shape[1:], 0)
    for f in range(n_t * frames):
        hot[f] = (spot == levels[f]).astype(jnp.float32)
    for r in range(frames):
        level = levels[t * frames + r]
        for k in range(chips):
            columns = pl.ds(pl.multiple_of((2 * (chip ^ k) + core) * width, LANES), width)
            gate_a[k, r : r + 1, :] = gate[pl.ds(level, 1), columns]
    mine = pl.ds(pl.multiple_of((2 * t + core) * width, LANES), width)
    for k in range(n_t):
        level = levels[(t ^ k) * frames + chip * (rows // chips) // QF]
        gate_b[k] = gate[pl.ds(level, 1), mine]


def stats_kernel(n_t, bias, keys, *refs):
    packed, out = refs[:n_t], refs[n_t]
    rows = packed[0].shape[1]
    for p in range(0, n_t, 2):
        q = jnp.concatenate([packed[p][0], packed[p + 1][0]], axis=0)
        scores = []
        for kf in range(bias.shape[0]):
            mask = bias[kf : kf + 1, p * rows : (p + 2) * rows]
            scores.append(dot(keys[kf * SPF : (kf + 1) * SPF, :], q, 1, 1) * SCALE + mask)
        top = functools.reduce(jnp.maximum, [jnp.max(x, axis=0, keepdims=True) for x in scores])
        total = sum(jnp.sum(jnp.exp(x - top), axis=0, keepdims=True) for x in scores)
        for i in range(2):
            out[p + i : p + i + 1, :] = top[:, i * rows : (i + 1) * rows]
            out[n_t + p + i : n_t + p + i + 1, :] = total[:, i * rows : (i + 1) * rows]


def head_kernel(chips, frames, packed, kept, received, gate_a, *refs):
    pieces, (mine, other, terms) = refs[:chips], refs[chips:]
    _, chip, _ = place()
    width = pieces[0].shape[1]
    tiles = width // LANES
    saved = jnp.concatenate([packed[1], received[:, chips * width : chips * width + HD]], axis=1)
    head = None
    for k in range(chips):
        weight = jnp.concatenate([kept[k], received[:, k * width : (k + 1) * width]], axis=0)
        wide = pieces[k][...].astype(jnp.float32)
        gated = jnp.concatenate(
            [
                (wide[r * QF : (r + 1) * QF] * gate_a[k, r : r + 1, :]).astype(jnp.bfloat16)
                for r in range(frames)
            ],
            axis=0,
        )
        part = dot(gated, weight, 1, 1)
        head = part if head is None else head + part
        product = wide * dot(saved, weight, 1, 0)
        for r in range(frames):
            term = jnp.sum(product[r * QF : (r + 1) * QF], axis=0, keepdims=True)
            for j in range(tiles):
                row = ((chip ^ k) * frames + r) * tiles + j
                terms[pl.ds(row, 1), :] = term[:, j * LANES : (j + 1) * LANES]
    mine[...] = head[:, :HD]
    other[...] = head[:, HD:]


def sections(rows, chips, tiles, n_t, count):
    starts = [0, rows]
    starts.append(starts[-1] + tiles * (rows // chips))
    starts.append(starts[-1] + -(-(SPLIT * 2 * n_t + count) // 16) * 16)
    return starts


def padded(x, rows):
    if x.shape[0] == rows:
        return x
    return jnp.concatenate([x, jnp.zeros((rows - x.shape[0], x.shape[1]), x.dtype)], axis=0)


def join_kernel(n_t, chips, starts, mine, received, stats, terms, *refs):
    pieces, outs, (wide, held) = refs[:chips], refs[chips : chips + n_t][::-1], refs[chips + n_t :]
    t, chip, _ = place()
    part, tiles = held.shape[1], held.shape[2] // LANES
    for k in range(chips):
        wide[...] = pieces[k][...].astype(jnp.float32)
        held[k] = wide[pl.ds(pl.multiple_of(chip * part, part), part), :]
    head = (mine[...] + received[...]).astype(jnp.bfloat16)
    rest = stats[...]
    split = []
    for _ in range(SPLIT):
        piece = rest.astype(jnp.bfloat16).astype(jnp.float32)
        split.append(piece)
        rest = rest - piece
    last = padded(jnp.concatenate(split + [terms[...]], axis=0), starts[3] - starts[2])
    last = last.astype(jnp.bfloat16)
    for k in range(n_t):
        rows = held[chip ^ t ^ k]
        rows = jnp.concatenate([rows[:, j * LANES : (j + 1) * LANES] for j in range(tiles)], axis=0)
        outs[k][: starts[1], :] = head
        outs[k][starts[1] : starts[2], :] = rows.astype(jnp.bfloat16)
        outs[k][starts[2] :, :] = last


def bundle_kernel(n_t, starts, count, gate_b, *refs):
    heads, out = refs[:n_t][::-1], refs[n_t]
    tiles = gate_b.shape[2] // LANES
    part = (starts[2] - starts[1]) // tiles
    wide = [heads[k][starts[1] : starts[2], :].astype(jnp.float32) for k in range(n_t)]
    for j in range(tiles):
        gated = jnp.concatenate(
            [
                wide[k][j * part : (j + 1) * part] * gate_b[k, :, j * LANES : (j + 1) * LANES]
                for k in range(n_t)
            ],
            axis=0,
        )
        out[j * n_t * part : (j + 1) * n_t * part, :] = gated.astype(jnp.bfloat16)
    first = SPLIT * 2 * n_t
    terms = [heads[k][starts[2] :, :].astype(jnp.float32)[first : first + count] for k in range(n_t)]
    out[tiles * n_t * part :, :] = jnp.concatenate(terms, axis=0).astype(jnp.bfloat16)


def collect_kernel(chips, base, *refs):
    pieces, out, held = refs[:chips], refs[chips], refs[chips + 1]
    chip = place()[1]
    for k in range(chips):
        out[k * base : (k + 1) * base, :] = pieces[k][:base, :]
        held[chip ^ k] = pieces[k][base:, :].astype(jnp.float32)
    total = held[0]
    for k in range(1, chips):
        total = total + held[k]
    high = total.astype(jnp.bfloat16)
    count = total.shape[0]
    out[chips * base : chips * base + count, :] = high
    out[chips * base + count :, :] = (total - high.astype(jnp.float32)).astype(jnp.bfloat16)


def grads_kernel(n_t, starts, bias, keys, values, *refs):
    packed, heads = refs[:n_t], refs[n_t : 2 * n_t][::-1]
    key_out, value_out = refs[2 * n_t : 2 * n_t + 2]
    outs = refs[2 * n_t + 2 : 3 * n_t + 2][::-1]
    key_acc, value_acc = refs[3 * n_t + 2 :]
    rows = packed[0].shape[1]
    ones = jnp.ones((8, HD), jnp.float32)
    keys_t = jnp.transpose(keys[...])
    stats = []
    for k in range(n_t):
        parts = heads[k][starts[2] :, :].astype(jnp.float32)
        stats.append(sum(parts[i * 2 * n_t : (i + 1) * 2 * n_t] for i in range(SPLIT)))
    for p in range(0, n_t, 2):
        q = jnp.concatenate([packed[p][0], packed[p + 1][0]], axis=0)
        o = jnp.concatenate([packed[p][1], packed[p + 1][1]], axis=0)
        g = jnp.concatenate([heads[p][:rows, :], heads[p + 1][:rows, :]], axis=0)
        delta = lax.dot_general(
            ones,
            g.astype(jnp.float32) * o.astype(jnp.float32),
            (((1,), (1,)), ((), ())),
            precision=lax.Precision.HIGHEST,
            preferred_element_type=jnp.float32,
        )[0:1]
        lse = []
        for i in (p, p + 1):
            tops = [stats[k][i ^ k : (i ^ k) + 1] for k in range(n_t)]
            sums = [stats[k][n_t + (i ^ k) : n_t + (i ^ k) + 1] for k in range(n_t)]
            top = functools.reduce(jnp.maximum, tops)
            lse.append(top + jnp.log(sum(b * jnp.exp(a - top) for a, b in zip(tops, sums))))
        lse = jnp.concatenate(lse, axis=1)
        query_part = None
        for kf in range(bias.shape[0]):
            span = slice(kf * SPF, (kf + 1) * SPF)
            shift = bias[kf : kf + 1, p * rows : (p + 2) * rows] - lse
            probs = jnp.exp(dot(keys[span, :], q, 1, 1) * SCALE + shift)
            score_grad = (probs * (dot(values[span, :], g, 1, 1) - delta)).astype(jnp.bfloat16)
            value_add = dot(probs.astype(jnp.bfloat16), g, 1, 0)
            key_add = dot(score_grad, q, 1, 0)
            if p > 0:
                value_add = value_add + value_acc[span, :]
                key_add = key_add + key_acc[span, :]
            if p + 2 < n_t:
                value_acc[span, :] = value_add
                key_acc[span, :] = key_add
            else:
                value_out[span, :] = value_add.astype(jnp.bfloat16)
                key_out[span, :] = (key_add * SCALE).astype(jnp.bfloat16)
            part = dot(keys_t[:, span], score_grad, 1, 0)
            query_part = part if query_part is None else query_part + part
        outs[p][...] = query_part[:, :rows].astype(jnp.bfloat16)
        outs[p + 1][...] = query_part[:, rows:].astype(jnp.bfloat16)


def query_kernel(n_t, *refs):
    total = refs[0][...].astype(jnp.float32)
    for k in range(1, n_t):
        total = total + refs[k][...].astype(jnp.float32)
    refs[n_t][...] = jnp.transpose(total * SCALE).astype(jnp.bfloat16)


def half_results(n_t, chips, frames, hot, ref, packed, saved, held, tiles):
    t, chip, _ = place()
    rows = saved.shape[1]
    part = rows // chips
    base = tiles * n_t * part
    for k in range(n_t):
        saved[k] = packed[k][1].astype(jnp.float32)
    ordered = []
    for c in range(chips):
        mine = pl.ds(pl.multiple_of((chip ^ c) * part, part), part)
        ordered += [saved[k, mine, :] for k in range(n_t)]
    ordered = jnp.transpose(jnp.concatenate(ordered, axis=0)).astype(jnp.bfloat16)
    gated = jnp.concatenate(
        [
            jnp.concatenate(
                [
                    ref[c * base + j * n_t * part : c * base + (j + 1) * n_t * part, :]
                    for c in range(chips)
                ],
                axis=0,
            )
            for j in range(tiles)
        ],
        axis=1,
    )
    count = (ref.shape[0] - chips * base) // 2
    each = count // n_t
    terms = ref[chips * base : chips * base + count, :].astype(jnp.float32)
    terms = terms + ref[chips * base + count :, :].astype(jnp.float32)
    for k in range(n_t):
        held[t ^ k] = terms[k * each : (k + 1) * each]

    def gate_tile(a, j):
        total = jnp.zeros(hot.shape[1:], jnp.float32)
        for f in range(n_t * frames):
            row = (a * frames + f % frames) * tiles + j
            total = total + hot[f] * held[f // frames, row : row + 1, :]
        return total

    return dot(ordered, gated, 1, 0), gate_tile


def own_kernel(n_t, chips, frames, hot, own, *refs):
    packed, (weight_out, gate_out, saved, held) = refs[:n_t], refs[n_t:]
    tiles = weight_out.shape[1] // LANES
    result, gate_tile = half_results(n_t, chips, frames, hot, own, packed, saved, held, tiles)
    weight_out[...] = result
    for a in range(chips):
        for j in range(tiles):
            gate_out[:, (a * tiles + j) * LANES : (a * tiles + j + 1) * LANES] = gate_tile(a, j)


def final_kernel(n_t, chips, frames, hot, other, own_weight, own_gate, *refs):
    packed, (weight_out, gate_out, saved, held) = refs[:n_t], refs[n_t:]
    core = place()[2]
    width = own_weight.shape[1]
    tiles = width // LANES
    result, gate_tile = half_results(n_t, chips, frames, hot, other, packed, saved, held, tiles)
    mine = own_weight[...]
    weight_out[:, :width] = jnp.where(core == 0, mine, result)
    weight_out[:, width:] = jnp.where(core == 0, result, mine)
    for a in range(chips):
        for j in range(tiles):
            first = gate_tile(a, j)
            second = own_gate[:, (a * tiles + j) * LANES : (a * tiles + j + 1) * LANES]
            column = 2 * a * width + j * LANES
            gate_out[:, column : column + LANES] = jnp.where(core == 0, second, first)
            column += width
            gate_out[:, column : column + LANES] = jnp.where(core == 0, first, second)


def call(kernel, args, out_shape, scratch=(), flops=0, in_place=False, in_smem=0):
    vmem = pl.BlockSpec(memory_space=pltpu.VMEM)
    single = not isinstance(out_shape, (list, tuple))
    nbytes = sum(a.size * a.dtype.itemsize for a in args)
    return pl.pallas_call(
        kernel,
        out_shape=out_shape,
        in_specs=[pl.BlockSpec(memory_space=pltpu.SMEM)] * in_smem
        + [pl.BlockSpec(memory_space=pltpu.HBM) if in_place else vmem] * (len(args) - in_smem),
        out_specs=vmem if single else [vmem] * len(out_shape),
        scratch_shapes=list(scratch),
        compiler_params=pltpu.CompilerParams(vmem_limit_bytes=PREP_VMEM if in_place else VMEM_LIMIT),
        cost_estimate=pl.CostEstimate(flops=flops, bytes_accessed=nbytes, transcendentals=0),
    )(*args)


def padded_shards(table, n_s, width):
    rows, columns = table.shape
    cut = table.reshape(rows, n_s, columns // n_s)
    cut = jnp.pad(cut, ((0, 0), (0, 0), (0, width - columns // n_s)))
    return cut.reshape(rows, n_s * width)


def without_padding(table, shards, shard):
    rows, columns = table.shape
    return table.reshape(rows, shards, columns // shards)[:, :, :shard].reshape(rows, shards * shard)


def body(
    queries, keys, values, saved_out, out_grad, proj_weight, gate_table, noise_levels, clip_lengths
):
    n_t, n_s = lax.axis_size("tm"), lax.axis_size("space")
    chips = n_s // 2
    rows, shard = out_grad.shape
    k_rows = keys.shape[0]
    frames = rows // QF
    levels = gate_table.shape[0]
    bf16, f32 = jnp.bfloat16, jnp.float32
    width = -(-shard // LANES) * LANES
    if width != shard:
        out_grad = jnp.pad(out_grad, ((0, 0), (0, width - shard)))
        proj_weight = padded_shards(proj_weight, n_s, width)
        gate_table = padded_shards(gate_table, n_s, width)

    def shape(dtype, *dims):
        return jax.ShapeDtypeStruct(dims, dtype)

    def over_chips(x):
        return [x] + [
            lax.ppermute(x, "space", [(s, s ^ (2 * k)) for s in range(n_s)]) for k in range(1, chips)
        ]

    def over_cores(x):
        return lax.ppermute(x, "space", [(s, s ^ 1) for s in range(n_s)])

    def over_time(x, k):
        return lax.ppermute(x, "tm", [(t, t ^ k) for t in range(n_t)])

    tiles = width // LANES
    part = rows // chips
    count = chips * frames * tiles
    starts = sections(rows, chips, tiles, n_t, count)

    def time_swaps(messages):
        got = {k: over_time(messages[k], k) for k in range(n_t - 1, 0, -1)}
        return [messages[0]] + [got[k] for k in range(1, n_t)]

    pieces = over_chips(out_grad)
    kept, sent = call(
        functools.partial(cut_kernel, chips),
        [proj_weight, saved_out],
        [shape(bf16, chips, HD, width), shape(bf16, HD, chips * width + HD)],
        [pltpu.SemaphoreType.DMA((2 * chips + 1,))],
        in_place=True,
    )
    received = over_cores(sent)
    packed, _ = lax.optimization_barrier((jnp.stack([queries, saved_out]), received))
    packed_all = [packed]
    for k in range(1, n_t):
        low = k & -k
        packed_all.append(over_time(packed_all[k - low], low))
    gate_table, _ = lax.optimization_barrier((gate_table, received))
    bias, gate_a, gate_b, hot = call(
        functools.partial(masks_kernel, n_t, chips, frames, rows),
        [noise_levels, clip_lengths, gate_table],
        [
            shape(f32, frames, n_t * rows),
            shape(f32, chips, frames, width),
            shape(f32, n_t, 1, width),
            shape(f32, n_t * frames, levels, LANES),
        ],
        in_smem=2,
    )
    mine, other, terms = call(
        functools.partial(head_kernel, chips, frames),
        [packed, kept, received, gate_a] + pieces,
        [shape(f32, rows, HD), shape(f32, rows, HD), shape(f32, count, LANES)],
        flops=4 * rows * chips * width * 2 * HD,
    )
    later_bias, _ = lax.optimization_barrier((bias, mine))
    stats = call(
        functools.partial(stats_kernel, n_t),
        [later_bias, keys] + packed_all,
        shape(f32, 2 * n_t, LANES),
        flops=2 * n_t * rows * k_rows * HD,
    )
    heads = call(
        functools.partial(join_kernel, n_t, chips, starts),
        [mine, over_cores(other), stats, terms] + pieces,
        [shape(bf16, starts[-1], LANES)] * n_t,
        [pltpu.VMEM((rows, width), f32), pltpu.VMEM((chips, part, width), f32)],
    )
    heads_all = time_swaps(heads[::-1])
    base = tiles * n_t * part
    bundle = call(
        functools.partial(bundle_kernel, n_t, starts, count),
        [gate_b] + heads_all[::-1],
        shape(bf16, base + n_t * count, LANES),
    )
    bundles = over_chips(bundle)
    later_bias, _ = lax.optimization_barrier((bias, bundle))
    outs = call(
        functools.partial(grads_kernel, n_t, starts),
        [later_bias, keys, values] + packed_all + heads_all[::-1],
        [shape(bf16, k_rows, HD)] * 2 + [shape(bf16, HD, rows)] * n_t,
        [pltpu.VMEM((k_rows, HD), f32)] * 2,
        flops=10 * n_t * rows * k_rows * HD,
    )
    key_grad, value_grad = outs[:2]
    parts = time_swaps(outs[2:][::-1])
    bundles, _ = lax.optimization_barrier((bundles, parts[::-1]))
    collected = call(
        functools.partial(collect_kernel, chips, base),
        bundles,
        shape(bf16, chips * base + 2 * n_t * count, LANES),
        [pltpu.VMEM((chips, n_t * count, LANES), f32)],
    )
    query_grad = call(functools.partial(query_kernel, n_t), parts[::-1], shape(bf16, rows, HD))
    scratch = [pltpu.VMEM((n_t, rows, HD), f32), pltpu.VMEM((n_t, count, LANES), f32)]
    own_halves = call(
        functools.partial(own_kernel, n_t, chips, frames),
        [hot, collected] + packed_all,
        [shape(f32, HD, width), shape(f32, levels, chips * width)],
        scratch,
        flops=2 * n_t * rows * width * HD,
    )
    weight_grad, gate_grad = call(
        functools.partial(final_kernel, n_t, chips, frames),
        [hot, over_cores(collected), *own_halves] + packed_all,
        [shape(f32, HD, 2 * width), shape(f32, levels, n_s * width)],
        scratch,
        flops=2 * n_t * rows * width * HD,
    )
    if width != shard:
        weight_grad = without_padding(weight_grad, 2, shard)
        gate_grad = without_padding(gate_grad, n_s, shard)
    return (query_grad, key_grad, value_grad, weight_grad, gate_grad)


def solution(mesh):
    return jax.shard_map(
        body,
        mesh=mesh,
        in_specs=(
            P("tm", "space"),
            P("tm", "space"),
            P("tm", "space"),
            P("tm", "space"),
            P("tm", "space"),
            P("space", None),
            P(),
            P(),
            P(),
        ),
        out_specs=(P("tm", "space"), P("tm", "space"), P("tm", "space"), P("space", "tm"), P()),
        check_vma=False,
    )
```

```python
import functools
import math

import jax
import jax.numpy as jnp
from jax import lax
from jax.experimental import pallas as pl
from jax.experimental.pallas import tpu as pltpu
from jax.sharding import PartitionSpec as P

HD = 128
SPF = 512
QF = 64
LANES = 128
NEG_BIG = -1e30
SCALE = 1.0 / math.sqrt(HD)
VMEM_LIMIT = 32 * 1024 * 1024
PREP_VMEM = 52 * 1024 * 1024
SPLIT = 3


def dot(a, b, on_a, on_b):
    return lax.dot_general(
        a, b, (((on_a,), (on_b,)), ((), ())), preferred_element_type=jnp.float32
    )


def place():
    s = lax.axis_index("space")
    return lax.axis_index("tm"), s // 2, s % 2


def clip_numbers(clips_ref):
    bounds = []
    so_far = 0
    for c in range(clips_ref.shape[0]):
        so_far = so_far + clips_ref[c]
        bounds.append(so_far)
    return lambda frame: sum((frame >= bound).astype(jnp.int32) for bound in bounds)


def cut_kernel(chips, weight_in, saved_in, kept, sent, sems):
    _, chip, core = place()
    width = kept.shape[2]
    moves = [(saved_in, sent.at[:, chips * width : chips * width + HD])]
    for k in range(chips):
        for c, out in ((1 - core, sent.at[:, k * width : (k + 1) * width]), (core, kept.at[k])):
            columns = pl.ds(pl.multiple_of((2 * (chip ^ k) + c) * width, LANES), width)
            moves.append((weight_in.at[:, columns], out))
    copies = [pltpu.make_async_copy(a, b, sems.at[i]) for i, (a, b) in enumerate(moves)]
    for copy in copies:
        copy.start()
    for copy in copies:
        copy.wait()


def masks_kernel(n_t, chips, frames, rows, levels, clips, gate, bias, gate_a, gate_b, hot):
    t, chip, core = place()
    width = gate_a.shape[2]
    clip_of = clip_numbers(clips)
    lane = lax.broadcasted_iota(jnp.int32, (1, rows), 1)
    for kf in range(frames):
        key_frame = t * frames + kf
        key_clip = clip_of(key_frame)
        for k in range(n_t):
            row = jnp.full((1, rows), NEG_BIG, jnp.float32)
            for r in range(frames):
                frame = (t ^ k) * frames + r
                visible = (key_frame >= frame) & (clip_of(frame) == key_clip)
                value = jnp.where(visible, 0.0, NEG_BIG).astype(jnp.float32)
                row = jnp.where((lane >= r * QF) & (lane < (r + 1) * QF), value, row)
            bias[kf : kf + 1, k * rows : (k + 1) * rows] = row
    spot = lax.broadcasted_iota(jnp.int32, hot.shape[1:], 0)
    for f in range(n_t * frames):
        hot[f] = (spot == levels[f]).astype(jnp.float32)
    for r in range(frames):
        level = levels[t * frames + r]
        for k in range(chips):
            columns = pl.ds(pl.multiple_of((2 * (chip ^ k) + core) * width, LANES), width)
            gate_a[k, r : r + 1, :] = gate[pl.ds(level, 1), columns]
    mine = pl.ds(pl.multiple_of((2 * t + core) * width, LANES), width)
    for k in range(n_t):
        level = levels[(t ^ k) * frames + chip * (rows // chips) // QF]
        gate_b[k] = gate[pl.ds(level, 1), mine]


def stats_kernel(n_t, bias, keys, *refs):
    packed, out = refs[:n_t], refs[n_t]
    rows = packed[0].shape[1]
    for p in range(0, n_t, 2):
        q = jnp.concatenate([packed[p][0], packed[p + 1][0]], axis=0)
        scores = []
        for kf in range(bias.shape[0]):
            mask = bias[kf : kf + 1, p * rows : (p + 2) * rows]
            scores.append(dot(keys[kf * SPF : (kf + 1) * SPF, :], q, 1, 1) * SCALE + mask)
        top = functools.reduce(jnp.maximum, [jnp.max(x, axis=0, keepdims=True) for x in scores])
        total = sum(jnp.sum(jnp.exp(x - top), axis=0, keepdims=True) for x in scores)
        for i in range(2):
            out[p + i : p + i + 1, :] = top[:, i * rows : (i + 1) * rows]
            out[n_t + p + i : n_t + p + i + 1, :] = total[:, i * rows : (i + 1) * rows]


def head_kernel(chips, frames, packed, kept, received, gate_a, *refs):
    pieces, (mine, other) = refs[:chips], refs[chips : chips + 2]
    messages, (terms, whole, held) = refs[chips + 2 : -3][::-1], refs[-3:]
    t, chip, _ = place()
    width = pieces[0].shape[1]
    tiles = width // LANES
    part = held.shape[1]
    saved = jnp.concatenate([packed[1], received[:, chips * width : chips * width + HD]], axis=1)
    head = None
    for k in range(chips):
        weight = jnp.concatenate([kept[k], received[:, k * width : (k + 1) * width]], axis=0)
        wide = pieces[k][...].astype(jnp.float32)
        whole[...] = wide
        held[k] = whole[pl.ds(pl.multiple_of(chip * part, part), part), :]
        gated = jnp.concatenate(
            [
                (wide[r * QF : (r + 1) * QF] * gate_a[k, r : r + 1, :]).astype(jnp.bfloat16)
                for r in range(frames)
            ],
            axis=0,
        )
        add = dot(gated, weight, 1, 1)
        head = add if head is None else head + add
        product = wide * dot(saved, weight, 1, 0)
        for r in range(frames):
            term = jnp.sum(product[r * QF : (r + 1) * QF], axis=0, keepdims=True)
            for j in range(tiles):
                row = ((chip ^ k) * frames + r) * tiles + j
                terms[pl.ds(row, 1), :] = term[:, j * LANES : (j + 1) * LANES]
    mine[...] = head[:, :HD]
    other[...] = head[:, HD:]
    for k in range(chips):
        rows = held[chip ^ t ^ k]
        rows = [rows[:, j * LANES : (j + 1) * LANES] for j in range(tiles)]
        out = padded(jnp.concatenate(rows + [terms[...]], axis=0), messages[k].shape[0])
        messages[k][...] = out.astype(jnp.bfloat16)


def padded(x, rows):
    if x.shape[0] == rows:
        return x
    return jnp.concatenate([x, jnp.zeros((rows - x.shape[0], x.shape[1]), x.dtype)], axis=0)


def join_kernel(mine, received, stats, out):
    rows = mine.shape[0]
    out[:rows, :] = (mine[...] + received[...]).astype(jnp.bfloat16)
    rest = stats[...]
    split = []
    for _ in range(SPLIT):
        piece = rest.astype(jnp.bfloat16).astype(jnp.float32)
        split.append(piece)
        rest = rest - piece
    split = padded(jnp.concatenate(split, axis=0), out.shape[0] - rows)
    out[rows:, :] = split.astype(jnp.bfloat16)


def bundle_kernel(n_t, part, count, gate_b, *refs):
    messages, out = refs[:n_t], refs[n_t]
    tiles = gate_b.shape[2] // LANES
    wide = [messages[k][...].astype(jnp.float32) for k in range(n_t)]
    for j in range(tiles):
        gated = jnp.concatenate(
            [
                wide[k][j * part : (j + 1) * part] * gate_b[k, :, j * LANES : (j + 1) * LANES]
                for k in range(n_t)
            ],
            axis=0,
        )
        out[j * n_t * part : (j + 1) * n_t * part, :] = gated.astype(jnp.bfloat16)
    terms = [wide[k][tiles * part : tiles * part + count] for k in range(n_t)]
    out[tiles * n_t * part :, :] = jnp.concatenate(terms, axis=0).astype(jnp.bfloat16)


def collect_kernel(chips, base, *refs):
    pieces, out, held = refs[:chips], refs[chips], refs[chips + 1]
    chip = place()[1]
    for k in range(chips):
        out[k * base : (k + 1) * base, :] = pieces[k][:base, :]
        held[chip ^ k] = pieces[k][base:, :].astype(jnp.float32)
    total = held[0]
    for k in range(1, chips):
        total = total + held[k]
    high = total.astype(jnp.bfloat16)
    count = total.shape[0]
    out[chips * base : chips * base + count, :] = high
    out[chips * base + count :, :] = (total - high.astype(jnp.float32)).astype(jnp.bfloat16)


def grads_kernel(n_t, bias, keys, values, *refs):
    packed, heads = refs[:n_t], refs[n_t : 2 * n_t]
    key_out, value_out = refs[2 * n_t : 2 * n_t + 2]
    outs = refs[2 * n_t + 2 : 3 * n_t + 2][::-1]
    key_acc, value_acc = refs[3 * n_t + 2 :]
    rows = packed[0].shape[1]
    ones = jnp.ones((8, HD), jnp.float32)
    keys_t = jnp.transpose(keys[...])
    stats = []
    for k in range(n_t):
        parts = heads[k][rows:, :].astype(jnp.float32)
        stats.append(sum(parts[i * 2 * n_t : (i + 1) * 2 * n_t] for i in range(SPLIT)))
    for p in range(0, n_t, 2):
        q = jnp.concatenate([packed[p][0], packed[p + 1][0]], axis=0)
        o = jnp.concatenate([packed[p][1], packed[p + 1][1]], axis=0)
        g = jnp.concatenate([heads[p][:rows, :], heads[p + 1][:rows, :]], axis=0)
        delta = lax.dot_general(
            ones,
            g.astype(jnp.float32) * o.astype(jnp.float32),
            (((1,), (1,)), ((), ())),
            precision=lax.Precision.HIGHEST,
            preferred_element_type=jnp.float32,
        )[0:1]
        lse = []
        for i in (p, p + 1):
            tops = [stats[k][i ^ k : (i ^ k) + 1] for k in range(n_t)]
            sums = [stats[k][n_t + (i ^ k) : n_t + (i ^ k) + 1] for k in range(n_t)]
            top = functools.reduce(jnp.maximum, tops)
            lse.append(top + jnp.log(sum(b * jnp.exp(a - top) for a, b in zip(tops, sums))))
        lse = jnp.concatenate(lse, axis=1)
        query_part = None
        for kf in range(bias.shape[0]):
            span = slice(kf * SPF, (kf + 1) * SPF)
            shift = bias[kf : kf + 1, p * rows : (p + 2) * rows] - lse
            probs = jnp.exp(dot(keys[span, :], q, 1, 1) * SCALE + shift)
            score_grad = (probs * (dot(values[span, :], g, 1, 1) - delta)).astype(jnp.bfloat16)
            value_add = dot(probs.astype(jnp.bfloat16), g, 1, 0)
            key_add = dot(score_grad, q, 1, 0)
            if p > 0:
                value_add = value_add + value_acc[span, :]
                key_add = key_add + key_acc[span, :]
            if p + 2 < n_t:
                value_acc[span, :] = value_add
                key_acc[span, :] = key_add
            else:
                value_out[span, :] = value_add.astype(jnp.bfloat16)
                key_out[span, :] = (key_add * SCALE).astype(jnp.bfloat16)
            part = dot(keys_t[:, span], score_grad, 1, 0)
            query_part = part if query_part is None else query_part + part
        outs[p][...] = query_part[:, :rows].astype(jnp.bfloat16)
        outs[p + 1][...] = query_part[:, rows:].astype(jnp.bfloat16)


def query_kernel(n_t, *refs):
    total = refs[0][...].astype(jnp.float32)
    for k in range(1, n_t):
        total = total + refs[k][...].astype(jnp.float32)
    refs[n_t][...] = jnp.transpose(total * SCALE).astype(jnp.bfloat16)


def half_results(n_t, chips, frames, hot, ref, packed, saved, held, tiles):
    t, chip, _ = place()
    rows = saved.shape[1]
    part = rows // chips
    base = tiles * n_t * part
    for k in range(n_t):
        saved[k] = packed[k][1].astype(jnp.float32)
    ordered = []
    for c in range(chips):
        mine = pl.ds(pl.multiple_of((chip ^ c) * part, part), part)
        ordered += [saved[k, mine, :] for k in range(n_t)]
    ordered = jnp.transpose(jnp.concatenate(ordered, axis=0)).astype(jnp.bfloat16)
    gated = jnp.concatenate(
        [
            jnp.concatenate(
                [
                    ref[c * base + j * n_t * part : c * base + (j + 1) * n_t * part, :]
                    for c in range(chips)
                ],
                axis=0,
            )
            for j in range(tiles)
        ],
        axis=1,
    )
    count = (ref.shape[0] - chips * base) // 2
    each = count // n_t
    terms = ref[chips * base : chips * base + count, :].astype(jnp.float32)
    terms = terms + ref[chips * base + count :, :].astype(jnp.float32)
    for k in range(n_t):
        held[t ^ k] = terms[k * each : (k + 1) * each]

    def gate_tile(a, j):
        total = jnp.zeros(hot.shape[1:], jnp.float32)
        for f in range(n_t * frames):
            row = (a * frames + f % frames) * tiles + j
            total = total + hot[f] * held[f // frames, row : row + 1, :]
        return total

    return dot(ordered, gated, 1, 0), gate_tile


def own_kernel(n_t, chips, frames, hot, own, *refs):
    packed, (weight_out, gate_out, saved, held) = refs[:n_t], refs[n_t:]
    tiles = weight_out.shape[1] // LANES
    result, gate_tile = half_results(n_t, chips, frames, hot, own, packed, saved, held, tiles)
    weight_out[...] = result
    for a in range(chips):
        for j in range(tiles):
            gate_out[:, (a * tiles + j) * LANES : (a * tiles + j + 1) * LANES] = gate_tile(a, j)


def final_kernel(n_t, chips, frames, hot, other, own_weight, own_gate, *refs):
    packed, (weight_out, gate_out, saved, held) = refs[:n_t], refs[n_t:]
    core = place()[2]
    width = own_weight.shape[1]
    tiles = width // LANES
    result, gate_tile = half_results(n_t, chips, frames, hot, other, packed, saved, held, tiles)
    mine = own_weight[...]
    weight_out[:, :width] = jnp.where(core == 0, mine, result)
    weight_out[:, width:] = jnp.where(core == 0, result, mine)
    for a in range(chips):
        for j in range(tiles):
            first = gate_tile(a, j)
            second = own_gate[:, (a * tiles + j) * LANES : (a * tiles + j + 1) * LANES]
            column = 2 * a * width + j * LANES
            gate_out[:, column : column + LANES] = jnp.where(core == 0, second, first)
            column += width
            gate_out[:, column : column + LANES] = jnp.where(core == 0, first, second)


def call(kernel, args, out_shape, scratch=(), flops=0, in_place=False, in_smem=0):
    vmem = pl.BlockSpec(memory_space=pltpu.VMEM)
    single = not isinstance(out_shape, (list, tuple))
    nbytes = sum(a.size * a.dtype.itemsize for a in args)
    return pl.pallas_call(
        kernel,
        out_shape=out_shape,
        in_specs=[pl.BlockSpec(memory_space=pltpu.SMEM)] * in_smem
        + [pl.BlockSpec(memory_space=pltpu.HBM) if in_place else vmem] * (len(args) - in_smem),
        out_specs=vmem if single else [vmem] * len(out_shape),
        scratch_shapes=list(scratch),
        compiler_params=pltpu.CompilerParams(vmem_limit_bytes=PREP_VMEM if in_place else VMEM_LIMIT),
        cost_estimate=pl.CostEstimate(flops=flops, bytes_accessed=nbytes, transcendentals=0),
    )(*args)


def padded_shards(table, n_s, width):
    rows, columns = table.shape
    cut = table.reshape(rows, n_s, columns // n_s)
    cut = jnp.pad(cut, ((0, 0), (0, 0), (0, width - columns // n_s)))
    return cut.reshape(rows, n_s * width)


def without_padding(table, shards, shard):
    rows, columns = table.shape
    return table.reshape(rows, shards, columns // shards)[:, :, :shard].reshape(rows, shards * shard)


def body(
    queries, keys, values, saved_out, out_grad, proj_weight, gate_table, noise_levels, clip_lengths
):
    n_t, n_s = lax.axis_size("tm"), lax.axis_size("space")
    chips = n_s // 2
    rows, shard = out_grad.shape
    k_rows = keys.shape[0]
    frames = rows // QF
    levels = gate_table.shape[0]
    bf16, f32 = jnp.bfloat16, jnp.float32
    width = -(-shard // LANES) * LANES
    if width != shard:
        out_grad = jnp.pad(out_grad, ((0, 0), (0, width - shard)))
        proj_weight = padded_shards(proj_weight, n_s, width)
        gate_table = padded_shards(gate_table, n_s, width)

    def shape(dtype, *dims):
        return jax.ShapeDtypeStruct(dims, dtype)

    def over_chips(x):
        return [x] + [
            lax.ppermute(x, "space", [(s, s ^ (2 * k)) for s in range(n_s)]) for k in range(1, chips)
        ]

    def over_cores(x):
        return lax.ppermute(x, "space", [(s, s ^ 1) for s in range(n_s)])

    def over_time(x, k):
        return lax.ppermute(x, "tm", [(t, t ^ k) for t in range(n_t)])

    tiles = width // LANES
    part = rows // chips
    count = chips * frames * tiles

    def time_swaps(messages):
        got = {k: over_time(messages[k], k) for k in range(n_t - 1, 0, -1)}
        return [messages[0]] + [got[k] for k in range(1, n_t)]

    pieces = over_chips(out_grad)
    kept, sent = call(
        functools.partial(cut_kernel, chips),
        [proj_weight, saved_out],
        [shape(bf16, chips, HD, width), shape(bf16, HD, chips * width + HD)],
        [pltpu.SemaphoreType.DMA((2 * chips + 1,))],
        in_place=True,
    )
    received = over_cores(sent)
    packed, _ = lax.optimization_barrier((jnp.stack([queries, saved_out]), received))
    packed_all = [packed]
    for k in range(1, n_t):
        low = k & -k
        packed_all.append(over_time(packed_all[k - low], low))
    gate_table, _ = lax.optimization_barrier((gate_table, received))
    bias, gate_a, gate_b, hot = call(
        functools.partial(masks_kernel, n_t, chips, frames, rows),
        [noise_levels, clip_lengths, gate_table],
        [
            shape(f32, frames, n_t * rows),
            shape(f32, chips, frames, width),
            shape(f32, n_t, 1, width),
            shape(f32, n_t * frames, levels, LANES),
        ],
        in_smem=2,
    )
    base = tiles * n_t * part
    length = -(-(tiles * part + count) // 16) * 16
    mine, other, *shares = call(
        functools.partial(head_kernel, chips, frames),
        [packed, kept, received, gate_a] + pieces,
        [shape(f32, rows, HD)] * 2 + [shape(bf16, length, LANES)] * n_t,
        [
            pltpu.VMEM((count, LANES), f32),
            pltpu.VMEM((rows, width), f32),
            pltpu.VMEM((chips, part, width), f32),
        ],
        flops=4 * rows * chips * width * 2 * HD,
    )
    shares = time_swaps(shares[::-1])
    later_bias, _ = lax.optimization_barrier((bias, mine))
    stats = call(
        functools.partial(stats_kernel, n_t),
        [later_bias, keys] + packed_all,
        shape(f32, 2 * n_t, LANES),
        flops=2 * n_t * rows * k_rows * HD,
    )
    message = call(
        join_kernel,
        [mine, over_cores(other), stats],
        shape(bf16, rows + -(-SPLIT * 2 * n_t // 16) * 16, LANES),
    )
    heads_all = time_swaps([message] * n_t)
    bundle = call(
        functools.partial(bundle_kernel, n_t, part, count),
        [gate_b] + shares,
        shape(bf16, base + n_t * count, LANES),
    )
    bundles = over_chips(bundle)
    later_bias, _ = lax.optimization_barrier((bias, bundle))
    outs = call(
        functools.partial(grads_kernel, n_t),
        [later_bias, keys, values] + packed_all + heads_all,
        [shape(bf16, k_rows, HD)] * 2 + [shape(bf16, HD, rows)] * n_t,
        [pltpu.VMEM((k_rows, HD), f32)] * 2,
        flops=10 * n_t * rows * k_rows * HD,
    )
    key_grad, value_grad = outs[:2]
    parts = time_swaps(outs[2:][::-1])
    bundles, _ = lax.optimization_barrier((bundles, parts[::-1]))
    collected = call(
        functools.partial(collect_kernel, chips, base),
        bundles,
        shape(bf16, chips * base + 2 * n_t * count, LANES),
        [pltpu.VMEM((chips, n_t * count, LANES), f32)],
    )
    query_grad = call(functools.partial(query_kernel, n_t), parts[::-1], shape(bf16, rows, HD))
    scratch = [pltpu.VMEM((n_t, rows, HD), f32), pltpu.VMEM((n_t, count, LANES), f32)]
    own_halves = call(
        functools.partial(own_kernel, n_t, chips, frames),
        [hot, collected] + packed_all,
        [shape(f32, HD, width), shape(f32, levels, chips * width)],
        scratch,
        flops=2 * n_t * rows * width * HD,
    )
    weight_grad, gate_grad = call(
        functools.partial(final_kernel, n_t, chips, frames),
        [hot, over_cores(collected), *own_halves] + packed_all,
        [shape(f32, HD, 2 * width), shape(f32, levels, n_s * width)],
        scratch,
        flops=2 * n_t * rows * width * HD,
    )
    if width != shard:
        weight_grad = without_padding(weight_grad, 2, shard)
        gate_grad = without_padding(gate_grad, n_s, shard)
    return (query_grad, key_grad, value_grad, weight_grad, gate_grad)


def solution(mesh):
    return jax.shard_map(
        body,
        mesh=mesh,
        in_specs=(
            P("tm", "space"),
            P("tm", "space"),
            P("tm", "space"),
            P("tm", "space"),
            P("tm", "space"),
            P("space", None),
            P(),
            P(),
            P(),
        ),
        out_specs=(P("tm", "space"), P("tm", "space"), P("tm", "space"), P("space", "tm"), P()),
        check_vma=False,
    )
```

```python
import functools
import math

import jax
import jax.numpy as jnp
from jax import lax
from jax.experimental import pallas as pl
from jax.experimental.pallas import tpu as pltpu
from jax.sharding import PartitionSpec as P

HD = 128
SPF = 512
QF = 64
LANES = 128
NEG_BIG = -1e30
SCALE = 1.0 / math.sqrt(HD)
VMEM_LIMIT = 32 * 1024 * 1024
PREP_VMEM = 52 * 1024 * 1024
SPLIT = 3


def dot(a, b, on_a, on_b):
    return lax.dot_general(
        a, b, (((on_a,), (on_b,)), ((), ())), preferred_element_type=jnp.float32
    )


def place():
    s = lax.axis_index("space")
    return lax.axis_index("tm"), s // 2, s % 2


def clip_numbers(clips_ref):
    bounds = []
    so_far = 0
    for c in range(clips_ref.shape[0]):
        so_far = so_far + clips_ref[c]
        bounds.append(so_far)
    return lambda frame: sum((frame >= bound).astype(jnp.int32) for bound in bounds)


def cut_kernel(chips, weight_in, saved_in, kept, sent, sems):
    _, chip, core = place()
    width = kept.shape[2]
    moves = [(saved_in, sent.at[:, chips * width : chips * width + HD])]
    for k in range(chips):
        for c, out in ((1 - core, sent.at[:, k * width : (k + 1) * width]), (core, kept.at[k])):
            columns = pl.ds(pl.multiple_of((2 * (chip ^ k) + c) * width, LANES), width)
            moves.append((weight_in.at[:, columns], out))
    copies = [pltpu.make_async_copy(a, b, sems.at[i]) for i, (a, b) in enumerate(moves)]
    for copy in copies:
        copy.start()
    for copy in copies:
        copy.wait()


def masks_kernel(n_t, chips, frames, rows, levels, clips, gate, bias, gate_a, gate_b, hot):
    t, chip, core = place()
    width = gate_a.shape[2]
    clip_of = clip_numbers(clips)
    lane = lax.broadcasted_iota(jnp.int32, (1, rows), 1)
    for kf in range(frames):
        key_frame = t * frames + kf
        key_clip = clip_of(key_frame)
        for k in range(n_t):
            row = jnp.full((1, rows), NEG_BIG, jnp.float32)
            for r in range(frames):
                frame = (t ^ k) * frames + r
                visible = (key_frame >= frame) & (clip_of(frame) == key_clip)
                value = jnp.where(visible, 0.0, NEG_BIG).astype(jnp.float32)
                row = jnp.where((lane >= r * QF) & (lane < (r + 1) * QF), value, row)
            bias[kf : kf + 1, k * rows : (k + 1) * rows] = row
    spot = lax.broadcasted_iota(jnp.int32, hot.shape[1:], 0)
    for f in range(n_t * frames):
        hot[f] = (spot == levels[f]).astype(jnp.float32)
    for r in range(frames):
        level = levels[t * frames + r]
        for k in range(chips):
            columns = pl.ds(pl.multiple_of((2 * (chip ^ k) + core) * width, LANES), width)
            gate_a[k, r : r + 1, :] = gate[pl.ds(level, 1), columns]
    mine = pl.ds(pl.multiple_of((2 * t + core) * width, LANES), width)
    for k in range(n_t):
        level = levels[(t ^ k) * frames + chip * (rows // chips) // QF]
        gate_b[k] = gate[pl.ds(level, 1), mine]


def stats_kernel(n_t, bias, keys, *refs):
    packed, out = refs[:n_t], refs[n_t]
    rows = packed[0].shape[1]
    for p in range(0, n_t, 2):
        q = jnp.concatenate([packed[p][0], packed[p + 1][0]], axis=0)
        scores = []
        for kf in range(bias.shape[0]):
            mask = bias[kf : kf + 1, p * rows : (p + 2) * rows]
            scores.append(dot(keys[kf * SPF : (kf + 1) * SPF, :], q, 1, 1) * SCALE + mask)
        top = functools.reduce(jnp.maximum, [jnp.max(x, axis=0, keepdims=True) for x in scores])
        total = sum(jnp.sum(jnp.exp(x - top), axis=0, keepdims=True) for x in scores)
        for i in range(2):
            out[p + i : p + i + 1, :] = top[:, i * rows : (i + 1) * rows]
            out[n_t + p + i : n_t + p + i + 1, :] = total[:, i * rows : (i + 1) * rows]


def head_kernel(chips, frames, packed, kept, received, gate_a, *refs):
    pieces, (mine, other, terms) = refs[:chips], refs[chips:]
    _, chip, _ = place()
    width = pieces[0].shape[1]
    tiles = width // LANES
    saved = jnp.concatenate([packed[1], received[:, chips * width : chips * width + HD]], axis=1)
    head = None
    for k in range(chips):
        weight = jnp.concatenate([kept[k], received[:, k * width : (k + 1) * width]], axis=0)
        wide = pieces[k][...].astype(jnp.float32)
        gated = jnp.concatenate(
            [
                (wide[r * QF : (r + 1) * QF] * gate_a[k, r : r + 1, :]).astype(jnp.bfloat16)
                for r in range(frames)
            ],
            axis=0,
        )
        part = dot(gated, weight, 1, 1)
        head = part if head is None else head + part
        product = wide * dot(saved, weight, 1, 0)
        for r in range(frames):
            term = jnp.sum(product[r * QF : (r + 1) * QF], axis=0, keepdims=True)
            for j in range(tiles):
                row = ((chip ^ k) * frames + r) * tiles + j
                terms[pl.ds(row, 1), :] = term[:, j * LANES : (j + 1) * LANES]
    mine[...] = head[:, :HD]
    other[...] = head[:, HD:]


def sections(rows, chips, tiles, n_t, count):
    starts = [0, rows]
    starts.append(starts[-1] + tiles * (rows // chips))
    starts.append(starts[-1] + -(-(SPLIT * 2 * n_t + count) // 16) * 16)
    return starts


def padded(x, rows):
    if x.shape[0] == rows:
        return x
    return jnp.concatenate([x, jnp.zeros((rows - x.shape[0], x.shape[1]), x.dtype)], axis=0)


def join_kernel(n_t, chips, starts, mine, received, stats, terms, *refs):
    pieces, outs, (wide, held) = refs[:chips], refs[chips : chips + n_t][::-1], refs[chips + n_t :]
    t, chip, _ = place()
    part, tiles = held.shape[1], held.shape[2] // LANES
    for k in range(chips):
        wide[...] = pieces[k][...].astype(jnp.float32)
        held[k] = wide[pl.ds(pl.multiple_of(chip * part, part), part), :]
    head = (mine[...] + received[...]).astype(jnp.bfloat16)
    rest = stats[...]
    split = []
    for _ in range(SPLIT):
        piece = rest.astype(jnp.bfloat16).astype(jnp.float32)
        split.append(piece)
        rest = rest - piece
    last = padded(jnp.concatenate(split + [terms[...]], axis=0), starts[3] - starts[2])
    last = last.astype(jnp.bfloat16)
    for k in range(n_t):
        rows = held[chip ^ t ^ k]
        rows = jnp.concatenate([rows[:, j * LANES : (j + 1) * LANES] for j in range(tiles)], axis=0)
        outs[k][: starts[1], :] = head
        outs[k][starts[1] : starts[2], :] = rows.astype(jnp.bfloat16)
        outs[k][starts[2] :, :] = last


def bundle_kernel(n_t, starts, count, gate_b, *refs):
    heads, out = refs[:n_t][::-1], refs[n_t]
    tiles = gate_b.shape[2] // LANES
    part = (starts[2] - starts[1]) // tiles
    wide = [heads[k][starts[1] : starts[2], :].astype(jnp.float32) for k in range(n_t)]
    for j in range(tiles):
        gated = jnp.concatenate(
            [
                wide[k][j * part : (j + 1) * part] * gate_b[k, :, j * LANES : (j + 1) * LANES]
                for k in range(n_t)
            ],
            axis=0,
        )
        out[j * n_t * part : (j + 1) * n_t * part, :] = gated.astype(jnp.bfloat16)
    first = SPLIT * 2 * n_t
    terms = [heads[k][starts[2] :, :].astype(jnp.float32)[first : first + count] for k in range(n_t)]
    out[tiles * n_t * part :, :] = jnp.concatenate(terms, axis=0).astype(jnp.bfloat16)


def collect_kernel(chips, base, *refs):
    pieces, out, held = refs[:chips], refs[chips], refs[chips + 1]
    chip = place()[1]
    for k in range(chips):
        out[k * base : (k + 1) * base, :] = pieces[k][:base, :]
        held[chip ^ k] = pieces[k][base:, :].astype(jnp.float32)
    total = held[0]
    for k in range(1, chips):
        total = total + held[k]
    high = total.astype(jnp.bfloat16)
    count = total.shape[0]
    out[chips * base : chips * base + count, :] = high
    out[chips * base + count :, :] = (total - high.astype(jnp.float32)).astype(jnp.bfloat16)


def grads_kernel(n_t, starts, bias, keys, values, *refs):
    packed, heads = refs[:n_t], refs[n_t : 2 * n_t][::-1]
    key_out, value_out = refs[2 * n_t : 2 * n_t + 2]
    outs = refs[2 * n_t + 2 : 3 * n_t + 2][::-1]
    key_acc, value_acc = refs[3 * n_t + 2 :]
    rows = packed[0].shape[1]
    ones = jnp.ones((8, HD), jnp.float32)
    keys_t = jnp.transpose(keys[...])
    stats = []
    for k in range(n_t):
        parts = heads[k][starts[2] :, :].astype(jnp.float32)
        stats.append(sum(parts[i * 2 * n_t : (i + 1) * 2 * n_t] for i in range(SPLIT)))
    for p in range(0, n_t, 2):
        q = jnp.concatenate([packed[p][0], packed[p + 1][0]], axis=0)
        o = jnp.concatenate([packed[p][1], packed[p + 1][1]], axis=0)
        g = jnp.concatenate([heads[p][:rows, :], heads[p + 1][:rows, :]], axis=0)
        delta = lax.dot_general(
            ones,
            g.astype(jnp.float32) * o.astype(jnp.float32),
            (((1,), (1,)), ((), ())),
            precision=lax.Precision.HIGHEST,
            preferred_element_type=jnp.float32,
        )[0:1]
        lse = []
        for i in (p, p + 1):
            tops = [stats[k][i ^ k : (i ^ k) + 1] for k in range(n_t)]
            sums = [stats[k][n_t + (i ^ k) : n_t + (i ^ k) + 1] for k in range(n_t)]
            top = functools.reduce(jnp.maximum, tops)
            lse.append(top + jnp.log(sum(b * jnp.exp(a - top) for a, b in zip(tops, sums))))
        lse = jnp.concatenate(lse, axis=1)
        query_part = None
        for kf in range(bias.shape[0]):
            span = slice(kf * SPF, (kf + 1) * SPF)
            shift = bias[kf : kf + 1, p * rows : (p + 2) * rows] - lse
            probs = jnp.exp(dot(keys[span, :], q, 1, 1) * SCALE + shift)
            score_grad = (probs * (dot(values[span, :], g, 1, 1) - delta)).astype(jnp.bfloat16)
            value_add = dot(probs.astype(jnp.bfloat16), g, 1, 0)
            key_add = dot(score_grad, q, 1, 0)
            if p > 0:
                value_add = value_add + value_acc[span, :]
                key_add = key_add + key_acc[span, :]
            if p + 2 < n_t:
                value_acc[span, :] = value_add
                key_acc[span, :] = key_add
            else:
                value_out[span, :] = value_add.astype(jnp.bfloat16)
                key_out[span, :] = (key_add * SCALE).astype(jnp.bfloat16)
            part = dot(keys_t[:, span], score_grad, 1, 0)
            query_part = part if query_part is None else query_part + part
        outs[p][...] = query_part[:, :rows].astype(jnp.bfloat16)
        outs[p + 1][...] = query_part[:, rows:].astype(jnp.bfloat16)


def query_kernel(n_t, *refs):
    total = refs[0][...].astype(jnp.float32)
    for k in range(1, n_t):
        total = total + refs[k][...].astype(jnp.float32)
    refs[n_t][...] = jnp.transpose(total * SCALE).astype(jnp.bfloat16)


def half_results(n_t, chips, frames, hot, ref, packed, saved, held, tiles):
    t, chip, _ = place()
    rows = saved.shape[1]
    part = rows // chips
    base = tiles * n_t * part
    for k in range(n_t):
        saved[k] = packed[k][1].astype(jnp.float32)
    ordered = []
    for c in range(chips):
        mine = pl.ds(pl.multiple_of((chip ^ c) * part, part), part)
        ordered += [saved[k, mine, :] for k in range(n_t)]
    ordered = jnp.transpose(jnp.concatenate(ordered, axis=0)).astype(jnp.bfloat16)
    gated = jnp.concatenate(
        [
            jnp.concatenate(
                [
                    ref[c * base + j * n_t * part : c * base + (j + 1) * n_t * part, :]
                    for c in range(chips)
                ],
                axis=0,
            )
            for j in range(tiles)
        ],
        axis=1,
    )
    count = (ref.shape[0] - chips * base) // 2
    each = count // n_t
    terms = ref[chips * base : chips * base + count, :].astype(jnp.float32)
    terms = terms + ref[chips * base + count :, :].astype(jnp.float32)
    for k in range(n_t):
        held[t ^ k] = terms[k * each : (k + 1) * each]

    def gate_tile(a, j):
        total = jnp.zeros(hot.shape[1:], jnp.float32)
        for f in range(n_t * frames):
            row = (a * frames + f % frames) * tiles + j
            total = total + hot[f] * held[f // frames, row : row + 1, :]
        return total

    return dot(ordered, gated, 1, 0), gate_tile


def own_kernel(n_t, chips, frames, hot, own, *refs):
    packed, (weight_out, gate_out, saved, held) = refs[:n_t], refs[n_t:]
    tiles = weight_out.shape[1] // LANES
    result, gate_tile = half_results(n_t, chips, frames, hot, own, packed, saved, held, tiles)
    weight_out[...] = result
    for a in range(chips):
        for j in range(tiles):
            gate_out[:, (a * tiles + j) * LANES : (a * tiles + j + 1) * LANES] = gate_tile(a, j)


def final_kernel(n_t, chips, frames, hot, other, own_weight, own_gate, *refs):
    packed, (weight_out, gate_out, saved, held) = refs[:n_t], refs[n_t:]
    core = place()[2]
    width = own_weight.shape[1]
    tiles = width // LANES
    result, gate_tile = half_results(n_t, chips, frames, hot, other, packed, saved, held, tiles)
    mine = own_weight[...]
    weight_out[:, :width] = jnp.where(core == 0, mine, result)
    weight_out[:, width:] = jnp.where(core == 0, result, mine)
    for a in range(chips):
        for j in range(tiles):
            first = gate_tile(a, j)
            second = own_gate[:, (a * tiles + j) * LANES : (a * tiles + j + 1) * LANES]
            column = 2 * a * width + j * LANES
            gate_out[:, column : column + LANES] = jnp.where(core == 0, second, first)
            column += width
            gate_out[:, column : column + LANES] = jnp.where(core == 0, first, second)


def call(kernel, args, out_shape, scratch=(), flops=0, in_place=False, in_smem=0):
    vmem = pl.BlockSpec(memory_space=pltpu.VMEM)
    single = not isinstance(out_shape, (list, tuple))
    nbytes = sum(a.size * a.dtype.itemsize for a in args)
    return pl.pallas_call(
        kernel,
        out_shape=out_shape,
        in_specs=[pl.BlockSpec(memory_space=pltpu.SMEM)] * in_smem
        + [pl.BlockSpec(memory_space=pltpu.HBM) if in_place else vmem] * (len(args) - in_smem),
        out_specs=vmem if single else [vmem] * len(out_shape),
        scratch_shapes=list(scratch),
        compiler_params=pltpu.CompilerParams(vmem_limit_bytes=PREP_VMEM if in_place else VMEM_LIMIT),
        cost_estimate=pl.CostEstimate(flops=flops, bytes_accessed=nbytes, transcendentals=0),
    )(*args)


def padded_shards(table, n_s, width):
    rows, columns = table.shape
    cut = table.reshape(rows, n_s, columns // n_s)
    cut = jnp.pad(cut, ((0, 0), (0, 0), (0, width - columns // n_s)))
    return cut.reshape(rows, n_s * width)


def without_padding(table, shards, shard):
    rows, columns = table.shape
    return table.reshape(rows, shards, columns // shards)[:, :, :shard].reshape(rows, shards * shard)


def body(
    queries, keys, values, saved_out, out_grad, proj_weight, gate_table, noise_levels, clip_lengths
):
    n_t, n_s = lax.axis_size("tm"), lax.axis_size("space")
    chips = n_s // 2
    rows, shard = out_grad.shape
    k_rows = keys.shape[0]
    frames = rows // QF
    levels = gate_table.shape[0]
    bf16, f32 = jnp.bfloat16, jnp.float32
    width = -(-shard // LANES) * LANES
    if width != shard:
        out_grad = jnp.pad(out_grad, ((0, 0), (0, width - shard)))
        proj_weight = padded_shards(proj_weight, n_s, width)
        gate_table = padded_shards(gate_table, n_s, width)

    def shape(dtype, *dims):
        return jax.ShapeDtypeStruct(dims, dtype)

    def over_chips(x):
        return [x] + [
            lax.ppermute(x, "space", [(s, s ^ (2 * k)) for s in range(n_s)]) for k in range(1, chips)
        ]

    def over_cores(x):
        return lax.ppermute(x, "space", [(s, s ^ 1) for s in range(n_s)])

    def over_time(x, k):
        return lax.ppermute(x, "tm", [(t, t ^ k) for t in range(n_t)])

    tiles = width // LANES
    part = rows // chips
    count = chips * frames * tiles
    starts = sections(rows, chips, tiles, n_t, count)

    def time_swaps(messages):
        got = {k: over_time(messages[k], k) for k in range(n_t - 1, 0, -1)}
        return [messages[0]] + [got[k] for k in range(1, n_t)]

    pieces = over_chips(out_grad)
    kept, sent = call(
        functools.partial(cut_kernel, chips),
        [proj_weight, saved_out],
        [shape(bf16, chips, HD, width), shape(bf16, HD, chips * width + HD)],
        [pltpu.SemaphoreType.DMA((2 * chips + 1,))],
        in_place=True,
    )
    received = over_cores(sent)
    packed, _ = lax.optimization_barrier((jnp.stack([queries, saved_out]), received))
    packed_all = [packed]
    for k in range(1, n_t):
        low = k & -k
        packed_all.append(over_time(packed_all[k - low], low))
    gate_table, _ = lax.optimization_barrier((gate_table, received))
    bias, gate_a, gate_b, hot = call(
        functools.partial(masks_kernel, n_t, chips, frames, rows),
        [noise_levels, clip_lengths, gate_table],
        [
            shape(f32, frames, n_t * rows),
            shape(f32, chips, frames, width),
            shape(f32, n_t, 1, width),
            shape(f32, n_t * frames, levels, LANES),
        ],
        in_smem=2,
    )
    mine, other, terms = call(
        functools.partial(head_kernel, chips, frames),
        [packed, kept, received, gate_a] + pieces,
        [shape(f32, rows, HD), shape(f32, rows, HD), shape(f32, count, LANES)],
        flops=4 * rows * chips * width * 2 * HD,
    )
    later_bias, _ = lax.optimization_barrier((bias, mine))
    stats = call(
        functools.partial(stats_kernel, n_t),
        [later_bias, keys] + packed_all,
        shape(f32, 2 * n_t, LANES),
        flops=2 * n_t * rows * k_rows * HD,
    )
    heads = call(
        functools.partial(join_kernel, n_t, chips, starts),
        [mine, over_cores(other), stats, terms] + pieces,
        [shape(bf16, starts[-1], LANES)] * n_t,
        [pltpu.VMEM((rows, width), f32), pltpu.VMEM((chips, part, width), f32)],
    )
    heads_all = time_swaps(heads[::-1])
    base = tiles * n_t * part
    bundle = call(
        functools.partial(bundle_kernel, n_t, starts, count),
        [gate_b] + heads_all[::-1],
        shape(bf16, base + n_t * count, LANES),
    )
    bundles = over_chips(bundle)
    later_bias, _ = lax.optimization_barrier((bias, bundle))
    outs = call(
        functools.partial(grads_kernel, n_t, starts),
        [later_bias, keys, values] + packed_all + heads_all[::-1],
        [shape(bf16, k_rows, HD)] * 2 + [shape(bf16, HD, rows)] * n_t,
        [pltpu.VMEM((k_rows, HD), f32)] * 2,
        flops=10 * n_t * rows * k_rows * HD,
    )
    key_grad, value_grad = outs[:2]
    parts = time_swaps(outs[2:][::-1])
    bundles, _ = lax.optimization_barrier((bundles, parts[: n_t // 2 - 1 : -1]))
    collected = call(
        functools.partial(collect_kernel, chips, base),
        bundles,
        shape(bf16, chips * base + 2 * n_t * count, LANES),
        [pltpu.VMEM((chips, n_t * count, LANES), f32)],
    )
    scratch = [pltpu.VMEM((n_t, rows, HD), f32), pltpu.VMEM((n_t, count, LANES), f32)]
    own_halves = call(
        functools.partial(own_kernel, n_t, chips, frames),
        [hot, collected] + packed_all,
        [shape(f32, HD, width), shape(f32, levels, chips * width)],
        scratch,
        flops=2 * n_t * rows * width * HD,
    )
    weight_grad, gate_grad = call(
        functools.partial(final_kernel, n_t, chips, frames),
        [hot, over_cores(collected), *own_halves] + packed_all,
        [shape(f32, HD, 2 * width), shape(f32, levels, n_s * width)],
        scratch,
        flops=2 * n_t * rows * width * HD,
    )
    parts[0], _ = lax.optimization_barrier((parts[0], gate_grad))
    query_grad = call(functools.partial(query_kernel, n_t), parts[::-1], shape(bf16, rows, HD))
    if width != shard:
        weight_grad = without_padding(weight_grad, 2, shard)
        gate_grad = without_padding(gate_grad, n_s, shard)
    return (query_grad, key_grad, value_grad, weight_grad, gate_grad)


def solution(mesh):
    return jax.shard_map(
        body,
        mesh=mesh,
        in_specs=(
            P("tm", "space"),
            P("tm", "space"),
            P("tm", "space"),
            P("tm", "space"),
            P("tm", "space"),
            P("space", None),
            P(),
            P(),
            P(),
        ),
        out_specs=(P("tm", "space"), P("tm", "space"), P("tm", "space"), P("space", "tm"), P()),
        check_vma=False,
    )
```

```python
import functools
import math

import jax
import jax.numpy as jnp
from jax import lax
from jax.experimental import pallas as pl
from jax.experimental.pallas import tpu as pltpu
from jax.sharding import PartitionSpec as P

HD = 128
SPF = 512
QF = 64
LANES = 128
NEG_BIG = -1e30
SCALE = 1.0 / math.sqrt(HD)
VMEM_LIMIT = 32 * 1024 * 1024
PREP_VMEM = 52 * 1024 * 1024
SPLIT = 3


def dot(a, b, on_a, on_b):
    return lax.dot_general(
        a, b, (((on_a,), (on_b,)), ((), ())), preferred_element_type=jnp.float32
    )


def place():
    s = lax.axis_index("space")
    return lax.axis_index("tm"), s // 2, s % 2


def clip_numbers(clips_ref):
    bounds = []
    so_far = 0
    for c in range(clips_ref.shape[0]):
        so_far = so_far + clips_ref[c]
        bounds.append(so_far)
    return lambda frame: sum((frame >= bound).astype(jnp.int32) for bound in bounds)


def cut_kernel(chips, weight_in, saved_in, kept, sent, sems):
    _, chip, core = place()
    width = kept.shape[2]
    moves = [(saved_in, sent.at[:, chips * width : chips * width + HD])]
    for k in range(chips):
        for c, out in ((1 - core, sent.at[:, k * width : (k + 1) * width]), (core, kept.at[k])):
            columns = pl.ds(pl.multiple_of((2 * (chip ^ k) + c) * width, LANES), width)
            moves.append((weight_in.at[:, columns], out))
    copies = [pltpu.make_async_copy(a, b, sems.at[i]) for i, (a, b) in enumerate(moves)]
    for copy in copies:
        copy.start()
    for copy in copies:
        copy.wait()


def masks_kernel(n_t, chips, frames, rows, levels, clips, gate, bias, gate_a, gate_b, hot):
    t, chip, core = place()
    width = gate_a.shape[2]
    clip_of = clip_numbers(clips)
    lane = lax.broadcasted_iota(jnp.int32, (1, rows), 1)
    for kf in range(frames):
        key_frame = t * frames + kf
        key_clip = clip_of(key_frame)
        for k in range(n_t):
            row = jnp.full((1, rows), NEG_BIG, jnp.float32)
            for r in range(frames):
                frame = (t ^ k) * frames + r
                visible = (key_frame >= frame) & (clip_of(frame) == key_clip)
                value = jnp.where(visible, 0.0, NEG_BIG).astype(jnp.float32)
                row = jnp.where((lane >= r * QF) & (lane < (r + 1) * QF), value, row)
            bias[kf : kf + 1, k * rows : (k + 1) * rows] = row
    spot = lax.broadcasted_iota(jnp.int32, hot.shape[1:], 0)
    for f in range(n_t * frames):
        hot[f] = (spot == levels[f]).astype(jnp.float32)
    for r in range(frames):
        level = levels[t * frames + r]
        for k in range(chips):
            columns = pl.ds(pl.multiple_of((2 * (chip ^ k) + core) * width, LANES), width)
            gate_a[k, r : r + 1, :] = gate[pl.ds(level, 1), columns]
    mine = pl.ds(pl.multiple_of((2 * t + core) * width, LANES), width)
    for k in range(n_t):
        level = levels[(t ^ k) * frames + chip * (rows // chips) // QF]
        gate_b[k] = gate[pl.ds(level, 1), mine]


def stats_kernel(n_t, bias, keys, *refs):
    packed, out = refs[:n_t], refs[n_t]
    rows = packed[0].shape[1]
    for p in range(0, n_t, 2):
        q = jnp.concatenate([packed[p][0], packed[p + 1][0]], axis=0)
        scores = []
        for kf in range(bias.shape[0]):
            mask = bias[kf : kf + 1, p * rows : (p + 2) * rows]
            scores.append(dot(keys[kf * SPF : (kf + 1) * SPF, :], q, 1, 1) * SCALE + mask)
        top = functools.reduce(jnp.maximum, [jnp.max(x, axis=0, keepdims=True) for x in scores])
        total = sum(jnp.sum(jnp.exp(x - top), axis=0, keepdims=True) for x in scores)
        for i in range(2):
            out[p + i : p + i + 1, :] = top[:, i * rows : (i + 1) * rows]
            out[n_t + p + i : n_t + p + i + 1, :] = total[:, i * rows : (i + 1) * rows]


def head_kernel(chips, frames, packed, kept, received, gate_a, *refs):
    pieces, (mine, other, terms) = refs[:chips], refs[chips:]
    _, chip, _ = place()
    width = pieces[0].shape[1]
    tiles = width // LANES
    saved = jnp.concatenate([packed[1], received[:, chips * width : chips * width + HD]], axis=1)
    head = None
    for k in range(chips):
        weight = jnp.concatenate([kept[k], received[:, k * width : (k + 1) * width]], axis=0)
        wide = pieces[k][...].astype(jnp.float32)
        gated = jnp.concatenate(
            [
                (wide[r * QF : (r + 1) * QF] * gate_a[k, r : r + 1, :]).astype(jnp.bfloat16)
                for r in range(frames)
            ],
            axis=0,
        )
        part = dot(gated, weight, 1, 1)
        head = part if head is None else head + part
        product = wide * dot(saved, weight, 1, 0)
        for r in range(frames):
            term = jnp.sum(product[r * QF : (r + 1) * QF], axis=0, keepdims=True)
            for j in range(tiles):
                row = ((chip ^ k) * frames + r) * tiles + j
                terms[pl.ds(row, 1), :] = term[:, j * LANES : (j + 1) * LANES]
    mine[...] = head[:, :HD]
    other[...] = head[:, HD:]


def sections(rows, chips, tiles, n_t, count):
    starts = [0, rows]
    starts.append(starts[-1] + tiles * (rows // chips))
    starts.append(starts[-1] + -(-(SPLIT * 2 * n_t + count) // 16) * 16)
    return starts


def padded(x, rows):
    if x.shape[0] == rows:
        return x
    return jnp.concatenate([x, jnp.zeros((rows - x.shape[0], x.shape[1]), x.dtype)], axis=0)


def join_kernel(n_t, chips, starts, mine, received, stats, terms, *refs):
    pieces, outs, (wide, held) = refs[:chips], refs[chips : chips + n_t][::-1], refs[chips + n_t :]
    t, chip, _ = place()
    part, tiles = held.shape[1], held.shape[2] // LANES
    for k in range(chips):
        wide[...] = pieces[k][...].astype(jnp.float32)
        held[k] = wide[pl.ds(pl.multiple_of(chip * part, part), part), :]
    head = (mine[...] + received[...]).astype(jnp.bfloat16)
    rest = stats[...]
    split = []
    for _ in range(SPLIT):
        piece = rest.astype(jnp.bfloat16).astype(jnp.float32)
        split.append(piece)
        rest = rest - piece
    last = padded(jnp.concatenate(split + [terms[...]], axis=0), starts[3] - starts[2])
    last = last.astype(jnp.bfloat16)
    for k in range(n_t):
        rows = held[chip ^ t ^ k]
        rows = jnp.concatenate([rows[:, j * LANES : (j + 1) * LANES] for j in range(tiles)], axis=0)
        outs[k][: starts[1], :] = head
        outs[k][starts[1] : starts[2], :] = rows.astype(jnp.bfloat16)
        outs[k][starts[2] :, :] = last


def bundle_kernel(n_t, starts, count, gate_b, *refs):
    heads, out = refs[:n_t][::-1], refs[n_t]
    tiles = gate_b.shape[2] // LANES
    part = (starts[2] - starts[1]) // tiles
    wide = [heads[k][starts[1] : starts[2], :].astype(jnp.float32) for k in range(n_t)]
    for j in range(tiles):
        gated = jnp.concatenate(
            [
                wide[k][j * part : (j + 1) * part] * gate_b[k, :, j * LANES : (j + 1) * LANES]
                for k in range(n_t)
            ],
            axis=0,
        )
        out[j * n_t * part : (j + 1) * n_t * part, :] = gated.astype(jnp.bfloat16)
    first = SPLIT * 2 * n_t
    terms = [heads[k][starts[2] :, :].astype(jnp.float32)[first : first + count] for k in range(n_t)]
    out[tiles * n_t * part :, :] = jnp.concatenate(terms, axis=0).astype(jnp.bfloat16)


def collect_kernel(chips, base, *refs):
    pieces, out, held = refs[:chips], refs[chips], refs[chips + 1]
    chip = place()[1]
    for k in range(chips):
        out[k * base : (k + 1) * base, :] = pieces[k][:base, :]
        held[chip ^ k] = pieces[k][base:, :].astype(jnp.float32)
    total = held[0]
    for k in range(1, chips):
        total = total + held[k]
    high = total.astype(jnp.bfloat16)
    count = total.shape[0]
    out[chips * base : chips * base + count, :] = high
    out[chips * base + count :, :] = (total - high.astype(jnp.float32)).astype(jnp.bfloat16)


def grads_kernel(n_t, starts, first, last, bias, keys, values, *refs):
    packed, heads = refs[:n_t], refs[n_t : 2 * n_t][::-1]
    refs = refs[2 * n_t :]
    if first == 0:
        sums, refs = refs[:2], refs[2:]
    key_out, value_out = refs[:2]
    outs = refs[2 : 2 + last - first][::-1]
    accs = refs[2 + last - first :]
    rows = packed[0].shape[1]
    ones = jnp.ones((8, HD), jnp.float32)
    keys_t = jnp.transpose(keys[...])
    stats = []
    for k in range(n_t):
        parts = heads[k][starts[2] :, :].astype(jnp.float32)
        stats.append(sum(parts[i * 2 * n_t : (i + 1) * 2 * n_t] for i in range(SPLIT)))
    for p in range(first, last, 2):
        q = jnp.concatenate([packed[p][0], packed[p + 1][0]], axis=0)
        o = jnp.concatenate([packed[p][1], packed[p + 1][1]], axis=0)
        g = jnp.concatenate([heads[p][:rows, :], heads[p + 1][:rows, :]], axis=0)
        delta = lax.dot_general(
            ones,
            g.astype(jnp.float32) * o.astype(jnp.float32),
            (((1,), (1,)), ((), ())),
            precision=lax.Precision.HIGHEST,
            preferred_element_type=jnp.float32,
        )[0:1]
        lse = []
        for i in (p, p + 1):
            tops = [stats[k][i ^ k : (i ^ k) + 1] for k in range(n_t)]
            sums_of = [stats[k][n_t + (i ^ k) : n_t + (i ^ k) + 1] for k in range(n_t)]
            top = functools.reduce(jnp.maximum, tops)
            lse.append(top + jnp.log(sum(b * jnp.exp(a - top) for a, b in zip(tops, sums_of))))
        lse = jnp.concatenate(lse, axis=1)
        query_part = None
        for kf in range(bias.shape[0]):
            span = slice(kf * SPF, (kf + 1) * SPF)
            shift = bias[kf : kf + 1, p * rows : (p + 2) * rows] - lse
            probs = jnp.exp(dot(keys[span, :], q, 1, 1) * SCALE + shift)
            score_grad = (probs * (dot(values[span, :], g, 1, 1) - delta)).astype(jnp.bfloat16)
            value_add = dot(probs.astype(jnp.bfloat16), g, 1, 0)
            key_add = dot(score_grad, q, 1, 0)
            if p > first:
                value_add = value_add + accs[1][span, :]
                key_add = key_add + accs[0][span, :]
            if p + 2 < last:
                accs[1][span, :] = value_add
                accs[0][span, :] = key_add
            elif first:
                value_out[span, :] = value_add
                key_out[span, :] = key_add
            else:
                value_out[span, :] = (value_add + sums[1][span, :]).astype(jnp.bfloat16)
                key_out[span, :] = ((key_add + sums[0][span, :]) * SCALE).astype(jnp.bfloat16)
            part = dot(keys_t[:, span], score_grad, 1, 0)
            query_part = part if query_part is None else query_part + part
        outs[p - first][...] = query_part[:, :rows].astype(jnp.bfloat16)
        outs[p + 1 - first][...] = query_part[:, rows:].astype(jnp.bfloat16)


def query_kernel(n_t, *refs):
    total = refs[0][...].astype(jnp.float32)
    for k in range(1, n_t):
        total = total + refs[k][...].astype(jnp.float32)
    refs[n_t][...] = jnp.transpose(total * SCALE).astype(jnp.bfloat16)


def half_results(n_t, chips, frames, hot, ref, packed, saved, held, tiles):
    t, chip, _ = place()
    rows = saved.shape[1]
    part = rows // chips
    base = tiles * n_t * part
    for k in range(n_t):
        saved[k] = packed[k][1].astype(jnp.float32)
    ordered = []
    for c in range(chips):
        mine = pl.ds(pl.multiple_of((chip ^ c) * part, part), part)
        ordered += [saved[k, mine, :] for k in range(n_t)]
    ordered = jnp.transpose(jnp.concatenate(ordered, axis=0)).astype(jnp.bfloat16)
    gated = jnp.concatenate(
        [
            jnp.concatenate(
                [
                    ref[c * base + j * n_t * part : c * base + (j + 1) * n_t * part, :]
                    for c in range(chips)
                ],
                axis=0,
            )
            for j in range(tiles)
        ],
        axis=1,
    )
    count = (ref.shape[0] - chips * base) // 2
    each = count // n_t
    terms = ref[chips * base : chips * base + count, :].astype(jnp.float32)
    terms = terms + ref[chips * base + count :, :].astype(jnp.float32)
    for k in range(n_t):
        held[t ^ k] = terms[k * each : (k + 1) * each]

    def gate_tile(a, j):
        total = jnp.zeros(hot.shape[1:], jnp.float32)
        for f in range(n_t * frames):
            row = (a * frames + f % frames) * tiles + j
            total = total + hot[f] * held[f // frames, row : row + 1, :]
        return total

    return dot(ordered, gated, 1, 0), gate_tile


def own_kernel(n_t, chips, frames, hot, own, *refs):
    packed, (weight_out, gate_out, saved, held) = refs[:n_t], refs[n_t:]
    tiles = weight_out.shape[1] // LANES
    result, gate_tile = half_results(n_t, chips, frames, hot, own, packed, saved, held, tiles)
    weight_out[...] = result
    for a in range(chips):
        for j in range(tiles):
            gate_out[:, (a * tiles + j) * LANES : (a * tiles + j + 1) * LANES] = gate_tile(a, j)


def final_kernel(n_t, chips, frames, hot, other, own_weight, own_gate, *refs):
    packed, (weight_out, gate_out, saved, held) = refs[:n_t], refs[n_t:]
    core = place()[2]
    width = own_weight.shape[1]
    tiles = width // LANES
    result, gate_tile = half_results(n_t, chips, frames, hot, other, packed, saved, held, tiles)
    mine = own_weight[...]
    weight_out[:, :width] = jnp.where(core == 0, mine, result)
    weight_out[:, width:] = jnp.where(core == 0, result, mine)
    for a in range(chips):
        for j in range(tiles):
            first = gate_tile(a, j)
            second = own_gate[:, (a * tiles + j) * LANES : (a * tiles + j + 1) * LANES]
            column = 2 * a * width + j * LANES
            gate_out[:, column : column + LANES] = jnp.where(core == 0, second, first)
            column += width
            gate_out[:, column : column + LANES] = jnp.where(core == 0, first, second)


def call(kernel, args, out_shape, scratch=(), flops=0, in_place=False, in_smem=0):
    vmem = pl.BlockSpec(memory_space=pltpu.VMEM)
    single = not isinstance(out_shape, (list, tuple))
    nbytes = sum(a.size * a.dtype.itemsize for a in args)
    return pl.pallas_call(
        kernel,
        out_shape=out_shape,
        in_specs=[pl.BlockSpec(memory_space=pltpu.SMEM)] * in_smem
        + [pl.BlockSpec(memory_space=pltpu.HBM) if in_place else vmem] * (len(args) - in_smem),
        out_specs=vmem if single else [vmem] * len(out_shape),
        scratch_shapes=list(scratch),
        compiler_params=pltpu.CompilerParams(vmem_limit_bytes=PREP_VMEM if in_place else VMEM_LIMIT),
        cost_estimate=pl.CostEstimate(flops=flops, bytes_accessed=nbytes, transcendentals=0),
    )(*args)


def padded_shards(table, n_s, width):
    rows, columns = table.shape
    cut = table.reshape(rows, n_s, columns // n_s)
    cut = jnp.pad(cut, ((0, 0), (0, 0), (0, width - columns // n_s)))
    return cut.reshape(rows, n_s * width)


def without_padding(table, shards, shard):
    rows, columns = table.shape
    return table.reshape(rows, shards, columns // shards)[:, :, :shard].reshape(rows, shards * shard)


def body(
    queries, keys, values, saved_out, out_grad, proj_weight, gate_table, noise_levels, clip_lengths
):
    n_t, n_s = lax.axis_size("tm"), lax.axis_size("space")
    chips = n_s // 2
    rows, shard = out_grad.shape
    k_rows = keys.shape[0]
    frames = rows // QF
    levels = gate_table.shape[0]
    bf16, f32 = jnp.bfloat16, jnp.float32
    width = -(-shard // LANES) * LANES
    if width != shard:
        out_grad = jnp.pad(out_grad, ((0, 0), (0, width - shard)))
        proj_weight = padded_shards(proj_weight, n_s, width)
        gate_table = padded_shards(gate_table, n_s, width)

    def shape(dtype, *dims):
        return jax.ShapeDtypeStruct(dims, dtype)

    def over_chips(x):
        return [x] + [
            lax.ppermute(x, "space", [(s, s ^ (2 * k)) for s in range(n_s)]) for k in range(1, chips)
        ]

    def over_cores(x):
        return lax.ppermute(x, "space", [(s, s ^ 1) for s in range(n_s)])

    def over_time(x, k):
        return lax.ppermute(x, "tm", [(t, t ^ k) for t in range(n_t)])

    tiles = width // LANES
    part = rows // chips
    count = chips * frames * tiles
    starts = sections(rows, chips, tiles, n_t, count)

    def time_swaps(messages):
        got = {k: over_time(messages[k], k) for k in range(n_t - 1, 0, -1)}
        return [messages[0]] + [got[k] for k in range(1, n_t)]

    pieces = over_chips(out_grad)
    kept, sent = call(
        functools.partial(cut_kernel, chips),
        [proj_weight, saved_out],
        [shape(bf16, chips, HD, width), shape(bf16, HD, chips * width + HD)],
        [pltpu.SemaphoreType.DMA((2 * chips + 1,))],
        in_place=True,
    )
    received = over_cores(sent)
    packed, _ = lax.optimization_barrier((jnp.stack([queries, saved_out]), received))
    packed_all = [packed]
    for k in range(1, n_t):
        low = k & -k
        packed_all.append(over_time(packed_all[k - low], low))
    gate_table, _ = lax.optimization_barrier((gate_table, received))
    bias, gate_a, gate_b, hot = call(
        functools.partial(masks_kernel, n_t, chips, frames, rows),
        [noise_levels, clip_lengths, gate_table],
        [
            shape(f32, frames, n_t * rows),
            shape(f32, chips, frames, width),
            shape(f32, n_t, 1, width),
            shape(f32, n_t * frames, levels, LANES),
        ],
        in_smem=2,
    )
    mine, other, terms = call(
        functools.partial(head_kernel, chips, frames),
        [packed, kept, received, gate_a] + pieces,
        [shape(f32, rows, HD), shape(f32, rows, HD), shape(f32, count, LANES)],
        flops=4 * rows * chips * width * 2 * HD,
    )
    later_bias, _ = lax.optimization_barrier((bias, mine))
    stats = call(
        functools.partial(stats_kernel, n_t),
        [later_bias, keys] + packed_all,
        shape(f32, 2 * n_t, LANES),
        flops=2 * n_t * rows * k_rows * HD,
    )
    heads = call(
        functools.partial(join_kernel, n_t, chips, starts),
        [mine, over_cores(other), stats, terms] + pieces,
        [shape(bf16, starts[-1], LANES)] * n_t,
        [pltpu.VMEM((rows, width), f32), pltpu.VMEM((chips, part, width), f32)],
    )
    heads_all = time_swaps(heads[::-1])
    base = tiles * n_t * part
    bundle = call(
        functools.partial(bundle_kernel, n_t, starts, count),
        [gate_b] + heads_all[::-1],
        shape(bf16, base + n_t * count, LANES),
    )
    bundles = over_chips(bundle)
    later_bias, _ = lax.optimization_barrier((bias, bundle))
    accs = [pltpu.VMEM((k_rows, HD), f32)] * 2
    far = call(
        functools.partial(grads_kernel, n_t, starts, 2, n_t),
        [later_bias, keys, values] + packed_all + heads_all[::-1],
        [shape(f32, k_rows, HD)] * 2 + [shape(bf16, HD, rows)] * (n_t - 2),
        accs,
        flops=10 * (n_t - 2) * rows * k_rows * HD,
    )
    parts = {k: over_time(far[1 + n_t - k], k) for k in range(n_t - 1, 1, -1)}
    near_bias, _ = lax.optimization_barrier((bias, parts[n_t - 1]))
    near = call(
        functools.partial(grads_kernel, n_t, starts, 0, 2),
        [near_bias, keys, values] + packed_all + heads_all[::-1] + list(far[:2]),
        [shape(bf16, k_rows, HD)] * 2 + [shape(bf16, HD, rows)] * 2,
        flops=20 * rows * k_rows * HD,
    )
    key_grad, value_grad = near[:2]
    parts[0], parts[1] = near[3], over_time(near[2], 1)
    parts = [parts[k] for k in range(n_t)]
    bundles, _ = lax.optimization_barrier((bundles, (key_grad, parts[: n_t // 2 - 1 : -1])))
    collected = call(
        functools.partial(collect_kernel, chips, base),
        bundles,
        shape(bf16, chips * base + 2 * n_t * count, LANES),
        [pltpu.VMEM((chips, n_t * count, LANES), f32)],
    )
    scratch = [pltpu.VMEM((n_t, rows, HD), f32), pltpu.VMEM((n_t, count, LANES), f32)]
    own_halves = call(
        functools.partial(own_kernel, n_t, chips, frames),
        [hot, collected] + packed_all,
        [shape(f32, HD, width), shape(f32, levels, chips * width)],
        scratch,
        flops=2 * n_t * rows * width * HD,
    )
    weight_grad, gate_grad = call(
        functools.partial(final_kernel, n_t, chips, frames),
        [hot, over_cores(collected), *own_halves] + packed_all,
        [shape(f32, HD, 2 * width), shape(f32, levels, n_s * width)],
        scratch,
        flops=2 * n_t * rows * width * HD,
    )
    parts[0], _ = lax.optimization_barrier((parts[0], gate_grad))
    query_grad = call(functools.partial(query_kernel, n_t), parts[::-1], shape(bf16, rows, HD))
    if width != shard:
        weight_grad = without_padding(weight_grad, 2, shard)
        gate_grad = without_padding(gate_grad, n_s, shard)
    return (query_grad, key_grad, value_grad, weight_grad, gate_grad)


def solution(mesh):
    return jax.shard_map(
        body,
        mesh=mesh,
        in_specs=(
            P("tm", "space"),
            P("tm", "space"),
            P("tm", "space"),
            P("tm", "space"),
            P("tm", "space"),
            P("space", None),
            P(),
            P(),
            P(),
        ),
        out_specs=(P("tm", "space"), P("tm", "space"), P("tm", "space"), P("space", "tm"), P()),
        check_vma=False,
    )
```

```python
import functools
import math

import jax
import jax.numpy as jnp
from jax import lax
from jax.experimental import pallas as pl
from jax.experimental.pallas import tpu as pltpu
from jax.sharding import PartitionSpec as P

HD = 128
SPF = 512
QF = 64
LANES = 128
NEG_BIG = -1e30
SCALE = 1.0 / math.sqrt(HD)
VMEM_LIMIT = 32 * 1024 * 1024
PREP_VMEM = 52 * 1024 * 1024
SPLIT = 3


def dot(a, b, on_a, on_b):
    return lax.dot_general(
        a, b, (((on_a,), (on_b,)), ((), ())), preferred_element_type=jnp.float32
    )


def two_first(blocks):
    blocks = list(blocks)
    return blocks[:1] + blocks[2:3] + blocks[1:2] + blocks[3:]


def place():
    s = lax.axis_index("space")
    return lax.axis_index("tm"), s // 2, s % 2


def clip_numbers(clips_ref):
    bounds = []
    so_far = 0
    for c in range(clips_ref.shape[0]):
        so_far = so_far + clips_ref[c]
        bounds.append(so_far)
    return lambda frame: sum((frame >= bound).astype(jnp.int32) for bound in bounds)


def cut_kernel(chips, weight_in, saved_in, kept, sent, sems):
    _, chip, core = place()
    width = kept.shape[2]
    moves = [(saved_in, sent.at[:, chips * width : chips * width + HD])]
    for k in range(chips):
        for c, out in ((1 - core, sent.at[:, k * width : (k + 1) * width]), (core, kept.at[k])):
            columns = pl.ds(pl.multiple_of((2 * (chip ^ k) + c) * width, LANES), width)
            moves.append((weight_in.at[:, columns], out))
    copies = [pltpu.make_async_copy(a, b, sems.at[i]) for i, (a, b) in enumerate(moves)]
    for copy in copies:
        copy.start()
    for copy in copies:
        copy.wait()


def masks_kernel(n_t, chips, frames, rows, levels, clips, gate, bias, gate_a, gate_b, hot):
    t, chip, core = place()
    width = gate_a.shape[2]
    clip_of = clip_numbers(clips)
    lane = lax.broadcasted_iota(jnp.int32, (1, rows), 1)
    for kf in range(frames):
        key_frame = t * frames + kf
        key_clip = clip_of(key_frame)
        for k in range(n_t):
            row = jnp.full((1, rows), NEG_BIG, jnp.float32)
            for r in range(frames):
                frame = (t ^ k) * frames + r
                visible = (key_frame >= frame) & (clip_of(frame) == key_clip)
                value = jnp.where(visible, 0.0, NEG_BIG).astype(jnp.float32)
                row = jnp.where((lane >= r * QF) & (lane < (r + 1) * QF), value, row)
            bias[kf : kf + 1, k * rows : (k + 1) * rows] = row
    spot = lax.broadcasted_iota(jnp.int32, hot.shape[1:], 0)
    for f in range(n_t * frames):
        hot[f] = (spot == levels[f]).astype(jnp.float32)
    for r in range(frames):
        level = levels[t * frames + r]
        for k in range(chips):
            columns = pl.ds(pl.multiple_of((2 * (chip ^ k) + core) * width, LANES), width)
            gate_a[k, r : r + 1, :] = gate[pl.ds(level, 1), columns]
    mine = pl.ds(pl.multiple_of((2 * t + core) * width, LANES), width)
    for k in range(n_t):
        level = levels[(t ^ k) * frames + chip * (rows // chips) // QF]
        gate_b[k] = gate[pl.ds(level, 1), mine]


def stats_kernel(n_t, bias, keys, *refs):
    packed, out = refs[:n_t], refs[n_t]
    rows = packed[0].shape[1]
    for p in range(0, n_t, 2):
        q = jnp.concatenate([packed[p][0], packed[p + 1][0]], axis=0)
        scores = []
        for kf in range(bias.shape[0]):
            mask = bias[kf : kf + 1, p * rows : (p + 2) * rows]
            scores.append(dot(keys[kf * SPF : (kf + 1) * SPF, :], q, 1, 1) * SCALE + mask)
        top = functools.reduce(jnp.maximum, [jnp.max(x, axis=0, keepdims=True) for x in scores])
        total = sum(jnp.sum(jnp.exp(x - top), axis=0, keepdims=True) for x in scores)
        for i in range(2):
            out[p + i : p + i + 1, :] = top[:, i * rows : (i + 1) * rows]
            out[n_t + p + i : n_t + p + i + 1, :] = total[:, i * rows : (i + 1) * rows]


def head_kernel(chips, frames, packed, kept, received, gate_a, *refs):
    pieces, (mine, other, terms) = refs[:chips], refs[chips:]
    _, chip, _ = place()
    width = pieces[0].shape[1]
    tiles = width // LANES
    saved = jnp.concatenate([packed[1], received[:, chips * width : chips * width + HD]], axis=1)
    head = None
    for k in range(chips):
        weight = jnp.concatenate([kept[k], received[:, k * width : (k + 1) * width]], axis=0)
        wide = pieces[k][...].astype(jnp.float32)
        gated = jnp.concatenate(
            [
                (wide[r * QF : (r + 1) * QF] * gate_a[k, r : r + 1, :]).astype(jnp.bfloat16)
                for r in range(frames)
            ],
            axis=0,
        )
        part = dot(gated, weight, 1, 1)
        head = part if head is None else head + part
        product = wide * dot(saved, weight, 1, 0)
        for r in range(frames):
            term = jnp.sum(product[r * QF : (r + 1) * QF], axis=0, keepdims=True)
            for j in range(tiles):
                row = ((chip ^ k) * frames + r) * tiles + j
                terms[pl.ds(row, 1), :] = term[:, j * LANES : (j + 1) * LANES]
    mine[...] = head[:, :HD]
    other[...] = head[:, HD:]


def sections(rows, chips, tiles, n_t, count):
    starts = [0, rows]
    starts.append(starts[-1] + tiles * (rows // chips))
    starts.append(starts[-1] + -(-(SPLIT * 2 * n_t + count) // 16) * 16)
    return starts


def padded(x, rows):
    if x.shape[0] == rows:
        return x
    return jnp.concatenate([x, jnp.zeros((rows - x.shape[0], x.shape[1]), x.dtype)], axis=0)


def join_kernel(n_t, chips, starts, mine, received, stats, terms, *refs):
    pieces, outs, (wide, held) = refs[:chips], refs[chips : chips + n_t][::-1], refs[chips + n_t :]
    t, chip, _ = place()
    part, tiles = held.shape[1], held.shape[2] // LANES
    for k in range(chips):
        wide[...] = pieces[k][...].astype(jnp.float32)
        held[k] = wide[pl.ds(pl.multiple_of(chip * part, part), part), :]
    head = (mine[...] + received[...]).astype(jnp.bfloat16)
    rest = stats[...]
    split = []
    for _ in range(SPLIT):
        piece = rest.astype(jnp.bfloat16).astype(jnp.float32)
        split.append(piece)
        rest = rest - piece
    last = padded(jnp.concatenate(split + [terms[...]], axis=0), starts[3] - starts[2])
    last = last.astype(jnp.bfloat16)
    for k in range(n_t):
        rows = held[chip ^ t ^ k]
        rows = jnp.concatenate([rows[:, j * LANES : (j + 1) * LANES] for j in range(tiles)], axis=0)
        outs[k][: starts[1], :] = head
        outs[k][starts[1] : starts[2], :] = rows.astype(jnp.bfloat16)
        outs[k][starts[2] :, :] = last


def bundle_kernel(n_t, starts, count, gate_b, *refs):
    heads, out = two_first(refs[:n_t]), refs[n_t]
    tiles = gate_b.shape[2] // LANES
    part = (starts[2] - starts[1]) // tiles
    wide = [heads[k][starts[1] : starts[2], :].astype(jnp.float32) for k in range(n_t)]
    for j in range(tiles):
        gated = jnp.concatenate(
            [
                wide[k][j * part : (j + 1) * part] * gate_b[k, :, j * LANES : (j + 1) * LANES]
                for k in range(n_t)
            ],
            axis=0,
        )
        out[j * n_t * part : (j + 1) * n_t * part, :] = gated.astype(jnp.bfloat16)
    first = SPLIT * 2 * n_t
    terms = [heads[k][starts[2] :, :].astype(jnp.float32)[first : first + count] for k in range(n_t)]
    out[tiles * n_t * part :, :] = jnp.concatenate(terms, axis=0).astype(jnp.bfloat16)


def collect_kernel(chips, base, *refs):
    pieces, out, held = refs[:chips], refs[chips], refs[chips + 1]
    chip = place()[1]
    for k in range(chips):
        out[k * base : (k + 1) * base, :] = pieces[k][:base, :]
        held[chip ^ k] = pieces[k][base:, :].astype(jnp.float32)
    total = held[0]
    for k in range(1, chips):
        total = total + held[k]
    high = total.astype(jnp.bfloat16)
    count = total.shape[0]
    out[chips * base : chips * base + count, :] = high
    out[chips * base + count :, :] = (total - high.astype(jnp.float32)).astype(jnp.bfloat16)


def grads_kernel(n_t, starts, first, last, bias, keys, values, *refs):
    packed, heads = refs[:n_t], refs[n_t : 2 * n_t][::-1]
    refs = refs[2 * n_t :]
    if first == 0:
        sums, refs = refs[:2], refs[2:]
    key_out, value_out = refs[:2]
    outs = refs[2 : 2 + last - first][::-1]
    accs = refs[2 + last - first :]
    rows = packed[0].shape[1]
    ones = jnp.ones((8, HD), jnp.float32)
    keys_t = jnp.transpose(keys[...])
    stats = []
    for k in range(n_t):
        parts = heads[k][starts[2] :, :].astype(jnp.float32)
        stats.append(sum(parts[i * 2 * n_t : (i + 1) * 2 * n_t] for i in range(SPLIT)))
    for p in range(first, last, 2):
        q = jnp.concatenate([packed[p][0], packed[p + 1][0]], axis=0)
        o = jnp.concatenate([packed[p][1], packed[p + 1][1]], axis=0)
        g = jnp.concatenate([heads[p][:rows, :], heads[p + 1][:rows, :]], axis=0)
        delta = lax.dot_general(
            ones,
            g.astype(jnp.float32) * o.astype(jnp.float32),
            (((1,), (1,)), ((), ())),
            precision=lax.Precision.HIGHEST,
            preferred_element_type=jnp.float32,
        )[0:1]
        lse = []
        for i in (p, p + 1):
            tops = [stats[k][i ^ k : (i ^ k) + 1] for k in range(n_t)]
            sums_of = [stats[k][n_t + (i ^ k) : n_t + (i ^ k) + 1] for k in range(n_t)]
            top = functools.reduce(jnp.maximum, tops)
            lse.append(top + jnp.log(sum(b * jnp.exp(a - top) for a, b in zip(tops, sums_of))))
        lse = jnp.concatenate(lse, axis=1)
        query_part = None
        for kf in range(bias.shape[0]):
            span = slice(kf * SPF, (kf + 1) * SPF)
            shift = bias[kf : kf + 1, p * rows : (p + 2) * rows] - lse
            probs = jnp.exp(dot(keys[span, :], q, 1, 1) * SCALE + shift)
            score_grad = (probs * (dot(values[span, :], g, 1, 1) - delta)).astype(jnp.bfloat16)
            value_add = dot(probs.astype(jnp.bfloat16), g, 1, 0)
            key_add = dot(score_grad, q, 1, 0)
            if p > first:
                value_add = value_add + accs[1][span, :]
                key_add = key_add + accs[0][span, :]
            if p + 2 < last:
                accs[1][span, :] = value_add
                accs[0][span, :] = key_add
            elif first:
                value_out[span, :] = value_add
                key_out[span, :] = key_add
            else:
                value_out[span, :] = (value_add + sums[1][span, :]).astype(jnp.bfloat16)
                key_out[span, :] = ((key_add + sums[0][span, :]) * SCALE).astype(jnp.bfloat16)
            part = dot(keys_t[:, span], score_grad, 1, 0)
            query_part = part if query_part is None else query_part + part
        outs[p - first][...] = query_part[:, :rows].astype(jnp.bfloat16)
        outs[p + 1 - first][...] = query_part[:, rows:].astype(jnp.bfloat16)


def query_kernel(n_t, *refs):
    total = refs[0][...].astype(jnp.float32)
    for k in range(1, n_t):
        total = total + refs[k][...].astype(jnp.float32)
    refs[n_t][...] = jnp.transpose(total * SCALE).astype(jnp.bfloat16)


def half_results(n_t, chips, frames, hot, ref, packed, saved, held, tiles):
    t, chip, _ = place()
    rows = saved.shape[1]
    part = rows // chips
    base = tiles * n_t * part
    for k in range(n_t):
        saved[k] = packed[k][1].astype(jnp.float32)
    ordered = []
    for c in range(chips):
        mine = pl.ds(pl.multiple_of((chip ^ c) * part, part), part)
        ordered += [saved[k, mine, :] for k in range(n_t)]
    ordered = jnp.transpose(jnp.concatenate(ordered, axis=0)).astype(jnp.bfloat16)
    gated = jnp.concatenate(
        [
            jnp.concatenate(
                [
                    ref[c * base + j * n_t * part : c * base + (j + 1) * n_t * part, :]
                    for c in range(chips)
                ],
                axis=0,
            )
            for j in range(tiles)
        ],
        axis=1,
    )
    count = (ref.shape[0] - chips * base) // 2
    each = count // n_t
    terms = ref[chips * base : chips * base + count, :].astype(jnp.float32)
    terms = terms + ref[chips * base + count :, :].astype(jnp.float32)
    for k in range(n_t):
        held[t ^ k] = terms[k * each : (k + 1) * each]

    def gate_tile(a, j):
        total = jnp.zeros(hot.shape[1:], jnp.float32)
        for f in range(n_t * frames):
            row = (a * frames + f % frames) * tiles + j
            total = total + hot[f] * held[f // frames, row : row + 1, :]
        return total

    return dot(ordered, gated, 1, 0), gate_tile


def own_kernel(n_t, chips, frames, hot, own, *refs):
    packed, (weight_out, gate_out, saved, held) = refs[:n_t], refs[n_t:]
    tiles = weight_out.shape[1] // LANES
    result, gate_tile = half_results(n_t, chips, frames, hot, own, packed, saved, held, tiles)
    weight_out[...] = result
    for a in range(chips):
        for j in range(tiles):
            gate_out[:, (a * tiles + j) * LANES : (a * tiles + j + 1) * LANES] = gate_tile(a, j)


def final_kernel(n_t, chips, frames, hot, other, own_weight, own_gate, *refs):
    packed, (weight_out, gate_out, saved, held) = refs[:n_t], refs[n_t:]
    core = place()[2]
    width = own_weight.shape[1]
    tiles = width // LANES
    result, gate_tile = half_results(n_t, chips, frames, hot, other, packed, saved, held, tiles)
    mine = own_weight[...]
    weight_out[:, :width] = jnp.where(core == 0, mine, result)
    weight_out[:, width:] = jnp.where(core == 0, result, mine)
    for a in range(chips):
        for j in range(tiles):
            first = gate_tile(a, j)
            second = own_gate[:, (a * tiles + j) * LANES : (a * tiles + j + 1) * LANES]
            column = 2 * a * width + j * LANES
            gate_out[:, column : column + LANES] = jnp.where(core == 0, second, first)
            column += width
            gate_out[:, column : column + LANES] = jnp.where(core == 0, first, second)


def call(kernel, args, out_shape, scratch=(), flops=0, in_place=False, in_smem=0):
    vmem = pl.BlockSpec(memory_space=pltpu.VMEM)
    single = not isinstance(out_shape, (list, tuple))
    nbytes = sum(a.size * a.dtype.itemsize for a in args)
    return pl.pallas_call(
        kernel,
        out_shape=out_shape,
        in_specs=[pl.BlockSpec(memory_space=pltpu.SMEM)] * in_smem
        + [pl.BlockSpec(memory_space=pltpu.HBM) if in_place else vmem] * (len(args) - in_smem),
        out_specs=vmem if single else [vmem] * len(out_shape),
        scratch_shapes=list(scratch),
        compiler_params=pltpu.CompilerParams(vmem_limit_bytes=PREP_VMEM if in_place else VMEM_LIMIT),
        cost_estimate=pl.CostEstimate(flops=flops, bytes_accessed=nbytes, transcendentals=0),
    )(*args)


def padded_shards(table, n_s, width):
    rows, columns = table.shape
    cut = table.reshape(rows, n_s, columns // n_s)
    cut = jnp.pad(cut, ((0, 0), (0, 0), (0, width - columns // n_s)))
    return cut.reshape(rows, n_s * width)


def without_padding(table, shards, shard):
    rows, columns = table.shape
    return table.reshape(rows, shards, columns // shards)[:, :, :shard].reshape(rows, shards * shard)


def body(
    queries, keys, values, saved_out, out_grad, proj_weight, gate_table, noise_levels, clip_lengths
):
    n_t, n_s = lax.axis_size("tm"), lax.axis_size("space")
    chips = n_s // 2
    rows, shard = out_grad.shape
    k_rows = keys.shape[0]
    frames = rows // QF
    levels = gate_table.shape[0]
    bf16, f32 = jnp.bfloat16, jnp.float32
    width = -(-shard // LANES) * LANES
    if width != shard:
        out_grad = jnp.pad(out_grad, ((0, 0), (0, width - shard)))
        proj_weight = padded_shards(proj_weight, n_s, width)
        gate_table = padded_shards(gate_table, n_s, width)

    def shape(dtype, *dims):
        return jax.ShapeDtypeStruct(dims, dtype)

    def over_chips(x):
        return [x] + [
            lax.ppermute(x, "space", [(s, s ^ (2 * k)) for s in range(n_s)]) for k in range(1, chips)
        ]

    def over_cores(x):
        return lax.ppermute(x, "space", [(s, s ^ 1) for s in range(n_s)])

    def over_time(x, k):
        return lax.ppermute(x, "tm", [(t, t ^ k) for t in range(n_t)])

    tiles = width // LANES
    part = rows // chips
    count = chips * frames * tiles
    starts = sections(rows, chips, tiles, n_t, count)

    def time_swaps(messages):
        got = {k: over_time(messages[k], k) for k in range(n_t - 1, 0, -1)}
        return [messages[0]] + [got[k] for k in range(1, n_t)]

    pieces = over_chips(out_grad)
    kept, sent = call(
        functools.partial(cut_kernel, chips),
        [proj_weight, saved_out],
        [shape(bf16, chips, HD, width), shape(bf16, HD, chips * width + HD)],
        [pltpu.SemaphoreType.DMA((2 * chips + 1,))],
        in_place=True,
    )
    received = over_cores(sent)
    packed, _ = lax.optimization_barrier((jnp.stack([queries, saved_out]), received))
    packed_all = [packed]
    for k in range(1, n_t):
        low = k & -k
        packed_all.append(over_time(packed_all[k - low], low))
    gate_table, _ = lax.optimization_barrier((gate_table, received))
    bias, gate_a, gate_b, hot = call(
        functools.partial(masks_kernel, n_t, chips, frames, rows),
        [noise_levels, clip_lengths, gate_table],
        [
            shape(f32, frames, n_t * rows),
            shape(f32, chips, frames, width),
            shape(f32, n_t, 1, width),
            shape(f32, n_t * frames, levels, LANES),
        ],
        in_smem=2,
    )
    mine, other, terms = call(
        functools.partial(head_kernel, chips, frames),
        [packed, kept, received, gate_a] + pieces,
        [shape(f32, rows, HD), shape(f32, rows, HD), shape(f32, count, LANES)],
        flops=4 * rows * chips * width * 2 * HD,
    )
    later_bias, _ = lax.optimization_barrier((bias, mine))
    stats = call(
        functools.partial(stats_kernel, n_t),
        [later_bias, keys] + packed_all,
        shape(f32, 2 * n_t, LANES),
        flops=2 * n_t * rows * k_rows * HD,
    )
    heads = call(
        functools.partial(join_kernel, n_t, chips, starts),
        [mine, over_cores(other), stats, terms] + pieces,
        [shape(bf16, starts[-1], LANES)] * n_t,
        [pltpu.VMEM((rows, width), f32), pltpu.VMEM((chips, part, width), f32)],
    )
    heads_all = time_swaps(heads[::-1])
    base = tiles * n_t * part
    bundle = call(
        functools.partial(bundle_kernel, n_t, starts, count),
        [gate_b] + two_first(heads_all),
        shape(bf16, base + n_t * count, LANES),
    )
    bundles = over_chips(bundle)
    later_bias, _ = lax.optimization_barrier((bias, bundle))
    accs = [pltpu.VMEM((k_rows, HD), f32)] * 2
    far = call(
        functools.partial(grads_kernel, n_t, starts, 2, n_t),
        [later_bias, keys, values] + packed_all + heads_all[::-1],
        [shape(f32, k_rows, HD)] * 2 + [shape(bf16, HD, rows)] * (n_t - 2),
        accs,
        flops=10 * (n_t - 2) * rows * k_rows * HD,
    )
    parts = {k: over_time(far[1 + n_t - k], k) for k in range(n_t - 1, 1, -1)}
    near = call(
        functools.partial(grads_kernel, n_t, starts, 0, 2),
        [bias, keys, values] + packed_all + heads_all[::-1] + list(far[:2]),
        [shape(bf16, k_rows, HD)] * 2 + [shape(bf16, HD, rows)] * 2,
        flops=20 * rows * k_rows * HD,
    )
    key_grad, value_grad = near[:2]
    parts[0], parts[1] = near[3], over_time(near[2], 1)
    parts = [parts[k] for k in range(n_t)]
    bundles, _ = lax.optimization_barrier((bundles, (key_grad, parts[: n_t // 2 - 1 : -1])))
    collected = call(
        functools.partial(collect_kernel, chips, base),
        bundles,
        shape(bf16, chips * base + 2 * n_t * count, LANES),
        [pltpu.VMEM((chips, n_t * count, LANES), f32)],
    )
    scratch = [pltpu.VMEM((n_t, rows, HD), f32), pltpu.VMEM((n_t, count, LANES), f32)]
    own_halves = call(
        functools.partial(own_kernel, n_t, chips, frames),
        [hot, collected] + packed_all,
        [shape(f32, HD, width), shape(f32, levels, chips * width)],
        scratch,
        flops=2 * n_t * rows * width * HD,
    )
    weight_grad, gate_grad = call(
        functools.partial(final_kernel, n_t, chips, frames),
        [hot, over_cores(collected), *own_halves] + packed_all,
        [shape(f32, HD, 2 * width), shape(f32, levels, n_s * width)],
        scratch,
        flops=2 * n_t * rows * width * HD,
    )
    parts[0], _ = lax.optimization_barrier((parts[0], gate_grad))
    query_grad = call(functools.partial(query_kernel, n_t), parts[::-1], shape(bf16, rows, HD))
    if width != shard:
        weight_grad = without_padding(weight_grad, 2, shard)
        gate_grad = without_padding(gate_grad, n_s, shard)
    return (query_grad, key_grad, value_grad, weight_grad, gate_grad)


def solution(mesh):
    return jax.shard_map(
        body,
        mesh=mesh,
        in_specs=(
            P("tm", "space"),
            P("tm", "space"),
            P("tm", "space"),
            P("tm", "space"),
            P("tm", "space"),
            P("space", None),
            P(),
            P(),
            P(),
        ),
        out_specs=(P("tm", "space"), P("tm", "space"), P("tm", "space"), P("space", "tm"), P()),
        check_vma=False,
    )
```

```python
import functools
import math

import jax
import jax.numpy as jnp
from jax import lax
from jax.experimental import pallas as pl
from jax.experimental.pallas import tpu as pltpu
from jax.sharding import PartitionSpec as P

HD = 128
SPF = 512
QF = 64
LANES = 128
NEG_BIG = -1e30
SCALE = 1.0 / math.sqrt(HD)
VMEM_LIMIT = 32 * 1024 * 1024
PREP_VMEM = 52 * 1024 * 1024
SPLIT = 3


def dot(a, b, on_a, on_b):
    return lax.dot_general(
        a, b, (((on_a,), (on_b,)), ((), ())), preferred_element_type=jnp.float32
    )


def far_first(blocks):
    blocks = list(blocks)
    return blocks[:1] + blocks[:0:-1]


def place():
    s = lax.axis_index("space")
    return lax.axis_index("tm"), s // 2, s % 2


def clip_numbers(clips_ref):
    bounds = []
    so_far = 0
    for c in range(clips_ref.shape[0]):
        so_far = so_far + clips_ref[c]
        bounds.append(so_far)
    return lambda frame: sum((frame >= bound).astype(jnp.int32) for bound in bounds)


def cut_kernel(chips, weight_in, saved_in, kept, sent, sems):
    _, chip, core = place()
    width = kept.shape[2]
    moves = [(saved_in, sent.at[:, chips * width : chips * width + HD])]
    for k in range(chips):
        for c, out in ((1 - core, sent.at[:, k * width : (k + 1) * width]), (core, kept.at[k])):
            columns = pl.ds(pl.multiple_of((2 * (chip ^ k) + c) * width, LANES), width)
            moves.append((weight_in.at[:, columns], out))
    copies = [pltpu.make_async_copy(a, b, sems.at[i]) for i, (a, b) in enumerate(moves)]
    for copy in copies:
        copy.start()
    for copy in copies:
        copy.wait()


def masks_kernel(n_t, chips, frames, rows, levels, clips, gate, bias, gate_a, gate_b, hot):
    t, chip, core = place()
    width = gate_a.shape[2]
    clip_of = clip_numbers(clips)
    lane = lax.broadcasted_iota(jnp.int32, (1, rows), 1)
    for kf in range(frames):
        key_frame = t * frames + kf
        key_clip = clip_of(key_frame)
        for k in range(n_t):
            row = jnp.full((1, rows), NEG_BIG, jnp.float32)
            for r in range(frames):
                frame = (t ^ k) * frames + r
                visible = (key_frame >= frame) & (clip_of(frame) == key_clip)
                value = jnp.where(visible, 0.0, NEG_BIG).astype(jnp.float32)
                row = jnp.where((lane >= r * QF) & (lane < (r + 1) * QF), value, row)
            bias[kf : kf + 1, k * rows : (k + 1) * rows] = row
    spot = lax.broadcasted_iota(jnp.int32, hot.shape[1:], 0)
    for f in range(n_t * frames):
        hot[f] = (spot == levels[f]).astype(jnp.float32)
    for r in range(frames):
        level = levels[t * frames + r]
        for k in range(chips):
            columns = pl.ds(pl.multiple_of((2 * (chip ^ k) + core) * width, LANES), width)
            gate_a[k, r : r + 1, :] = gate[pl.ds(level, 1), columns]
    mine = pl.ds(pl.multiple_of((2 * t + core) * width, LANES), width)
    for k in range(n_t):
        level = levels[(t ^ k) * frames + chip * (rows // chips) // QF]
        gate_b[k] = gate[pl.ds(level, 1), mine]


def stats_kernel(n_t, bias, keys, *refs):
    packed, out = refs[:n_t], refs[n_t]
    rows = packed[0].shape[1]
    for p in range(0, n_t, 2):
        q = jnp.concatenate([packed[p][0], packed[p + 1][0]], axis=0)
        scores = []
        for kf in range(bias.shape[0]):
            mask = bias[kf : kf + 1, p * rows : (p + 2) * rows]
            scores.append(dot(keys[kf * SPF : (kf + 1) * SPF, :], q, 1, 1) * SCALE + mask)
        top = functools.reduce(jnp.maximum, [jnp.max(x, axis=0, keepdims=True) for x in scores])
        total = sum(jnp.sum(jnp.exp(x - top), axis=0, keepdims=True) for x in scores)
        for i in range(2):
            out[p + i : p + i + 1, :] = top[:, i * rows : (i + 1) * rows]
            out[n_t + p + i : n_t + p + i + 1, :] = total[:, i * rows : (i + 1) * rows]


def head_kernel(chips, frames, packed, kept, received, gate_a, *refs):
    pieces, (mine, other, terms) = refs[:chips], refs[chips:]
    _, chip, _ = place()
    width = pieces[0].shape[1]
    tiles = width // LANES
    saved = jnp.concatenate([packed[1], received[:, chips * width : chips * width + HD]], axis=1)
    head = None
    for k in range(chips):
        weight = jnp.concatenate([kept[k], received[:, k * width : (k + 1) * width]], axis=0)
        wide = pieces[k][...].astype(jnp.float32)
        gated = jnp.concatenate(
            [
                (wide[r * QF : (r + 1) * QF] * gate_a[k, r : r + 1, :]).astype(jnp.bfloat16)
                for r in range(frames)
            ],
            axis=0,
        )
        part = dot(gated, weight, 1, 1)
        head = part if head is None else head + part
        product = wide * dot(saved, weight, 1, 0)
        for r in range(frames):
            term = jnp.sum(product[r * QF : (r + 1) * QF], axis=0, keepdims=True)
            for j in range(tiles):
                row = ((chip ^ k) * frames + r) * tiles + j
                terms[pl.ds(row, 1), :] = term[:, j * LANES : (j + 1) * LANES]
    mine[...] = head[:, :HD]
    other[...] = head[:, HD:]


def sections(rows, chips, tiles, n_t, count):
    starts = [0, rows]
    starts.append(starts[-1] + tiles * (rows // chips))
    starts.append(starts[-1] + -(-(SPLIT * 2 * n_t + count) // 16) * 16)
    return starts


def padded(x, rows):
    if x.shape[0] == rows:
        return x
    return jnp.concatenate([x, jnp.zeros((rows - x.shape[0], x.shape[1]), x.dtype)], axis=0)


def join_kernel(n_t, chips, starts, mine, received, stats, terms, *refs):
    pieces, outs, (wide, held) = refs[:chips], refs[chips : chips + n_t][::-1], refs[chips + n_t :]
    t, chip, _ = place()
    part, tiles = held.shape[1], held.shape[2] // LANES
    for k in range(chips):
        wide[...] = pieces[k][...].astype(jnp.float32)
        held[k] = wide[pl.ds(pl.multiple_of(chip * part, part), part), :]
    head = (mine[...] + received[...]).astype(jnp.bfloat16)
    rest = stats[...]
    split = []
    for _ in range(SPLIT):
        piece = rest.astype(jnp.bfloat16).astype(jnp.float32)
        split.append(piece)
        rest = rest - piece
    last = padded(jnp.concatenate(split + [terms[...]], axis=0), starts[3] - starts[2])
    last = last.astype(jnp.bfloat16)
    for k in range(n_t):
        rows = held[chip ^ t ^ k]
        rows = jnp.concatenate([rows[:, j * LANES : (j + 1) * LANES] for j in range(tiles)], axis=0)
        outs[k][: starts[1], :] = head
        outs[k][starts[1] : starts[2], :] = rows.astype(jnp.bfloat16)
        outs[k][starts[2] :, :] = last


def bundle_kernel(n_t, starts, count, gate_b, *refs):
    heads, out = far_first(refs[:n_t]), refs[n_t]
    tiles = gate_b.shape[2] // LANES
    part = (starts[2] - starts[1]) // tiles
    wide = [heads[k][starts[1] : starts[2], :].astype(jnp.float32) for k in range(n_t)]
    for j in range(tiles):
        gated = jnp.concatenate(
            [
                wide[k][j * part : (j + 1) * part] * gate_b[k, :, j * LANES : (j + 1) * LANES]
                for k in range(n_t)
            ],
            axis=0,
        )
        out[j * n_t * part : (j + 1) * n_t * part, :] = gated.astype(jnp.bfloat16)
    first = SPLIT * 2 * n_t
    terms = [heads[k][starts[2] :, :].astype(jnp.float32)[first : first + count] for k in range(n_t)]
    out[tiles * n_t * part :, :] = jnp.concatenate(terms, axis=0).astype(jnp.bfloat16)


def collect_kernel(chips, base, *refs):
    pieces, out, held = refs[:chips], refs[chips], refs[chips + 1]
    chip = place()[1]
    for k in range(chips):
        out[k * base : (k + 1) * base, :] = pieces[k][:base, :]
        held[chip ^ k] = pieces[k][base:, :].astype(jnp.float32)
    total = held[0]
    for k in range(1, chips):
        total = total + held[k]
    high = total.astype(jnp.bfloat16)
    count = total.shape[0]
    out[chips * base : chips * base + count, :] = high
    out[chips * base + count :, :] = (total - high.astype(jnp.float32)).astype(jnp.bfloat16)


def grads_kernel(n_t, starts, first, last, bias, keys, values, *refs):
    packed, heads = refs[:n_t], refs[n_t : 2 * n_t][::-1]
    refs = refs[2 * n_t :]
    if first == 0:
        sums, refs = refs[:2], refs[2:]
    key_out, value_out = refs[:2]
    outs = refs[2 : 2 + last - first][::-1]
    accs = refs[2 + last - first :]
    rows = packed[0].shape[1]
    ones = jnp.ones((8, HD), jnp.float32)
    keys_t = jnp.transpose(keys[...])
    stats = []
    for k in range(n_t):
        parts = heads[k][starts[2] :, :].astype(jnp.float32)
        stats.append(sum(parts[i * 2 * n_t : (i + 1) * 2 * n_t] for i in range(SPLIT)))
    for p in range(first, last, 2):
        q = jnp.concatenate([packed[p][0], packed[p + 1][0]], axis=0)
        o = jnp.concatenate([packed[p][1], packed[p + 1][1]], axis=0)
        g = jnp.concatenate([heads[p][:rows, :], heads[p + 1][:rows, :]], axis=0)
        delta = lax.dot_general(
            ones,
            g.astype(jnp.float32) * o.astype(jnp.float32),
            (((1,), (1,)), ((), ())),
            precision=lax.Precision.HIGHEST,
            preferred_element_type=jnp.float32,
        )[0:1]
        lse = []
        for i in (p, p + 1):
            tops = [stats[k][i ^ k : (i ^ k) + 1] for k in range(n_t)]
            sums_of = [stats[k][n_t + (i ^ k) : n_t + (i ^ k) + 1] for k in range(n_t)]
            top = functools.reduce(jnp.maximum, tops)
            lse.append(top + jnp.log(sum(b * jnp.exp(a - top) for a, b in zip(tops, sums_of))))
        lse = jnp.concatenate(lse, axis=1)
        query_part = None
        for kf in range(bias.shape[0]):
            span = slice(kf * SPF, (kf + 1) * SPF)
            shift = bias[kf : kf + 1, p * rows : (p + 2) * rows] - lse
            probs = jnp.exp(dot(keys[span, :], q, 1, 1) * SCALE + shift)
            score_grad = (probs * (dot(values[span, :], g, 1, 1) - delta)).astype(jnp.bfloat16)
            value_add = dot(probs.astype(jnp.bfloat16), g, 1, 0)
            key_add = dot(score_grad, q, 1, 0)
            if p > first:
                value_add = value_add + accs[1][span, :]
                key_add = key_add + accs[0][span, :]
            if p + 2 < last:
                accs[1][span, :] = value_add
                accs[0][span, :] = key_add
            elif first:
                value_out[span, :] = value_add
                key_out[span, :] = key_add
            else:
                value_out[span, :] = (value_add + sums[1][span, :]).astype(jnp.bfloat16)
                key_out[span, :] = ((key_add + sums[0][span, :]) * SCALE).astype(jnp.bfloat16)
            part = dot(keys_t[:, span], score_grad, 1, 0)
            query_part = part if query_part is None else query_part + part
        outs[p - first][...] = query_part[:, :rows].astype(jnp.bfloat16)
        outs[p + 1 - first][...] = query_part[:, rows:].astype(jnp.bfloat16)


def query_kernel(n_t, *refs):
    total = refs[0][...].astype(jnp.float32)
    for k in range(1, n_t):
        total = total + refs[k][...].astype(jnp.float32)
    refs[n_t][...] = jnp.transpose(total * SCALE).astype(jnp.bfloat16)


def half_results(n_t, chips, frames, hot, ref, packed, saved, held, tiles):
    t, chip, _ = place()
    rows = saved.shape[1]
    part = rows // chips
    base = tiles * n_t * part
    for k in range(n_t):
        saved[k] = packed[k][1].astype(jnp.float32)
    ordered = []
    for c in range(chips):
        mine = pl.ds(pl.multiple_of((chip ^ c) * part, part), part)
        ordered += [saved[k, mine, :] for k in range(n_t)]
    ordered = jnp.transpose(jnp.concatenate(ordered, axis=0)).astype(jnp.bfloat16)
    gated = jnp.concatenate(
        [
            jnp.concatenate(
                [
                    ref[c * base + j * n_t * part : c * base + (j + 1) * n_t * part, :]
                    for c in range(chips)
                ],
                axis=0,
            )
            for j in range(tiles)
        ],
        axis=1,
    )
    count = (ref.shape[0] - chips * base) // 2
    each = count // n_t
    terms = ref[chips * base : chips * base + count, :].astype(jnp.float32)
    terms = terms + ref[chips * base + count :, :].astype(jnp.float32)
    for k in range(n_t):
        held[t ^ k] = terms[k * each : (k + 1) * each]

    def gate_tile(a, j):
        total = jnp.zeros(hot.shape[1:], jnp.float32)
        for f in range(n_t * frames):
            row = (a * frames + f % frames) * tiles + j
            total = total + hot[f] * held[f // frames, row : row + 1, :]
        return total

    return dot(ordered, gated, 1, 0), gate_tile


def own_kernel(n_t, chips, frames, hot, own, *refs):
    packed, (weight_out, gate_out, saved, held) = refs[:n_t], refs[n_t:]
    tiles = weight_out.shape[1] // LANES
    result, gate_tile = half_results(n_t, chips, frames, hot, own, packed, saved, held, tiles)
    weight_out[...] = result
    for a in range(chips):
        for j in range(tiles):
            gate_out[:, (a * tiles + j) * LANES : (a * tiles + j + 1) * LANES] = gate_tile(a, j)


def final_kernel(n_t, chips, frames, hot, other, own_weight, own_gate, *refs):
    packed, (weight_out, gate_out, saved, held) = refs[:n_t], refs[n_t:]
    core = place()[2]
    width = own_weight.shape[1]
    tiles = width // LANES
    result, gate_tile = half_results(n_t, chips, frames, hot, other, packed, saved, held, tiles)
    mine = own_weight[...]
    weight_out[:, :width] = jnp.where(core == 0, mine, result)
    weight_out[:, width:] = jnp.where(core == 0, result, mine)
    for a in range(chips):
        for j in range(tiles):
            first = gate_tile(a, j)
            second = own_gate[:, (a * tiles + j) * LANES : (a * tiles + j + 1) * LANES]
            column = 2 * a * width + j * LANES
            gate_out[:, column : column + LANES] = jnp.where(core == 0, second, first)
            column += width
            gate_out[:, column : column + LANES] = jnp.where(core == 0, first, second)


def call(kernel, args, out_shape, scratch=(), flops=0, in_place=False, in_smem=0):
    vmem = pl.BlockSpec(memory_space=pltpu.VMEM)
    single = not isinstance(out_shape, (list, tuple))
    nbytes = sum(a.size * a.dtype.itemsize for a in args)
    return pl.pallas_call(
        kernel,
        out_shape=out_shape,
        in_specs=[pl.BlockSpec(memory_space=pltpu.SMEM)] * in_smem
        + [pl.BlockSpec(memory_space=pltpu.HBM) if in_place else vmem] * (len(args) - in_smem),
        out_specs=vmem if single else [vmem] * len(out_shape),
        scratch_shapes=list(scratch),
        compiler_params=pltpu.CompilerParams(vmem_limit_bytes=PREP_VMEM if in_place else VMEM_LIMIT),
        cost_estimate=pl.CostEstimate(flops=flops, bytes_accessed=nbytes, transcendentals=0),
    )(*args)


def padded_shards(table, n_s, width):
    rows, columns = table.shape
    cut = table.reshape(rows, n_s, columns // n_s)
    cut = jnp.pad(cut, ((0, 0), (0, 0), (0, width - columns // n_s)))
    return cut.reshape(rows, n_s * width)


def without_padding(table, shards, shard):
    rows, columns = table.shape
    return table.reshape(rows, shards, columns // shards)[:, :, :shard].reshape(rows, shards * shard)


def body(
    queries, keys, values, saved_out, out_grad, proj_weight, gate_table, noise_levels, clip_lengths
):
    n_t, n_s = lax.axis_size("tm"), lax.axis_size("space")
    chips = n_s // 2
    rows, shard = out_grad.shape
    k_rows = keys.shape[0]
    frames = rows // QF
    levels = gate_table.shape[0]
    bf16, f32 = jnp.bfloat16, jnp.float32
    width = -(-shard // LANES) * LANES
    if width != shard:
        out_grad = jnp.pad(out_grad, ((0, 0), (0, width - shard)))
        proj_weight = padded_shards(proj_weight, n_s, width)
        gate_table = padded_shards(gate_table, n_s, width)

    def shape(dtype, *dims):
        return jax.ShapeDtypeStruct(dims, dtype)

    def over_chips(x):
        return [x] + [
            lax.ppermute(x, "space", [(s, s ^ (2 * k)) for s in range(n_s)]) for k in range(1, chips)
        ]

    def over_cores(x):
        return lax.ppermute(x, "space", [(s, s ^ 1) for s in range(n_s)])

    def over_time(x, k):
        return lax.ppermute(x, "tm", [(t, t ^ k) for t in range(n_t)])

    tiles = width // LANES
    part = rows // chips
    count = chips * frames * tiles
    starts = sections(rows, chips, tiles, n_t, count)

    def time_swaps(messages):
        got = {k: over_time(messages[k], k) for k in range(n_t - 1, 0, -1)}
        return [messages[0]] + [got[k] for k in range(1, n_t)]

    pieces = over_chips(out_grad)
    kept, sent = call(
        functools.partial(cut_kernel, chips),
        [proj_weight, saved_out],
        [shape(bf16, chips, HD, width), shape(bf16, HD, chips * width + HD)],
        [pltpu.SemaphoreType.DMA((2 * chips + 1,))],
        in_place=True,
    )
    received = over_cores(sent)
    packed, _ = lax.optimization_barrier((jnp.stack([queries, saved_out]), received))
    packed_all = [packed]
    for k in range(1, n_t):
        low = k & -k
        packed_all.append(over_time(packed_all[k - low], low))
    gate_table, _ = lax.optimization_barrier((gate_table, received))
    bias, gate_a, gate_b, hot = call(
        functools.partial(masks_kernel, n_t, chips, frames, rows),
        [noise_levels, clip_lengths, gate_table],
        [
            shape(f32, frames, n_t * rows),
            shape(f32, chips, frames, width),
            shape(f32, n_t, 1, width),
            shape(f32, n_t * frames, levels, LANES),
        ],
        in_smem=2,
    )
    mine, other, terms = call(
        functools.partial(head_kernel, chips, frames),
        [packed, kept, received, gate_a] + pieces,
        [shape(f32, rows, HD), shape(f32, rows, HD), shape(f32, count, LANES)],
        flops=4 * rows * chips * width * 2 * HD,
    )
    later_bias, _ = lax.optimization_barrier((bias, mine))
    stats = call(
        functools.partial(stats_kernel, n_t),
        [later_bias, keys] + packed_all,
        shape(f32, 2 * n_t, LANES),
        flops=2 * n_t * rows * k_rows * HD,
    )
    heads = call(
        functools.partial(join_kernel, n_t, chips, starts),
        [mine, over_cores(other), stats, terms] + pieces,
        [shape(bf16, starts[-1], LANES)] * n_t,
        [pltpu.VMEM((rows, width), f32), pltpu.VMEM((chips, part, width), f32)],
    )
    heads_all = time_swaps(heads[::-1])
    base = tiles * n_t * part
    bundle = call(
        functools.partial(bundle_kernel, n_t, starts, count),
        [gate_b] + far_first(heads_all),
        shape(bf16, base + n_t * count, LANES),
    )
    bundles = over_chips(bundle)
    later_bias, _ = lax.optimization_barrier((bias, bundle))
    accs = [pltpu.VMEM((k_rows, HD), f32)] * 2
    far = call(
        functools.partial(grads_kernel, n_t, starts, 2, n_t),
        [later_bias, keys, values] + packed_all + heads_all[::-1],
        [shape(f32, k_rows, HD)] * 2 + [shape(bf16, HD, rows)] * (n_t - 2),
        accs,
        flops=10 * (n_t - 2) * rows * k_rows * HD,
    )
    parts = {k: over_time(far[1 + n_t - k], k) for k in range(n_t - 1, 1, -1)}
    near = call(
        functools.partial(grads_kernel, n_t, starts, 0, 2),
        [bias, keys, values] + packed_all + heads_all[::-1] + list(far[:2]),
        [shape(bf16, k_rows, HD)] * 2 + [shape(bf16, HD, rows)] * 2,
        flops=20 * rows * k_rows * HD,
    )
    key_grad, value_grad = near[:2]
    parts[0], parts[1] = near[3], over_time(near[2], 1)
    parts = [parts[k] for k in range(n_t)]
    bundles, _ = lax.optimization_barrier((bundles, (key_grad, parts[n_t - 1])))
    collected = call(
        functools.partial(collect_kernel, chips, base),
        bundles,
        shape(bf16, chips * base + 2 * n_t * count, LANES),
        [pltpu.VMEM((chips, n_t * count, LANES), f32)],
    )
    scratch = [pltpu.VMEM((n_t, rows, HD), f32), pltpu.VMEM((n_t, count, LANES), f32)]
    own_halves = call(
        functools.partial(own_kernel, n_t, chips, frames),
        [hot, collected] + packed_all,
        [shape(f32, HD, width), shape(f32, levels, chips * width)],
        scratch,
        flops=2 * n_t * rows * width * HD,
    )
    weight_grad, gate_grad = call(
        functools.partial(final_kernel, n_t, chips, frames),
        [hot, over_cores(collected), *own_halves] + packed_all,
        [shape(f32, HD, 2 * width), shape(f32, levels, n_s * width)],
        scratch,
        flops=2 * n_t * rows * width * HD,
    )
    parts[0], _ = lax.optimization_barrier((parts[0], gate_grad))
    query_grad = call(functools.partial(query_kernel, n_t), parts[::-1], shape(bf16, rows, HD))
    if width != shard:
        weight_grad = without_padding(weight_grad, 2, shard)
        gate_grad = without_padding(gate_grad, n_s, shard)
    return (query_grad, key_grad, value_grad, weight_grad, gate_grad)


def solution(mesh):
    return jax.shard_map(
        body,
        mesh=mesh,
        in_specs=(
            P("tm", "space"),
            P("tm", "space"),
            P("tm", "space"),
            P("tm", "space"),
            P("tm", "space"),
            P("space", None),
            P(),
            P(),
            P(),
        ),
        out_specs=(P("tm", "space"), P("tm", "space"), P("tm", "space"), P("space", "tm"), P()),
        check_vma=False,
    )
```

```python
import functools
import math

import jax
import jax.numpy as jnp
from jax import lax
from jax.experimental import pallas as pl
from jax.experimental.pallas import tpu as pltpu
from jax.sharding import PartitionSpec as P

HD = 128
SPF = 512
QF = 64
LANES = 128
NEG_BIG = -1e30
SCALE = 1.0 / math.sqrt(HD)
VMEM_LIMIT = 32 * 1024 * 1024
PREP_VMEM = 52 * 1024 * 1024
SPLIT = 3


def dot(a, b, on_a, on_b):
    return lax.dot_general(
        a, b, (((on_a,), (on_b,)), ((), ())), preferred_element_type=jnp.float32
    )


def far_first(blocks):
    blocks = list(blocks)
    return blocks[:1] + blocks[:0:-1]


def place():
    s = lax.axis_index("space")
    return lax.axis_index("tm"), s // 2, s % 2


def clip_numbers(clips_ref):
    bounds = []
    so_far = 0
    for c in range(clips_ref.shape[0]):
        so_far = so_far + clips_ref[c]
        bounds.append(so_far)
    return lambda frame: sum((frame >= bound).astype(jnp.int32) for bound in bounds)


def cut_kernel(chips, weight_in, saved_in, kept, sent, sems):
    _, chip, core = place()
    width = kept.shape[2]
    moves = [(saved_in, sent.at[:, chips * width : chips * width + HD])]
    for k in range(chips):
        for c, out in ((1 - core, sent.at[:, k * width : (k + 1) * width]), (core, kept.at[k])):
            columns = pl.ds(pl.multiple_of((2 * (chip ^ k) + c) * width, LANES), width)
            moves.append((weight_in.at[:, columns], out))
    copies = [pltpu.make_async_copy(a, b, sems.at[i]) for i, (a, b) in enumerate(moves)]
    for copy in copies:
        copy.start()
    for copy in copies:
        copy.wait()


def masks_kernel(n_t, chips, frames, rows, levels, clips, gate, bias, gate_a, gate_b, hot):
    t, chip, core = place()
    width = gate_a.shape[2]
    clip_of = clip_numbers(clips)
    lane = lax.broadcasted_iota(jnp.int32, (1, rows), 1)
    for kf in range(frames):
        key_frame = t * frames + kf
        key_clip = clip_of(key_frame)
        for k in range(n_t):
            row = jnp.full((1, rows), NEG_BIG, jnp.float32)
            for r in range(frames):
                frame = (t ^ k) * frames + r
                visible = (key_frame >= frame) & (clip_of(frame) == key_clip)
                value = jnp.where(visible, 0.0, NEG_BIG).astype(jnp.float32)
                row = jnp.where((lane >= r * QF) & (lane < (r + 1) * QF), value, row)
            bias[kf : kf + 1, k * rows : (k + 1) * rows] = row
    spot = lax.broadcasted_iota(jnp.int32, hot.shape[1:], 0)
    for f in range(n_t * frames):
        hot[f] = (spot == levels[f]).astype(jnp.float32)
    for r in range(frames):
        level = levels[t * frames + r]
        for k in range(chips):
            columns = pl.ds(pl.multiple_of((2 * (chip ^ k) + core) * width, LANES), width)
            gate_a[k, r : r + 1, :] = gate[pl.ds(level, 1), columns]
    mine = pl.ds(pl.multiple_of((2 * t + core) * width, LANES), width)
    for k in range(n_t):
        level = levels[(t ^ k) * frames + chip * (rows // chips) // QF]
        gate_b[k] = gate[pl.ds(level, 1), mine]


def stats_kernel(n_t, bias, keys, *refs):
    packed, out = refs[:n_t], refs[n_t]
    rows = packed[0].shape[1]
    for p in range(0, n_t, 2):
        q = jnp.concatenate([packed[p][0], packed[p + 1][0]], axis=0)
        scores = []
        for kf in range(bias.shape[0]):
            mask = bias[kf : kf + 1, p * rows : (p + 2) * rows]
            scores.append(dot(keys[kf * SPF : (kf + 1) * SPF, :], q, 1, 1) * SCALE + mask)
        top = functools.reduce(jnp.maximum, [jnp.max(x, axis=0, keepdims=True) for x in scores])
        total = sum(jnp.sum(jnp.exp(x - top), axis=0, keepdims=True) for x in scores)
        for i in range(2):
            out[p + i : p + i + 1, :] = top[:, i * rows : (i + 1) * rows]
            out[n_t + p + i : n_t + p + i + 1, :] = total[:, i * rows : (i + 1) * rows]


def head_kernel(chips, frames, packed, kept, received, gate_a, *refs):
    pieces, (mine, other, terms) = refs[:chips], refs[chips:]
    _, chip, _ = place()
    width = pieces[0].shape[1]
    tiles = width // LANES
    saved = jnp.concatenate([packed[1], received[:, chips * width : chips * width + HD]], axis=1)
    head = None
    for k in range(chips):
        weight = jnp.concatenate([kept[k], received[:, k * width : (k + 1) * width]], axis=0)
        wide = pieces[k][...].astype(jnp.float32)
        gated = jnp.concatenate(
            [
                (wide[r * QF : (r + 1) * QF] * gate_a[k, r : r + 1, :]).astype(jnp.bfloat16)
                for r in range(frames)
            ],
            axis=0,
        )
        part = dot(gated, weight, 1, 1)
        head = part if head is None else head + part
        product = wide * dot(saved, weight, 1, 0)
        for r in range(frames):
            term = jnp.sum(product[r * QF : (r + 1) * QF], axis=0, keepdims=True)
            for j in range(tiles):
                row = ((chip ^ k) * frames + r) * tiles + j
                terms[pl.ds(row, 1), :] = term[:, j * LANES : (j + 1) * LANES]
    mine[...] = head[:, :HD]
    other[...] = head[:, HD:]


def sections(rows, chips, tiles, n_t):
    starts = [0, rows]
    starts.append(starts[-1] + tiles * (rows // chips))
    starts.append(starts[-1] + -(-SPLIT * 2 * n_t // 16) * 16)
    return starts


def padded(x, rows):
    if x.shape[0] == rows:
        return x
    return jnp.concatenate([x, jnp.zeros((rows - x.shape[0], x.shape[1]), x.dtype)], axis=0)


def join_kernel(n_t, chips, starts, mine, received, stats, own_terms, other_terms, *refs):
    pieces, outs, (both, wide, held) = refs[:chips], refs[chips : chips + n_t][::-1], refs[chips + n_t :]
    t, chip, core = place()
    own, other = own_terms[...], other_terms[...]
    count = own.shape[0]
    both[:count, :] = jnp.where(core == 0, own, other)
    both[count:, :] = jnp.where(core == 0, other, own)
    part, tiles = held.shape[1], held.shape[2] // LANES
    for k in range(chips):
        wide[...] = pieces[k][...].astype(jnp.float32)
        held[k] = wide[pl.ds(pl.multiple_of(chip * part, part), part), :]
    head = (mine[...] + received[...]).astype(jnp.bfloat16)
    rest = stats[...]
    split = []
    for _ in range(SPLIT):
        piece = rest.astype(jnp.bfloat16).astype(jnp.float32)
        split.append(piece)
        rest = rest - piece
    last = padded(jnp.concatenate(split, axis=0), starts[3] - starts[2])
    last = last.astype(jnp.bfloat16)
    for k in range(n_t):
        rows = held[chip ^ t ^ k]
        rows = jnp.concatenate([rows[:, j * LANES : (j + 1) * LANES] for j in range(tiles)], axis=0)
        outs[k][: starts[1], :] = head
        outs[k][starts[1] : starts[2], :] = rows.astype(jnp.bfloat16)
        outs[k][starts[2] :, :] = last


def bundle_kernel(n_t, starts, gate_b, *refs):
    heads, out = far_first(refs[:n_t]), refs[n_t]
    tiles = gate_b.shape[2] // LANES
    part = (starts[2] - starts[1]) // tiles
    wide = [heads[k][starts[1] : starts[2], :].astype(jnp.float32) for k in range(n_t)]
    for j in range(tiles):
        gated = jnp.concatenate(
            [
                wide[k][j * part : (j + 1) * part] * gate_b[k, :, j * LANES : (j + 1) * LANES]
                for k in range(n_t)
            ],
            axis=0,
        )
        out[j * n_t * part : (j + 1) * n_t * part, :] = gated.astype(jnp.bfloat16)


def collect_kernel(chips, *refs):
    base = refs[0].shape[0]
    for k in range(chips):
        refs[chips][k * base : (k + 1) * base, :] = refs[k][...]


def grads_kernel(n_t, starts, first, last, bias, keys, values, terms, *refs):
    packed, heads = refs[:n_t], refs[n_t : 2 * n_t][::-1]
    refs = refs[2 * n_t :]
    if first == 0:
        sums, refs = refs[:2], refs[2:]
    key_out, value_out = refs[:2]
    outs = refs[2 : 2 + last - first][::-1]
    accs = refs[2 + last - first :]
    rows = packed[0].shape[1]
    ones = jnp.ones((8, HD), jnp.float32)
    keys_t = jnp.transpose(keys[...])
    stats = []
    for k in range(n_t):
        parts = heads[k][starts[2] :, :].astype(jnp.float32)
        stats.append(sum(parts[i * 2 * n_t : (i + 1) * 2 * n_t] for i in range(SPLIT)))
    for out in outs:
        out[rows:, :] = terms[...].astype(jnp.bfloat16)
    for p in range(first, last, 2):
        q = jnp.concatenate([packed[p][0], packed[p + 1][0]], axis=0)
        o = jnp.concatenate([packed[p][1], packed[p + 1][1]], axis=0)
        g = jnp.concatenate([heads[p][:rows, :], heads[p + 1][:rows, :]], axis=0)
        delta = lax.dot_general(
            ones,
            g.astype(jnp.float32) * o.astype(jnp.float32),
            (((1,), (1,)), ((), ())),
            precision=lax.Precision.HIGHEST,
            preferred_element_type=jnp.float32,
        )[0:1]
        lse = []
        for i in (p, p + 1):
            tops = [stats[k][i ^ k : (i ^ k) + 1] for k in range(n_t)]
            sums_of = [stats[k][n_t + (i ^ k) : n_t + (i ^ k) + 1] for k in range(n_t)]
            top = functools.reduce(jnp.maximum, tops)
            lse.append(top + jnp.log(sum(b * jnp.exp(a - top) for a, b in zip(tops, sums_of))))
        lse = jnp.concatenate(lse, axis=1)
        query_part = None
        for kf in range(bias.shape[0]):
            span = slice(kf * SPF, (kf + 1) * SPF)
            shift = bias[kf : kf + 1, p * rows : (p + 2) * rows] - lse
            probs = jnp.exp(dot(keys[span, :], q, 1, 1) * SCALE + shift)
            score_grad = (probs * (dot(values[span, :], g, 1, 1) - delta)).astype(jnp.bfloat16)
            value_add = dot(probs.astype(jnp.bfloat16), g, 1, 0)
            key_add = dot(score_grad, q, 1, 0)
            if p > first:
                value_add = value_add + accs[1][span, :]
                key_add = key_add + accs[0][span, :]
            if p + 2 < last:
                accs[1][span, :] = value_add
                accs[0][span, :] = key_add
            elif first:
                value_out[span, :] = value_add
                key_out[span, :] = key_add
            else:
                value_out[span, :] = (value_add + sums[1][span, :]).astype(jnp.bfloat16)
                key_out[span, :] = ((key_add + sums[0][span, :]) * SCALE).astype(jnp.bfloat16)
            part = dot(keys_t[:, span], score_grad, 1, 0)
            query_part = part if query_part is None else query_part + part
        outs[p - first][:rows, :] = query_part[:, :rows].astype(jnp.bfloat16)
        outs[p + 1 - first][:rows, :] = query_part[:, rows:].astype(jnp.bfloat16)


def finish_kernel(n_t, chips, frames, hot, *refs):
    parts, (query_out, gate_out, held) = refs[:n_t][::-1], refs[n_t:]
    t = lax.axis_index("tm")
    rows = query_out.shape[0]
    total = parts[0][:rows, :].astype(jnp.float32)
    for k in range(1, n_t):
        total = total + parts[k][:rows, :].astype(jnp.float32)
    query_out[...] = jnp.transpose(total * SCALE).astype(jnp.bfloat16)
    for k in range(n_t):
        held[t ^ k] = parts[k][rows:, :].astype(jnp.float32)
    tiles = gate_out.shape[1] // (2 * chips * LANES)
    for core in range(2):
        for a in range(chips):
            for j in range(tiles):
                total = jnp.zeros(hot.shape[1:], jnp.float32)
                for f in range(n_t * frames):
                    row = ((core * chips + a) * frames + f % frames) * tiles + j
                    total = total + hot[f] * held[f // frames, row : row + 1, :]
                column = ((2 * a + core) * tiles + j) * LANES
                gate_out[:, column : column + LANES] = total


def half_result(n_t, chips, ref, packed, saved, tiles):
    _, chip, _ = place()
    rows = saved.shape[1]
    part = rows // chips
    base = tiles * n_t * part
    for k in range(n_t):
        saved[k] = packed[k][1].astype(jnp.float32)
    ordered = []
    for c in range(chips):
        mine = pl.ds(pl.multiple_of((chip ^ c) * part, part), part)
        ordered += [saved[k, mine, :] for k in range(n_t)]
    ordered = jnp.transpose(jnp.concatenate(ordered, axis=0)).astype(jnp.bfloat16)
    gated = jnp.concatenate(
        [
            jnp.concatenate(
                [
                    ref[c * base + j * n_t * part : c * base + (j + 1) * n_t * part, :]
                    for c in range(chips)
                ],
                axis=0,
            )
            for j in range(tiles)
        ],
        axis=1,
    )
    return dot(ordered, gated, 1, 0)


def own_kernel(n_t, chips, own, *refs):
    packed, (weight_out, saved) = refs[:n_t], refs[n_t:]
    weight_out[...] = half_result(n_t, chips, own, packed, saved, weight_out.shape[1] // LANES)


def final_kernel(n_t, chips, other, own_weight, *refs):
    packed, (weight_out, saved) = refs[:n_t], refs[n_t:]
    core = place()[2]
    width = own_weight.shape[1]
    result = half_result(n_t, chips, other, packed, saved, width // LANES)
    mine = own_weight[...]
    weight_out[:, :width] = jnp.where(core == 0, mine, result)
    weight_out[:, width:] = jnp.where(core == 0, result, mine)


def call(kernel, args, out_shape, scratch=(), flops=0, in_place=False, in_smem=0):
    vmem = pl.BlockSpec(memory_space=pltpu.VMEM)
    single = not isinstance(out_shape, (list, tuple))
    nbytes = sum(a.size * a.dtype.itemsize for a in args)
    return pl.pallas_call(
        kernel,
        out_shape=out_shape,
        in_specs=[pl.BlockSpec(memory_space=pltpu.SMEM)] * in_smem
        + [pl.BlockSpec(memory_space=pltpu.HBM) if in_place else vmem] * (len(args) - in_smem),
        out_specs=vmem if single else [vmem] * len(out_shape),
        scratch_shapes=list(scratch),
        compiler_params=pltpu.CompilerParams(vmem_limit_bytes=PREP_VMEM if in_place else VMEM_LIMIT),
        cost_estimate=pl.CostEstimate(flops=flops, bytes_accessed=nbytes, transcendentals=0),
    )(*args)


def padded_shards(table, n_s, width):
    rows, columns = table.shape
    cut = table.reshape(rows, n_s, columns // n_s)
    cut = jnp.pad(cut, ((0, 0), (0, 0), (0, width - columns // n_s)))
    return cut.reshape(rows, n_s * width)


def without_padding(table, shards, shard):
    rows, columns = table.shape
    return table.reshape(rows, shards, columns // shards)[:, :, :shard].reshape(rows, shards * shard)


def body(
    queries, keys, values, saved_out, out_grad, proj_weight, gate_table, noise_levels, clip_lengths
):
    n_t, n_s = lax.axis_size("tm"), lax.axis_size("space")
    chips = n_s // 2
    rows, shard = out_grad.shape
    k_rows = keys.shape[0]
    frames = rows // QF
    levels = gate_table.shape[0]
    bf16, f32 = jnp.bfloat16, jnp.float32
    width = -(-shard // LANES) * LANES
    if width != shard:
        out_grad = jnp.pad(out_grad, ((0, 0), (0, width - shard)))
        proj_weight = padded_shards(proj_weight, n_s, width)
        gate_table = padded_shards(gate_table, n_s, width)

    def shape(dtype, *dims):
        return jax.ShapeDtypeStruct(dims, dtype)

    def over_chip(x, k):
        return lax.ppermute(x, "space", [(s, s ^ (2 * k)) for s in range(n_s)])

    def over_chips(x):
        return [x] + [over_chip(x, k) for k in range(1, chips)]

    def over_cores(x):
        return lax.ppermute(x, "space", [(s, s ^ 1) for s in range(n_s)])

    def over_time(x, k):
        return lax.ppermute(x, "tm", [(t, t ^ k) for t in range(n_t)])

    tiles = width // LANES
    part = rows // chips
    count = chips * frames * tiles
    starts = sections(rows, chips, tiles, n_t)

    def time_swaps(messages):
        got = {k: over_time(messages[k], k) for k in range(n_t - 1, 0, -1)}
        return [messages[0]] + [got[k] for k in range(1, n_t)]

    pieces = over_chips(out_grad)
    kept, sent = call(
        functools.partial(cut_kernel, chips),
        [proj_weight, saved_out],
        [shape(bf16, chips, HD, width), shape(bf16, HD, chips * width + HD)],
        [pltpu.SemaphoreType.DMA((2 * chips + 1,))],
        in_place=True,
    )
    received = over_cores(sent)
    packed, _ = lax.optimization_barrier((jnp.stack([queries, saved_out]), received))
    packed_all = [packed]
    for k in range(1, n_t):
        low = k & -k
        packed_all.append(over_time(packed_all[k - low], low))
    gate_table, _ = lax.optimization_barrier((gate_table, received))
    bias, gate_a, gate_b, hot = call(
        functools.partial(masks_kernel, n_t, chips, frames, rows),
        [noise_levels, clip_lengths, gate_table],
        [
            shape(f32, frames, n_t * rows),
            shape(f32, chips, frames, width),
            shape(f32, n_t, 1, width),
            shape(f32, n_t * frames, levels, LANES),
        ],
        in_smem=2,
    )
    mine, other, own_terms = call(
        functools.partial(head_kernel, chips, frames),
        [packed, kept, received, gate_a] + pieces,
        [shape(f32, rows, HD), shape(f32, rows, HD), shape(f32, count, LANES)],
        flops=4 * rows * chips * width * 2 * HD,
    )
    later_bias, _ = lax.optimization_barrier((bias, mine))
    stats = call(
        functools.partial(stats_kernel, n_t),
        [later_bias, keys] + packed_all,
        shape(f32, 2 * n_t, LANES),
        flops=2 * n_t * rows * k_rows * HD,
    )
    *heads, terms = call(
        functools.partial(join_kernel, n_t, chips, starts),
        [mine, over_cores(other), stats, own_terms, over_cores(own_terms)] + pieces,
        [shape(bf16, starts[-1], LANES)] * n_t + [shape(f32, 2 * count, LANES)],
        [pltpu.VMEM((rows, width), f32), pltpu.VMEM((chips, part, width), f32)],
    )
    heads_all = time_swaps(heads[::-1])
    step = 1
    while step < chips:
        terms = terms + over_chip(terms, step)
        step *= 2
    base = tiles * n_t * part
    gate_b, _ = lax.optimization_barrier((gate_b, terms))
    bundle = call(
        functools.partial(bundle_kernel, n_t, starts),
        [gate_b] + far_first(heads_all),
        shape(bf16, base, LANES),
    )
    bundles = over_chips(bundle)
    later_bias, _ = lax.optimization_barrier((bias, bundle))
    accs = [pltpu.VMEM((k_rows, HD), f32)] * 2
    message = shape(bf16, HD + 2 * count, rows)
    far = call(
        functools.partial(grads_kernel, n_t, starts, 2, n_t),
        [later_bias, keys, values, terms] + packed_all + heads_all[::-1],
        [shape(f32, k_rows, HD)] * 2 + [message] * (n_t - 2),
        accs,
        flops=10 * (n_t - 2) * rows * k_rows * HD,
    )
    parts = {k: over_time(far[1 + n_t - k], k) for k in range(n_t - 1, 1, -1)}
    near = call(
        functools.partial(grads_kernel, n_t, starts, 0, 2),
        [bias, keys, values, terms] + packed_all + heads_all[::-1] + list(far[:2]),
        [shape(bf16, k_rows, HD)] * 2 + [message] * 2,
        flops=20 * rows * k_rows * HD,
    )
    key_grad, value_grad = near[:2]
    parts[0], parts[1] = near[3], over_time(near[2], 1)
    parts = [parts[k] for k in range(n_t)]
    bundles, _ = lax.optimization_barrier((bundles, (key_grad, parts[: n_t // 2 - 1 : -1])))
    collected = call(
        functools.partial(collect_kernel, chips), bundles, shape(bf16, chips * base, LANES)
    )
    scratch = [pltpu.VMEM((n_t, rows, HD), f32)]
    own_half = call(
        functools.partial(own_kernel, n_t, chips),
        [collected] + packed_all,
        shape(f32, HD, width),
        scratch,
        flops=2 * n_t * rows * width * HD,
    )
    weight_grad = call(
        functools.partial(final_kernel, n_t, chips),
        [over_cores(collected), own_half] + packed_all,
        shape(f32, HD, 2 * width),
        scratch,
        flops=2 * n_t * rows * width * HD,
    )
    hot, _ = lax.optimization_barrier((hot, weight_grad))
    query_grad, gate_grad = call(
        functools.partial(finish_kernel, n_t, chips, frames),
        [hot] + parts[::-1],
        [shape(bf16, rows, HD), shape(f32, levels, n_s * width)],
        [pltpu.VMEM((n_t, 2 * count, LANES), f32)],
    )
    if width != shard:
        weight_grad = without_padding(weight_grad, 2, shard)
        gate_grad = without_padding(gate_grad, n_s, shard)
    return (query_grad, key_grad, value_grad, weight_grad, gate_grad)


def solution(mesh):
    return jax.shard_map(
        body,
        mesh=mesh,
        in_specs=(
            P("tm", "space"),
            P("tm", "space"),
            P("tm", "space"),
            P("tm", "space"),
            P("tm", "space"),
            P("space", None),
            P(),
            P(),
            P(),
        ),
        out_specs=(P("tm", "space"), P("tm", "space"), P("tm", "space"), P("space", "tm"), P()),
        check_vma=False,
    )
```

```python
import functools
import math

import jax
import jax.numpy as jnp
from jax import lax
from jax.experimental import pallas as pl
from jax.experimental.pallas import tpu as pltpu
from jax.sharding import PartitionSpec as P

HD = 128
SPF = 512
QF = 64
LANES = 128
NEG_BIG = -1e30
SCALE = 1.0 / math.sqrt(HD)
VMEM_LIMIT = 32 * 1024 * 1024
PREP_VMEM = 52 * 1024 * 1024
SPLIT = 3


def dot(a, b, on_a, on_b):
    return lax.dot_general(
        a, b, (((on_a,), (on_b,)), ((), ())), preferred_element_type=jnp.float32
    )


def far_first(blocks):
    blocks = list(blocks)
    return blocks[:1] + blocks[:0:-1]


def place():
    s = lax.axis_index("space")
    return lax.axis_index("tm"), s // 2, s % 2


def clip_numbers(clips_ref):
    bounds = []
    so_far = 0
    for c in range(clips_ref.shape[0]):
        so_far = so_far + clips_ref[c]
        bounds.append(so_far)
    return lambda frame: sum((frame >= bound).astype(jnp.int32) for bound in bounds)


def cut_kernel(chips, weight_in, saved_in, kept, sent, sems):
    _, chip, core = place()
    width = kept.shape[2]
    moves = [(saved_in, sent.at[:, chips * width : chips * width + HD])]
    for k in range(chips):
        for c, out in ((1 - core, sent.at[:, k * width : (k + 1) * width]), (core, kept.at[k])):
            columns = pl.ds(pl.multiple_of((2 * (chip ^ k) + c) * width, LANES), width)
            moves.append((weight_in.at[:, columns], out))
    copies = [pltpu.make_async_copy(a, b, sems.at[i]) for i, (a, b) in enumerate(moves)]
    for copy in copies:
        copy.start()
    for copy in copies:
        copy.wait()


def masks_kernel(n_t, chips, frames, rows, levels, clips, gate, bias, gate_a, gate_b, hot):
    t, chip, core = place()
    width = gate_a.shape[2]
    clip_of = clip_numbers(clips)
    lane = lax.broadcasted_iota(jnp.int32, (1, rows), 1)
    for kf in range(frames):
        key_frame = t * frames + kf
        key_clip = clip_of(key_frame)
        for k in range(n_t):
            row = jnp.full((1, rows), NEG_BIG, jnp.float32)
            for r in range(frames):
                frame = (t ^ k) * frames + r
                visible = (key_frame >= frame) & (clip_of(frame) == key_clip)
                value = jnp.where(visible, 0.0, NEG_BIG).astype(jnp.float32)
                row = jnp.where((lane >= r * QF) & (lane < (r + 1) * QF), value, row)
            bias[kf : kf + 1, k * rows : (k + 1) * rows] = row
    spot = lax.broadcasted_iota(jnp.int32, hot.shape[1:], 0)
    for f in range(n_t * frames):
        hot[f] = (spot == levels[f]).astype(jnp.float32)
    for r in range(frames):
        level = levels[t * frames + r]
        for k in range(chips):
            columns = pl.ds(pl.multiple_of((2 * (chip ^ k) + core) * width, LANES), width)
            gate_a[k, r : r + 1, :] = gate[pl.ds(level, 1), columns]
    mine = pl.ds(pl.multiple_of((2 * t + core) * width, LANES), width)
    for k in range(n_t):
        level = levels[(t ^ k) * frames + chip * (rows // chips) // QF]
        gate_b[k] = gate[pl.ds(level, 1), mine]


def stats_kernel(n_t, bias, keys, *refs):
    packed, out = refs[:n_t], refs[n_t]
    rows = packed[0].shape[1]
    for p in range(0, n_t, 2):
        q = jnp.concatenate([packed[p][0], packed[p + 1][0]], axis=0)
        scores = []
        for kf in range(bias.shape[0]):
            mask = bias[kf : kf + 1, p * rows : (p + 2) * rows]
            scores.append(dot(keys[kf * SPF : (kf + 1) * SPF, :], q, 1, 1) * SCALE + mask)
        top = functools.reduce(jnp.maximum, [jnp.max(x, axis=0, keepdims=True) for x in scores])
        total = sum(jnp.sum(jnp.exp(x - top), axis=0, keepdims=True) for x in scores)
        for i in range(2):
            out[p + i : p + i + 1, :] = top[:, i * rows : (i + 1) * rows]
            out[n_t + p + i : n_t + p + i + 1, :] = total[:, i * rows : (i + 1) * rows]


def head_kernel(chips, frames, packed, kept, received, gate_a, *refs):
    pieces, (mine, other, terms) = refs[:chips], refs[chips:]
    _, chip, _ = place()
    width = pieces[0].shape[1]
    tiles = width // LANES
    saved = jnp.concatenate([packed[1], received[:, chips * width : chips * width + HD]], axis=1)
    head = None
    for k in range(chips):
        weight = jnp.concatenate([kept[k], received[:, k * width : (k + 1) * width]], axis=0)
        wide = pieces[k][...].astype(jnp.float32)
        gated = jnp.concatenate(
            [
                (wide[r * QF : (r + 1) * QF] * gate_a[k, r : r + 1, :]).astype(jnp.bfloat16)
                for r in range(frames)
            ],
            axis=0,
        )
        part = dot(gated, weight, 1, 1)
        head = part if head is None else head + part
        product = wide * dot(saved, weight, 1, 0)
        for r in range(frames):
            term = jnp.sum(product[r * QF : (r + 1) * QF], axis=0, keepdims=True)
            for j in range(tiles):
                row = ((chip ^ k) * frames + r) * tiles + j
                terms[pl.ds(row, 1), :] = term[:, j * LANES : (j + 1) * LANES]
    mine[...] = head[:, :HD]
    other[...] = head[:, HD:]


def sections(rows, chips, tiles, n_t, count):
    starts = [0, rows]
    starts.append(starts[-1] + tiles * (rows // chips))
    starts.append(starts[-1] + -(-(SPLIT * 2 * n_t + count) // 16) * 16)
    return starts


def padded(x, rows):
    if x.shape[0] == rows:
        return x
    return jnp.concatenate([x, jnp.zeros((rows - x.shape[0], x.shape[1]), x.dtype)], axis=0)


def join_kernel(n_t, chips, starts, mine, received, stats, terms, *refs):
    pieces, outs, (wide, held) = refs[:chips], refs[chips : chips + n_t][::-1], refs[chips + n_t :]
    t, chip, _ = place()
    part, tiles = held.shape[1], held.shape[2] // LANES
    for k in range(chips):
        wide[...] = pieces[k][...].astype(jnp.float32)
        held[k] = wide[pl.ds(pl.multiple_of(chip * part, part), part), :]
    head = (mine[...] + received[...]).astype(jnp.bfloat16)
    rest = stats[...]
    split = []
    for _ in range(SPLIT):
        piece = rest.astype(jnp.bfloat16).astype(jnp.float32)
        split.append(piece)
        rest = rest - piece
    last = padded(jnp.concatenate(split + [terms[...]], axis=0), starts[3] - starts[2])
    last = last.astype(jnp.bfloat16)
    for k in range(n_t):
        rows = held[chip ^ t ^ k]
        rows = jnp.concatenate([rows[:, j * LANES : (j + 1) * LANES] for j in range(tiles)], axis=0)
        outs[k][: starts[1], :] = head
        outs[k][starts[1] : starts[2], :] = rows.astype(jnp.bfloat16)
        outs[k][starts[2] :, :] = last


def bundle_kernel(n_t, starts, count, gate_b, *refs):
    heads, out = far_first(refs[:n_t]), refs[n_t]
    tiles = gate_b.shape[2] // LANES
    part = (starts[2] - starts[1]) // tiles
    wide = [heads[k][starts[1] : starts[2], :].astype(jnp.float32) for k in range(n_t)]
    for j in range(tiles):
        gated = jnp.concatenate(
            [
                wide[k][j * part : (j + 1) * part] * gate_b[k, :, j * LANES : (j + 1) * LANES]
                for k in range(n_t)
            ],
            axis=0,
        )
        out[j * n_t * part : (j + 1) * n_t * part, :] = gated.astype(jnp.bfloat16)
    first = SPLIT * 2 * n_t
    terms = [heads[k][starts[2] :, :].astype(jnp.float32)[first : first + count] for k in range(n_t)]
    out[tiles * n_t * part :, :] = jnp.concatenate(terms, axis=0).astype(jnp.bfloat16)


def grads_kernel(n_t, starts, first, last, bias, keys, values, *refs):
    packed, heads = refs[:n_t], refs[n_t : 2 * n_t][::-1]
    refs = refs[2 * n_t :]
    if first == 0:
        sums, refs = refs[:2], refs[2:]
    key_out, value_out = refs[:2]
    outs = refs[2 : 2 + last - first][::-1]
    accs = refs[2 + last - first :]
    rows = packed[0].shape[1]
    ones = jnp.ones((8, HD), jnp.float32)
    keys_t = jnp.transpose(keys[...])
    stats = []
    for k in range(n_t):
        parts = heads[k][starts[2] :, :].astype(jnp.float32)
        stats.append(sum(parts[i * 2 * n_t : (i + 1) * 2 * n_t] for i in range(SPLIT)))
    for p in range(first, last, 2):
        q = jnp.concatenate([packed[p][0], packed[p + 1][0]], axis=0)
        o = jnp.concatenate([packed[p][1], packed[p + 1][1]], axis=0)
        g = jnp.concatenate([heads[p][:rows, :], heads[p + 1][:rows, :]], axis=0)
        delta = lax.dot_general(
            ones,
            g.astype(jnp.float32) * o.astype(jnp.float32),
            (((1,), (1,)), ((), ())),
            precision=lax.Precision.HIGHEST,
            preferred_element_type=jnp.float32,
        )[0:1]
        lse = []
        for i in (p, p + 1):
            tops = [stats[k][i ^ k : (i ^ k) + 1] for k in range(n_t)]
            sums_of = [stats[k][n_t + (i ^ k) : n_t + (i ^ k) + 1] for k in range(n_t)]
            top = functools.reduce(jnp.maximum, tops)
            lse.append(top + jnp.log(sum(b * jnp.exp(a - top) for a, b in zip(tops, sums_of))))
        lse = jnp.concatenate(lse, axis=1)
        query_part = None
        for kf in range(bias.shape[0]):
            span = slice(kf * SPF, (kf + 1) * SPF)
            shift = bias[kf : kf + 1, p * rows : (p + 2) * rows] - lse
            probs = jnp.exp(dot(keys[span, :], q, 1, 1) * SCALE + shift)
            score_grad = (probs * (dot(values[span, :], g, 1, 1) - delta)).astype(jnp.bfloat16)
            value_add = dot(probs.astype(jnp.bfloat16), g, 1, 0)
            key_add = dot(score_grad, q, 1, 0)
            if p > first:
                value_add = value_add + accs[1][span, :]
                key_add = key_add + accs[0][span, :]
            if p + 2 < last:
                accs[1][span, :] = value_add
                accs[0][span, :] = key_add
            elif first:
                value_out[span, :] = value_add
                key_out[span, :] = key_add
            else:
                value_out[span, :] = (value_add + sums[1][span, :]).astype(jnp.bfloat16)
                key_out[span, :] = ((key_add + sums[0][span, :]) * SCALE).astype(jnp.bfloat16)
            part = dot(keys_t[:, span], score_grad, 1, 0)
            query_part = part if query_part is None else query_part + part
        outs[p - first][...] = query_part[:, :rows].astype(jnp.bfloat16)
        outs[p + 1 - first][...] = query_part[:, rows:].astype(jnp.bfloat16)


def query_kernel(n_t, *refs):
    total = refs[0][...].astype(jnp.float32)
    for k in range(1, n_t):
        total = total + refs[k][...].astype(jnp.float32)
    refs[n_t][...] = jnp.transpose(total * SCALE).astype(jnp.bfloat16)


def half_results(n_t, chips, frames, hot, gated_refs, packed, saved, held, tiles):
    t, chip, _ = place()
    rows = saved.shape[1]
    part = rows // chips
    base = tiles * n_t * part
    for k in range(n_t):
        saved[k] = packed[k][1].astype(jnp.float32)
    ordered = []
    for c in range(chips):
        mine = pl.ds(pl.multiple_of((chip ^ c) * part, part), part)
        ordered += [saved[k, mine, :] for k in range(n_t)]
        held[chip ^ c] = gated_refs[c][base:, :].astype(jnp.float32)
    ordered = jnp.transpose(jnp.concatenate(ordered, axis=0)).astype(jnp.bfloat16)
    gated = jnp.concatenate(
        [
            jnp.concatenate(
                [ref[j * n_t * part : (j + 1) * n_t * part, :] for ref in gated_refs], axis=0
            )
            for j in range(tiles)
        ],
        axis=1,
    )
    terms = held[0]
    for c in range(1, chips):
        terms = terms + held[c]
    count = terms.shape[0] // n_t
    for k in range(n_t):
        held[0, pl.ds(pl.multiple_of((t ^ k) * count, 8), count), :] = terms[k * count : (k + 1) * count]

    def gate_tile(a, j):
        total = jnp.zeros(hot.shape[1:], jnp.float32)
        for f in range(n_t * frames):
            row = (f // frames) * count + (a * frames + f % frames) * tiles + j
            total = total + hot[f] * held[0, row : row + 1, :]
        return total

    return dot(ordered, gated, 1, 0), gate_tile


def own_kernel(n_t, chips, frames, hot, *refs):
    gated, packed = refs[:chips], refs[chips : chips + n_t]
    weight_out, gate_out, saved, held = refs[chips + n_t :]
    tiles = weight_out.shape[1] // LANES
    result, gate_tile = half_results(n_t, chips, frames, hot, gated, packed, saved, held, tiles)
    weight_out[...] = result
    for a in range(chips):
        for j in range(tiles):
            gate_out[:, (a * tiles + j) * LANES : (a * tiles + j + 1) * LANES] = gate_tile(a, j)


def final_kernel(n_t, chips, frames, hot, own_weight, own_gate, *refs):
    gated, packed = refs[:chips], refs[chips : chips + n_t]
    weight_out, gate_out, saved, held = refs[chips + n_t :]
    core = place()[2]
    width = own_weight.shape[1]
    tiles = width // LANES
    result, gate_tile = half_results(n_t, chips, frames, hot, gated, packed, saved, held, tiles)
    mine = own_weight[...]
    weight_out[:, :width] = jnp.where(core == 0, mine, result)
    weight_out[:, width:] = jnp.where(core == 0, result, mine)
    for a in range(chips):
        for j in range(tiles):
            first = gate_tile(a, j)
            second = own_gate[:, (a * tiles + j) * LANES : (a * tiles + j + 1) * LANES]
            column = 2 * a * width + j * LANES
            gate_out[:, column : column + LANES] = jnp.where(core == 0, second, first)
            column += width
            gate_out[:, column : column + LANES] = jnp.where(core == 0, first, second)


def call(kernel, args, out_shape, scratch=(), flops=0, in_place=False, in_smem=0):
    vmem = pl.BlockSpec(memory_space=pltpu.VMEM)
    single = not isinstance(out_shape, (list, tuple))
    nbytes = sum(a.size * a.dtype.itemsize for a in args)
    return pl.pallas_call(
        kernel,
        out_shape=out_shape,
        in_specs=[pl.BlockSpec(memory_space=pltpu.SMEM)] * in_smem
        + [pl.BlockSpec(memory_space=pltpu.HBM) if in_place else vmem] * (len(args) - in_smem),
        out_specs=vmem if single else [vmem] * len(out_shape),
        scratch_shapes=list(scratch),
        compiler_params=pltpu.CompilerParams(vmem_limit_bytes=PREP_VMEM if in_place else VMEM_LIMIT),
        cost_estimate=pl.CostEstimate(flops=flops, bytes_accessed=nbytes, transcendentals=0),
    )(*args)


def padded_shards(table, n_s, width):
    rows, columns = table.shape
    cut = table.reshape(rows, n_s, columns // n_s)
    cut = jnp.pad(cut, ((0, 0), (0, 0), (0, width - columns // n_s)))
    return cut.reshape(rows, n_s * width)


def without_padding(table, shards, shard):
    rows, columns = table.shape
    return table.reshape(rows, shards, columns // shards)[:, :, :shard].reshape(rows, shards * shard)


def body(
    queries, keys, values, saved_out, out_grad, proj_weight, gate_table, noise_levels, clip_lengths
):
    n_t, n_s = lax.axis_size("tm"), lax.axis_size("space")
    chips = n_s // 2
    rows, shard = out_grad.shape
    k_rows = keys.shape[0]
    frames = rows // QF
    levels = gate_table.shape[0]
    bf16, f32 = jnp.bfloat16, jnp.float32
    width = -(-shard // LANES) * LANES
    if width != shard:
        out_grad = jnp.pad(out_grad, ((0, 0), (0, width - shard)))
        proj_weight = padded_shards(proj_weight, n_s, width)
        gate_table = padded_shards(gate_table, n_s, width)

    def shape(dtype, *dims):
        return jax.ShapeDtypeStruct(dims, dtype)

    def over_chips(x):
        return [x] + [
            lax.ppermute(x, "space", [(s, s ^ (2 * k)) for s in range(n_s)]) for k in range(1, chips)
        ]

    def over_cores(x):
        return lax.ppermute(x, "space", [(s, s ^ 1) for s in range(n_s)])

    def over_time(x, k):
        return lax.ppermute(x, "tm", [(t, t ^ k) for t in range(n_t)])

    tiles = width // LANES
    part = rows // chips
    count = chips * frames * tiles
    starts = sections(rows, chips, tiles, n_t, count)

    def time_swaps(messages):
        got = {k: over_time(messages[k], k) for k in range(n_t - 1, 0, -1)}
        return [messages[0]] + [got[k] for k in range(1, n_t)]

    pieces = over_chips(out_grad)
    kept, sent = call(
        functools.partial(cut_kernel, chips),
        [proj_weight, saved_out],
        [shape(bf16, chips, HD, width), shape(bf16, HD, chips * width + HD)],
        [pltpu.SemaphoreType.DMA((2 * chips + 1,))],
        in_place=True,
    )
    received = over_cores(sent)
    packed, _ = lax.optimization_barrier((jnp.stack([queries, saved_out]), received))
    packed_all = [packed]
    for k in range(1, n_t):
        low = k & -k
        packed_all.append(over_time(packed_all[k - low], low))
    gate_table, _ = lax.optimization_barrier((gate_table, received))
    bias, gate_a, gate_b, hot = call(
        functools.partial(masks_kernel, n_t, chips, frames, rows),
        [noise_levels, clip_lengths, gate_table],
        [
            shape(f32, frames, n_t * rows),
            shape(f32, chips, frames, width),
            shape(f32, n_t, 1, width),
            shape(f32, n_t * frames, levels, LANES),
        ],
        in_smem=2,
    )
    mine, other, terms = call(
        functools.partial(head_kernel, chips, frames),
        [packed, kept, received, gate_a] + pieces,
        [shape(f32, rows, HD), shape(f32, rows, HD), shape(f32, count, LANES)],
        flops=4 * rows * chips * width * 2 * HD,
    )
    later_bias, _ = lax.optimization_barrier((bias, mine))
    stats = call(
        functools.partial(stats_kernel, n_t),
        [later_bias, keys] + packed_all,
        shape(f32, 2 * n_t, LANES),
        flops=2 * n_t * rows * k_rows * HD,
    )
    heads = call(
        functools.partial(join_kernel, n_t, chips, starts),
        [mine, over_cores(other), stats, terms] + pieces,
        [shape(bf16, starts[-1], LANES)] * n_t,
        [pltpu.VMEM((rows, width), f32), pltpu.VMEM((chips, part, width), f32)],
    )
    heads_all = time_swaps(heads[::-1])
    base = tiles * n_t * part
    bundle = call(
        functools.partial(bundle_kernel, n_t, starts, count),
        [gate_b] + far_first(heads_all),
        shape(bf16, base + n_t * count, LANES),
    )
    bundles = over_chips(bundle)
    later_bias, _ = lax.optimization_barrier((bias, bundle))
    accs = [pltpu.VMEM((k_rows, HD), f32)] * 2
    far = call(
        functools.partial(grads_kernel, n_t, starts, 2, n_t),
        [later_bias, keys, values] + packed_all + heads_all[::-1],
        [shape(f32, k_rows, HD)] * 2 + [shape(bf16, HD, rows)] * (n_t - 2),
        accs,
        flops=10 * (n_t - 2) * rows * k_rows * HD,
    )
    parts = {k: over_time(far[1 + n_t - k], k) for k in range(n_t - 1, 1, -1)}
    near = call(
        functools.partial(grads_kernel, n_t, starts, 0, 2),
        [bias, keys, values] + packed_all + heads_all[::-1] + list(far[:2]),
        [shape(bf16, k_rows, HD)] * 2 + [shape(bf16, HD, rows)] * 2,
        flops=20 * rows * k_rows * HD,
    )
    key_grad, value_grad = near[:2]
    parts[0], parts[1] = near[3], over_time(near[2], 1)
    parts = [parts[k] for k in range(n_t)]
    bundles, _ = lax.optimization_barrier((bundles, (key_grad, parts[: n_t // 2 - 1 : -1])))
    scratch = [pltpu.VMEM((n_t, rows, HD), f32), pltpu.VMEM((chips, n_t * count, LANES), f32)]
    own_halves = call(
        functools.partial(own_kernel, n_t, chips, frames),
        [hot] + bundles + packed_all,
        [shape(f32, HD, width), shape(f32, levels, chips * width)],
        scratch,
        flops=2 * n_t * rows * width * HD,
    )
    weight_grad, gate_grad = call(
        functools.partial(final_kernel, n_t, chips, frames),
        [hot, *own_halves] + [over_cores(x) for x in bundles] + packed_all,
        [shape(f32, HD, 2 * width), shape(f32, levels, n_s * width)],
        scratch,
        flops=2 * n_t * rows * width * HD,
    )
    parts[0], _ = lax.optimization_barrier((parts[0], gate_grad))
    query_grad = call(functools.partial(query_kernel, n_t), parts[::-1], shape(bf16, rows, HD))
    if width != shard:
        weight_grad = without_padding(weight_grad, 2, shard)
        gate_grad = without_padding(gate_grad, n_s, shard)
    return (query_grad, key_grad, value_grad, weight_grad, gate_grad)


def solution(mesh):
    return jax.shard_map(
        body,
        mesh=mesh,
        in_specs=(
            P("tm", "space"),
            P("tm", "space"),
            P("tm", "space"),
            P("tm", "space"),
            P("tm", "space"),
            P("space", None),
            P(),
            P(),
            P(),
        ),
        out_specs=(P("tm", "space"), P("tm", "space"), P("tm", "space"), P("space", "tm"), P()),
        check_vma=False,
    )
```

```python
import functools
import math

import jax
import jax.numpy as jnp
from jax import lax
from jax.experimental import pallas as pl
from jax.experimental.pallas import tpu as pltpu
from jax.sharding import PartitionSpec as P

HD = 128
SPF = 512
QF = 64
LANES = 128
NEG_BIG = -1e30
SCALE = 1.0 / math.sqrt(HD)
VMEM_LIMIT = 32 * 1024 * 1024
PREP_VMEM = 52 * 1024 * 1024
SPLIT = 3


def dot(a, b, on_a, on_b):
    return lax.dot_general(
        a, b, (((on_a,), (on_b,)), ((), ())), preferred_element_type=jnp.float32
    )


def last_swapped(blocks):
    blocks = list(blocks)
    return blocks[:-2] + blocks[:-3:-1]


def place():
    s = lax.axis_index("space")
    return lax.axis_index("tm"), s // 2, s % 2


def clip_numbers(clips_ref):
    bounds = []
    so_far = 0
    for c in range(clips_ref.shape[0]):
        so_far = so_far + clips_ref[c]
        bounds.append(so_far)
    return lambda frame: sum((frame >= bound).astype(jnp.int32) for bound in bounds)


def fetch_kernel(chips, weight_in, grad_in, kept, grad, sems):
    _, chip, core = place()
    width = kept.shape[2]
    copies = [pltpu.make_async_copy(grad_in, grad, sems.at[chips])]
    for k in range(chips):
        columns = pl.ds(pl.multiple_of((2 * (chip ^ k) + core) * width, LANES), width)
        copies.append(pltpu.make_async_copy(weight_in.at[:, columns], kept.at[k], sems.at[k]))
    for copy in copies:
        copy.start()
    for copy in copies:
        copy.wait()


def masks_kernel(n_t, chips, frames, rows, levels, clips, gate, bias, gate_a, gate_b, hot):
    t, chip, core = place()
    width = gate_a.shape[2]
    clip_of = clip_numbers(clips)
    lane = lax.broadcasted_iota(jnp.int32, (1, rows), 1)
    for kf in range(frames):
        key_frame = t * frames + kf
        key_clip = clip_of(key_frame)
        for k in range(n_t):
            row = jnp.full((1, rows), NEG_BIG, jnp.float32)
            for r in range(frames):
                frame = (t ^ k) * frames + r
                visible = (key_frame >= frame) & (clip_of(frame) == key_clip)
                value = jnp.where(visible, 0.0, NEG_BIG).astype(jnp.float32)
                row = jnp.where((lane >= r * QF) & (lane < (r + 1) * QF), value, row)
            bias[kf : kf + 1, k * rows : (k + 1) * rows] = row
    spot = lax.broadcasted_iota(jnp.int32, hot.shape[1:], 0)
    for f in range(n_t * frames):
        hot[f] = (spot == levels[f]).astype(jnp.float32)
    for r in range(frames):
        level = levels[t * frames + r]
        for k in range(chips):
            columns = pl.ds(pl.multiple_of((2 * (chip ^ k) + core) * width, LANES), width)
            gate_a[k, r : r + 1, :] = gate[pl.ds(level, 1), columns]
    mine = pl.ds(pl.multiple_of((2 * t + core) * width, LANES), width)
    for k in range(n_t):
        level = levels[(t ^ k) * frames + chip * (rows // chips) // QF]
        gate_b[k] = gate[pl.ds(level, 1), mine]


def stats_kernel(n_t, bias, keys, *refs):
    packed, out = refs[:n_t], refs[n_t]
    rows = packed[0].shape[1]
    for p in range(0, n_t, 2):
        q = jnp.concatenate([packed[p][0], packed[p + 1][0]], axis=0)
        scores = []
        for kf in range(bias.shape[0]):
            mask = bias[kf : kf + 1, p * rows : (p + 2) * rows]
            scores.append(dot(keys[kf * SPF : (kf + 1) * SPF, :], q, 1, 1) * SCALE + mask)
        top = functools.reduce(jnp.maximum, [jnp.max(x, axis=0, keepdims=True) for x in scores])
        total = sum(jnp.sum(jnp.exp(x - top), axis=0, keepdims=True) for x in scores)
        for i in range(2):
            out[p + i : p + i + 1, :] = top[:, i * rows : (i + 1) * rows]
            out[n_t + p + i : n_t + p + i + 1, :] = total[:, i * rows : (i + 1) * rows]


def head_kernel(chips, frames, packed, other_saved, kept, received, gate_a, *refs):
    pieces, (mine, other, terms) = refs[:chips], refs[chips:]
    _, chip, core = place()
    width = pieces[0].shape[1]
    tiles = width // LANES
    saved = jnp.concatenate([packed[1], other_saved[...]], axis=1)
    head = None
    for k in range(chips):
        columns = pl.ds(pl.multiple_of((2 * (chip ^ k) + core) * width, LANES), width)
        weight = jnp.concatenate([kept[k], received[:, columns]], axis=0)
        wide = pieces[k][...].astype(jnp.float32)
        gated = jnp.concatenate(
            [
                (wide[r * QF : (r + 1) * QF] * gate_a[k, r : r + 1, :]).astype(jnp.bfloat16)
                for r in range(frames)
            ],
            axis=0,
        )
        part = dot(gated, weight, 1, 1)
        head = part if head is None else head + part
        product = wide * dot(saved, weight, 1, 0)
        for r in range(frames):
            term = jnp.sum(product[r * QF : (r + 1) * QF], axis=0, keepdims=True)
            for j in range(tiles):
                row = ((chip ^ k) * frames + r) * tiles + j
                terms[pl.ds(row, 1), :] = term[:, j * LANES : (j + 1) * LANES]
    mine[...] = head[:, :HD]
    other[...] = head[:, HD:]


def sections(rows, chips, tiles, n_t, count):
    starts = [0, rows]
    starts.append(starts[-1] + tiles * (rows // chips))
    starts.append(starts[-1] + -(-(SPLIT * 2 * n_t + count) // 16) * 16)
    return starts


def padded(x, rows):
    if x.shape[0] == rows:
        return x
    return jnp.concatenate([x, jnp.zeros((rows - x.shape[0], x.shape[1]), x.dtype)], axis=0)


def join_kernel(n_t, chips, starts, mine, received, stats, terms, *refs):
    pieces, outs, (wide, held) = refs[:chips], refs[chips : chips + n_t][::-1], refs[chips + n_t :]
    t, chip, _ = place()
    part, tiles = held.shape[1], held.shape[2] // LANES
    for k in range(chips):
        wide[...] = pieces[k][...].astype(jnp.float32)
        held[k] = wide[pl.ds(pl.multiple_of(chip * part, part), part), :]
    head = (mine[...] + received[...]).astype(jnp.bfloat16)
    rest = stats[...]
    split = []
    for _ in range(SPLIT):
        piece = rest.astype(jnp.bfloat16).astype(jnp.float32)
        split.append(piece)
        rest = rest - piece
    last = padded(jnp.concatenate(split + [terms[...]], axis=0), starts[3] - starts[2])
    last = last.astype(jnp.bfloat16)
    for k in range(n_t):
        rows = held[chip ^ t ^ k]
        rows = jnp.concatenate([rows[:, j * LANES : (j + 1) * LANES] for j in range(tiles)], axis=0)
        outs[k][: starts[1], :] = head
        outs[k][starts[1] : starts[2], :] = rows.astype(jnp.bfloat16)
        outs[k][starts[2] :, :] = last


def bundle_kernel(n_t, starts, count, gate_b, *refs):
    heads, out = last_swapped(refs[:n_t]), refs[n_t]
    tiles = gate_b.shape[2] // LANES
    part = (starts[2] - starts[1]) // tiles
    wide = [heads[k][starts[1] : starts[2], :].astype(jnp.float32) for k in range(n_t)]
    for j in range(tiles):
        gated = jnp.concatenate(
            [
                wide[k][j * part : (j + 1) * part] * gate_b[k, :, j * LANES : (j + 1) * LANES]
                for k in range(n_t)
            ],
            axis=0,
        )
        out[j * n_t * part : (j + 1) * n_t * part, :] = gated.astype(jnp.bfloat16)
    first = SPLIT * 2 * n_t
    terms = [heads[k][starts[2] :, :].astype(jnp.float32)[first : first + count] for k in range(n_t)]
    out[tiles * n_t * part :, :] = jnp.concatenate(terms, axis=0).astype(jnp.bfloat16)


def collect_kernel(chips, base, *refs):
    pieces, out, held = refs[:chips], refs[chips], refs[chips + 1]
    chip = place()[1]
    for k in range(chips):
        out[k * base : (k + 1) * base, :] = pieces[k][:base, :]
        held[chip ^ k] = pieces[k][base:, :].astype(jnp.float32)
    total = held[0]
    for k in range(1, chips):
        total = total + held[k]
    high = total.astype(jnp.bfloat16)
    count = total.shape[0]
    out[chips * base : chips * base + count, :] = high
    out[chips * base + count :, :] = (total - high.astype(jnp.float32)).astype(jnp.bfloat16)


def grads_kernel(n_t, starts, first, last, bias, keys, values, *refs):
    packed, heads = refs[:n_t], refs[n_t : 2 * n_t][::-1]
    refs = refs[2 * n_t :]
    if first == 0:
        sums, refs = refs[:2], refs[2:]
    key_out, value_out = refs[:2]
    outs = refs[2 : 2 + last - first][::-1]
    accs = refs[2 + last - first :]
    rows = packed[0].shape[1]
    ones = jnp.ones((8, HD), jnp.float32)
    keys_t = jnp.transpose(keys[...])
    stats = []
    for k in range(n_t):
        parts = heads[k][starts[2] :, :].astype(jnp.float32)
        stats.append(sum(parts[i * 2 * n_t : (i + 1) * 2 * n_t] for i in range(SPLIT)))
    for p in range(first, last, 2):
        q = jnp.concatenate([packed[p][0], packed[p + 1][0]], axis=0)
        o = jnp.concatenate([packed[p][1], packed[p + 1][1]], axis=0)
        g = jnp.concatenate([heads[p][:rows, :], heads[p + 1][:rows, :]], axis=0)
        delta = lax.dot_general(
            ones,
            g.astype(jnp.float32) * o.astype(jnp.float32),
            (((1,), (1,)), ((), ())),
            precision=lax.Precision.HIGHEST,
            preferred_element_type=jnp.float32,
        )[0:1]
        lse = []
        for i in (p, p + 1):
            tops = [stats[k][i ^ k : (i ^ k) + 1] for k in range(n_t)]
            sums_of = [stats[k][n_t + (i ^ k) : n_t + (i ^ k) + 1] for k in range(n_t)]
            top = functools.reduce(jnp.maximum, tops)
            lse.append(top + jnp.log(sum(b * jnp.exp(a - top) for a, b in zip(tops, sums_of))))
        lse = jnp.concatenate(lse, axis=1)
        query_part = None
        for kf in range(bias.shape[0]):
            span = slice(kf * SPF, (kf + 1) * SPF)
            shift = bias[kf : kf + 1, p * rows : (p + 2) * rows] - lse
            probs = jnp.exp(dot(keys[span, :], q, 1, 1) * SCALE + shift)
            score_grad = (probs * (dot(values[span, :], g, 1, 1) - delta)).astype(jnp.bfloat16)
            value_add = dot(probs.astype(jnp.bfloat16), g, 1, 0)
            key_add = dot(score_grad, q, 1, 0)
            if p > first:
                value_add = value_add + accs[1][span, :]
                key_add = key_add + accs[0][span, :]
            if p + 2 < last:
                accs[1][span, :] = value_add
                accs[0][span, :] = key_add
            elif first:
                value_out[span, :] = value_add
                key_out[span, :] = key_add
            else:
                value_out[span, :] = (value_add + sums[1][span, :]).astype(jnp.bfloat16)
                key_out[span, :] = ((key_add + sums[0][span, :]) * SCALE).astype(jnp.bfloat16)
            part = dot(keys_t[:, span], score_grad, 1, 0)
            query_part = part if query_part is None else query_part + part
        outs[p - first][...] = query_part[:, :rows].astype(jnp.bfloat16)
        outs[p + 1 - first][...] = query_part[:, rows:].astype(jnp.bfloat16)


def query_kernel(n_t, *refs):
    total = refs[0][...].astype(jnp.float32)
    for k in range(1, n_t):
        total = total + refs[k][...].astype(jnp.float32)
    refs[n_t][...] = jnp.transpose(total * SCALE).astype(jnp.bfloat16)


def half_results(n_t, chips, frames, hot, ref, packed, saved, held, tiles):
    t, chip, _ = place()
    rows = saved.shape[1]
    part = rows // chips
    base = tiles * n_t * part
    for k in range(n_t):
        saved[k] = packed[k][1].astype(jnp.float32)
    ordered = []
    for c in range(chips):
        mine = pl.ds(pl.multiple_of((chip ^ c) * part, part), part)
        ordered += [saved[k, mine, :] for k in range(n_t)]
    ordered = jnp.transpose(jnp.concatenate(ordered, axis=0)).astype(jnp.bfloat16)
    gated = jnp.concatenate(
        [
            jnp.concatenate(
                [
                    ref[c * base + j * n_t * part : c * base + (j + 1) * n_t * part, :]
                    for c in range(chips)
                ],
                axis=0,
            )
            for j in range(tiles)
        ],
        axis=1,
    )
    count = (ref.shape[0] - chips * base) // 2
    each = count // n_t
    terms = ref[chips * base : chips * base + count, :].astype(jnp.float32)
    terms = terms + ref[chips * base + count :, :].astype(jnp.float32)
    for k in range(n_t):
        held[t ^ k] = terms[k * each : (k + 1) * each]

    def gate_tile(a, j):
        total = jnp.zeros(hot.shape[1:], jnp.float32)
        for f in range(n_t * frames):
            row = (a * frames + f % frames) * tiles + j
            total = total + hot[f] * held[f // frames, row : row + 1, :]
        return total

    return dot(ordered, gated, 1, 0), gate_tile


def own_kernel(n_t, chips, frames, hot, own, *refs):
    packed, (weight_out, gate_out, saved, held) = refs[:n_t], refs[n_t:]
    tiles = weight_out.shape[1] // LANES
    result, gate_tile = half_results(n_t, chips, frames, hot, own, packed, saved, held, tiles)
    weight_out[...] = result
    for a in range(chips):
        for j in range(tiles):
            gate_out[:, (a * tiles + j) * LANES : (a * tiles + j + 1) * LANES] = gate_tile(a, j)


def final_kernel(n_t, chips, frames, hot, other, own_weight, own_gate, *refs):
    packed, (weight_out, gate_out, saved, held) = refs[:n_t], refs[n_t:]
    core = place()[2]
    width = own_weight.shape[1]
    tiles = width // LANES
    result, gate_tile = half_results(n_t, chips, frames, hot, other, packed, saved, held, tiles)
    mine = own_weight[...]
    weight_out[:, :width] = jnp.where(core == 0, mine, result)
    weight_out[:, width:] = jnp.where(core == 0, result, mine)
    for a in range(chips):
        for j in range(tiles):
            first = gate_tile(a, j)
            second = own_gate[:, (a * tiles + j) * LANES : (a * tiles + j + 1) * LANES]
            column = 2 * a * width + j * LANES
            gate_out[:, column : column + LANES] = jnp.where(core == 0, second, first)
            column += width
            gate_out[:, column : column + LANES] = jnp.where(core == 0, first, second)


def call(kernel, args, out_shape, scratch=(), flops=0, in_place=False, in_smem=0):
    vmem = pl.BlockSpec(memory_space=pltpu.VMEM)
    single = not isinstance(out_shape, (list, tuple))
    nbytes = sum(a.size * a.dtype.itemsize for a in args)
    return pl.pallas_call(
        kernel,
        out_shape=out_shape,
        in_specs=[pl.BlockSpec(memory_space=pltpu.SMEM)] * in_smem
        + [pl.BlockSpec(memory_space=pltpu.HBM) if in_place else vmem] * (len(args) - in_smem),
        out_specs=vmem if single else [vmem] * len(out_shape),
        scratch_shapes=list(scratch),
        compiler_params=pltpu.CompilerParams(vmem_limit_bytes=PREP_VMEM if in_place else VMEM_LIMIT),
        cost_estimate=pl.CostEstimate(flops=flops, bytes_accessed=nbytes, transcendentals=0),
    )(*args)


def padded_shards(table, n_s, width):
    rows, columns = table.shape
    cut = table.reshape(rows, n_s, columns // n_s)
    cut = jnp.pad(cut, ((0, 0), (0, 0), (0, width - columns // n_s)))
    return cut.reshape(rows, n_s * width)


def without_padding(table, shards, shard):
    rows, columns = table.shape
    return table.reshape(rows, shards, columns // shards)[:, :, :shard].reshape(rows, shards * shard)


def body(
    queries, keys, values, saved_out, out_grad, proj_weight, gate_table, noise_levels, clip_lengths
):
    n_t, n_s = lax.axis_size("tm"), lax.axis_size("space")
    chips = n_s // 2
    rows, shard = out_grad.shape
    k_rows = keys.shape[0]
    frames = rows // QF
    levels = gate_table.shape[0]
    bf16, f32 = jnp.bfloat16, jnp.float32
    width = -(-shard // LANES) * LANES
    if width != shard:
        out_grad = jnp.pad(out_grad, ((0, 0), (0, width - shard)))
        proj_weight = padded_shards(proj_weight, n_s, width)
        gate_table = padded_shards(gate_table, n_s, width)

    def shape(dtype, *dims):
        return jax.ShapeDtypeStruct(dims, dtype)

    def over_chips(x):
        return [x] + [
            lax.ppermute(x, "space", [(s, s ^ (2 * k)) for s in range(n_s)]) for k in range(1, chips)
        ]

    def over_cores(x):
        return lax.ppermute(x, "space", [(s, s ^ 1) for s in range(n_s)])

    def over_time(x, k):
        return lax.ppermute(x, "tm", [(t, t ^ k) for t in range(n_t)])

    tiles = width // LANES
    part = rows // chips
    count = chips * frames * tiles
    starts = sections(rows, chips, tiles, n_t, count)

    def time_swaps(messages):
        got = {k: over_time(messages[k], k) for k in range(n_t - 1, 0, -1)}
        return [messages[0]] + [got[k] for k in range(1, n_t)]

    pieces = over_chips(out_grad)
    received, other_saved = over_cores(proj_weight), over_cores(saved_out)
    packed, _ = lax.optimization_barrier(
        (jnp.stack([queries, saved_out]), (received, other_saved))
    )
    packed_all = [packed]
    for k in range(1, n_t):
        low = k & -k
        packed_all.append(over_time(packed_all[k - low], low))
    (to_fetch, own_grad), _ = lax.optimization_barrier(((proj_weight, out_grad), received))
    kept, pieces[0] = call(
        functools.partial(fetch_kernel, chips),
        [to_fetch, own_grad],
        [shape(bf16, chips, HD, width), shape(bf16, rows, width)],
        [pltpu.SemaphoreType.DMA((chips + 1,))],
        in_place=True,
    )
    gate_table, _ = lax.optimization_barrier((gate_table, received))
    bias, gate_a, gate_b, hot = call(
        functools.partial(masks_kernel, n_t, chips, frames, rows),
        [noise_levels, clip_lengths, gate_table],
        [
            shape(f32, frames, n_t * rows),
            shape(f32, chips, frames, width),
            shape(f32, n_t, 1, width),
            shape(f32, n_t * frames, levels, LANES),
        ],
        in_smem=2,
    )
    mine, other, terms = call(
        functools.partial(head_kernel, chips, frames),
        [packed, other_saved, kept, received, gate_a] + pieces,
        [shape(f32, rows, HD), shape(f32, rows, HD), shape(f32, count, LANES)],
        flops=4 * rows * chips * width * 2 * HD,
    )
    later_bias, _ = lax.optimization_barrier((bias, mine))
    stats = call(
        functools.partial(stats_kernel, n_t),
        [later_bias, keys] + packed_all,
        shape(f32, 2 * n_t, LANES),
        flops=2 * n_t * rows * k_rows * HD,
    )
    heads = call(
        functools.partial(join_kernel, n_t, chips, starts),
        [mine, over_cores(other), stats, terms] + pieces,
        [shape(bf16, starts[-1], LANES)] * n_t,
        [pltpu.VMEM((rows, width), f32), pltpu.VMEM((chips, part, width), f32)],
    )
    heads_all = time_swaps(heads[::-1])
    base = tiles * n_t * part
    bundle = call(
        functools.partial(bundle_kernel, n_t, starts, count),
        [gate_b] + last_swapped(heads_all),
        shape(bf16, base + n_t * count, LANES),
    )
    bundles = over_chips(bundle)
    later_bias, _ = lax.optimization_barrier((bias, bundle))
    accs = [pltpu.VMEM((k_rows, HD), f32)] * 2
    far = call(
        functools.partial(grads_kernel, n_t, starts, 2, n_t),
        [later_bias, keys, values] + packed_all + heads_all[::-1],
        [shape(f32, k_rows, HD)] * 2 + [shape(bf16, HD, rows)] * (n_t - 2),
        accs,
        flops=10 * (n_t - 2) * rows * k_rows * HD,
    )
    parts = {k: over_time(far[1 + n_t - k], k) for k in range(n_t - 1, 1, -1)}
    near = call(
        functools.partial(grads_kernel, n_t, starts, 0, 2),
        [bias, keys, values] + packed_all + heads_all[::-1] + list(far[:2]),
        [shape(bf16, k_rows, HD)] * 2 + [shape(bf16, HD, rows)] * 2,
        flops=20 * rows * k_rows * HD,
    )
    key_grad, value_grad = near[:2]
    parts[0], parts[1] = near[3], over_time(near[2], 1)
    parts = [parts[k] for k in range(n_t)]
    bundles, _ = lax.optimization_barrier((bundles, (key_grad, parts[: n_t // 2 - 1 : -1])))
    collected = call(
        functools.partial(collect_kernel, chips, base),
        bundles,
        shape(bf16, chips * base + 2 * n_t * count, LANES),
        [pltpu.VMEM((chips, n_t * count, LANES), f32)],
    )
    scratch = [pltpu.VMEM((n_t, rows, HD), f32), pltpu.VMEM((n_t, count, LANES), f32)]
    own_halves = call(
        functools.partial(own_kernel, n_t, chips, frames),
        [hot, collected] + packed_all,
        [shape(f32, HD, width), shape(f32, levels, chips * width)],
        scratch,
        flops=2 * n_t * rows * width * HD,
    )
    weight_grad, gate_grad = call(
        functools.partial(final_kernel, n_t, chips, frames),
        [hot, over_cores(collected), *own_halves] + packed_all,
        [shape(f32, HD, 2 * width), shape(f32, levels, n_s * width)],
        scratch,
        flops=2 * n_t * rows * width * HD,
    )
    parts[0], _ = lax.optimization_barrier((parts[0], gate_grad))
    query_grad = call(functools.partial(query_kernel, n_t), parts[::-1], shape(bf16, rows, HD))
    if width != shard:
        weight_grad = without_padding(weight_grad, 2, shard)
        gate_grad = without_padding(gate_grad, n_s, shard)
    return (query_grad, key_grad, value_grad, weight_grad, gate_grad)


def solution(mesh):
    return jax.shard_map(
        body,
        mesh=mesh,
        in_specs=(
            P("tm", "space"),
            P("tm", "space"),
            P("tm", "space"),
            P("tm", "space"),
            P("tm", "space"),
            P("space", None),
            P(),
            P(),
            P(),
        ),
        out_specs=(P("tm", "space"), P("tm", "space"), P("tm", "space"), P("space", "tm"), P()),
        check_vma=False,
    )
```

```python
import functools
import math

import jax
import jax.numpy as jnp
from jax import lax
from jax.experimental import pallas as pl
from jax.experimental.pallas import tpu as pltpu
from jax.sharding import PartitionSpec as P

HD = 128
SPF = 512
QF = 64
LANES = 128
NEG_BIG = -1e30
SCALE = 1.0 / math.sqrt(HD)
VMEM_LIMIT = 32 * 1024 * 1024
PREP_VMEM = 52 * 1024 * 1024
SPLIT = 3


def dot(a, b, on_a, on_b):
    return lax.dot_general(
        a, b, (((on_a,), (on_b,)), ((), ())), preferred_element_type=jnp.float32
    )


def far_first(blocks):
    blocks = list(blocks)
    return blocks[:1] + blocks[:0:-1]


def last_swapped(blocks):
    blocks = list(blocks)
    return blocks[:-2] + blocks[:-3:-1]


def place():
    s = lax.axis_index("space")
    return lax.axis_index("tm"), s // 2, s % 2


def clip_numbers(clips_ref):
    bounds = []
    so_far = 0
    for c in range(clips_ref.shape[0]):
        so_far = so_far + clips_ref[c]
        bounds.append(so_far)
    return lambda frame: sum((frame >= bound).astype(jnp.int32) for bound in bounds)


def fetch_kernel(chips, weight_in, grad_in, kept, grad, sems):
    _, chip, core = place()
    width = kept.shape[2]
    copies = [pltpu.make_async_copy(grad_in, grad, sems.at[chips])]
    for k in range(chips):
        columns = pl.ds(pl.multiple_of((2 * (chip ^ k) + core) * width, LANES), width)
        copies.append(pltpu.make_async_copy(weight_in.at[:, columns], kept.at[k], sems.at[k]))
    for copy in copies:
        copy.start()
    for copy in copies:
        copy.wait()


def masks_kernel(n_t, chips, frames, rows, levels, clips, gate, bias, gate_a, gate_b, hot):
    t, chip, core = place()
    width = gate_a.shape[2]
    clip_of = clip_numbers(clips)
    lane = lax.broadcasted_iota(jnp.int32, (1, rows), 1)
    for kf in range(frames):
        key_frame = t * frames + kf
        key_clip = clip_of(key_frame)
        for k in range(n_t):
            row = jnp.full((1, rows), NEG_BIG, jnp.float32)
            for r in range(frames):
                frame = (t ^ k) * frames + r
                visible = (key_frame >= frame) & (clip_of(frame) == key_clip)
                value = jnp.where(visible, 0.0, NEG_BIG).astype(jnp.float32)
                row = jnp.where((lane >= r * QF) & (lane < (r + 1) * QF), value, row)
            bias[kf : kf + 1, k * rows : (k + 1) * rows] = row
    spot = lax.broadcasted_iota(jnp.int32, hot.shape[1:], 0)
    for f in range(n_t * frames):
        hot[f] = (spot == levels[f]).astype(jnp.float32)
    for r in range(frames):
        level = levels[t * frames + r]
        for k in range(chips):
            columns = pl.ds(pl.multiple_of((2 * (chip ^ k) + core) * width, LANES), width)
            gate_a[k, r : r + 1, :] = gate[pl.ds(level, 1), columns]
    mine = pl.ds(pl.multiple_of((2 * t + core) * width, LANES), width)
    for k in range(n_t):
        level = levels[(t ^ k) * frames + chip * (rows // chips) // QF]
        gate_b[k] = gate[pl.ds(level, 1), mine]


def stats_kernel(n_t, bias, keys, *refs):
    packed, out = far_first(refs[:n_t]), refs[n_t]
    rows = packed[0].shape[1]
    for p in range(0, n_t, 2):
        q = jnp.concatenate([packed[p][0], packed[p + 1][0]], axis=0)
        scores = []
        for kf in range(bias.shape[0]):
            mask = bias[kf : kf + 1, p * rows : (p + 2) * rows]
            scores.append(dot(keys[kf * SPF : (kf + 1) * SPF, :], q, 1, 1) * SCALE + mask)
        top = functools.reduce(jnp.maximum, [jnp.max(x, axis=0, keepdims=True) for x in scores])
        total = sum(jnp.sum(jnp.exp(x - top), axis=0, keepdims=True) for x in scores)
        for i in range(2):
            out[p + i : p + i + 1, :] = top[:, i * rows : (i + 1) * rows]
            out[n_t + p + i : n_t + p + i + 1, :] = total[:, i * rows : (i + 1) * rows]


def head_kernel(chips, frames, packed, other_saved, kept, received, gate_a, *refs):
    pieces, (mine, other, terms) = refs[:chips], refs[chips:]
    _, chip, core = place()
    width = pieces[0].shape[1]
    tiles = width // LANES
    saved = jnp.concatenate([packed[1], other_saved[...]], axis=1)
    head = None
    for k in range(chips):
        columns = pl.ds(pl.multiple_of((2 * (chip ^ k) + core) * width, LANES), width)
        weight = jnp.concatenate([kept[k], received[:, columns]], axis=0)
        wide = pieces[k][...].astype(jnp.float32)
        gated = jnp.concatenate(
            [
                (wide[r * QF : (r + 1) * QF] * gate_a[k, r : r + 1, :]).astype(jnp.bfloat16)
                for r in range(frames)
            ],
            axis=0,
        )
        part = dot(gated, weight, 1, 1)
        head = part if head is None else head + part
        product = wide * dot(saved, weight, 1, 0)
        for r in range(frames):
            term = jnp.sum(product[r * QF : (r + 1) * QF], axis=0, keepdims=True)
            for j in range(tiles):
                row = ((chip ^ k) * frames + r) * tiles + j
                terms[pl.ds(row, 1), :] = term[:, j * LANES : (j + 1) * LANES]
    mine[...] = head[:, :HD]
    other[...] = head[:, HD:]


def sections(rows, chips, tiles, n_t, count):
    starts = [0, rows]
    starts.append(starts[-1] + tiles * (rows // chips))
    starts.append(starts[-1] + -(-(SPLIT * 2 * n_t + count) // 16) * 16)
    return starts


def padded(x, rows):
    if x.shape[0] == rows:
        return x
    return jnp.concatenate([x, jnp.zeros((rows - x.shape[0], x.shape[1]), x.dtype)], axis=0)


def join_kernel(n_t, chips, starts, mine, received, stats, terms, *refs):
    pieces, outs, (wide, held) = refs[:chips], refs[chips : chips + n_t][::-1], refs[chips + n_t :]
    t, chip, _ = place()
    part, tiles = held.shape[1], held.shape[2] // LANES
    for k in range(chips):
        wide[...] = pieces[k][...].astype(jnp.float32)
        held[k] = wide[pl.ds(pl.multiple_of(chip * part, part), part), :]
    head = (mine[...] + received[...]).astype(jnp.bfloat16)
    rest = stats[...]
    split = []
    for _ in range(SPLIT):
        piece = rest.astype(jnp.bfloat16).astype(jnp.float32)
        split.append(piece)
        rest = rest - piece
    last = padded(jnp.concatenate(split + [terms[...]], axis=0), starts[3] - starts[2])
    last = last.astype(jnp.bfloat16)
    for k in range(n_t):
        rows = held[chip ^ t ^ k]
        rows = jnp.concatenate([rows[:, j * LANES : (j + 1) * LANES] for j in range(tiles)], axis=0)
        outs[k][: starts[1], :] = head
        outs[k][starts[1] : starts[2], :] = rows.astype(jnp.bfloat16)
        outs[k][starts[2] :, :] = last


def bundle_kernel(n_t, starts, count, gate_b, *refs):
    heads, out = last_swapped(refs[:n_t]), refs[n_t]
    tiles = gate_b.shape[2] // LANES
    part = (starts[2] - starts[1]) // tiles
    wide = [heads[k][starts[1] : starts[2], :].astype(jnp.float32) for k in range(n_t)]
    for j in range(tiles):
        gated = jnp.concatenate(
            [
                wide[k][j * part : (j + 1) * part] * gate_b[k, :, j * LANES : (j + 1) * LANES]
                for k in range(n_t)
            ],
            axis=0,
        )
        out[j * n_t * part : (j + 1) * n_t * part, :] = gated.astype(jnp.bfloat16)
    first = SPLIT * 2 * n_t
    terms = [heads[k][starts[2] :, :].astype(jnp.float32)[first : first + count] for k in range(n_t)]
    out[tiles * n_t * part :, :] = jnp.concatenate(terms, axis=0).astype(jnp.bfloat16)


def collect_kernel(chips, base, *refs):
    pieces, out, held = refs[:chips], refs[chips], refs[chips + 1]
    chip = place()[1]
    for k in range(chips):
        out[k * base : (k + 1) * base, :] = pieces[k][:base, :]
        held[chip ^ k] = pieces[k][base:, :].astype(jnp.float32)
    total = held[0]
    for k in range(1, chips):
        total = total + held[k]
    high = total.astype(jnp.bfloat16)
    count = total.shape[0]
    out[chips * base : chips * base + count, :] = high
    out[chips * base + count :, :] = (total - high.astype(jnp.float32)).astype(jnp.bfloat16)


def grads_kernel(n_t, starts, first, last, bias, keys, values, *refs):
    packed, heads = refs[:n_t], refs[n_t : 2 * n_t][::-1]
    refs = refs[2 * n_t :]
    if first == 0:
        sums, refs = refs[:2], refs[2:]
    key_out, value_out = refs[:2]
    outs = refs[2 : 2 + last - first][::-1]
    accs = refs[2 + last - first :]
    rows = packed[0].shape[1]
    ones = jnp.ones((8, HD), jnp.float32)
    keys_t = jnp.transpose(keys[...])
    stats = []
    for k in range(n_t):
        parts = heads[k][starts[2] :, :].astype(jnp.float32)
        stats.append(sum(parts[i * 2 * n_t : (i + 1) * 2 * n_t] for i in range(SPLIT)))
    for p in range(first, last, 2):
        q = jnp.concatenate([packed[p][0], packed[p + 1][0]], axis=0)
        o = jnp.concatenate([packed[p][1], packed[p + 1][1]], axis=0)
        g = jnp.concatenate([heads[p][:rows, :], heads[p + 1][:rows, :]], axis=0)
        delta = lax.dot_general(
            ones,
            g.astype(jnp.float32) * o.astype(jnp.float32),
            (((1,), (1,)), ((), ())),
            precision=lax.Precision.HIGHEST,
            preferred_element_type=jnp.float32,
        )[0:1]
        lse = []
        for i in (p, p + 1):
            tops = [stats[k][i ^ k : (i ^ k) + 1] for k in range(n_t)]
            sums_of = [stats[k][n_t + (i ^ k) : n_t + (i ^ k) + 1] for k in range(n_t)]
            top = functools.reduce(jnp.maximum, tops)
            lse.append(top + jnp.log(sum(b * jnp.exp(a - top) for a, b in zip(tops, sums_of))))
        lse = jnp.concatenate(lse, axis=1)
        query_part = None
        for kf in range(bias.shape[0]):
            span = slice(kf * SPF, (kf + 1) * SPF)
            shift = bias[kf : kf + 1, p * rows : (p + 2) * rows] - lse
            probs = jnp.exp(dot(keys[span, :], q, 1, 1) * SCALE + shift)
            score_grad = (probs * (dot(values[span, :], g, 1, 1) - delta)).astype(jnp.bfloat16)
            value_add = dot(probs.astype(jnp.bfloat16), g, 1, 0)
            key_add = dot(score_grad, q, 1, 0)
            if p > first:
                value_add = value_add + accs[1][span, :]
                key_add = key_add + accs[0][span, :]
            if p + 2 < last:
                accs[1][span, :] = value_add
                accs[0][span, :] = key_add
            elif first:
                value_out[span, :] = value_add
                key_out[span, :] = key_add
            else:
                value_out[span, :] = (value_add + sums[1][span, :]).astype(jnp.bfloat16)
                key_out[span, :] = ((key_add + sums[0][span, :]) * SCALE).astype(jnp.bfloat16)
            part = dot(keys_t[:, span], score_grad, 1, 0)
            query_part = part if query_part is None else query_part + part
        outs[p - first][...] = query_part[:, :rows].astype(jnp.bfloat16)
        outs[p + 1 - first][...] = query_part[:, rows:].astype(jnp.bfloat16)


def query_kernel(n_t, *refs):
    total = refs[0][...].astype(jnp.float32)
    for k in range(1, n_t):
        total = total + refs[k][...].astype(jnp.float32)
    refs[n_t][...] = jnp.transpose(total * SCALE).astype(jnp.bfloat16)


def half_results(n_t, chips, frames, hot, ref, packed, saved, held, tiles):
    t, chip, _ = place()
    rows = saved.shape[1]
    part = rows // chips
    base = tiles * n_t * part
    for k in range(n_t):
        saved[k] = packed[k][1].astype(jnp.float32)
    ordered = []
    for c in range(chips):
        mine = pl.ds(pl.multiple_of((chip ^ c) * part, part), part)
        ordered += [saved[k, mine, :] for k in range(n_t)]
    ordered = jnp.transpose(jnp.concatenate(ordered, axis=0)).astype(jnp.bfloat16)
    gated = jnp.concatenate(
        [
            jnp.concatenate(
                [
                    ref[c * base + j * n_t * part : c * base + (j + 1) * n_t * part, :]
                    for c in range(chips)
                ],
                axis=0,
            )
            for j in range(tiles)
        ],
        axis=1,
    )
    count = (ref.shape[0] - chips * base) // 2
    each = count // n_t
    terms = ref[chips * base : chips * base + count, :].astype(jnp.float32)
    terms = terms + ref[chips * base + count :, :].astype(jnp.float32)
    for k in range(n_t):
        held[t ^ k] = terms[k * each : (k + 1) * each]

    def gate_tile(a, j):
        total = jnp.zeros(hot.shape[1:], jnp.float32)
        for f in range(n_t * frames):
            row = (a * frames + f % frames) * tiles + j
            total = total + hot[f] * held[f // frames, row : row + 1, :]
        return total

    return dot(ordered, gated, 1, 0), gate_tile


def own_kernel(n_t, chips, frames, hot, own, *refs):
    packed, (weight_out, gate_out, saved, held) = refs[:n_t], refs[n_t:]
    tiles = weight_out.shape[1] // LANES
    result, gate_tile = half_results(n_t, chips, frames, hot, own, packed, saved, held, tiles)
    weight_out[...] = result
    for a in range(chips):
        for j in range(tiles):
            gate_out[:, (a * tiles + j) * LANES : (a * tiles + j + 1) * LANES] = gate_tile(a, j)


def final_kernel(n_t, chips, frames, hot, other, own_weight, own_gate, *refs):
    packed, (weight_out, gate_out, saved, held) = refs[:n_t], refs[n_t:]
    core = place()[2]
    width = own_weight.shape[1]
    tiles = width // LANES
    result, gate_tile = half_results(n_t, chips, frames, hot, other, packed, saved, held, tiles)
    mine = own_weight[...]
    weight_out[:, :width] = jnp.where(core == 0, mine, result)
    weight_out[:, width:] = jnp.where(core == 0, result, mine)
    for a in range(chips):
        for j in range(tiles):
            first = gate_tile(a, j)
            second = own_gate[:, (a * tiles + j) * LANES : (a * tiles + j + 1) * LANES]
            column = 2 * a * width + j * LANES
            gate_out[:, column : column + LANES] = jnp.where(core == 0, second, first)
            column += width
            gate_out[:, column : column + LANES] = jnp.where(core == 0, first, second)


def call(kernel, args, out_shape, scratch=(), flops=0, in_place=False, in_smem=0):
    vmem = pl.BlockSpec(memory_space=pltpu.VMEM)
    single = not isinstance(out_shape, (list, tuple))
    nbytes = sum(a.size * a.dtype.itemsize for a in args)
    return pl.pallas_call(
        kernel,
        out_shape=out_shape,
        in_specs=[pl.BlockSpec(memory_space=pltpu.SMEM)] * in_smem
        + [pl.BlockSpec(memory_space=pltpu.HBM) if in_place else vmem] * (len(args) - in_smem),
        out_specs=vmem if single else [vmem] * len(out_shape),
        scratch_shapes=list(scratch),
        compiler_params=pltpu.CompilerParams(vmem_limit_bytes=PREP_VMEM if in_place else VMEM_LIMIT),
        cost_estimate=pl.CostEstimate(flops=flops, bytes_accessed=nbytes, transcendentals=0),
    )(*args)


def padded_shards(table, n_s, width):
    rows, columns = table.shape
    cut = table.reshape(rows, n_s, columns // n_s)
    cut = jnp.pad(cut, ((0, 0), (0, 0), (0, width - columns // n_s)))
    return cut.reshape(rows, n_s * width)


def without_padding(table, shards, shard):
    rows, columns = table.shape
    return table.reshape(rows, shards, columns // shards)[:, :, :shard].reshape(rows, shards * shard)


def body(
    queries, keys, values, saved_out, out_grad, proj_weight, gate_table, noise_levels, clip_lengths
):
    n_t, n_s = lax.axis_size("tm"), lax.axis_size("space")
    chips = n_s // 2
    rows, shard = out_grad.shape
    k_rows = keys.shape[0]
    frames = rows // QF
    levels = gate_table.shape[0]
    bf16, f32 = jnp.bfloat16, jnp.float32
    width = -(-shard // LANES) * LANES
    if width != shard:
        out_grad = jnp.pad(out_grad, ((0, 0), (0, width - shard)))
        proj_weight = padded_shards(proj_weight, n_s, width)
        gate_table = padded_shards(gate_table, n_s, width)

    def shape(dtype, *dims):
        return jax.ShapeDtypeStruct(dims, dtype)

    def over_chips(x):
        return [x] + [
            lax.ppermute(x, "space", [(s, s ^ (2 * k)) for s in range(n_s)]) for k in range(1, chips)
        ]

    def over_cores(x):
        return lax.ppermute(x, "space", [(s, s ^ 1) for s in range(n_s)])

    def over_time(x, k):
        return lax.ppermute(x, "tm", [(t, t ^ k) for t in range(n_t)])

    tiles = width // LANES
    part = rows // chips
    count = chips * frames * tiles
    starts = sections(rows, chips, tiles, n_t, count)

    def time_swaps(messages):
        got = {k: over_time(messages[k], k) for k in range(n_t - 1, 0, -1)}
        return [messages[0]] + [got[k] for k in range(1, n_t)]

    pieces = over_chips(out_grad)
    received, other_saved = over_cores(proj_weight), over_cores(saved_out)
    packed, _ = lax.optimization_barrier(
        (jnp.stack([queries, saved_out]), (received, other_saved))
    )
    packed_all = time_swaps([packed] * n_t)
    (to_fetch, own_grad), _ = lax.optimization_barrier(((proj_weight, out_grad), received))
    kept, pieces[0] = call(
        functools.partial(fetch_kernel, chips),
        [to_fetch, own_grad],
        [shape(bf16, chips, HD, width), shape(bf16, rows, width)],
        [pltpu.SemaphoreType.DMA((chips + 1,))],
        in_place=True,
    )
    gate_table, _ = lax.optimization_barrier((gate_table, received))
    bias, gate_a, gate_b, hot = call(
        functools.partial(masks_kernel, n_t, chips, frames, rows),
        [noise_levels, clip_lengths, gate_table],
        [
            shape(f32, frames, n_t * rows),
            shape(f32, chips, frames, width),
            shape(f32, n_t, 1, width),
            shape(f32, n_t * frames, levels, LANES),
        ],
        in_smem=2,
    )
    mine, other, terms = call(
        functools.partial(head_kernel, chips, frames),
        [packed, other_saved, kept, received, gate_a] + pieces,
        [shape(f32, rows, HD), shape(f32, rows, HD), shape(f32, count, LANES)],
        flops=4 * rows * chips * width * 2 * HD,
    )
    later_bias, _ = lax.optimization_barrier((bias, mine))
    stats = call(
        functools.partial(stats_kernel, n_t),
        [later_bias, keys] + far_first(packed_all),
        shape(f32, 2 * n_t, LANES),
        flops=2 * n_t * rows * k_rows * HD,
    )
    heads = call(
        functools.partial(join_kernel, n_t, chips, starts),
        [mine, over_cores(other), stats, terms] + pieces,
        [shape(bf16, starts[-1], LANES)] * n_t,
        [pltpu.VMEM((rows, width), f32), pltpu.VMEM((chips, part, width), f32)],
    )
    heads_all = time_swaps(heads[::-1])
    base = tiles * n_t * part
    bundle = call(
        functools.partial(bundle_kernel, n_t, starts, count),
        [gate_b] + last_swapped(heads_all),
        shape(bf16, base + n_t * count, LANES),
    )
    bundles = over_chips(bundle)
    later_bias, _ = lax.optimization_barrier((bias, bundle))
    accs = [pltpu.VMEM((k_rows, HD), f32)] * 2
    far = call(
        functools.partial(grads_kernel, n_t, starts, 2, n_t),
        [later_bias, keys, values] + packed_all + heads_all[::-1],
        [shape(f32, k_rows, HD)] * 2 + [shape(bf16, HD, rows)] * (n_t - 2),
        accs,
        flops=10 * (n_t - 2) * rows * k_rows * HD,
    )
    parts = {k: over_time(far[1 + n_t - k], k) for k in range(n_t - 1, 1, -1)}
    near = call(
        functools.partial(grads_kernel, n_t, starts, 0, 2),
        [bias, keys, values] + packed_all + heads_all[::-1] + list(far[:2]),
        [shape(bf16, k_rows, HD)] * 2 + [shape(bf16, HD, rows)] * 2,
        flops=20 * rows * k_rows * HD,
    )
    key_grad, value_grad = near[:2]
    parts[0], parts[1] = near[3], over_time(near[2], 1)
    parts = [parts[k] for k in range(n_t)]
    bundles, _ = lax.optimization_barrier((bundles, (key_grad, parts[: n_t // 2 - 1 : -1])))
    collected = call(
        functools.partial(collect_kernel, chips, base),
        bundles,
        shape(bf16, chips * base + 2 * n_t * count, LANES),
        [pltpu.VMEM((chips, n_t * count, LANES), f32)],
    )
    scratch = [pltpu.VMEM((n_t, rows, HD), f32), pltpu.VMEM((n_t, count, LANES), f32)]
    own_halves = call(
        functools.partial(own_kernel, n_t, chips, frames),
        [hot, collected] + packed_all,
        [shape(f32, HD, width), shape(f32, levels, chips * width)],
        scratch,
        flops=2 * n_t * rows * width * HD,
    )
    weight_grad, gate_grad = call(
        functools.partial(final_kernel, n_t, chips, frames),
        [hot, over_cores(collected), *own_halves] + packed_all,
        [shape(f32, HD, 2 * width), shape(f32, levels, n_s * width)],
        scratch,
        flops=2 * n_t * rows * width * HD,
    )
    parts[0], _ = lax.optimization_barrier((parts[0], gate_grad))
    query_grad = call(functools.partial(query_kernel, n_t), parts[::-1], shape(bf16, rows, HD))
    if width != shard:
        weight_grad = without_padding(weight_grad, 2, shard)
        gate_grad = without_padding(gate_grad, n_s, shard)
    return (query_grad, key_grad, value_grad, weight_grad, gate_grad)


def solution(mesh):
    return jax.shard_map(
        body,
        mesh=mesh,
        in_specs=(
            P("tm", "space"),
            P("tm", "space"),
            P("tm", "space"),
            P("tm", "space"),
            P("tm", "space"),
            P("space", None),
            P(),
            P(),
            P(),
        ),
        out_specs=(P("tm", "space"), P("tm", "space"), P("tm", "space"), P("space", "tm"), P()),
        check_vma=False,
    )
```

```python
import functools
import math

import jax
import jax.numpy as jnp
from jax import lax
from jax.experimental import pallas as pl
from jax.experimental.pallas import tpu as pltpu
from jax.sharding import PartitionSpec as P

HD = 128
SPF = 512
QF = 64
LANES = 128
NEG_BIG = -1e30
SCALE = 1.0 / math.sqrt(HD)
VMEM_LIMIT = 32 * 1024 * 1024
PREP_VMEM = 52 * 1024 * 1024
SPLIT = 3


def dot(a, b, on_a, on_b):
    return lax.dot_general(
        a, b, (((on_a,), (on_b,)), ((), ())), preferred_element_type=jnp.float32
    )


def far_first(blocks):
    blocks = list(blocks)
    return blocks[:1] + blocks[:0:-1]


def last_swapped(blocks):
    blocks = list(blocks)
    return blocks[:-2] + blocks[:-3:-1]


def place():
    s = lax.axis_index("space")
    return lax.axis_index("tm"), s // 2, s % 2


def clip_numbers(clips_ref):
    bounds = []
    so_far = 0
    for c in range(clips_ref.shape[0]):
        so_far = so_far + clips_ref[c]
        bounds.append(so_far)
    return lambda frame: sum((frame >= bound).astype(jnp.int32) for bound in bounds)


def fetch_kernel(chips, weight_in, grad_in, kept, grad, sems):
    _, chip, core = place()
    width = kept.shape[2]
    copies = [pltpu.make_async_copy(grad_in, grad, sems.at[chips])]
    for k in range(chips):
        columns = pl.ds(pl.multiple_of((2 * (chip ^ k) + core) * width, LANES), width)
        copies.append(pltpu.make_async_copy(weight_in.at[:, columns], kept.at[k], sems.at[k]))
    for copy in copies:
        copy.start()
    for copy in copies:
        copy.wait()


def masks_kernel(n_t, chips, frames, rows, levels, clips, gate, bias, gate_a, gate_b, hot):
    t, chip, core = place()
    width = gate_a.shape[2]
    clip_of = clip_numbers(clips)
    lane = lax.broadcasted_iota(jnp.int32, (1, rows), 1)
    for kf in range(frames):
        key_frame = t * frames + kf
        key_clip = clip_of(key_frame)
        for k in range(n_t):
            row = jnp.full((1, rows), NEG_BIG, jnp.float32)
            for r in range(frames):
                frame = (t ^ k) * frames + r
                visible = (key_frame >= frame) & (clip_of(frame) == key_clip)
                value = jnp.where(visible, 0.0, NEG_BIG).astype(jnp.float32)
                row = jnp.where((lane >= r * QF) & (lane < (r + 1) * QF), value, row)
            bias[kf : kf + 1, k * rows : (k + 1) * rows] = row
    spot = lax.broadcasted_iota(jnp.int32, hot.shape[1:], 0)
    for f in range(n_t * frames):
        hot[f] = (spot == levels[f]).astype(jnp.float32)
    for r in range(frames):
        level = levels[t * frames + r]
        for k in range(chips):
            columns = pl.ds(pl.multiple_of((2 * (chip ^ k) + core) * width, LANES), width)
            gate_a[k, r : r + 1, :] = gate[pl.ds(level, 1), columns]
    mine = pl.ds(pl.multiple_of((2 * t + core) * width, LANES), width)
    for k in range(n_t):
        level = levels[(t ^ k) * frames + chip * (rows // chips) // QF]
        gate_b[k] = gate[pl.ds(level, 1), mine]


def stats_kernel(n_t, bias, keys, *refs):
    packed, out = far_first(refs[:n_t]), refs[n_t]
    rows = packed[0].shape[1]
    for p in range(0, n_t, 2):
        q = jnp.concatenate([packed[p][0], packed[p + 1][0]], axis=0)
        scores = []
        for kf in range(bias.shape[0]):
            mask = bias[kf : kf + 1, p * rows : (p + 2) * rows]
            scores.append(dot(keys[kf * SPF : (kf + 1) * SPF, :], q, 1, 1) * SCALE + mask)
        top = functools.reduce(jnp.maximum, [jnp.max(x, axis=0, keepdims=True) for x in scores])
        total = sum(jnp.sum(jnp.exp(x - top), axis=0, keepdims=True) for x in scores)
        for i in range(2):
            out[p + i : p + i + 1, :] = top[:, i * rows : (i + 1) * rows]
            out[n_t + p + i : n_t + p + i + 1, :] = total[:, i * rows : (i + 1) * rows]


def head_kernel(chips, frames, packed, other_saved, kept, received, gate_a, *refs):
    pieces, (mine, other, terms) = refs[:chips], refs[chips:]
    _, chip, core = place()
    width = pieces[0].shape[1]
    tiles = width // LANES
    saved = jnp.concatenate([packed[1], other_saved[...]], axis=1)
    head = None
    for k in range(chips):
        columns = pl.ds(pl.multiple_of((2 * (chip ^ k) + core) * width, LANES), width)
        weight = jnp.concatenate([kept[k], received[:, columns]], axis=0)
        wide = pieces[k][...].astype(jnp.float32)
        gated = jnp.concatenate(
            [
                (wide[r * QF : (r + 1) * QF] * gate_a[k, r : r + 1, :]).astype(jnp.bfloat16)
                for r in range(frames)
            ],
            axis=0,
        )
        part = dot(gated, weight, 1, 1)
        head = part if head is None else head + part
        product = wide * dot(saved, weight, 1, 0)
        for r in range(frames):
            term = jnp.sum(product[r * QF : (r + 1) * QF], axis=0, keepdims=True)
            for j in range(tiles):
                row = ((chip ^ k) * frames + r) * tiles + j
                terms[pl.ds(row, 1), :] = term[:, j * LANES : (j + 1) * LANES]
    mine[...] = head[:, :HD]
    other[...] = head[:, HD:]


def sections(rows, chips, tiles, n_t, count):
    starts = [0, rows]
    starts.append(starts[-1] + tiles * (rows // chips))
    starts.append(starts[-1] + -(-(SPLIT * 2 * n_t + count) // 16) * 16)
    return starts


def padded(x, rows):
    if x.shape[0] == rows:
        return x
    return jnp.concatenate([x, jnp.zeros((rows - x.shape[0], x.shape[1]), x.dtype)], axis=0)


def join_kernel(n_t, chips, starts, mine, received, stats, terms, *refs):
    pieces, outs, (wide, held) = refs[:chips], refs[chips : chips + n_t][::-1], refs[chips + n_t :]
    t, chip, _ = place()
    part, tiles = held.shape[1], held.shape[2] // LANES
    for k in range(chips):
        wide[...] = pieces[k][...].astype(jnp.float32)
        held[k] = wide[pl.ds(pl.multiple_of(chip * part, part), part), :]
    head = (mine[...] + received[...]).astype(jnp.bfloat16)
    rest = stats[...]
    split = []
    for _ in range(SPLIT):
        piece = rest.astype(jnp.bfloat16).astype(jnp.float32)
        split.append(piece)
        rest = rest - piece
    last = padded(jnp.concatenate(split + [terms[...]], axis=0), starts[3] - starts[2])
    last = last.astype(jnp.bfloat16)
    for k in range(n_t):
        rows = held[chip ^ t ^ k]
        rows = jnp.concatenate([rows[:, j * LANES : (j + 1) * LANES] for j in range(tiles)], axis=0)
        outs[k][: starts[1], :] = head
        outs[k][starts[1] : starts[2], :] = rows.astype(jnp.bfloat16)
        outs[k][starts[2] :, :] = last


def bundle_kernel(n_t, starts, count, gate_b, *refs):
    heads, out = last_swapped(refs[:n_t]), refs[n_t]
    tiles = gate_b.shape[2] // LANES
    part = (starts[2] - starts[1]) // tiles
    wide = [heads[k][starts[1] : starts[2], :].astype(jnp.float32) for k in range(n_t)]
    for j in range(tiles):
        gated = jnp.concatenate(
            [
                wide[k][j * part : (j + 1) * part] * gate_b[k, :, j * LANES : (j + 1) * LANES]
                for k in range(n_t)
            ],
            axis=0,
        )
        out[j * n_t * part : (j + 1) * n_t * part, :] = gated.astype(jnp.bfloat16)
    first = SPLIT * 2 * n_t
    terms = [heads[k][starts[2] :, :].astype(jnp.float32)[first : first + count] for k in range(n_t)]
    out[tiles * n_t * part :, :] = jnp.concatenate(terms, axis=0).astype(jnp.bfloat16)


def collect_kernel(chips, base, *refs):
    pieces, out, held = refs[:chips], refs[chips], refs[chips + 1]
    chip = place()[1]
    for k in range(chips):
        out[k * base : (k + 1) * base, :] = pieces[k][:base, :]
        held[chip ^ k] = pieces[k][base:, :].astype(jnp.float32)
    total = held[0]
    for k in range(1, chips):
        total = total + held[k]
    high = total.astype(jnp.bfloat16)
    count = total.shape[0]
    out[chips * base : chips * base + count, :] = high
    out[chips * base + count :, :] = (total - high.astype(jnp.float32)).astype(jnp.bfloat16)


def grads_kernel(n_t, starts, first, last, bias, keys, values, *refs):
    packed, heads = refs[:n_t], refs[n_t : 2 * n_t][::-1]
    refs = refs[2 * n_t :]
    if first == 0:
        sums, refs = refs[:2], refs[2:]
    key_out, value_out = refs[:2]
    outs = refs[2 : 2 + last - first][::-1]
    accs = refs[2 + last - first :]
    rows = packed[0].shape[1]
    ones = jnp.ones((8, HD), jnp.float32)
    keys_t = jnp.transpose(keys[...])
    stats = []
    for k in range(n_t):
        parts = heads[k][starts[2] :, :].astype(jnp.float32)
        stats.append(sum(parts[i * 2 * n_t : (i + 1) * 2 * n_t] for i in range(SPLIT)))
    for p in range(first, last, 2):
        q = jnp.concatenate([packed[p][0], packed[p + 1][0]], axis=0)
        o = jnp.concatenate([packed[p][1], packed[p + 1][1]], axis=0)
        g = jnp.concatenate([heads[p][:rows, :], heads[p + 1][:rows, :]], axis=0)
        delta = lax.dot_general(
            ones,
            g.astype(jnp.float32) * o.astype(jnp.float32),
            (((1,), (1,)), ((), ())),
            precision=lax.Precision.HIGHEST,
            preferred_element_type=jnp.float32,
        )[0:1]
        lse = []
        for i in (p, p + 1):
            tops = [stats[k][i ^ k : (i ^ k) + 1] for k in range(n_t)]
            sums_of = [stats[k][n_t + (i ^ k) : n_t + (i ^ k) + 1] for k in range(n_t)]
            top = functools.reduce(jnp.maximum, tops)
            lse.append(top + jnp.log(sum(b * jnp.exp(a - top) for a, b in zip(tops, sums_of))))
        lse = jnp.concatenate(lse, axis=1)
        query_part = None
        for kf in range(bias.shape[0]):
            span = slice(kf * SPF, (kf + 1) * SPF)
            shift = bias[kf : kf + 1, p * rows : (p + 2) * rows] - lse
            probs = jnp.exp(dot(keys[span, :], q, 1, 1) * SCALE + shift)
            score_grad = (probs * (dot(values[span, :], g, 1, 1) - delta)).astype(jnp.bfloat16)
            value_add = dot(probs.astype(jnp.bfloat16), g, 1, 0)
            key_add = dot(score_grad, q, 1, 0)
            if p > first:
                value_add = value_add + accs[1][span, :]
                key_add = key_add + accs[0][span, :]
            if p + 2 < last:
                accs[1][span, :] = value_add
                accs[0][span, :] = key_add
            elif first:
                value_out[span, :] = value_add
                key_out[span, :] = key_add
            else:
                value_out[span, :] = (value_add + sums[1][span, :]).astype(jnp.bfloat16)
                key_out[span, :] = ((key_add + sums[0][span, :]) * SCALE).astype(jnp.bfloat16)
            part = dot(keys_t[:, span], score_grad, 1, 0)
            query_part = part if query_part is None else query_part + part
        outs[p - first][...] = query_part[:, :rows].astype(jnp.bfloat16)
        outs[p + 1 - first][...] = query_part[:, rows:].astype(jnp.bfloat16)


def query_kernel(n_t, *refs):
    total = refs[0][...].astype(jnp.float32)
    for k in range(1, n_t):
        total = total + refs[k][...].astype(jnp.float32)
    refs[n_t][...] = jnp.transpose(total * SCALE).astype(jnp.bfloat16)


def order_kernel(n_t, chips, *refs):
    packed, (out, saved) = refs[:n_t], refs[n_t:]
    chip = place()[1]
    part = saved.shape[1] // chips
    for k in range(n_t):
        saved[k] = packed[k][1].astype(jnp.float32)
    ordered = []
    for c in range(chips):
        mine = pl.ds(pl.multiple_of((chip ^ c) * part, part), part)
        ordered += [saved[k, mine, :] for k in range(n_t)]
    out[...] = jnp.transpose(jnp.concatenate(ordered, axis=0)).astype(jnp.bfloat16)


def half_results(n_t, chips, frames, hot, ref, ordered, held, tiles):
    t = lax.axis_index("tm")
    part = ordered.shape[1] // (n_t * chips)
    base = tiles * n_t * part
    gated = jnp.concatenate(
        [
            jnp.concatenate(
                [
                    ref[c * base + j * n_t * part : c * base + (j + 1) * n_t * part, :]
                    for c in range(chips)
                ],
                axis=0,
            )
            for j in range(tiles)
        ],
        axis=1,
    )
    count = (ref.shape[0] - chips * base) // 2
    each = count // n_t
    terms = ref[chips * base : chips * base + count, :].astype(jnp.float32)
    terms = terms + ref[chips * base + count :, :].astype(jnp.float32)
    for k in range(n_t):
        held[t ^ k] = terms[k * each : (k + 1) * each]

    def gate_tile(a, j):
        total = jnp.zeros(hot.shape[1:], jnp.float32)
        for f in range(n_t * frames):
            row = (a * frames + f % frames) * tiles + j
            total = total + hot[f] * held[f // frames, row : row + 1, :]
        return total

    return dot(ordered[...], gated, 1, 0), gate_tile


def own_kernel(n_t, chips, frames, hot, own, ordered, weight_out, gate_out, held):
    tiles = weight_out.shape[1] // LANES
    result, gate_tile = half_results(n_t, chips, frames, hot, own, ordered, held, tiles)
    weight_out[...] = result
    for a in range(chips):
        for j in range(tiles):
            gate_out[:, (a * tiles + j) * LANES : (a * tiles + j + 1) * LANES] = gate_tile(a, j)


def final_kernel(
    n_t, chips, frames, hot, other, own_weight, own_gate, ordered, weight_out, gate_out, held
):
    core = place()[2]
    width = own_weight.shape[1]
    tiles = width // LANES
    result, gate_tile = half_results(n_t, chips, frames, hot, other, ordered, held, tiles)
    mine = own_weight[...]
    weight_out[:, :width] = jnp.where(core == 0, mine, result)
    weight_out[:, width:] = jnp.where(core == 0, result, mine)
    for a in range(chips):
        for j in range(tiles):
            first = gate_tile(a, j)
            second = own_gate[:, (a * tiles + j) * LANES : (a * tiles + j + 1) * LANES]
            column = 2 * a * width + j * LANES
            gate_out[:, column : column + LANES] = jnp.where(core == 0, second, first)
            column += width
            gate_out[:, column : column + LANES] = jnp.where(core == 0, first, second)


def call(kernel, args, out_shape, scratch=(), flops=0, in_place=False, in_smem=0):
    vmem = pl.BlockSpec(memory_space=pltpu.VMEM)
    single = not isinstance(out_shape, (list, tuple))
    nbytes = sum(a.size * a.dtype.itemsize for a in args)
    return pl.pallas_call(
        kernel,
        out_shape=out_shape,
        in_specs=[pl.BlockSpec(memory_space=pltpu.SMEM)] * in_smem
        + [pl.BlockSpec(memory_space=pltpu.HBM) if in_place else vmem] * (len(args) - in_smem),
        out_specs=vmem if single else [vmem] * len(out_shape),
        scratch_shapes=list(scratch),
        compiler_params=pltpu.CompilerParams(vmem_limit_bytes=PREP_VMEM if in_place else VMEM_LIMIT),
        cost_estimate=pl.CostEstimate(flops=flops, bytes_accessed=nbytes, transcendentals=0),
    )(*args)


def padded_shards(table, n_s, width):
    rows, columns = table.shape
    cut = table.reshape(rows, n_s, columns // n_s)
    cut = jnp.pad(cut, ((0, 0), (0, 0), (0, width - columns // n_s)))
    return cut.reshape(rows, n_s * width)


def without_padding(table, shards, shard):
    rows, columns = table.shape
    return table.reshape(rows, shards, columns // shards)[:, :, :shard].reshape(rows, shards * shard)


def body(
    queries, keys, values, saved_out, out_grad, proj_weight, gate_table, noise_levels, clip_lengths
):
    n_t, n_s = lax.axis_size("tm"), lax.axis_size("space")
    chips = n_s // 2
    rows, shard = out_grad.shape
    k_rows = keys.shape[0]
    frames = rows // QF
    levels = gate_table.shape[0]
    bf16, f32 = jnp.bfloat16, jnp.float32
    width = -(-shard // LANES) * LANES
    if width != shard:
        out_grad = jnp.pad(out_grad, ((0, 0), (0, width - shard)))
        proj_weight = padded_shards(proj_weight, n_s, width)
        gate_table = padded_shards(gate_table, n_s, width)

    def shape(dtype, *dims):
        return jax.ShapeDtypeStruct(dims, dtype)

    def over_chips(x):
        return [x] + [
            lax.ppermute(x, "space", [(s, s ^ (2 * k)) for s in range(n_s)]) for k in range(1, chips)
        ]

    def over_cores(x):
        return lax.ppermute(x, "space", [(s, s ^ 1) for s in range(n_s)])

    def over_time(x, k):
        return lax.ppermute(x, "tm", [(t, t ^ k) for t in range(n_t)])

    tiles = width // LANES
    part = rows // chips
    count = chips * frames * tiles
    starts = sections(rows, chips, tiles, n_t, count)

    def time_swaps(messages):
        got = {k: over_time(messages[k], k) for k in range(n_t - 1, 0, -1)}
        return [messages[0]] + [got[k] for k in range(1, n_t)]

    pieces = over_chips(out_grad)
    received, other_saved = over_cores(proj_weight), over_cores(saved_out)
    packed, _ = lax.optimization_barrier(
        (jnp.stack([queries, saved_out]), (received, other_saved))
    )
    packed_all = time_swaps([packed] * n_t)
    (to_fetch, own_grad), _ = lax.optimization_barrier(((proj_weight, out_grad), received))
    kept, pieces[0] = call(
        functools.partial(fetch_kernel, chips),
        [to_fetch, own_grad],
        [shape(bf16, chips, HD, width), shape(bf16, rows, width)],
        [pltpu.SemaphoreType.DMA((chips + 1,))],
        in_place=True,
    )
    gate_table, _ = lax.optimization_barrier((gate_table, received))
    bias, gate_a, gate_b, hot = call(
        functools.partial(masks_kernel, n_t, chips, frames, rows),
        [noise_levels, clip_lengths, gate_table],
        [
            shape(f32, frames, n_t * rows),
            shape(f32, chips, frames, width),
            shape(f32, n_t, 1, width),
            shape(f32, n_t * frames, levels, LANES),
        ],
        in_smem=2,
    )
    mine, other, terms = call(
        functools.partial(head_kernel, chips, frames),
        [packed, other_saved, kept, received, gate_a] + pieces,
        [shape(f32, rows, HD), shape(f32, rows, HD), shape(f32, count, LANES)],
        flops=4 * rows * chips * width * 2 * HD,
    )
    later_bias, _ = lax.optimization_barrier((bias, mine))
    stats = call(
        functools.partial(stats_kernel, n_t),
        [later_bias, keys] + far_first(packed_all),
        shape(f32, 2 * n_t, LANES),
        flops=2 * n_t * rows * k_rows * HD,
    )
    heads = call(
        functools.partial(join_kernel, n_t, chips, starts),
        [mine, over_cores(other), stats, terms] + pieces,
        [shape(bf16, starts[-1], LANES)] * n_t,
        [pltpu.VMEM((rows, width), f32), pltpu.VMEM((chips, part, width), f32)],
    )
    heads_all = time_swaps(heads[::-1])
    base = tiles * n_t * part
    bundle = call(
        functools.partial(bundle_kernel, n_t, starts, count),
        [gate_b] + last_swapped(heads_all),
        shape(bf16, base + n_t * count, LANES),
    )
    bundles = over_chips(bundle)
    later_bias, _ = lax.optimization_barrier((bias, bundle))
    accs = [pltpu.VMEM((k_rows, HD), f32)] * 2
    far = call(
        functools.partial(grads_kernel, n_t, starts, 2, n_t),
        [later_bias, keys, values] + packed_all + heads_all[::-1],
        [shape(f32, k_rows, HD)] * 2 + [shape(bf16, HD, rows)] * (n_t - 2),
        accs,
        flops=10 * (n_t - 2) * rows * k_rows * HD,
    )
    parts = {k: over_time(far[1 + n_t - k], k) for k in range(n_t - 1, 1, -1)}
    near = call(
        functools.partial(grads_kernel, n_t, starts, 0, 2),
        [bias, keys, values] + packed_all + heads_all[::-1] + list(far[:2]),
        [shape(bf16, k_rows, HD)] * 2 + [shape(bf16, HD, rows)] * 2,
        flops=20 * rows * k_rows * HD,
    )
    key_grad, value_grad = near[:2]
    parts[0], parts[1] = near[3], over_time(near[2], 1)
    parts = [parts[k] for k in range(n_t)]
    to_order, _ = lax.optimization_barrier((packed_all, key_grad))
    ordered = call(
        functools.partial(order_kernel, n_t, chips),
        to_order,
        shape(bf16, HD, n_t * rows),
        [pltpu.VMEM((n_t, rows, HD), f32)],
    )
    bundles, _ = lax.optimization_barrier((bundles, (ordered, key_grad, parts[: n_t // 2 - 1 : -1])))
    collected = call(
        functools.partial(collect_kernel, chips, base),
        bundles,
        shape(bf16, chips * base + 2 * n_t * count, LANES),
        [pltpu.VMEM((chips, n_t * count, LANES), f32)],
    )
    scratch = [pltpu.VMEM((n_t, count, LANES), f32)]
    own_halves = call(
        functools.partial(own_kernel, n_t, chips, frames),
        [hot, collected, ordered],
        [shape(f32, HD, width), shape(f32, levels, chips * width)],
        scratch,
        flops=2 * n_t * rows * width * HD,
    )
    weight_grad, gate_grad = call(
        functools.partial(final_kernel, n_t, chips, frames),
        [hot, over_cores(collected), *own_halves, ordered],
        [shape(f32, HD, 2 * width), shape(f32, levels, n_s * width)],
        scratch,
        flops=2 * n_t * rows * width * HD,
    )
    parts[0], _ = lax.optimization_barrier((parts[0], gate_grad))
    query_grad = call(functools.partial(query_kernel, n_t), parts[::-1], shape(bf16, rows, HD))
    if width != shard:
        weight_grad = without_padding(weight_grad, 2, shard)
        gate_grad = without_padding(gate_grad, n_s, shard)
    return (query_grad, key_grad, value_grad, weight_grad, gate_grad)


def solution(mesh):
    return jax.shard_map(
        body,
        mesh=mesh,
        in_specs=(
            P("tm", "space"),
            P("tm", "space"),
            P("tm", "space"),
            P("tm", "space"),
            P("tm", "space"),
            P("space", None),
            P(),
            P(),
            P(),
        ),
        out_specs=(P("tm", "space"), P("tm", "space"), P("tm", "space"), P("space", "tm"), P()),
        check_vma=False,
    )
```

```python
import functools
import math

import jax
import jax.numpy as jnp
from jax import lax
from jax.experimental import pallas as pl
from jax.experimental.pallas import tpu as pltpu
from jax.sharding import PartitionSpec as P

HD = 128
SPF = 512
QF = 64
LANES = 128
NEG_BIG = -1e30
SCALE = 1.0 / math.sqrt(HD)
VMEM_LIMIT = 32 * 1024 * 1024
PREP_VMEM = 52 * 1024 * 1024
SPLIT = 3


def dot(a, b, on_a, on_b):
    return lax.dot_general(
        a, b, (((on_a,), (on_b,)), ((), ())), preferred_element_type=jnp.float32
    )


def far_first(blocks):
    blocks = list(blocks)
    return blocks[:1] + blocks[:0:-1]


def last_swapped(blocks):
    blocks = list(blocks)
    return blocks[:-2] + blocks[:-3:-1]


def place():
    s = lax.axis_index("space")
    return lax.axis_index("tm"), s // 2, s % 2


def clip_numbers(clips_ref):
    bounds = []
    so_far = 0
    for c in range(clips_ref.shape[0]):
        so_far = so_far + clips_ref[c]
        bounds.append(so_far)
    return lambda frame: sum((frame >= bound).astype(jnp.int32) for bound in bounds)


def fetch_kernel(chips, weight_in, grad_in, kept, grad, sems):
    _, chip, core = place()
    width = kept.shape[2]
    copies = [pltpu.make_async_copy(grad_in, grad, sems.at[chips])]
    for k in range(chips):
        columns = pl.ds(pl.multiple_of((2 * (chip ^ k) + core) * width, LANES), width)
        copies.append(pltpu.make_async_copy(weight_in.at[:, columns], kept.at[k], sems.at[k]))
    for copy in copies:
        copy.start()
    for copy in copies:
        copy.wait()


def masks_kernel(n_t, chips, frames, rows, levels, clips, gate, bias, gate_a, gate_b, hot):
    t, chip, core = place()
    width = gate_a.shape[2]
    clip_of = clip_numbers(clips)
    lane = lax.broadcasted_iota(jnp.int32, (1, rows), 1)
    for kf in range(frames):
        key_frame = t * frames + kf
        key_clip = clip_of(key_frame)
        for k in range(n_t):
            row = jnp.full((1, rows), NEG_BIG, jnp.float32)
            for r in range(frames):
                frame = (t ^ k) * frames + r
                visible = (key_frame >= frame) & (clip_of(frame) == key_clip)
                value = jnp.where(visible, 0.0, NEG_BIG).astype(jnp.float32)
                row = jnp.where((lane >= r * QF) & (lane < (r + 1) * QF), value, row)
            bias[kf : kf + 1, k * rows : (k + 1) * rows] = row
    spot = lax.broadcasted_iota(jnp.int32, hot.shape[1:], 0)
    for f in range(n_t * frames):
        hot[f] = (spot == levels[f]).astype(jnp.float32)
    for r in range(frames):
        level = levels[t * frames + r]
        for k in range(chips):
            columns = pl.ds(pl.multiple_of((2 * (chip ^ k) + core) * width, LANES), width)
            gate_a[k, r : r + 1, :] = gate[pl.ds(level, 1), columns]
    mine = pl.ds(pl.multiple_of((2 * t + core) * width, LANES), width)
    for k in range(n_t):
        level = levels[(t ^ k) * frames + chip * (rows // chips) // QF]
        gate_b[k] = gate[pl.ds(level, 1), mine]


def stats_kernel(n_t, bias, keys, *refs):
    packed, out = far_first(refs[:n_t]), refs[n_t]
    rows = packed[0].shape[1]
    for p in range(0, n_t, 2):
        q = jnp.concatenate([packed[p][0], packed[p + 1][0]], axis=0)
        scores = []
        for kf in range(bias.shape[0]):
            mask = bias[kf : kf + 1, p * rows : (p + 2) * rows]
            scores.append(dot(keys[kf * SPF : (kf + 1) * SPF, :], q, 1, 1) * SCALE + mask)
        top = functools.reduce(jnp.maximum, [jnp.max(x, axis=0, keepdims=True) for x in scores])
        total = sum(jnp.sum(jnp.exp(x - top), axis=0, keepdims=True) for x in scores)
        for i in range(2):
            out[p + i : p + i + 1, :] = top[:, i * rows : (i + 1) * rows]
            out[n_t + p + i : n_t + p + i + 1, :] = total[:, i * rows : (i + 1) * rows]


def head_kernel(chips, frames, packed, other_saved, kept, received, gate_a, *refs):
    pieces, (mine, other, terms) = refs[:chips], refs[chips:]
    _, chip, core = place()
    width = pieces[0].shape[1]
    tiles = width // LANES
    saved = jnp.concatenate([packed[1], other_saved[...]], axis=1)
    head = None
    for k in range(chips):
        columns = pl.ds(pl.multiple_of((2 * (chip ^ k) + core) * width, LANES), width)
        weight = jnp.concatenate([kept[k], received[:, columns]], axis=0)
        wide = pieces[k][...].astype(jnp.float32)
        gated = jnp.concatenate(
            [
                (wide[r * QF : (r + 1) * QF] * gate_a[k, r : r + 1, :]).astype(jnp.bfloat16)
                for r in range(frames)
            ],
            axis=0,
        )
        part = dot(gated, weight, 1, 1)
        head = part if head is None else head + part
        product = wide * dot(saved, weight, 1, 0)
        for r in range(frames):
            term = jnp.sum(product[r * QF : (r + 1) * QF], axis=0, keepdims=True)
            for j in range(tiles):
                row = ((chip ^ k) * frames + r) * tiles + j
                terms[pl.ds(row, 1), :] = term[:, j * LANES : (j + 1) * LANES]
    mine[...] = head[:, :HD]
    other[...] = head[:, HD:]


def sections(rows, chips, tiles, n_t, count):
    starts = [0, rows]
    starts.append(starts[-1] + tiles * (rows // chips))
    starts.append(starts[-1] + -(-(SPLIT * 2 * n_t + count) // 16) * 16)
    return starts


def padded(x, rows):
    if x.shape[0] == rows:
        return x
    return jnp.concatenate([x, jnp.zeros((rows - x.shape[0], x.shape[1]), x.dtype)], axis=0)


def join_kernel(n_t, chips, starts, mine, received, stats, terms, *refs):
    pieces, outs, (wide, held) = refs[:chips], refs[chips : chips + n_t][::-1], refs[chips + n_t :]
    t, chip, _ = place()
    part, tiles = held.shape[1], held.shape[2] // LANES
    for k in range(chips):
        wide[...] = pieces[k][...].astype(jnp.float32)
        held[k] = wide[pl.ds(pl.multiple_of(chip * part, part), part), :]
    head = (mine[...] + received[...]).astype(jnp.bfloat16)
    rest = stats[...]
    split = []
    for _ in range(SPLIT):
        piece = rest.astype(jnp.bfloat16).astype(jnp.float32)
        split.append(piece)
        rest = rest - piece
    last = padded(jnp.concatenate(split + [terms[...]], axis=0), starts[3] - starts[2])
    last = last.astype(jnp.bfloat16)
    for k in range(n_t):
        rows = held[chip ^ t ^ k]
        rows = jnp.concatenate([rows[:, j * LANES : (j + 1) * LANES] for j in range(tiles)], axis=0)
        outs[k][: starts[1], :] = head
        outs[k][starts[1] : starts[2], :] = rows.astype(jnp.bfloat16)
        outs[k][starts[2] :, :] = last


def bundle_kernel(n_t, starts, count, gate_b, *refs):
    heads, out = last_swapped(refs[:n_t]), refs[n_t]
    tiles = gate_b.shape[2] // LANES
    part = (starts[2] - starts[1]) // tiles
    wide = [heads[k][starts[1] : starts[2], :].astype(jnp.float32) for k in range(n_t)]
    for j in range(tiles):
        gated = jnp.concatenate(
            [
                wide[k][j * part : (j + 1) * part] * gate_b[k, :, j * LANES : (j + 1) * LANES]
                for k in range(n_t)
            ],
            axis=0,
        )
        out[j * n_t * part : (j + 1) * n_t * part, :] = gated.astype(jnp.bfloat16)
    first = SPLIT * 2 * n_t
    terms = [heads[k][starts[2] :, :].astype(jnp.float32)[first : first + count] for k in range(n_t)]
    out[tiles * n_t * part :, :] = jnp.concatenate(terms, axis=0).astype(jnp.bfloat16)


def collect_kernel(chips, base, *refs):
    pieces, out, held = refs[:chips], refs[chips], refs[chips + 1]
    chip = place()[1]
    for k in range(chips):
        out[k * base : (k + 1) * base, :] = pieces[k][:base, :]
        held[chip ^ k] = pieces[k][base:, :].astype(jnp.float32)
    total = held[0]
    for k in range(1, chips):
        total = total + held[k]
    high = total.astype(jnp.bfloat16)
    count = total.shape[0]
    out[chips * base : chips * base + count, :] = high
    out[chips * base + count :, :] = (total - high.astype(jnp.float32)).astype(jnp.bfloat16)


def grads_kernel(n_t, starts, first, last, bias, keys, values, *refs):
    packed, heads = far_first(refs[:n_t]), last_swapped(refs[n_t : 2 * n_t])
    refs = refs[2 * n_t :]
    if first == 0:
        sums, refs = refs[:2], refs[2:]
    key_out, value_out = refs[:2]
    outs = refs[2 : 2 + last - first]
    accs = refs[2 + last - first :]
    rows = packed[0].shape[1]
    ones = jnp.ones((8, HD), jnp.float32)
    keys_t = jnp.transpose(keys[...])
    stats = []
    for k in range(n_t):
        parts = heads[k][starts[2] :, :].astype(jnp.float32)
        stats.append(sum(parts[i * 2 * n_t : (i + 1) * 2 * n_t] for i in range(SPLIT)))
    for p in range(first, last, 2):
        q = jnp.concatenate([packed[p][0], packed[p + 1][0]], axis=0)
        o = jnp.concatenate([packed[p][1], packed[p + 1][1]], axis=0)
        g = jnp.concatenate([heads[p][:rows, :], heads[p + 1][:rows, :]], axis=0)
        delta = lax.dot_general(
            ones,
            g.astype(jnp.float32) * o.astype(jnp.float32),
            (((1,), (1,)), ((), ())),
            precision=lax.Precision.HIGHEST,
            preferred_element_type=jnp.float32,
        )[0:1]
        lse = []
        for i in (p, p + 1):
            tops = [stats[k][i ^ k : (i ^ k) + 1] for k in range(n_t)]
            sums_of = [stats[k][n_t + (i ^ k) : n_t + (i ^ k) + 1] for k in range(n_t)]
            top = functools.reduce(jnp.maximum, tops)
            lse.append(top + jnp.log(sum(b * jnp.exp(a - top) for a, b in zip(tops, sums_of))))
        lse = jnp.concatenate(lse, axis=1)
        query_part = None
        for kf in range(bias.shape[0]):
            span = slice(kf * SPF, (kf + 1) * SPF)
            shift = bias[kf : kf + 1, p * rows : (p + 2) * rows] - lse
            probs = jnp.exp(dot(keys[span, :], q, 1, 1) * SCALE + shift)
            score_grad = (probs * (dot(values[span, :], g, 1, 1) - delta)).astype(jnp.bfloat16)
            value_add = dot(probs.astype(jnp.bfloat16), g, 1, 0)
            key_add = dot(score_grad, q, 1, 0)
            if p > first:
                value_add = value_add + accs[1][span, :]
                key_add = key_add + accs[0][span, :]
            if p + 2 < last:
                accs[1][span, :] = value_add
                accs[0][span, :] = key_add
            elif first:
                value_out[span, :] = value_add
                key_out[span, :] = key_add
            else:
                value_out[span, :] = (value_add + sums[1][span, :]).astype(jnp.bfloat16)
                key_out[span, :] = ((key_add + sums[0][span, :]) * SCALE).astype(jnp.bfloat16)
            part = dot(keys_t[:, span], score_grad, 1, 0)
            query_part = part if query_part is None else query_part + part
        outs[p - first][...] = query_part[:, :rows].astype(jnp.bfloat16)
        outs[p + 1 - first][...] = query_part[:, rows:].astype(jnp.bfloat16)


def query_kernel(n_t, *refs):
    total = refs[0][...].astype(jnp.float32)
    for k in range(1, n_t):
        total = total + refs[k][...].astype(jnp.float32)
    refs[n_t][...] = jnp.transpose(total * SCALE).astype(jnp.bfloat16)


def half_results(n_t, chips, frames, hot, ref, packed, saved, held, tiles):
    t, chip, _ = place()
    rows = saved.shape[1]
    part = rows // chips
    base = tiles * n_t * part
    for k in range(n_t):
        saved[k] = packed[k][1].astype(jnp.float32)
    ordered = []
    for c in range(chips):
        mine = pl.ds(pl.multiple_of((chip ^ c) * part, part), part)
        ordered += [saved[k, mine, :] for k in range(n_t)]
    ordered = jnp.transpose(jnp.concatenate(ordered, axis=0)).astype(jnp.bfloat16)
    gated = jnp.concatenate(
        [
            jnp.concatenate(
                [
                    ref[c * base + j * n_t * part : c * base + (j + 1) * n_t * part, :]
                    for c in range(chips)
                ],
                axis=0,
            )
            for j in range(tiles)
        ],
        axis=1,
    )
    count = (ref.shape[0] - chips * base) // 2
    each = count // n_t
    terms = ref[chips * base : chips * base + count, :].astype(jnp.float32)
    terms = terms + ref[chips * base + count :, :].astype(jnp.float32)
    for k in range(n_t):
        held[t ^ k] = terms[k * each : (k + 1) * each]

    def gate_tile(a, j):
        total = jnp.zeros(hot.shape[1:], jnp.float32)
        for f in range(n_t * frames):
            row = (a * frames + f % frames) * tiles + j
            total = total + hot[f] * held[f // frames, row : row + 1, :]
        return total

    return dot(ordered, gated, 1, 0), gate_tile


def own_kernel(n_t, chips, frames, hot, own, *refs):
    packed, (weight_out, gate_out, saved, held) = refs[:n_t], refs[n_t:]
    tiles = weight_out.shape[1] // LANES
    result, gate_tile = half_results(n_t, chips, frames, hot, own, packed, saved, held, tiles)
    weight_out[...] = result
    for a in range(chips):
        for j in range(tiles):
            gate_out[:, (a * tiles + j) * LANES : (a * tiles + j + 1) * LANES] = gate_tile(a, j)


def final_kernel(n_t, chips, frames, hot, other, own_weight, own_gate, *refs):
    packed, (weight_out, gate_out, saved, held) = refs[:n_t], refs[n_t:]
    core = place()[2]
    width = own_weight.shape[1]
    tiles = width // LANES
    result, gate_tile = half_results(n_t, chips, frames, hot, other, packed, saved, held, tiles)
    mine = own_weight[...]
    weight_out[:, :width] = jnp.where(core == 0, mine, result)
    weight_out[:, width:] = jnp.where(core == 0, result, mine)
    for a in range(chips):
        for j in range(tiles):
            first = gate_tile(a, j)
            second = own_gate[:, (a * tiles + j) * LANES : (a * tiles + j + 1) * LANES]
            column = 2 * a * width + j * LANES
            gate_out[:, column : column + LANES] = jnp.where(core == 0, second, first)
            column += width
            gate_out[:, column : column + LANES] = jnp.where(core == 0, first, second)


def call(kernel, args, out_shape, scratch=(), flops=0, in_place=False, in_smem=0):
    vmem = pl.BlockSpec(memory_space=pltpu.VMEM)
    single = not isinstance(out_shape, (list, tuple))
    nbytes = sum(a.size * a.dtype.itemsize for a in args)
    return pl.pallas_call(
        kernel,
        out_shape=out_shape,
        in_specs=[pl.BlockSpec(memory_space=pltpu.SMEM)] * in_smem
        + [pl.BlockSpec(memory_space=pltpu.HBM) if in_place else vmem] * (len(args) - in_smem),
        out_specs=vmem if single else [vmem] * len(out_shape),
        scratch_shapes=list(scratch),
        compiler_params=pltpu.CompilerParams(vmem_limit_bytes=PREP_VMEM if in_place else VMEM_LIMIT),
        cost_estimate=pl.CostEstimate(flops=flops, bytes_accessed=nbytes, transcendentals=0),
    )(*args)


def padded_shards(table, n_s, width):
    rows, columns = table.shape
    cut = table.reshape(rows, n_s, columns // n_s)
    cut = jnp.pad(cut, ((0, 0), (0, 0), (0, width - columns // n_s)))
    return cut.reshape(rows, n_s * width)


def without_padding(table, shards, shard):
    rows, columns = table.shape
    return table.reshape(rows, shards, columns // shards)[:, :, :shard].reshape(rows, shards * shard)


def body(
    queries, keys, values, saved_out, out_grad, proj_weight, gate_table, noise_levels, clip_lengths
):
    n_t, n_s = lax.axis_size("tm"), lax.axis_size("space")
    chips = n_s // 2
    rows, shard = out_grad.shape
    k_rows = keys.shape[0]
    frames = rows // QF
    levels = gate_table.shape[0]
    bf16, f32 = jnp.bfloat16, jnp.float32
    width = -(-shard // LANES) * LANES
    if width != shard:
        out_grad = jnp.pad(out_grad, ((0, 0), (0, width - shard)))
        proj_weight = padded_shards(proj_weight, n_s, width)
        gate_table = padded_shards(gate_table, n_s, width)

    def shape(dtype, *dims):
        return jax.ShapeDtypeStruct(dims, dtype)

    def over_chips(x):
        return [x] + [
            lax.ppermute(x, "space", [(s, s ^ (2 * k)) for s in range(n_s)]) for k in range(1, chips)
        ]

    def over_cores(x):
        return lax.ppermute(x, "space", [(s, s ^ 1) for s in range(n_s)])

    def over_time(x, k):
        return lax.ppermute(x, "tm", [(t, t ^ k) for t in range(n_t)])

    tiles = width // LANES
    part = rows // chips
    count = chips * frames * tiles
    starts = sections(rows, chips, tiles, n_t, count)

    def time_swaps(messages):
        got = {k: over_time(messages[k], k) for k in range(n_t - 1, 0, -1)}
        return [messages[0]] + [got[k] for k in range(1, n_t)]

    pieces = over_chips(out_grad)
    received, other_saved = over_cores(proj_weight), over_cores(saved_out)
    packed, _ = lax.optimization_barrier(
        (jnp.stack([queries, saved_out]), (received, other_saved))
    )
    packed_all = time_swaps([packed] * n_t)
    (to_fetch, own_grad), _ = lax.optimization_barrier(((proj_weight, out_grad), received))
    kept, pieces[0] = call(
        functools.partial(fetch_kernel, chips),
        [to_fetch, own_grad],
        [shape(bf16, chips, HD, width), shape(bf16, rows, width)],
        [pltpu.SemaphoreType.DMA((chips + 1,))],
        in_place=True,
    )
    gate_table, _ = lax.optimization_barrier((gate_table, received))
    bias, gate_a, gate_b, hot = call(
        functools.partial(masks_kernel, n_t, chips, frames, rows),
        [noise_levels, clip_lengths, gate_table],
        [
            shape(f32, frames, n_t * rows),
            shape(f32, chips, frames, width),
            shape(f32, n_t, 1, width),
            shape(f32, n_t * frames, levels, LANES),
        ],
        in_smem=2,
    )
    mine, other, terms = call(
        functools.partial(head_kernel, chips, frames),
        [packed, other_saved, kept, received, gate_a] + pieces,
        [shape(f32, rows, HD), shape(f32, rows, HD), shape(f32, count, LANES)],
        flops=4 * rows * chips * width * 2 * HD,
    )
    later_bias, _ = lax.optimization_barrier((bias, mine))
    stats = call(
        functools.partial(stats_kernel, n_t),
        [later_bias, keys] + far_first(packed_all),
        shape(f32, 2 * n_t, LANES),
        flops=2 * n_t * rows * k_rows * HD,
    )
    heads = call(
        functools.partial(join_kernel, n_t, chips, starts),
        [mine, over_cores(other), stats, terms] + pieces,
        [shape(bf16, starts[-1], LANES)] * n_t,
        [pltpu.VMEM((rows, width), f32), pltpu.VMEM((chips, part, width), f32)],
    )
    heads_all = time_swaps(heads[::-1])
    base = tiles * n_t * part
    bundle = call(
        functools.partial(bundle_kernel, n_t, starts, count),
        [gate_b] + last_swapped(heads_all),
        shape(bf16, base + n_t * count, LANES),
    )
    bundles = over_chips(bundle)
    later_bias, _ = lax.optimization_barrier((bias, bundle))
    accs = [pltpu.VMEM((k_rows, HD), f32)] * 2
    far = call(
        functools.partial(grads_kernel, n_t, starts, 2, n_t),
        [later_bias, keys, values] + far_first(packed_all) + last_swapped(heads_all),
        [shape(f32, k_rows, HD)] * 2 + [shape(bf16, HD, rows)] * (n_t - 2),
        accs,
        flops=10 * (n_t - 2) * rows * k_rows * HD,
    )
    parts = {k: over_time(far[k], k) for k in range(2, n_t)}
    near = call(
        functools.partial(grads_kernel, n_t, starts, 0, 2),
        [bias, keys, values] + far_first(packed_all) + last_swapped(heads_all) + list(far[:2]),
        [shape(bf16, k_rows, HD)] * 2 + [shape(bf16, HD, rows)] * 2,
        flops=20 * rows * k_rows * HD,
    )
    key_grad, value_grad = near[:2]
    parts[0], parts[1] = near[2], over_time(near[3], 1)
    parts = [parts[k] for k in range(n_t)]
    bundles, _ = lax.optimization_barrier((bundles, (key_grad, parts[n_t // 2 :])))
    collected = call(
        functools.partial(collect_kernel, chips, base),
        bundles,
        shape(bf16, chips * base + 2 * n_t * count, LANES),
        [pltpu.VMEM((chips, n_t * count, LANES), f32)],
    )
    scratch = [pltpu.VMEM((n_t, rows, HD), f32), pltpu.VMEM((n_t, count, LANES), f32)]
    own_halves = call(
        functools.partial(own_kernel, n_t, chips, frames),
        [hot, collected] + packed_all,
        [shape(f32, HD, width), shape(f32, levels, chips * width)],
        scratch,
        flops=2 * n_t * rows * width * HD,
    )
    weight_grad, gate_grad = call(
        functools.partial(final_kernel, n_t, chips, frames),
        [hot, over_cores(collected), *own_halves] + packed_all,
        [shape(f32, HD, 2 * width), shape(f32, levels, n_s * width)],
        scratch,
        flops=2 * n_t * rows * width * HD,
    )
    parts[0], _ = lax.optimization_barrier((parts[0], gate_grad))
    query_grad = call(functools.partial(query_kernel, n_t), parts, shape(bf16, rows, HD))
    if width != shard:
        weight_grad = without_padding(weight_grad, 2, shard)
        gate_grad = without_padding(gate_grad, n_s, shard)
    return (query_grad, key_grad, value_grad, weight_grad, gate_grad)


def solution(mesh):
    return jax.shard_map(
        body,
        mesh=mesh,
        in_specs=(
            P("tm", "space"),
            P("tm", "space"),
            P("tm", "space"),
            P("tm", "space"),
            P("tm", "space"),
            P("space", None),
            P(),
            P(),
            P(),
        ),
        out_specs=(P("tm", "space"), P("tm", "space"), P("tm", "space"), P("space", "tm"), P()),
        check_vma=False,
    )
```

```python
import functools
import math

import jax
import jax.numpy as jnp
from jax import lax
from jax.experimental import pallas as pl
from jax.experimental.pallas import tpu as pltpu
from jax.sharding import PartitionSpec as P

HD = 128
SPF = 512
QF = 64
LANES = 128
NEG_BIG = -1e30
SCALE = 1.0 / math.sqrt(HD)
VMEM_LIMIT = 32 * 1024 * 1024
PREP_VMEM = 52 * 1024 * 1024
SPLIT = 3


def dot(a, b, on_a, on_b):
    return lax.dot_general(
        a, b, (((on_a,), (on_b,)), ((), ())), preferred_element_type=jnp.float32
    )


def far_first(blocks):
    blocks = list(blocks)
    return blocks[:1] + blocks[:0:-1]


def last_swapped(blocks):
    blocks = list(blocks)
    return blocks[:-2] + blocks[:-3:-1]


def place():
    s = lax.axis_index("space")
    return lax.axis_index("tm"), s // 2, s % 2


def clip_numbers(clips_ref):
    bounds = []
    so_far = 0
    for c in range(clips_ref.shape[0]):
        so_far = so_far + clips_ref[c]
        bounds.append(so_far)
    return lambda frame: sum((frame >= bound).astype(jnp.int32) for bound in bounds)


def fetch_kernel(chips, weight_in, grad_in, kept, grad, sems):
    _, chip, core = place()
    width = kept.shape[2]
    copies = [pltpu.make_async_copy(grad_in, grad, sems.at[chips])]
    for k in range(chips):
        columns = pl.ds(pl.multiple_of((2 * (chip ^ k) + core) * width, LANES), width)
        copies.append(pltpu.make_async_copy(weight_in.at[:, columns], kept.at[k], sems.at[k]))
    for copy in copies:
        copy.start()
    for copy in copies:
        copy.wait()


def masks_kernel(n_t, chips, frames, rows, levels, clips, gate, bias, gate_a, gate_b, hot):
    t, chip, core = place()
    width = gate_a.shape[2]
    clip_of = clip_numbers(clips)
    lane = lax.broadcasted_iota(jnp.int32, (1, rows), 1)
    for kf in range(frames):
        key_frame = t * frames + kf
        key_clip = clip_of(key_frame)
        for k in range(n_t):
            row = jnp.full((1, rows), NEG_BIG, jnp.float32)
            for r in range(frames):
                frame = (t ^ k) * frames + r
                visible = (key_frame >= frame) & (clip_of(frame) == key_clip)
                value = jnp.where(visible, 0.0, NEG_BIG).astype(jnp.float32)
                row = jnp.where((lane >= r * QF) & (lane < (r + 1) * QF), value, row)
            bias[kf : kf + 1, k * rows : (k + 1) * rows] = row
    spot = lax.broadcasted_iota(jnp.int32, hot.shape[1:], 0)
    for f in range(n_t * frames):
        hot[f] = (spot == levels[f]).astype(jnp.float32)
    for r in range(frames):
        level = levels[t * frames + r]
        for k in range(chips):
            columns = pl.ds(pl.multiple_of((2 * (chip ^ k) + core) * width, LANES), width)
            gate_a[k, r : r + 1, :] = gate[pl.ds(level, 1), columns]
    mine = pl.ds(pl.multiple_of((2 * t + core) * width, LANES), width)
    for k in range(n_t):
        level = levels[(t ^ k) * frames + chip * (rows // chips) // QF]
        gate_b[k] = gate[pl.ds(level, 1), mine]


def stats_kernel(n_t, bias, keys, *refs):
    packed, out = far_first(refs[:n_t]), refs[n_t]
    rows = packed[0].shape[1]
    for p in range(0, n_t, 2):
        q = jnp.concatenate([packed[p][0], packed[p + 1][0]], axis=0)
        scores = []
        for kf in range(bias.shape[0]):
            mask = bias[kf : kf + 1, p * rows : (p + 2) * rows]
            scores.append(dot(keys[kf * SPF : (kf + 1) * SPF, :], q, 1, 1) * SCALE + mask)
        top = functools.reduce(jnp.maximum, [jnp.max(x, axis=0, keepdims=True) for x in scores])
        total = sum(jnp.sum(jnp.exp(x - top), axis=0, keepdims=True) for x in scores)
        for i in range(2):
            out[p + i : p + i + 1, :] = top[:, i * rows : (i + 1) * rows]
            out[n_t + p + i : n_t + p + i + 1, :] = total[:, i * rows : (i + 1) * rows]


def head_kernel(chips, frames, packed, other_saved, kept, received, gate_a, *refs):
    pieces, (mine, other, terms) = refs[:chips], refs[chips:]
    _, chip, core = place()
    width = pieces[0].shape[1]
    tiles = width // LANES
    saved = jnp.concatenate([packed[1], other_saved[...]], axis=1)
    head = None
    for k in range(chips):
        columns = pl.ds(pl.multiple_of((2 * (chip ^ k) + core) * width, LANES), width)
        weight = jnp.concatenate([kept[k], received[:, columns]], axis=0)
        wide = pieces[k][...].astype(jnp.float32)
        gated = jnp.concatenate(
            [
                (wide[r * QF : (r + 1) * QF] * gate_a[k, r : r + 1, :]).astype(jnp.bfloat16)
                for r in range(frames)
            ],
            axis=0,
        )
        part = dot(gated, weight, 1, 1)
        head = part if head is None else head + part
        product = wide * dot(saved, weight, 1, 0)
        for r in range(frames):
            term = jnp.sum(product[r * QF : (r + 1) * QF], axis=0, keepdims=True)
            for j in range(tiles):
                row = ((chip ^ k) * frames + r) * tiles + j
                terms[pl.ds(row, 1), :] = term[:, j * LANES : (j + 1) * LANES]
    mine[...] = head[:, :HD]
    other[...] = head[:, HD:]


def sections(rows, chips, tiles, n_t, count):
    starts = [0, rows]
    starts.append(starts[-1] + tiles * (rows // chips))
    starts.append(starts[-1] + -(-(SPLIT * 2 * n_t + count) // 16) * 16)
    return starts


def padded(x, rows):
    if x.shape[0] == rows:
        return x
    return jnp.concatenate([x, jnp.zeros((rows - x.shape[0], x.shape[1]), x.dtype)], axis=0)


def join_kernel(n_t, chips, starts, mine, received, stats, terms, *refs):
    pieces, outs, (wide, held) = refs[:chips], refs[chips : chips + n_t][::-1], refs[chips + n_t :]
    t, chip, _ = place()
    part, tiles = held.shape[1], held.shape[2] // LANES
    for k in range(chips):
        wide[...] = pieces[k][...].astype(jnp.float32)
        held[k] = wide[pl.ds(pl.multiple_of(chip * part, part), part), :]
    head = (mine[...] + received[...]).astype(jnp.bfloat16)
    rest = stats[...]
    split = []
    for _ in range(SPLIT):
        piece = rest.astype(jnp.bfloat16).astype(jnp.float32)
        split.append(piece)
        rest = rest - piece
    last = padded(jnp.concatenate(split + [terms[...]], axis=0), starts[3] - starts[2])
    last = last.astype(jnp.bfloat16)
    for k in range(n_t):
        rows = held[chip ^ t ^ k]
        rows = jnp.concatenate([rows[:, j * LANES : (j + 1) * LANES] for j in range(tiles)], axis=0)
        outs[k][: starts[1], :] = head
        outs[k][starts[1] : starts[2], :] = rows.astype(jnp.bfloat16)
        outs[k][starts[2] :, :] = last


def bundle_kernel(n_t, starts, count, gate_b, *refs):
    heads, out = last_swapped(refs[:n_t]), refs[n_t]
    tiles = gate_b.shape[2] // LANES
    part = (starts[2] - starts[1]) // tiles
    wide = [heads[k][starts[1] : starts[2], :].astype(jnp.float32) for k in range(n_t)]
    for j in range(tiles):
        gated = jnp.concatenate(
            [
                wide[k][j * part : (j + 1) * part] * gate_b[k, :, j * LANES : (j + 1) * LANES]
                for k in range(n_t)
            ],
            axis=0,
        )
        out[j * n_t * part : (j + 1) * n_t * part, :] = gated.astype(jnp.bfloat16)
    first = SPLIT * 2 * n_t
    terms = [heads[k][starts[2] :, :].astype(jnp.float32)[first : first + count] for k in range(n_t)]
    out[tiles * n_t * part :, :] = jnp.concatenate(terms, axis=0).astype(jnp.bfloat16)


def collect_kernel(chips, base, *refs):
    pieces, out, held = far_first(refs[:chips]), refs[chips], refs[chips + 1]
    chip = place()[1]
    for k in range(chips):
        out[k * base : (k + 1) * base, :] = pieces[k][:base, :]
        held[chip ^ k] = pieces[k][base:, :].astype(jnp.float32)
    total = held[0]
    for k in range(1, chips):
        total = total + held[k]
    high = total.astype(jnp.bfloat16)
    count = total.shape[0]
    out[chips * base : chips * base + count, :] = high
    out[chips * base + count :, :] = (total - high.astype(jnp.float32)).astype(jnp.bfloat16)


def grads_kernel(n_t, starts, first, last, bias, keys, values, *refs):
    packed, heads = far_first(refs[:n_t]), last_swapped(refs[n_t : 2 * n_t])
    refs = refs[2 * n_t :]
    if first == 0:
        sums, refs = refs[:2], refs[2:]
    key_out, value_out = refs[:2]
    outs = refs[2 : 2 + last - first]
    accs = refs[2 + last - first :]
    rows = packed[0].shape[1]
    ones = jnp.ones((8, HD), jnp.float32)
    keys_t = jnp.transpose(keys[...])
    stats = []
    for k in range(n_t):
        parts = heads[k][starts[2] :, :].astype(jnp.float32)
        stats.append(sum(parts[i * 2 * n_t : (i + 1) * 2 * n_t] for i in range(SPLIT)))
    for p in range(first, last, 2):
        q = jnp.concatenate([packed[p][0], packed[p + 1][0]], axis=0)
        o = jnp.concatenate([packed[p][1], packed[p + 1][1]], axis=0)
        g = jnp.concatenate([heads[p][:rows, :], heads[p + 1][:rows, :]], axis=0)
        delta = lax.dot_general(
            ones,
            g.astype(jnp.float32) * o.astype(jnp.float32),
            (((1,), (1,)), ((), ())),
            precision=lax.Precision.HIGHEST,
            preferred_element_type=jnp.float32,
        )[0:1]
        lse = []
        for i in (p, p + 1):
            tops = [stats[k][i ^ k : (i ^ k) + 1] for k in range(n_t)]
            sums_of = [stats[k][n_t + (i ^ k) : n_t + (i ^ k) + 1] for k in range(n_t)]
            top = functools.reduce(jnp.maximum, tops)
            lse.append(top + jnp.log(sum(b * jnp.exp(a - top) for a, b in zip(tops, sums_of))))
        lse = jnp.concatenate(lse, axis=1)
        query_part = None
        for kf in range(bias.shape[0]):
            span = slice(kf * SPF, (kf + 1) * SPF)
            shift = bias[kf : kf + 1, p * rows : (p + 2) * rows] - lse
            probs = jnp.exp(dot(keys[span, :], q, 1, 1) * SCALE + shift)
            score_grad = (probs * (dot(values[span, :], g, 1, 1) - delta)).astype(jnp.bfloat16)
            value_add = dot(probs.astype(jnp.bfloat16), g, 1, 0)
            key_add = dot(score_grad, q, 1, 0)
            if p > first:
                value_add = value_add + accs[1][span, :]
                key_add = key_add + accs[0][span, :]
            if p + 2 < last:
                accs[1][span, :] = value_add
                accs[0][span, :] = key_add
            elif first:
                value_out[span, :] = value_add
                key_out[span, :] = key_add
            else:
                value_out[span, :] = (value_add + sums[1][span, :]).astype(jnp.bfloat16)
                key_out[span, :] = ((key_add + sums[0][span, :]) * SCALE).astype(jnp.bfloat16)
            part = dot(keys_t[:, span], score_grad, 1, 0)
            query_part = part if query_part is None else query_part + part
        outs[p - first][...] = query_part[:, :rows].astype(jnp.bfloat16)
        outs[p + 1 - first][...] = query_part[:, rows:].astype(jnp.bfloat16)


def query_kernel(n_t, *refs):
    total = refs[0][...].astype(jnp.float32)
    for k in range(1, n_t):
        total = total + refs[k][...].astype(jnp.float32)
    refs[n_t][...] = jnp.transpose(total * SCALE).astype(jnp.bfloat16)


def half_results(n_t, chips, frames, hot, ref, packed, saved, held, tiles):
    t, chip, _ = place()
    rows = saved.shape[1]
    part = rows // chips
    base = tiles * n_t * part
    for k in range(n_t):
        saved[k] = packed[k][1].astype(jnp.float32)
    ordered = []
    for c in range(chips):
        mine = pl.ds(pl.multiple_of((chip ^ c) * part, part), part)
        ordered += [saved[k, mine, :] for k in range(n_t)]
    ordered = jnp.transpose(jnp.concatenate(ordered, axis=0)).astype(jnp.bfloat16)
    gated = jnp.concatenate(
        [
            jnp.concatenate(
                [
                    ref[c * base + j * n_t * part : c * base + (j + 1) * n_t * part, :]
                    for c in range(chips)
                ],
                axis=0,
            )
            for j in range(tiles)
        ],
        axis=1,
    )
    count = (ref.shape[0] - chips * base) // 2
    each = count // n_t
    terms = ref[chips * base : chips * base + count, :].astype(jnp.float32)
    terms = terms + ref[chips * base + count :, :].astype(jnp.float32)
    for k in range(n_t):
        held[t ^ k] = terms[k * each : (k + 1) * each]

    def gate_tile(a, j):
        total = jnp.zeros(hot.shape[1:], jnp.float32)
        for f in range(n_t * frames):
            row = (a * frames + f % frames) * tiles + j
            total = total + hot[f] * held[f // frames, row : row + 1, :]
        return total

    return dot(ordered, gated, 1, 0), gate_tile


def own_kernel(n_t, chips, frames, hot, own, *refs):
    packed, (weight_out, gate_out, saved, held) = refs[:n_t], refs[n_t:]
    tiles = weight_out.shape[1] // LANES
    result, gate_tile = half_results(n_t, chips, frames, hot, own, packed, saved, held, tiles)
    weight_out[...] = result
    for a in range(chips):
        for j in range(tiles):
            gate_out[:, (a * tiles + j) * LANES : (a * tiles + j + 1) * LANES] = gate_tile(a, j)


def final_kernel(n_t, chips, frames, hot, other, own_weight, own_gate, *refs):
    packed, (weight_out, gate_out, saved, held) = refs[:n_t], refs[n_t:]
    core = place()[2]
    width = own_weight.shape[1]
    tiles = width // LANES
    result, gate_tile = half_results(n_t, chips, frames, hot, other, packed, saved, held, tiles)
    mine = own_weight[...]
    weight_out[:, :width] = jnp.where(core == 0, mine, result)
    weight_out[:, width:] = jnp.where(core == 0, result, mine)
    for a in range(chips):
        for j in range(tiles):
            first = gate_tile(a, j)
            second = own_gate[:, (a * tiles + j) * LANES : (a * tiles + j + 1) * LANES]
            column = 2 * a * width + j * LANES
            gate_out[:, column : column + LANES] = jnp.where(core == 0, second, first)
            column += width
            gate_out[:, column : column + LANES] = jnp.where(core == 0, first, second)


def call(kernel, args, out_shape, scratch=(), flops=0, in_place=False, in_smem=0):
    vmem = pl.BlockSpec(memory_space=pltpu.VMEM)
    single = not isinstance(out_shape, (list, tuple))
    nbytes = sum(a.size * a.dtype.itemsize for a in args)
    return pl.pallas_call(
        kernel,
        out_shape=out_shape,
        in_specs=[pl.BlockSpec(memory_space=pltpu.SMEM)] * in_smem
        + [pl.BlockSpec(memory_space=pltpu.HBM) if in_place else vmem] * (len(args) - in_smem),
        out_specs=vmem if single else [vmem] * len(out_shape),
        scratch_shapes=list(scratch),
        compiler_params=pltpu.CompilerParams(vmem_limit_bytes=PREP_VMEM if in_place else VMEM_LIMIT),
        cost_estimate=pl.CostEstimate(flops=flops, bytes_accessed=nbytes, transcendentals=0),
    )(*args)


def padded_shards(table, n_s, width):
    rows, columns = table.shape
    cut = table.reshape(rows, n_s, columns // n_s)
    cut = jnp.pad(cut, ((0, 0), (0, 0), (0, width - columns // n_s)))
    return cut.reshape(rows, n_s * width)


def without_padding(table, shards, shard):
    rows, columns = table.shape
    return table.reshape(rows, shards, columns // shards)[:, :, :shard].reshape(rows, shards * shard)


def body(
    queries, keys, values, saved_out, out_grad, proj_weight, gate_table, noise_levels, clip_lengths
):
    n_t, n_s = lax.axis_size("tm"), lax.axis_size("space")
    chips = n_s // 2
    rows, shard = out_grad.shape
    k_rows = keys.shape[0]
    frames = rows // QF
    levels = gate_table.shape[0]
    bf16, f32 = jnp.bfloat16, jnp.float32
    width = -(-shard // LANES) * LANES
    if width != shard:
        out_grad = jnp.pad(out_grad, ((0, 0), (0, width - shard)))
        proj_weight = padded_shards(proj_weight, n_s, width)
        gate_table = padded_shards(gate_table, n_s, width)

    def shape(dtype, *dims):
        return jax.ShapeDtypeStruct(dims, dtype)

    def over_chips(x):
        return [x] + [
            lax.ppermute(x, "space", [(s, s ^ (2 * k)) for s in range(n_s)]) for k in range(1, chips)
        ]

    def over_cores(x):
        return lax.ppermute(x, "space", [(s, s ^ 1) for s in range(n_s)])

    def over_time(x, k):
        return lax.ppermute(x, "tm", [(t, t ^ k) for t in range(n_t)])

    tiles = width // LANES
    part = rows // chips
    count = chips * frames * tiles
    starts = sections(rows, chips, tiles, n_t, count)

    def time_swaps(messages):
        got = {k: over_time(messages[k], k) for k in range(n_t - 1, 0, -1)}
        return [messages[0]] + [got[k] for k in range(1, n_t)]

    pieces = over_chips(out_grad)
    received, other_saved = over_cores(proj_weight), over_cores(saved_out)
    packed, _ = lax.optimization_barrier(
        (jnp.stack([queries, saved_out]), (received, other_saved))
    )
    packed_all = time_swaps([packed] * n_t)
    (to_fetch, own_grad), _ = lax.optimization_barrier(((proj_weight, out_grad), received))
    kept, pieces[0] = call(
        functools.partial(fetch_kernel, chips),
        [to_fetch, own_grad],
        [shape(bf16, chips, HD, width), shape(bf16, rows, width)],
        [pltpu.SemaphoreType.DMA((chips + 1,))],
        in_place=True,
    )
    gate_table, _ = lax.optimization_barrier((gate_table, received))
    bias, gate_a, gate_b, hot = call(
        functools.partial(masks_kernel, n_t, chips, frames, rows),
        [noise_levels, clip_lengths, gate_table],
        [
            shape(f32, frames, n_t * rows),
            shape(f32, chips, frames, width),
            shape(f32, n_t, 1, width),
            shape(f32, n_t * frames, levels, LANES),
        ],
        in_smem=2,
    )
    mine, other, terms = call(
        functools.partial(head_kernel, chips, frames),
        [packed, other_saved, kept, received, gate_a] + pieces,
        [shape(f32, rows, HD), shape(f32, rows, HD), shape(f32, count, LANES)],
        flops=4 * rows * chips * width * 2 * HD,
    )
    later_bias, _ = lax.optimization_barrier((bias, mine))
    stats = call(
        functools.partial(stats_kernel, n_t),
        [later_bias, keys] + far_first(packed_all),
        shape(f32, 2 * n_t, LANES),
        flops=2 * n_t * rows * k_rows * HD,
    )
    heads = call(
        functools.partial(join_kernel, n_t, chips, starts),
        [mine, over_cores(other), stats, terms] + pieces,
        [shape(bf16, starts[-1], LANES)] * n_t,
        [pltpu.VMEM((rows, width), f32), pltpu.VMEM((chips, part, width), f32)],
    )
    heads_all = time_swaps(heads[::-1])
    base = tiles * n_t * part
    bundle = call(
        functools.partial(bundle_kernel, n_t, starts, count),
        [gate_b] + last_swapped(heads_all),
        shape(bf16, base + n_t * count, LANES),
    )
    bundles = over_chips(bundle)
    bundles = far_first(bundles)
    later_bias, _ = lax.optimization_barrier((bias, bundle))
    accs = [pltpu.VMEM((k_rows, HD), f32)] * 2
    far = call(
        functools.partial(grads_kernel, n_t, starts, 2, n_t),
        [later_bias, keys, values] + far_first(packed_all) + last_swapped(heads_all),
        [shape(f32, k_rows, HD)] * 2 + [shape(bf16, HD, rows)] * (n_t - 2),
        accs,
        flops=10 * (n_t - 2) * rows * k_rows * HD,
    )
    parts = {k: over_time(far[k], k) for k in range(2, n_t)}
    near = call(
        functools.partial(grads_kernel, n_t, starts, 0, 2),
        [bias, keys, values] + far_first(packed_all) + last_swapped(heads_all) + list(far[:2]),
        [shape(bf16, k_rows, HD)] * 2 + [shape(bf16, HD, rows)] * 2,
        flops=20 * rows * k_rows * HD,
    )
    key_grad, value_grad = near[:2]
    parts[0], parts[1] = near[2], over_time(near[3], 1)
    parts = [parts[k] for k in range(n_t)]
    bundles, _ = lax.optimization_barrier((bundles, (key_grad, parts[n_t // 2 :])))
    collected = call(
        functools.partial(collect_kernel, chips, base),
        bundles,
        shape(bf16, chips * base + 2 * n_t * count, LANES),
        [pltpu.VMEM((chips, n_t * count, LANES), f32)],
    )
    scratch = [pltpu.VMEM((n_t, rows, HD), f32), pltpu.VMEM((n_t, count, LANES), f32)]
    own_halves = call(
        functools.partial(own_kernel, n_t, chips, frames),
        [hot, collected] + packed_all,
        [shape(f32, HD, width), shape(f32, levels, chips * width)],
        scratch,
        flops=2 * n_t * rows * width * HD,
    )
    weight_grad, gate_grad = call(
        functools.partial(final_kernel, n_t, chips, frames),
        [hot, over_cores(collected), *own_halves] + packed_all,
        [shape(f32, HD, 2 * width), shape(f32, levels, n_s * width)],
        scratch,
        flops=2 * n_t * rows * width * HD,
    )
    parts[0], _ = lax.optimization_barrier((parts[0], gate_grad))
    query_grad = call(functools.partial(query_kernel, n_t), parts, shape(bf16, rows, HD))
    if width != shard:
        weight_grad = without_padding(weight_grad, 2, shard)
        gate_grad = without_padding(gate_grad, n_s, shard)
    return (query_grad, key_grad, value_grad, weight_grad, gate_grad)


def solution(mesh):
    return jax.shard_map(
        body,
        mesh=mesh,
        in_specs=(
            P("tm", "space"),
            P("tm", "space"),
            P("tm", "space"),
            P("tm", "space"),
            P("tm", "space"),
            P("space", None),
            P(),
            P(),
            P(),
        ),
        out_specs=(P("tm", "space"), P("tm", "space"), P("tm", "space"), P("space", "tm"), P()),
        check_vma=False,
    )
```

```python
import functools
import math

import jax
import jax.numpy as jnp
from jax import lax
from jax.experimental import pallas as pl
from jax.experimental.pallas import tpu as pltpu
from jax.sharding import PartitionSpec as P

HD = 128
SPF = 512
QF = 64
LANES = 128
NEG_BIG = -1e30
SCALE = 1.0 / math.sqrt(HD)
VMEM_LIMIT = 32 * 1024 * 1024
PREP_VMEM = 52 * 1024 * 1024
SPLIT = 3


def dot(a, b, on_a, on_b):
    return lax.dot_general(
        a, b, (((on_a,), (on_b,)), ((), ())), preferred_element_type=jnp.float32
    )


def far_first(blocks):
    blocks = list(blocks)
    return blocks[:1] + blocks[:0:-1]


def last_swapped(blocks):
    blocks = list(blocks)
    return blocks[:-2] + blocks[:-3:-1]


def place():
    s = lax.axis_index("space")
    return lax.axis_index("tm"), s // 2, s % 2


def clip_numbers(clips_ref):
    bounds = []
    so_far = 0
    for c in range(clips_ref.shape[0]):
        so_far = so_far + clips_ref[c]
        bounds.append(so_far)
    return lambda frame: sum((frame >= bound).astype(jnp.int32) for bound in bounds)


def fetch_kernel(chips, weight_in, grad_in, kept, grad, sems):
    _, chip, core = place()
    width = kept.shape[2]
    copies = [pltpu.make_async_copy(grad_in, grad, sems.at[chips])]
    for k in range(chips):
        columns = pl.ds(pl.multiple_of((2 * (chip ^ k) + core) * width, LANES), width)
        copies.append(pltpu.make_async_copy(weight_in.at[:, columns], kept.at[k], sems.at[k]))
    for copy in copies:
        copy.start()
    for copy in copies:
        copy.wait()


def masks_kernel(n_t, chips, frames, rows, levels, clips, gate, bias, gate_a, gate_b, hot):
    t, chip, core = place()
    width = gate_a.shape[2]
    clip_of = clip_numbers(clips)
    lane = lax.broadcasted_iota(jnp.int32, (1, rows), 1)
    for kf in range(frames):
        key_frame = t * frames + kf
        key_clip = clip_of(key_frame)
        for k in range(n_t):
            row = jnp.full((1, rows), NEG_BIG, jnp.float32)
            for r in range(frames):
                frame = (t ^ k) * frames + r
                visible = (key_frame >= frame) & (clip_of(frame) == key_clip)
                value = jnp.where(visible, 0.0, NEG_BIG).astype(jnp.float32)
                row = jnp.where((lane >= r * QF) & (lane < (r + 1) * QF), value, row)
            bias[kf : kf + 1, k * rows : (k + 1) * rows] = row
    spot = lax.broadcasted_iota(jnp.int32, hot.shape[1:], 0)
    for f in range(n_t * frames):
        hot[f] = (spot == levels[f]).astype(jnp.float32)
    for r in range(frames):
        level = levels[t * frames + r]
        for k in range(chips):
            columns = pl.ds(pl.multiple_of((2 * (chip ^ k) + core) * width, LANES), width)
            gate_a[k, r : r + 1, :] = gate[pl.ds(level, 1), columns]
    mine = pl.ds(pl.multiple_of((2 * t + core) * width, LANES), width)
    for k in range(n_t):
        level = levels[(t ^ k) * frames + chip * (rows // chips) // QF]
        gate_b[k] = gate[pl.ds(level, 1), mine]


def stats_kernel(first, last, bias, keys, *refs):
    packed, out = refs[:-1], refs[-1]
    rows = packed[0].shape[1]
    count = last - first
    for p in range(0, count, 2):
        q = jnp.concatenate([packed[p][0], packed[p + 1][0]], axis=0)
        scores = []
        for kf in range(bias.shape[0]):
            mask = bias[kf : kf + 1, (first + p) * rows : (first + p + 2) * rows]
            scores.append(dot(keys[kf * SPF : (kf + 1) * SPF, :], q, 1, 1) * SCALE + mask)
        top = functools.reduce(jnp.maximum, [jnp.max(x, axis=0, keepdims=True) for x in scores])
        total = sum(jnp.sum(jnp.exp(x - top), axis=0, keepdims=True) for x in scores)
        for i in range(2):
            out[p + i : p + i + 1, :] = top[:, i * rows : (i + 1) * rows]
            out[count + p + i : count + p + i + 1, :] = total[:, i * rows : (i + 1) * rows]


def head_kernel(chips, frames, packed, other_saved, kept, received, gate_a, *refs):
    pieces, (mine, other, terms) = refs[:chips], refs[chips:]
    _, chip, core = place()
    width = pieces[0].shape[1]
    tiles = width // LANES
    saved = jnp.concatenate([packed[1], other_saved[...]], axis=1)
    head = None
    for k in range(chips):
        columns = pl.ds(pl.multiple_of((2 * (chip ^ k) + core) * width, LANES), width)
        weight = jnp.concatenate([kept[k], received[:, columns]], axis=0)
        wide = pieces[k][...].astype(jnp.float32)
        gated = jnp.concatenate(
            [
                (wide[r * QF : (r + 1) * QF] * gate_a[k, r : r + 1, :]).astype(jnp.bfloat16)
                for r in range(frames)
            ],
            axis=0,
        )
        part = dot(gated, weight, 1, 1)
        head = part if head is None else head + part
        product = wide * dot(saved, weight, 1, 0)
        for r in range(frames):
            term = jnp.sum(product[r * QF : (r + 1) * QF], axis=0, keepdims=True)
            for j in range(tiles):
                row = ((chip ^ k) * frames + r) * tiles + j
                terms[pl.ds(row, 1), :] = term[:, j * LANES : (j + 1) * LANES]
    mine[...] = head[:, :HD]
    other[...] = head[:, HD:]


def sections(rows, chips, tiles, n_t, count):
    starts = [0, rows]
    starts.append(starts[-1] + tiles * (rows // chips))
    starts.append(starts[-1] + -(-(SPLIT * 2 * n_t + count) // 16) * 16)
    return starts


def padded(x, rows):
    if x.shape[0] == rows:
        return x
    return jnp.concatenate([x, jnp.zeros((rows - x.shape[0], x.shape[1]), x.dtype)], axis=0)


def join_kernel(n_t, chips, starts, mine, received, near_stats, far_stats, terms, *refs):
    pieces, outs, (wide, held) = refs[:chips], refs[chips : chips + n_t][::-1], refs[chips + n_t :]
    t, chip, _ = place()
    part, tiles = held.shape[1], held.shape[2] // LANES
    for k in range(chips):
        wide[...] = pieces[k][...].astype(jnp.float32)
        held[k] = wide[pl.ds(pl.multiple_of(chip * part, part), part), :]
    head = (mine[...] + received[...]).astype(jnp.bfloat16)
    near, far = near_stats[...], far_stats[...]
    each = far.shape[0] // 2
    rest = jnp.concatenate([near[:2], far[:each], near[2:], far[each:]], axis=0)
    split = []
    for _ in range(SPLIT):
        piece = rest.astype(jnp.bfloat16).astype(jnp.float32)
        split.append(piece)
        rest = rest - piece
    last = padded(jnp.concatenate(split + [terms[...]], axis=0), starts[3] - starts[2])
    last = last.astype(jnp.bfloat16)
    for k in range(n_t):
        rows = held[chip ^ t ^ k]
        rows = jnp.concatenate([rows[:, j * LANES : (j + 1) * LANES] for j in range(tiles)], axis=0)
        outs[k][: starts[1], :] = head
        outs[k][starts[1] : starts[2], :] = rows.astype(jnp.bfloat16)
        outs[k][starts[2] :, :] = last


def bundle_kernel(n_t, starts, count, gate_b, *refs):
    heads, out = last_swapped(refs[:n_t]), refs[n_t]
    tiles = gate_b.shape[2] // LANES
    part = (starts[2] - starts[1]) // tiles
    wide = [heads[k][starts[1] : starts[2], :].astype(jnp.float32) for k in range(n_t)]
    for j in range(tiles):
        gated = jnp.concatenate(
            [
                wide[k][j * part : (j + 1) * part] * gate_b[k, :, j * LANES : (j + 1) * LANES]
                for k in range(n_t)
            ],
            axis=0,
        )
        out[j * n_t * part : (j + 1) * n_t * part, :] = gated.astype(jnp.bfloat16)
    first = SPLIT * 2 * n_t
    terms = [heads[k][starts[2] :, :].astype(jnp.float32)[first : first + count] for k in range(n_t)]
    out[tiles * n_t * part :, :] = jnp.concatenate(terms, axis=0).astype(jnp.bfloat16)


def collect_kernel(chips, base, *refs):
    pieces, out, held = far_first(refs[:chips]), refs[chips], refs[chips + 1]
    chip = place()[1]
    for k in range(chips):
        out[k * base : (k + 1) * base, :] = pieces[k][:base, :]
        held[chip ^ k] = pieces[k][base:, :].astype(jnp.float32)
    total = held[0]
    for k in range(1, chips):
        total = total + held[k]
    high = total.astype(jnp.bfloat16)
    count = total.shape[0]
    out[chips * base : chips * base + count, :] = high
    out[chips * base + count :, :] = (total - high.astype(jnp.float32)).astype(jnp.bfloat16)


def grads_kernel(n_t, starts, first, last, bias, keys, values, *refs):
    packed, heads = far_first(refs[:n_t]), last_swapped(refs[n_t : 2 * n_t])
    refs = refs[2 * n_t :]
    if first == 0:
        sums, refs = refs[:2], refs[2:]
    key_out, value_out = refs[:2]
    outs = refs[2 : 2 + last - first]
    accs = refs[2 + last - first :]
    rows = packed[0].shape[1]
    ones = jnp.ones((8, HD), jnp.float32)
    keys_t = jnp.transpose(keys[...])
    stats = []
    for k in range(n_t):
        parts = heads[k][starts[2] :, :].astype(jnp.float32)
        stats.append(sum(parts[i * 2 * n_t : (i + 1) * 2 * n_t] for i in range(SPLIT)))
    for p in range(first, last, 2):
        q = jnp.concatenate([packed[p][0], packed[p + 1][0]], axis=0)
        o = jnp.concatenate([packed[p][1], packed[p + 1][1]], axis=0)
        g = jnp.concatenate([heads[p][:rows, :], heads[p + 1][:rows, :]], axis=0)
        delta = lax.dot_general(
            ones,
            g.astype(jnp.float32) * o.astype(jnp.float32),
            (((1,), (1,)), ((), ())),
            precision=lax.Precision.HIGHEST,
            preferred_element_type=jnp.float32,
        )[0:1]
        lse = []
        for i in (p, p + 1):
            tops = [stats[k][i ^ k : (i ^ k) + 1] for k in range(n_t)]
            sums_of = [stats[k][n_t + (i ^ k) : n_t + (i ^ k) + 1] for k in range(n_t)]
            top = functools.reduce(jnp.maximum, tops)
            lse.append(top + jnp.log(sum(b * jnp.exp(a - top) for a, b in zip(tops, sums_of))))
        lse = jnp.concatenate(lse, axis=1)
        query_part = None
        for kf in range(bias.shape[0]):
            span = slice(kf * SPF, (kf + 1) * SPF)
            shift = bias[kf : kf + 1, p * rows : (p + 2) * rows] - lse
            probs = jnp.exp(dot(keys[span, :], q, 1, 1) * SCALE + shift)
            score_grad = (probs * (dot(values[span, :], g, 1, 1) - delta)).astype(jnp.bfloat16)
            value_add = dot(probs.astype(jnp.bfloat16), g, 1, 0)
            key_add = dot(score_grad, q, 1, 0)
            if p > first:
                value_add = value_add + accs[1][span, :]
                key_add = key_add + accs[0][span, :]
            if p + 2 < last:
                accs[1][span, :] = value_add
                accs[0][span, :] = key_add
            elif first:
                value_out[span, :] = value_add
                key_out[span, :] = key_add
            else:
                value_out[span, :] = (value_add + sums[1][span, :]).astype(jnp.bfloat16)
                key_out[span, :] = ((key_add + sums[0][span, :]) * SCALE).astype(jnp.bfloat16)
            part = dot(keys_t[:, span], score_grad, 1, 0)
            query_part = part if query_part is None else query_part + part
        outs[p - first][...] = query_part[:, :rows].astype(jnp.bfloat16)
        outs[p + 1 - first][...] = query_part[:, rows:].astype(jnp.bfloat16)


def query_kernel(n_t, *refs):
    total = refs[0][...].astype(jnp.float32)
    for k in range(1, n_t):
        total = total + refs[k][...].astype(jnp.float32)
    refs[n_t][...] = jnp.transpose(total * SCALE).astype(jnp.bfloat16)


def half_results(n_t, chips, frames, hot, ref, packed, saved, held, tiles):
    t, chip, _ = place()
    rows = saved.shape[1]
    part = rows // chips
    base = tiles * n_t * part
    for k in range(n_t):
        saved[k] = packed[k][1].astype(jnp.float32)
    ordered = []
    for c in range(chips):
        mine = pl.ds(pl.multiple_of((chip ^ c) * part, part), part)
        ordered += [saved[k, mine, :] for k in range(n_t)]
    ordered = jnp.transpose(jnp.concatenate(ordered, axis=0)).astype(jnp.bfloat16)
    gated = jnp.concatenate(
        [
            jnp.concatenate(
                [
                    ref[c * base + j * n_t * part : c * base + (j + 1) * n_t * part, :]
                    for c in range(chips)
                ],
                axis=0,
            )
            for j in range(tiles)
        ],
        axis=1,
    )
    count = (ref.shape[0] - chips * base) // 2
    each = count // n_t
    terms = ref[chips * base : chips * base + count, :].astype(jnp.float32)
    terms = terms + ref[chips * base + count :, :].astype(jnp.float32)
    for k in range(n_t):
        held[t ^ k] = terms[k * each : (k + 1) * each]

    def gate_tile(a, j):
        total = jnp.zeros(hot.shape[1:], jnp.float32)
        for f in range(n_t * frames):
            row = (a * frames + f % frames) * tiles + j
            total = total + hot[f] * held[f // frames, row : row + 1, :]
        return total

    return dot(ordered, gated, 1, 0), gate_tile


def own_kernel(n_t, chips, frames, hot, own, *refs):
    packed, (weight_out, gate_out, saved, held) = refs[:n_t], refs[n_t:]
    tiles = weight_out.shape[1] // LANES
    result, gate_tile = half_results(n_t, chips, frames, hot, own, packed, saved, held, tiles)
    weight_out[...] = result
    for a in range(chips):
        for j in range(tiles):
            gate_out[:, (a * tiles + j) * LANES : (a * tiles + j + 1) * LANES] = gate_tile(a, j)


def final_kernel(n_t, chips, frames, hot, other, own_weight, own_gate, *refs):
    packed, (weight_out, gate_out, saved, held) = refs[:n_t], refs[n_t:]
    core = place()[2]
    width = own_weight.shape[1]
    tiles = width // LANES
    result, gate_tile = half_results(n_t, chips, frames, hot, other, packed, saved, held, tiles)
    mine = own_weight[...]
    weight_out[:, :width] = jnp.where(core == 0, mine, result)
    weight_out[:, width:] = jnp.where(core == 0, result, mine)
    for a in range(chips):
        for j in range(tiles):
            first = gate_tile(a, j)
            second = own_gate[:, (a * tiles + j) * LANES : (a * tiles + j + 1) * LANES]
            column = 2 * a * width + j * LANES
            gate_out[:, column : column + LANES] = jnp.where(core == 0, second, first)
            column += width
            gate_out[:, column : column + LANES] = jnp.where(core == 0, first, second)


def call(kernel, args, out_shape, scratch=(), flops=0, in_place=False, in_smem=0):
    vmem = pl.BlockSpec(memory_space=pltpu.VMEM)
    single = not isinstance(out_shape, (list, tuple))
    nbytes = sum(a.size * a.dtype.itemsize for a in args)
    return pl.pallas_call(
        kernel,
        out_shape=out_shape,
        in_specs=[pl.BlockSpec(memory_space=pltpu.SMEM)] * in_smem
        + [pl.BlockSpec(memory_space=pltpu.HBM) if in_place else vmem] * (len(args) - in_smem),
        out_specs=vmem if single else [vmem] * len(out_shape),
        scratch_shapes=list(scratch),
        compiler_params=pltpu.CompilerParams(vmem_limit_bytes=PREP_VMEM if in_place else VMEM_LIMIT),
        cost_estimate=pl.CostEstimate(flops=flops, bytes_accessed=nbytes, transcendentals=0),
    )(*args)


def padded_shards(table, n_s, width):
    rows, columns = table.shape
    cut = table.reshape(rows, n_s, columns // n_s)
    cut = jnp.pad(cut, ((0, 0), (0, 0), (0, width - columns // n_s)))
    return cut.reshape(rows, n_s * width)


def without_padding(table, shards, shard):
    rows, columns = table.shape
    return table.reshape(rows, shards, columns // shards)[:, :, :shard].reshape(rows, shards * shard)


def body(
    queries, keys, values, saved_out, out_grad, proj_weight, gate_table, noise_levels, clip_lengths
):
    n_t, n_s = lax.axis_size("tm"), lax.axis_size("space")
    chips = n_s // 2
    rows, shard = out_grad.shape
    k_rows = keys.shape[0]
    frames = rows // QF
    levels = gate_table.shape[0]
    bf16, f32 = jnp.bfloat16, jnp.float32
    width = -(-shard // LANES) * LANES
    if width != shard:
        out_grad = jnp.pad(out_grad, ((0, 0), (0, width - shard)))
        proj_weight = padded_shards(proj_weight, n_s, width)
        gate_table = padded_shards(gate_table, n_s, width)

    def shape(dtype, *dims):
        return jax.ShapeDtypeStruct(dims, dtype)

    def over_chips(x):
        return [x] + [
            lax.ppermute(x, "space", [(s, s ^ (2 * k)) for s in range(n_s)]) for k in range(1, chips)
        ]

    def over_cores(x):
        return lax.ppermute(x, "space", [(s, s ^ 1) for s in range(n_s)])

    def over_time(x, k):
        return lax.ppermute(x, "tm", [(t, t ^ k) for t in range(n_t)])

    tiles = width // LANES
    part = rows // chips
    count = chips * frames * tiles
    starts = sections(rows, chips, tiles, n_t, count)

    def time_swaps(messages):
        got = {k: over_time(messages[k], k) for k in range(n_t - 1, 0, -1)}
        return [messages[0]] + [got[k] for k in range(1, n_t)]

    pieces = over_chips(out_grad)
    received, other_saved = over_cores(proj_weight), over_cores(saved_out)
    packed, _ = lax.optimization_barrier(
        (jnp.stack([queries, saved_out]), (received, other_saved))
    )
    packed_all = time_swaps([packed] * n_t)
    (to_fetch, own_grad), _ = lax.optimization_barrier(((proj_weight, out_grad), received))
    kept, pieces[0] = call(
        functools.partial(fetch_kernel, chips),
        [to_fetch, own_grad],
        [shape(bf16, chips, HD, width), shape(bf16, rows, width)],
        [pltpu.SemaphoreType.DMA((chips + 1,))],
        in_place=True,
    )
    gate_table, _ = lax.optimization_barrier((gate_table, received))
    bias, gate_a, gate_b, hot = call(
        functools.partial(masks_kernel, n_t, chips, frames, rows),
        [noise_levels, clip_lengths, gate_table],
        [
            shape(f32, frames, n_t * rows),
            shape(f32, chips, frames, width),
            shape(f32, n_t, 1, width),
            shape(f32, n_t * frames, levels, LANES),
        ],
        in_smem=2,
    )
    mine, other, terms = call(
        functools.partial(head_kernel, chips, frames),
        [packed, other_saved, kept, received, gate_a] + pieces,
        [shape(f32, rows, HD), shape(f32, rows, HD), shape(f32, count, LANES)],
        flops=4 * rows * chips * width * 2 * HD,
    )
    later_bias, _ = lax.optimization_barrier((bias, mine))
    far_stats = call(
        functools.partial(stats_kernel, 2, n_t),
        [later_bias, keys] + packed_all[2:],
        shape(f32, 2 * (n_t - 2), LANES),
        flops=2 * (n_t - 2) * rows * k_rows * HD,
    )
    last_bias, _ = lax.optimization_barrier((bias, far_stats))
    near_stats = call(
        functools.partial(stats_kernel, 0, 2),
        [last_bias, keys] + packed_all[:2],
        shape(f32, 4, LANES),
        flops=4 * rows * k_rows * HD,
    )
    heads = call(
        functools.partial(join_kernel, n_t, chips, starts),
        [mine, over_cores(other), near_stats, far_stats, terms] + pieces,
        [shape(bf16, starts[-1], LANES)] * n_t,
        [pltpu.VMEM((rows, width), f32), pltpu.VMEM((chips, part, width), f32)],
    )
    heads_all = time_swaps(heads[::-1])
    base = tiles * n_t * part
    bundle = call(
        functools.partial(bundle_kernel, n_t, starts, count),
        [gate_b] + last_swapped(heads_all),
        shape(bf16, base + n_t * count, LANES),
    )
    bundles = over_chips(bundle)
    bundles = far_first(bundles)
    later_bias, _ = lax.optimization_barrier((bias, bundle))
    accs = [pltpu.VMEM((k_rows, HD), f32)] * 2
    far = call(
        functools.partial(grads_kernel, n_t, starts, 2, n_t),
        [later_bias, keys, values] + far_first(packed_all) + last_swapped(heads_all),
        [shape(f32, k_rows, HD)] * 2 + [shape(bf16, HD, rows)] * (n_t - 2),
        accs,
        flops=10 * (n_t - 2) * rows * k_rows * HD,
    )
    parts = {k: over_time(far[k], k) for k in range(2, n_t)}
    near = call(
        functools.partial(grads_kernel, n_t, starts, 0, 2),
        [bias, keys, values] + far_first(packed_all) + last_swapped(heads_all) + list(far[:2]),
        [shape(bf16, k_rows, HD)] * 2 + [shape(bf16, HD, rows)] * 2,
        flops=20 * rows * k_rows * HD,
    )
    key_grad, value_grad = near[:2]
    parts[0], parts[1] = near[2], over_time(near[3], 1)
    parts = [parts[k] for k in range(n_t)]
    bundles, _ = lax.optimization_barrier((bundles, (key_grad, parts[n_t // 2 :])))
    collected = call(
        functools.partial(collect_kernel, chips, base),
        bundles,
        shape(bf16, chips * base + 2 * n_t * count, LANES),
        [pltpu.VMEM((chips, n_t * count, LANES), f32)],
    )
    scratch = [pltpu.VMEM((n_t, rows, HD), f32), pltpu.VMEM((n_t, count, LANES), f32)]
    own_halves = call(
        functools.partial(own_kernel, n_t, chips, frames),
        [hot, collected] + packed_all,
        [shape(f32, HD, width), shape(f32, levels, chips * width)],
        scratch,
        flops=2 * n_t * rows * width * HD,
    )
    weight_grad, gate_grad = call(
        functools.partial(final_kernel, n_t, chips, frames),
        [hot, over_cores(collected), *own_halves] + packed_all,
        [shape(f32, HD, 2 * width), shape(f32, levels, n_s * width)],
        scratch,
        flops=2 * n_t * rows * width * HD,
    )
    parts[0], _ = lax.optimization_barrier((parts[0], gate_grad))
    query_grad = call(functools.partial(query_kernel, n_t), parts, shape(bf16, rows, HD))
    if width != shard:
        weight_grad = without_padding(weight_grad, 2, shard)
        gate_grad = without_padding(gate_grad, n_s, shard)
    return (query_grad, key_grad, value_grad, weight_grad, gate_grad)


def solution(mesh):
    return jax.shard_map(
        body,
        mesh=mesh,
        in_specs=(
            P("tm", "space"),
            P("tm", "space"),
            P("tm", "space"),
            P("tm", "space"),
            P("tm", "space"),
            P("space", None),
            P(),
            P(),
            P(),
        ),
        out_specs=(P("tm", "space"), P("tm", "space"), P("tm", "space"), P("space", "tm"), P()),
        check_vma=False,
    )
```

```python
import functools
import math

import jax
import jax.numpy as jnp
from jax import lax
from jax.experimental import pallas as pl
from jax.experimental.pallas import tpu as pltpu
from jax.sharding import PartitionSpec as P

HD = 128
SPF = 512
QF = 64
LANES = 128
NEG_BIG = -1e30
SCALE = 1.0 / math.sqrt(HD)
VMEM_LIMIT = 32 * 1024 * 1024
PREP_VMEM = 52 * 1024 * 1024
SPLIT = 3


def dot(a, b, on_a, on_b):
    return lax.dot_general(
        a, b, (((on_a,), (on_b,)), ((), ())), preferred_element_type=jnp.float32
    )


def far_first(blocks):
    blocks = list(blocks)
    return blocks[:1] + blocks[:0:-1]


def last_swapped(blocks):
    blocks = list(blocks)
    return blocks[:-2] + blocks[:-3:-1]


def place():
    s = lax.axis_index("space")
    return lax.axis_index("tm"), s // 2, s % 2


def clip_numbers(clips_ref):
    bounds = []
    so_far = 0
    for c in range(clips_ref.shape[0]):
        so_far = so_far + clips_ref[c]
        bounds.append(so_far)
    return lambda frame: sum((frame >= bound).astype(jnp.int32) for bound in bounds)


def fetch_kernel(chips, weight_in, grad_in, kept, grad, sems):
    _, chip, core = place()
    width = kept.shape[2]
    copies = [pltpu.make_async_copy(grad_in, grad, sems.at[chips])]
    for k in range(chips):
        columns = pl.ds(pl.multiple_of((2 * (chip ^ k) + core) * width, LANES), width)
        copies.append(pltpu.make_async_copy(weight_in.at[:, columns], kept.at[k], sems.at[k]))
    for copy in copies:
        copy.start()
    for copy in copies:
        copy.wait()


def masks_kernel(n_t, chips, frames, rows, levels, clips, gate, bias, gate_a, gate_b, hot):
    t, chip, core = place()
    width = gate_a.shape[2]
    clip_of = clip_numbers(clips)
    lane = lax.broadcasted_iota(jnp.int32, (1, rows), 1)
    for kf in range(frames):
        key_frame = t * frames + kf
        key_clip = clip_of(key_frame)
        for k in range(n_t):
            row = jnp.full((1, rows), NEG_BIG, jnp.float32)
            for r in range(frames):
                frame = (t ^ k) * frames + r
                visible = (key_frame >= frame) & (clip_of(frame) == key_clip)
                value = jnp.where(visible, 0.0, NEG_BIG).astype(jnp.float32)
                row = jnp.where((lane >= r * QF) & (lane < (r + 1) * QF), value, row)
            bias[kf : kf + 1, k * rows : (k + 1) * rows] = row
    spot = lax.broadcasted_iota(jnp.int32, hot.shape[1:], 0)
    for f in range(n_t * frames):
        hot[f] = (spot == levels[f]).astype(jnp.float32)
    for r in range(frames):
        level = levels[t * frames + r]
        for k in range(chips):
            columns = pl.ds(pl.multiple_of((2 * (chip ^ k) + core) * width, LANES), width)
            gate_a[k, r : r + 1, :] = gate[pl.ds(level, 1), columns]
    mine = pl.ds(pl.multiple_of((2 * t + core) * width, LANES), width)
    for k in range(n_t):
        level = levels[(t ^ k) * frames + chip * (rows // chips) // QF]
        gate_b[k] = gate[pl.ds(level, 1), mine]


def stats_kernel(first, last, bias, keys, *refs):
    packed, out = refs[:-1], refs[-1]
    rows = packed[0].shape[1]
    count = last - first
    for p in range(0, count, 2):
        q = jnp.concatenate([packed[p][0], packed[p + 1][0]], axis=0)
        scores = []
        for kf in range(bias.shape[0]):
            mask = bias[kf : kf + 1, (first + p) * rows : (first + p + 2) * rows]
            scores.append(dot(keys[kf * SPF : (kf + 1) * SPF, :], q, 1, 1) * SCALE + mask)
        top = functools.reduce(jnp.maximum, [jnp.max(x, axis=0, keepdims=True) for x in scores])
        total = sum(jnp.sum(jnp.exp(x - top), axis=0, keepdims=True) for x in scores)
        for i in range(2):
            out[p + i : p + i + 1, :] = top[:, i * rows : (i + 1) * rows]
            out[count + p + i : count + p + i + 1, :] = total[:, i * rows : (i + 1) * rows]


def head_kernel(chips, frames, packed, other_saved, kept, received, gate_a, *refs):
    pieces, (mine, other, terms) = refs[:chips], refs[chips:]
    _, chip, core = place()
    width = pieces[0].shape[1]
    tiles = width // LANES
    saved = jnp.concatenate([packed[1], other_saved[...]], axis=1)
    head = None
    for k in range(chips):
        columns = pl.ds(pl.multiple_of((2 * (chip ^ k) + core) * width, LANES), width)
        weight = jnp.concatenate([kept[k], received[:, columns]], axis=0)
        wide = pieces[k][...].astype(jnp.float32)
        gated = jnp.concatenate(
            [
                (wide[r * QF : (r + 1) * QF] * gate_a[k, r : r + 1, :]).astype(jnp.bfloat16)
                for r in range(frames)
            ],
            axis=0,
        )
        part = dot(gated, weight, 1, 1)
        head = part if head is None else head + part
        product = wide * dot(saved, weight, 1, 0)
        for r in range(frames):
            term = jnp.sum(product[r * QF : (r + 1) * QF], axis=0, keepdims=True)
            for j in range(tiles):
                row = ((chip ^ k) * frames + r) * tiles + j
                terms[pl.ds(row, 1), :] = term[:, j * LANES : (j + 1) * LANES]
    mine[...] = head[:, :HD]
    other[...] = head[:, HD:]


def sections(rows, chips, tiles, n_t, count):
    starts = [0, rows]
    starts.append(starts[-1] + tiles * (rows // chips))
    starts.append(starts[-1] + -(-(SPLIT * 2 * n_t + count) // 16) * 16)
    return starts


def padded(x, rows):
    if x.shape[0] == rows:
        return x
    return jnp.concatenate([x, jnp.zeros((rows - x.shape[0], x.shape[1]), x.dtype)], axis=0)


def join_kernel(n_t, chips, starts, mine, received, near_stats, far_stats, terms, *refs):
    pieces, outs, (wide, held) = refs[:chips], refs[chips : chips + n_t][::-1], refs[chips + n_t :]
    t, chip, _ = place()
    part, tiles = held.shape[1], held.shape[2] // LANES
    for k in range(chips):
        wide[...] = pieces[k][...].astype(jnp.float32)
        held[k] = wide[pl.ds(pl.multiple_of(chip * part, part), part), :]
    head = (mine[...] + received[...]).astype(jnp.bfloat16)
    near, far = near_stats[...], far_stats[...]
    each = far.shape[0] // 2
    rest = jnp.concatenate([near[:2], far[:each], near[2:], far[each:]], axis=0)
    split = []
    for _ in range(SPLIT):
        piece = rest.astype(jnp.bfloat16).astype(jnp.float32)
        split.append(piece)
        rest = rest - piece
    last = padded(jnp.concatenate(split + [terms[...]], axis=0), starts[3] - starts[2])
    last = last.astype(jnp.bfloat16)
    for k in range(n_t):
        rows = held[chip ^ t ^ k]
        rows = jnp.concatenate([rows[:, j * LANES : (j + 1) * LANES] for j in range(tiles)], axis=0)
        outs[k][: starts[1], :] = head
        outs[k][starts[1] : starts[2], :] = rows.astype(jnp.bfloat16)
        outs[k][starts[2] :, :] = last


def bundle_kernel(n_t, starts, count, gate_b, *refs):
    heads, out = last_swapped(refs[:n_t]), refs[n_t]
    tiles = gate_b.shape[2] // LANES
    part = (starts[2] - starts[1]) // tiles
    wide = [heads[k][starts[1] : starts[2], :].astype(jnp.float32) for k in range(n_t)]
    for j in range(tiles):
        gated = jnp.concatenate(
            [
                wide[k][j * part : (j + 1) * part] * gate_b[k, :, j * LANES : (j + 1) * LANES]
                for k in range(n_t)
            ],
            axis=0,
        )
        out[j * n_t * part : (j + 1) * n_t * part, :] = gated.astype(jnp.bfloat16)
    first = SPLIT * 2 * n_t
    terms = [heads[k][starts[2] :, :].astype(jnp.float32)[first : first + count] for k in range(n_t)]
    out[tiles * n_t * part :, :] = jnp.concatenate(terms, axis=0).astype(jnp.bfloat16)


def collect_kernel(chips, base, *refs):
    pieces, out, held = far_first(refs[:chips]), refs[chips], refs[chips + 1]
    chip = place()[1]
    for k in range(chips):
        out[k * base : (k + 1) * base, :] = pieces[k][:base, :]
        held[chip ^ k] = pieces[k][base:, :].astype(jnp.float32)
    total = held[0]
    for k in range(1, chips):
        total = total + held[k]
    high = total.astype(jnp.bfloat16)
    count = total.shape[0]
    out[chips * base : chips * base + count, :] = high
    out[chips * base + count :, :] = (total - high.astype(jnp.float32)).astype(jnp.bfloat16)


def grads_kernel(n_t, starts, first, last, bias, keys, values, *refs):
    packed, heads = far_first(refs[:n_t]), last_swapped(refs[n_t : 2 * n_t])
    refs = refs[2 * n_t :]
    if first == 0:
        sums, refs = refs[:2], refs[2:]
    key_out, value_out = refs[:2]
    outs = refs[2 : 2 + last - first]
    accs = refs[2 + last - first :]
    rows = packed[0].shape[1]
    ones = jnp.ones((8, HD), jnp.float32)
    keys_t = jnp.transpose(keys[...])
    stats = []
    for k in range(n_t):
        parts = heads[k][starts[2] :, :].astype(jnp.float32)
        stats.append(sum(parts[i * 2 * n_t : (i + 1) * 2 * n_t] for i in range(SPLIT)))
    for p in range(first, last, 2):
        q = jnp.concatenate([packed[p][0], packed[p + 1][0]], axis=0)
        o = jnp.concatenate([packed[p][1], packed[p + 1][1]], axis=0)
        g = jnp.concatenate([heads[p][:rows, :], heads[p + 1][:rows, :]], axis=0)
        delta = lax.dot_general(
            ones,
            g.astype(jnp.float32) * o.astype(jnp.float32),
            (((1,), (1,)), ((), ())),
            precision=lax.Precision.HIGHEST,
            preferred_element_type=jnp.float32,
        )[0:1]
        lse = []
        for i in (p, p + 1):
            tops = [stats[k][i ^ k : (i ^ k) + 1] for k in range(n_t)]
            sums_of = [stats[k][n_t + (i ^ k) : n_t + (i ^ k) + 1] for k in range(n_t)]
            top = functools.reduce(jnp.maximum, tops)
            lse.append(top + jnp.log(sum(b * jnp.exp(a - top) for a, b in zip(tops, sums_of))))
        lse = jnp.concatenate(lse, axis=1)
        query_part = None
        for kf in range(bias.shape[0]):
            span = slice(kf * SPF, (kf + 1) * SPF)
            shift = bias[kf : kf + 1, p * rows : (p + 2) * rows] - lse
            probs = jnp.exp(dot(keys[span, :], q, 1, 1) * SCALE + shift)
            score_grad = (probs * (dot(values[span, :], g, 1, 1) - delta)).astype(jnp.bfloat16)
            value_add = dot(probs.astype(jnp.bfloat16), g, 1, 0)
            key_add = dot(score_grad, q, 1, 0)
            if p > first:
                value_add = value_add + accs[1][span, :]
                key_add = key_add + accs[0][span, :]
            if p + 2 < last:
                accs[1][span, :] = value_add
                accs[0][span, :] = key_add
            elif first:
                value_out[span, :] = value_add
                key_out[span, :] = key_add
            else:
                value_out[span, :] = (value_add + sums[1][span, :]).astype(jnp.bfloat16)
                key_out[span, :] = ((key_add + sums[0][span, :]) * SCALE).astype(jnp.bfloat16)
            part = dot(keys_t[:, span], score_grad, 1, 0)
            query_part = part if query_part is None else query_part + part
        outs[p - first][...] = query_part[:, :rows].astype(jnp.bfloat16)
        outs[p + 1 - first][...] = query_part[:, rows:].astype(jnp.bfloat16)


def query_kernel(n_t, *refs):
    total = refs[0][...].astype(jnp.float32)
    for k in range(1, n_t):
        total = total + refs[k][...].astype(jnp.float32)
    refs[n_t][...] = jnp.transpose(total * SCALE).astype(jnp.bfloat16)


def order_kernel(n_t, chips, *refs):
    packed, (out, saved) = refs[:n_t], refs[n_t:]
    chip = place()[1]
    part = saved.shape[1] // chips
    for k in range(n_t):
        saved[k] = packed[k][1].astype(jnp.float32)
    ordered = []
    for c in range(chips):
        mine = pl.ds(pl.multiple_of((chip ^ c) * part, part), part)
        ordered += [saved[k, mine, :] for k in range(n_t)]
    out[...] = jnp.transpose(jnp.concatenate(ordered, axis=0)).astype(jnp.bfloat16)


def half_results(n_t, chips, frames, hot, ref, ordered, held, tiles):
    t = lax.axis_index("tm")
    part = ordered.shape[1] // (n_t * chips)
    base = tiles * n_t * part
    gated = jnp.concatenate(
        [
            jnp.concatenate(
                [
                    ref[c * base + j * n_t * part : c * base + (j + 1) * n_t * part, :]
                    for c in range(chips)
                ],
                axis=0,
            )
            for j in range(tiles)
        ],
        axis=1,
    )
    count = (ref.shape[0] - chips * base) // 2
    each = count // n_t
    terms = ref[chips * base : chips * base + count, :].astype(jnp.float32)
    terms = terms + ref[chips * base + count :, :].astype(jnp.float32)
    for k in range(n_t):
        held[t ^ k] = terms[k * each : (k + 1) * each]

    def gate_tile(a, j):
        total = jnp.zeros(hot.shape[1:], jnp.float32)
        for f in range(n_t * frames):
            row = (a * frames + f % frames) * tiles + j
            total = total + hot[f] * held[f // frames, row : row + 1, :]
        return total

    return dot(ordered[...], gated, 1, 0), gate_tile


def own_kernel(n_t, chips, frames, hot, own, ordered, weight_out, gate_out, held):
    tiles = weight_out.shape[1] // LANES
    result, gate_tile = half_results(n_t, chips, frames, hot, own, ordered, held, tiles)
    weight_out[...] = result
    for a in range(chips):
        for j in range(tiles):
            gate_out[:, (a * tiles + j) * LANES : (a * tiles + j + 1) * LANES] = gate_tile(a, j)


def final_kernel(
    n_t, chips, frames, hot, other, own_weight, own_gate, ordered, weight_out, gate_out, held
):
    core = place()[2]
    width = own_weight.shape[1]
    tiles = width // LANES
    result, gate_tile = half_results(n_t, chips, frames, hot, other, ordered, held, tiles)
    mine = own_weight[...]
    weight_out[:, :width] = jnp.where(core == 0, mine, result)
    weight_out[:, width:] = jnp.where(core == 0, result, mine)
    for a in range(chips):
        for j in range(tiles):
            first = gate_tile(a, j)
            second = own_gate[:, (a * tiles + j) * LANES : (a * tiles + j + 1) * LANES]
            column = 2 * a * width + j * LANES
            gate_out[:, column : column + LANES] = jnp.where(core == 0, second, first)
            column += width
            gate_out[:, column : column + LANES] = jnp.where(core == 0, first, second)


def call(kernel, args, out_shape, scratch=(), flops=0, in_place=False, in_smem=0):
    vmem = pl.BlockSpec(memory_space=pltpu.VMEM)
    single = not isinstance(out_shape, (list, tuple))
    nbytes = sum(a.size * a.dtype.itemsize for a in args)
    return pl.pallas_call(
        kernel,
        out_shape=out_shape,
        in_specs=[pl.BlockSpec(memory_space=pltpu.SMEM)] * in_smem
        + [pl.BlockSpec(memory_space=pltpu.HBM) if in_place else vmem] * (len(args) - in_smem),
        out_specs=vmem if single else [vmem] * len(out_shape),
        scratch_shapes=list(scratch),
        compiler_params=pltpu.CompilerParams(vmem_limit_bytes=PREP_VMEM if in_place else VMEM_LIMIT),
        cost_estimate=pl.CostEstimate(flops=flops, bytes_accessed=nbytes, transcendentals=0),
    )(*args)


def padded_shards(table, n_s, width):
    rows, columns = table.shape
    cut = table.reshape(rows, n_s, columns // n_s)
    cut = jnp.pad(cut, ((0, 0), (0, 0), (0, width - columns // n_s)))
    return cut.reshape(rows, n_s * width)


def without_padding(table, shards, shard):
    rows, columns = table.shape
    return table.reshape(rows, shards, columns // shards)[:, :, :shard].reshape(rows, shards * shard)


def body(
    queries, keys, values, saved_out, out_grad, proj_weight, gate_table, noise_levels, clip_lengths
):
    n_t, n_s = lax.axis_size("tm"), lax.axis_size("space")
    chips = n_s // 2
    rows, shard = out_grad.shape
    k_rows = keys.shape[0]
    frames = rows // QF
    levels = gate_table.shape[0]
    bf16, f32 = jnp.bfloat16, jnp.float32
    width = -(-shard // LANES) * LANES
    if width != shard:
        out_grad = jnp.pad(out_grad, ((0, 0), (0, width - shard)))
        proj_weight = padded_shards(proj_weight, n_s, width)
        gate_table = padded_shards(gate_table, n_s, width)

    def shape(dtype, *dims):
        return jax.ShapeDtypeStruct(dims, dtype)

    def over_chips(x):
        return [x] + [
            lax.ppermute(x, "space", [(s, s ^ (2 * k)) for s in range(n_s)]) for k in range(1, chips)
        ]

    def over_cores(x):
        return lax.ppermute(x, "space", [(s, s ^ 1) for s in range(n_s)])

    def over_time(x, k):
        return lax.ppermute(x, "tm", [(t, t ^ k) for t in range(n_t)])

    tiles = width // LANES
    part = rows // chips
    count = chips * frames * tiles
    starts = sections(rows, chips, tiles, n_t, count)

    def time_swaps(messages):
        got = {k: over_time(messages[k], k) for k in range(n_t - 1, 0, -1)}
        return [messages[0]] + [got[k] for k in range(1, n_t)]

    pieces = over_chips(out_grad)
    received, other_saved = over_cores(proj_weight), over_cores(saved_out)
    packed, _ = lax.optimization_barrier(
        (jnp.stack([queries, saved_out]), (received, other_saved))
    )
    packed_all = time_swaps([packed] * n_t)
    (to_fetch, own_grad), _ = lax.optimization_barrier(((proj_weight, out_grad), received))
    kept, pieces[0] = call(
        functools.partial(fetch_kernel, chips),
        [to_fetch, own_grad],
        [shape(bf16, chips, HD, width), shape(bf16, rows, width)],
        [pltpu.SemaphoreType.DMA((chips + 1,))],
        in_place=True,
    )
    gate_table, _ = lax.optimization_barrier((gate_table, received))
    bias, gate_a, gate_b, hot = call(
        functools.partial(masks_kernel, n_t, chips, frames, rows),
        [noise_levels, clip_lengths, gate_table],
        [
            shape(f32, frames, n_t * rows),
            shape(f32, chips, frames, width),
            shape(f32, n_t, 1, width),
            shape(f32, n_t * frames, levels, LANES),
        ],
        in_smem=2,
    )
    mine, other, terms = call(
        functools.partial(head_kernel, chips, frames),
        [packed, other_saved, kept, received, gate_a] + pieces,
        [shape(f32, rows, HD), shape(f32, rows, HD), shape(f32, count, LANES)],
        flops=4 * rows * chips * width * 2 * HD,
    )
    later_bias, _ = lax.optimization_barrier((bias, mine))
    far_stats = call(
        functools.partial(stats_kernel, 2, n_t),
        [later_bias, keys] + packed_all[2:],
        shape(f32, 2 * (n_t - 2), LANES),
        flops=2 * (n_t - 2) * rows * k_rows * HD,
    )
    last_bias, _ = lax.optimization_barrier((bias, far_stats))
    near_stats = call(
        functools.partial(stats_kernel, 0, 2),
        [last_bias, keys] + packed_all[:2],
        shape(f32, 4, LANES),
        flops=4 * rows * k_rows * HD,
    )
    heads = call(
        functools.partial(join_kernel, n_t, chips, starts),
        [mine, over_cores(other), near_stats, far_stats, terms] + pieces,
        [shape(bf16, starts[-1], LANES)] * n_t,
        [pltpu.VMEM((rows, width), f32), pltpu.VMEM((chips, part, width), f32)],
    )
    heads_all = time_swaps(heads[::-1])
    base = tiles * n_t * part
    bundle = call(
        functools.partial(bundle_kernel, n_t, starts, count),
        [gate_b] + last_swapped(heads_all),
        shape(bf16, base + n_t * count, LANES),
    )
    bundles = over_chips(bundle)
    bundles = far_first(bundles)
    later_bias, _ = lax.optimization_barrier((bias, bundle))
    accs = [pltpu.VMEM((k_rows, HD), f32)] * 2
    far = call(
        functools.partial(grads_kernel, n_t, starts, 2, n_t),
        [later_bias, keys, values] + far_first(packed_all) + last_swapped(heads_all),
        [shape(f32, k_rows, HD)] * 2 + [shape(bf16, HD, rows)] * (n_t - 2),
        accs,
        flops=10 * (n_t - 2) * rows * k_rows * HD,
    )
    parts = {k: over_time(far[k], k) for k in range(2, n_t)}
    near = call(
        functools.partial(grads_kernel, n_t, starts, 0, 2),
        [bias, keys, values] + far_first(packed_all) + last_swapped(heads_all) + list(far[:2]),
        [shape(bf16, k_rows, HD)] * 2 + [shape(bf16, HD, rows)] * 2,
        flops=20 * rows * k_rows * HD,
    )
    key_grad, value_grad = near[:2]
    parts[0], parts[1] = near[2], over_time(near[3], 1)
    parts = [parts[k] for k in range(n_t)]
    to_order, _ = lax.optimization_barrier((packed_all, key_grad))
    ordered = call(
        functools.partial(order_kernel, n_t, chips),
        to_order,
        shape(bf16, HD, n_t * rows),
        [pltpu.VMEM((n_t, rows, HD), f32)],
    )
    bundles, _ = lax.optimization_barrier((bundles, (ordered, key_grad, parts[n_t // 2 :])))
    collected = call(
        functools.partial(collect_kernel, chips, base),
        bundles,
        shape(bf16, chips * base + 2 * n_t * count, LANES),
        [pltpu.VMEM((chips, n_t * count, LANES), f32)],
    )
    scratch = [pltpu.VMEM((n_t, count, LANES), f32)]
    own_halves = call(
        functools.partial(own_kernel, n_t, chips, frames),
        [hot, collected, ordered],
        [shape(f32, HD, width), shape(f32, levels, chips * width)],
        scratch,
        flops=2 * n_t * rows * width * HD,
    )
    weight_grad, gate_grad = call(
        functools.partial(final_kernel, n_t, chips, frames),
        [hot, over_cores(collected), *own_halves, ordered],
        [shape(f32, HD, 2 * width), shape(f32, levels, n_s * width)],
        scratch,
        flops=2 * n_t * rows * width * HD,
    )
    parts[0], _ = lax.optimization_barrier((parts[0], gate_grad))
    query_grad = call(functools.partial(query_kernel, n_t), parts, shape(bf16, rows, HD))
    if width != shard:
        weight_grad = without_padding(weight_grad, 2, shard)
        gate_grad = without_padding(gate_grad, n_s, shard)
    return (query_grad, key_grad, value_grad, weight_grad, gate_grad)


def solution(mesh):
    return jax.shard_map(
        body,
        mesh=mesh,
        in_specs=(
            P("tm", "space"),
            P("tm", "space"),
            P("tm", "space"),
            P("tm", "space"),
            P("tm", "space"),
            P("space", None),
            P(),
            P(),
            P(),
        ),
        out_specs=(P("tm", "space"), P("tm", "space"), P("tm", "space"), P("space", "tm"), P()),
        check_vma=False,
    )
```
